32 devices in a mesh: tm: 4 (over y, core), height: 4 (over z), dp: 2 (over x).
Axes of the slice: x: 2, y: 2, z: 4, core: 2. Of those that a mesh axis runs over, the one named last changes fastest.
Arguments:
- queries: bfloat16 [4, 4, 4, 1, 192, 128], P('tm', 'height', 'dp'), may hold values from -4.5 to 4.5
- keys: bfloat16 [4, 4, 4, 1, 192, 128], P('tm', 'height', 'dp'), may hold values from -4.5 to 4.5
- values: bfloat16 [4, 4, 4, 1, 192, 128], P('tm', 'height', 'dp'), may hold values from -6 to 6
- grad_out: bfloat16 [4, 4, 4, 1, 192, 128], P('tm', 'height', 'dp'), may hold values from -24 to 24
- attn_out: bfloat16 [4, 4, 4, 1, 192, 128], P('tm', 'height', 'dp'), may hold values from -1.796875 to 1.796875
- window_mask: int32 [4, 4, 1, 27], P('tm', 'height'), may hold values 0 or 1
Outputs:
- grad_queries: bfloat16 [4, 4, 4, 1, 192, 128], P('tm', 'height', 'dp')
- grad_keys: bfloat16 [4, 4, 4, 1, 192, 128], P('tm', 'height', 'dp')
- grad_values: bfloat16 [4, 4, 4, 1, 192, 128], P('tm', 'height', 'dp')
The draws below stay inside these ranges and needn't reach their ends.
All inputs are finite; a program needn't handle non-finite values. No bound on the sum of `window_mask` on one device may be relied on, other than what follows from the above.
Results may differ from the reference program's by a relative error of at most 0.009.
Values may be sent and summed in bfloat16 or wider, within the bound.
No kernel may reach another device: no remote copies, remote signals or barrier semaphores. Data moves between devices by JAX's collectives and lax.ppermute only.
A program may use at most 64 MiB of HBM per device.

```python
import jax
import jax.numpy as jnp
from jax import lax

DH = 128
TOK = 192
WINDOW = 27
WT = 1
HEADS = 4
VIDEO_T = 4
VIDEO_H = 4
TILES_T = 4
TILES_H = 4


def paired_draw(key):
    full_shape = (TILES_T, TILES_H, HEADS, WT, TOK, DH)
    base_key = jax.random.fold_in(key, 29)
    query_key, key_key = jax.random.split(base_key, 2)
    query_vals = jnp.clip(jax.random.normal(query_key, full_shape, jnp.float32), -4.5, 4.5)
    key_vals = jnp.clip(jax.random.normal(key_key, full_shape, jnp.float32), -4.5, 4.5)
    return (query_vals, key_vals)


def draw_queries(key, part):
    return paired_draw(key)[0].astype(jnp.bfloat16)


def draw_keys(key, part):
    return paired_draw(key)[1].astype(jnp.bfloat16)


def touch_ends(array, stream_key, least, largest):
    place = [jax.random.randint(jax.random.fold_in(stream_key, axis), (), 0, length) for axis, length in enumerate(array.shape)]
    widest = array.shape.index(max(array.shape))
    neighbour = place[:widest] + [(place[widest] + 1) % array.shape[widest]] + place[widest + 1:]
    return array.at[tuple(place)].set(least).at[tuple(neighbour)].set(largest)


def shard_levels(key, dims, shards, least, largest):
    def one(dim, blocks):
        heights = jax.random.uniform(jax.random.fold_in(jax.random.fold_in(key, 6), dim), (blocks,), jnp.float32, least / len(shards), largest / len(shards))
        return jnp.repeat(jnp.exp(heights), dims[dim] // blocks).reshape((-1,) + (1,) * (len(dims) - dim - 1))

    factor_of = one(*shards[0])
    for cut in shards[1:]:
        factor_of = factor_of * one(*cut)
    return factor_of


def bell_draw(rng, shape, scale, most, cuts=(), kind=jnp.bfloat16):
    result = jax.random.normal(rng, shape, jnp.float32) * scale
    if len(cuts) > 0:
        result = shard_levels(rng, shape, cuts, -0.22, 0.18) * result
    return jnp.clip(result, min=-most, max=most).astype(kind)


def setup_inputs(seed: int = 0) -> dict:
    seeds = jax.random.split(jax.random.key(seed), 7)
    return {
        "queries": draw_queries(jax.random.fold_in(seeds[6], 71), 0),
        "keys": draw_keys(jax.random.fold_in(seeds[6], 71), 0),
        "values": bell_draw(seeds[2], (TILES_T, TILES_H, HEADS, WT, TOK, DH), 1.0, 6.0, ((0, 4), (1, 4), (2, 2))),
        "grad_out": bell_draw(seeds[3], (TILES_T, TILES_H, HEADS, WT, TOK, DH), 4.0, 24.0, ((0, 4), (1, 4), (2, 2))),
        "attn_out": bell_draw(seeds[4], (TILES_T, TILES_H, HEADS, WT, TOK, DH), 0.3, 1.796875, ((0, 4), (1, 4), (2, 2))),
        "window_mask": touch_ends((jax.random.randint(seeds[5], (TILES_T, TILES_H, WT, WINDOW), 0, 3) < 1).astype(jnp.int32), jax.random.fold_in(seeds[5], 1), 0, 1),
    }


def round_low(values_f32):
    return lax.optimization_barrier(values_f32.astype(jnp.bfloat16)).astype(jnp.float32)


def same_video(count, block, step):
    index_all = jnp.arange(count, dtype=jnp.int32)
    source = index_all + (step - 1)
    return (source >= 0) & (source < count) & (jnp.floor_divide(source, block) == jnp.floor_divide(index_all, block))


def reference(queries, keys, values, grad_out, attn_out, window_mask):
    score_scale = DH ** -0.5
    offsets = [(step_time, step_height, step_width) for step_time in range(3) for step_height in range(3) for step_width in range(3) if WT > 1 or step_width == 1]
    allowed = {}
    for step_time, step_height, step_width in offsets:
        window_slot = 9 * step_time + 3 * step_height + step_width
        picked = window_mask[:, :, :, window_slot] != 0
        if window_slot == 13:
            picked = jnp.ones_like(picked)
        time_ok = same_video(TILES_T, VIDEO_T, step_time)
        height_ok = same_video(TILES_H, VIDEO_H, step_height)
        width_ok = same_video(WT, WT, step_width)
        within = time_ok[:, None, None] & height_ok[None, :, None] & width_ok[None, None, :]
        allowed[(step_time, step_height, step_width)] = picked & within

    def one_head(packed):
        query_f32, key_f32, value_f32, grad_f32, output_f32 = [part.astype(jnp.float32) for part in packed]
        pad_five = ((1, 1), (1, 1), (1, 1), (0, 0), (0, 0))
        key_pad = jnp.pad(key_f32, pad_five)
        value_pad = jnp.pad(value_f32, pad_five)

        def nearby(source, step_time, step_height, step_width):
            return source[step_time:step_time + TILES_T, step_height:step_height + TILES_H, step_width:step_width + WT]

        def scores_at(offset):
            return jnp.einsum("thwqd,thwkd->thwqk", query_f32, nearby(key_pad, *offset)) * score_scale

        running_top = jnp.full(query_f32.shape[:-1], -1e30, jnp.float32)
        running_total = jnp.zeros(query_f32.shape[:-1], jnp.float32)
        for offset in offsets:
            scores = jnp.where(allowed[offset][..., None, None], scores_at(offset), -1e30)
            new_top = jnp.maximum(running_top, scores.max(-1))
            running_total = running_total * jnp.exp(running_top - new_top) + jnp.exp(scores - new_top[..., None]).sum(-1)
            running_top = new_top
        log_total = running_top + jnp.log(running_total)
        delta_rows = jnp.sum(grad_f32 * output_f32, axis=-1)
        row_grads = jnp.zeros(query_f32.shape, jnp.float32)
        columns = {}
        for offset in offsets:
            step_time, step_height, step_width = offset
            prob_weights = jnp.where(allowed[offset][..., None, None], jnp.exp(scores_at(offset) - log_total[..., None]), 0.0)
            probs_low = round_low(prob_weights)
            prob_grads = jnp.einsum("thwqd,thwkd->thwqk", grad_f32, nearby(value_pad, *offset))
            score_grads = round_low(prob_weights * (prob_grads - delta_rows[..., None]) * score_scale)
            row_grads = row_grads + jnp.einsum("thwqk,thwkd->thwqd", score_grads, nearby(key_pad, *offset))
            key_part = jnp.einsum("thwqk,thwqd->thwkd", score_grads, query_f32)
            value_part = jnp.einsum("thwqk,thwqd->thwkd", probs_low, grad_f32)
            both_parts = jnp.stack([key_part, value_part])
            shifted = jnp.pad(both_parts, ((0, 0), (step_time, 2 - step_time), (step_height, 2 - step_height), (step_width, 2 - step_width), (0, 0), (0, 0)))
            shifted = shifted[:, 1:TILES_T + 1, 1:TILES_H + 1, 1:WT + 1]
            column_key = (step_time, step_height)
            if column_key in columns:
                columns[column_key] = columns[column_key] + shifted
            else:
                columns[column_key] = shifted
        summed = jnp.zeros((2,) + query_f32.shape, jnp.float32)
        for column_key in columns:
            summed = summed + round_low(columns[column_key])
        return row_grads.astype(jnp.bfloat16), summed[0].astype(jnp.bfloat16), summed[1].astype(jnp.bfloat16)

    packed = tuple(jnp.moveaxis(source, 2, 0) for source in (queries, keys, values, grad_out, attn_out))
    grad_q, grad_k, grad_v = lax.map(one_head, packed)
    return jnp.moveaxis(grad_q, 0, 2), jnp.moveaxis(grad_k, 0, 2), jnp.moveaxis(grad_v, 0, 2)
```

```python
import functools

import jax
import jax.numpy as jnp
from jax import lax
from jax.experimental import pallas as pl
from jax.experimental.pallas import tpu as pltpu
from jax.sharding import PartitionSpec as P

VMEM = pl.BlockSpec(memory_space=pltpu.VMEM)
SMEM = pl.BlockSpec(memory_space=pltpu.SMEM)
LIMIT = pltpu.CompilerParams(vmem_limit_bytes=32 * 1024 * 1024)
ROWS_T = (((1,), (1,)), ((), ()))
COLS_T = (((0,), (0,)), ((), ()))


def dot(a, b, dims=(((1,), (0,)), ((), ()))):
    return lax.dot_general(a, b, dims, preferred_element_type=jnp.float32)


def place():
    t = lax.axis_index("tm")
    return t // 2, t % 2, lax.axis_index("height")


def flag(mask_ref, dt, dh):
    return (mask_ref[0, 0, 0, 9 * dt + 3 * dh + 1] != 0).astype(jnp.float32)


def pack_kernel(tok, k_ref, v_ref, q_ref, g_ref, o_ref, mask_ref, other_ref, cross_ref, along_ref):
    _, c, _ = place()
    for i, ref in enumerate((k_ref, v_ref, q_ref, g_ref, o_ref)):
        block = ref[0, 0, 1 - c, 0]
        other_ref[pl.ds(i * tok, tok), :] = block
        if i < 2:
            cross_ref[pl.ds(i * tok, tok), :] = block
            along_ref[pl.ds(i * tok, tok), :] = ref[0, 0, c, 0]
    row = lax.broadcasted_iota(jnp.int32, (16, other_ref.shape[1]), 0)
    flags = jnp.zeros(row.shape, jnp.float32)
    for dt in range(3):
        for dh in range(3):
            flags = jnp.where(row == 3 * dt + dh, flag(mask_ref, dt, dh), flags)
    other_ref[pl.ds(5 * tok, 16), :] = flags.astype(jnp.bfloat16)


def line_kernel(tok, chips, own_ref, par_ref, cross_ref, along_ref, line_ref):
    y, c, _ = place()
    for i in range(2):
        rows = pl.ds(i * tok, tok)
        line_ref[i, pl.ds(pl.multiple_of(c * tok, tok), tok), :] = own_ref[rows, :]
        line_ref[i, pl.ds(pl.multiple_of((1 - c) * tok, tok), tok), :] = par_ref[rows, :]
        if chips == 2:
            line_ref[i, pl.ds(2 * tok, tok), :] = jnp.where(
                c != y, cross_ref[rows, :], along_ref[rows, :]
            )
        else:
            line_ref[i, pl.ds(pl.multiple_of((2 + c) * tok, tok), tok), :] = cross_ref[rows, :]
            line_ref[i, pl.ds(pl.multiple_of((3 - c) * tok, tok), tok), :] = along_ref[rows, :]


def main_kernel(
    tok, chips, heights, scale,
    q_ref, g_ref, o_ref, mask_ref, par_ref, here_ref, before_ref, after_ref,
    down_ref, own_ref, up_ref, dq_ref,
    qs, gs, s_ref,
):
    y, c, z = place()
    two = 2 * tok
    slots = here_ref.shape[1] // tok
    mine = pl.ds(pl.multiple_of(c * tok, tok), tok)
    other = pl.ds(pl.multiple_of((1 - c) * tok, tok), tok)
    qs[mine, :] = q_ref[0, 0, c, 0]
    qs[other, :] = par_ref[pl.ds(2 * tok, tok), :]
    gs[mine, :] = g_ref[0, 0, c, 0]
    gs[other, :] = par_ref[pl.ds(3 * tok, tok), :]
    f32 = jnp.float32
    product_own = g_ref[0, 0, c, 0].astype(f32) * o_ref[0, 0, c, 0].astype(f32)
    product_par = par_ref[pl.ds(3 * tok, tok), :].astype(f32) * par_ref[pl.ds(4 * tok, tok), :].astype(f32)
    first = c == 0
    product = jnp.concatenate(
        [jnp.where(first, product_own, product_par), jnp.where(first, product_par, product_own)], axis=0
    )
    delta = jnp.sum(product.T, axis=0, keepdims=True)

    width = par_ref.shape[1]
    lane = lax.broadcasted_iota(jnp.int32, (1, width), 1)
    even, odd = {}, {}
    for dt in range(3):
        for dh in range(3):
            i = 3 * dt + dh
            if i == 4:
                even[i] = odd[i] = jnp.ones((1, width), f32)
                continue
            own = jnp.full((1, width), flag(mask_ref, dt, dh), f32)
            par = par_ref[pl.ds(5 * tok, 16), :].astype(f32)[i : i + 1]
            even[i], odd[i] = jnp.where(first, own, par), jnp.where(first, par, own)
    has_below = (y > 0).astype(f32)
    has_above = (y < chips - 1).astype(f32)
    none = jnp.zeros((1, width), f32)

    def bias(slot, dh):
        e, o = [
            lambda: (even[3 + dh], odd[dh]),
            lambda: (even[6 + dh], odd[3 + dh]),
            lambda: (even[dh] * has_below, odd[6 + dh] * has_above if chips == 2 else none),
            lambda: (none, odd[6 + dh] * has_above),
        ][slot]()
        row = spread(e, o)
        inside = ((z + dh - 1 >= 0) & (z + dh - 1 < heights)).astype(f32)
        return (row * inside - 1.0) * 1e30

    def spread(e, o):
        parts = []
        for start in range(0, two, width):
            parts.append(jnp.where(lane + start < tok, e, o))
        return jnp.concatenate(parts, axis=1)

    sources = (before_ref, here_ref, after_ref)
    blocks = [(dh, slot) for dh in (1, 0, 2) for slot in range(slots)]

    def rows_of(dh, slot):
        return pl.ds((dh * slots + slot) * tok, tok)

    top = jnp.full((8, two), -1e30, f32)
    for dh, slot in blocks:
        keys = sources[dh][0, pl.ds(slot * tok, tok), :]
        scores = dot(keys, qs[...], ROWS_T) * scale + bias(slot, dh)
        s_ref[rows_of(dh, slot), :] = scores
        top = jnp.maximum(top, jnp.max(scores.reshape(tok // 8, 8, two), axis=0))
    top = jnp.max(top, axis=0, keepdims=True)
    total = jnp.zeros((8, two), f32)
    for dh, slot in blocks:
        weights = jnp.exp(s_ref[rows_of(dh, slot), :] - top)
        s_ref[rows_of(dh, slot), :] = weights
        total = total + jnp.sum(weights.reshape(tok // 8, 8, two), axis=0)
    share = 1.0 / jnp.sum(total, axis=0, keepdims=True)

    dq = jnp.zeros((two, width), f32)
    results = (down_ref, own_ref, up_ref)
    for dh, slot in [(dh, slot) for dh in (0, 2, 1) for slot in range(slots)]:
        rows = pl.ds(slot * tok, tok)
        keys = sources[dh][0, rows, :]
        probs = s_ref[rows_of(dh, slot), :] * share
        grads = dot(sources[dh][1, rows, :], gs[...], ROWS_T)
        low = (probs * (grads - delta)).astype(jnp.bfloat16)
        results[dh][0, rows, :] = (dot(low, qs[...]) * scale).astype(jnp.bfloat16)
        results[dh][1, rows, :] = dot(probs.astype(jnp.bfloat16), gs[...]).astype(jnp.bfloat16)
        dq = dq + dot(low, keys, COLS_T)
    dq_ref[...] = (dq * scale).astype(jnp.bfloat16)


def sum_kernel(tok, own_ref, below_ref, above_ref, dq_ref, mine_ref, swap_ref, *halo_refs):
    _, c, _ = place()
    f32 = jnp.float32

    def total(i, start):
        rows = pl.ds(pl.multiple_of(start, tok), tok)
        return own_ref[i, rows, :].astype(f32) + below_ref[i, rows, :].astype(f32) + above_ref[i, rows, :].astype(f32)

    for i in range(2):
        mine_ref[i] = total(i, c * tok)
        swap_ref[i] = total(i, (1 - c) * tok).astype(jnp.bfloat16)
        if len(halo_refs) == 1:
            halo_refs[0][i] = total(i, 2 * tok).astype(jnp.bfloat16)
        else:
            halo_refs[0][i] = total(i, (2 + c) * tok).astype(jnp.bfloat16)
            halo_refs[1][i] = total(i, (3 - c) * tok).astype(jnp.bfloat16)
    swap_ref[2] = dq_ref[pl.ds(pl.multiple_of((1 - c) * tok, tok), tok), :]


def final_kernel(tok, mine_ref, swap_ref, cross_ref, along_ref, dq_ref, gq_ref, gk_ref, gv_ref):
    _, c, _ = place()
    f32 = jnp.float32
    gq_ref[0, 0, c, 0] = dq_ref[pl.ds(pl.multiple_of(c * tok, tok), tok), :]
    gq_ref[0, 0, 1 - c, 0] = swap_ref[2]
    for i, ref in enumerate((gk_ref, gv_ref)):
        ref[0, 0, c, 0] = (mine_ref[i] + along_ref[i].astype(f32)).astype(jnp.bfloat16)
        ref[0, 0, 1 - c, 0] = (swap_ref[i].astype(f32) + cross_ref[i].astype(f32)).astype(jnp.bfloat16)


def body(queries, keys, values, grad_out, attn_out, window_mask):
    tok, width = queries.shape[-2:]
    scale = width ** -0.5
    times, heights = lax.axis_size("tm"), lax.axis_size("height")
    chips = times // 2
    slots = 3 if chips == 2 else 4
    bf16, f32 = jnp.bfloat16, jnp.float32

    def call(kernel, shapes, specs, scratch=(), **kwargs):
        return pl.pallas_call(
            kernel,
            out_shape=[jax.ShapeDtypeStruct(*shape) for shape in shapes],
            in_specs=list(specs),
            out_specs=[VMEM] * len(shapes),
            scratch_shapes=list(scratch),
            compiler_params=LIMIT,
            **kwargs,
        )

    swap = [(t, t ^ 1) for t in range(times)]
    steps = {d: [(t, t + d if t % 2 else t - d) for t in range(times)] for d in (1, 2)}
    cross, along = ([(i, j) for i, j in steps[d] if 0 <= j < times] for d in (1, 2))
    up = [(i, i + 1) for i in range(heights - 1)]
    down = [(j, i) for i, j in up]

    def back(pairs):
        return [(j, i) for i, j in pairs]

    other, near, far = call(
        functools.partial(pack_kernel, tok),
        [((5 * tok + 16, width), bf16), ((2 * tok, width), bf16), ((2 * tok, width), bf16)],
        [VMEM] * 5 + [SMEM],
    )(keys, values, queries, grad_out, attn_out, window_mask)
    near_in = lax.ppermute(near, "tm", cross)
    far_in = lax.ppermute(far, "tm", along)
    par = lax.ppermute(other, "tm", swap)
    (line,) = call(
        functools.partial(line_kernel, tok, chips), [((2, slots * tok, width), bf16)], [VMEM] * 4
    )(far, par, near_in, far_in)
    before = lax.ppermute(line, "height", up)
    after = lax.ppermute(line, "height", down)
    part = ((2, slots * tok, width), bf16)
    to_before, own, to_after, dq = call(
        functools.partial(main_kernel, tok, chips, heights, scale),
        [part, part, part, ((2 * tok, width), bf16)],
        [VMEM] * 3 + [SMEM] + [VMEM] * 4,
        [
            pltpu.VMEM((2 * tok, width), bf16),
            pltpu.VMEM((2 * tok, width), bf16),
            pltpu.VMEM((3 * slots * tok, 2 * tok), f32),
        ],
    )(queries, grad_out, attn_out, window_mask, par, line, before, after)
    from_below = lax.ppermute(to_after, "height", up)
    from_above = lax.ppermute(to_before, "height", down)
    tile = (2, tok, width)
    mine, packed, *halos = call(
        functools.partial(sum_kernel, tok),
        [(tile, f32), ((3, tok, width), bf16)] + [(tile, bf16)] * (slots - 2),
        [VMEM] * 4,
    )(own, from_below, from_above, dq)
    near_back = lax.ppermute(halos[0], "tm", back(cross))
    far_back = lax.ppermute(halos[-1], "tm", back(along))
    swapped = lax.ppermute(packed, "tm", swap)
    return call(
        functools.partial(final_kernel, tok),
        [(queries.shape, bf16)] * 3,
        [VMEM] * 5,
    )(mine, swapped, near_back, far_back, dq)


def solution(mesh):
    placed = P("tm", "height", "dp", None, None, None)
    return jax.shard_map(
        body,
        mesh=mesh,
        in_specs=(placed,) * 5 + (P("tm", "height", None, None),),
        out_specs=(placed,) * 3,
        check_vma=False,
    )
```

```python
import functools

import jax
import jax.numpy as jnp
from jax import lax
from jax.experimental import pallas as pl
from jax.experimental.pallas import tpu as pltpu
from jax.sharding import PartitionSpec as P

VMEM = pl.BlockSpec(memory_space=pltpu.VMEM)
HBM = pl.BlockSpec(memory_space=pltpu.HBM)
LIMIT = pltpu.CompilerParams(vmem_limit_bytes=32 * 1024 * 1024)
ROWS_T = (((1,), (1,)), ((), ()))
COLS_T = (((0,), (0,)), ((), ()))


def dot(a, b, dims=(((1,), (0,)), ((), ()))):
    return lax.dot_general(a, b, dims, preferred_element_type=jnp.float32)


def place():
    t = lax.axis_index("tm")
    return t // 2, t % 2, lax.axis_index("height")


def pair(index, which):
    rising = (index % 2) == (0 if which == 0 else 1)
    return rising, jnp.where(rising, index + 1, index - 1)


def within(index, size):
    return (index >= 0) & (index < size)


def tile_rows(index, tok):
    return pl.ds(pl.multiple_of(index * tok, tok), tok)


def pack_kernel(tok, k_ref, v_ref, q_ref, g_ref, o_ref, mask_ref, own_ref, other_ref, flags, sems):
    _, c, _ = place()
    copies = [pltpu.make_async_copy(mask_ref, flags, sems.at[10])]
    for i, ref in enumerate((k_ref, v_ref, q_ref, g_ref, o_ref)):
        rows = pl.ds(i * tok, tok)
        copies.append(pltpu.make_async_copy(ref.at[0, 0, 1 - c, 0], other_ref.at[rows, :], sems.at[2 * i]))
        copies.append(pltpu.make_async_copy(ref.at[0, 0, c, 0], own_ref.at[rows, :], sems.at[2 * i + 1]))
    for copy in copies:
        copy.start()
    copies[0].wait()
    row = lax.broadcasted_iota(jnp.int32, (16, own_ref.shape[1]), 0)
    spread = jnp.zeros(row.shape, jnp.float32)
    for i in range(9):
        on = (flags[0, 0, 0, 9 * (i // 3) + 3 * (i % 3) + 1] != 0).astype(jnp.float32)
        spread = jnp.where(row == i, on, spread)
    own_ref[pl.ds(5 * tok, 16), :] = spread.astype(jnp.bfloat16)
    other_ref[pl.ds(5 * tok, 16), :] = spread.astype(jnp.bfloat16)
    for copy in copies[1:]:
        copy.wait()


def line_kernel(tok, own_ref, par_ref, line_ref, *border_refs):
    y, c, _ = place()
    for i in range(2):
        rows = pl.ds(i * tok, tok)
        line_ref[i, tile_rows(c, tok), :] = own_ref[rows, :]
        line_ref[i, tile_rows(1 - c, tok), :] = par_ref[rows, :]
        for which, ref in enumerate(border_refs):
            rising, _ = pair(y, which)
            ref[i] = jnp.where((c == 1) == rising, own_ref[rows, :], par_ref[rows, :])


def main_kernel(tok, chips, heights, sides, scale, *refs):
    own_ref, par_ref = refs[:2]
    count = 3 * (1 + sides)
    sources, results = refs[2 : 2 + count], refs[2 + count : 2 + 2 * count]
    dq_ref, qs, gs, s_ref = refs[2 + 2 * count :]
    y, c, z = place()
    two = 2 * tok
    width = own_ref.shape[1]
    f32, bf16 = jnp.float32, jnp.bfloat16
    first = c == 0

    def by_tile(part):
        own, par = own_ref[pl.ds(part * tok, tok), :], par_ref[pl.ds(part * tok, tok), :]
        return own, par

    for part, ref in ((2, qs), (3, gs)):
        own, par = by_tile(part)
        ref[tile_rows(c, tok), :] = own
        ref[tile_rows(1 - c, tok), :] = par
    (g_own, g_par), (o_own, o_par) = by_tile(3), by_tile(4)
    p_own, p_par = g_own.astype(f32) * o_own.astype(f32), g_par.astype(f32) * o_par.astype(f32)
    product = jnp.concatenate([jnp.where(first, p_own, p_par), jnp.where(first, p_par, p_own)], axis=0)
    delta = jnp.sum(product.T, axis=0, keepdims=True)

    lane = lax.broadcasted_iota(jnp.int32, (1, width), 1)
    own_flags = own_ref[pl.ds(5 * tok, 16), :].astype(f32)
    par_flags = par_ref[pl.ds(5 * tok, 16), :].astype(f32)
    flags = jnp.where(first, own_flags, par_flags), jnp.where(first, par_flags, own_flags)
    none = jnp.zeros((1, width), f32)

    def bias(line, slot):
        inside = True
        if line:
            z_rising, z_at = pair(z, line - 1)
            inside = within(z_at, heights)

        def at(tile, dt):
            row = flags[tile]
            if line == 0:
                return row[3 * dt + 1 : 3 * dt + 2] if dt != 1 else none + 1.0
            return jnp.where(z_rising, row[3 * dt + 2 : 3 * dt + 3], row[3 * dt : 3 * dt + 1])

        if slot == 0:
            even, odd = at(0, 1), at(1, 0)
        elif slot == 1:
            even, odd = at(0, 2), at(1, 1)
        else:
            y_rising, y_at = pair(y, slot - 2)
            inside = within(y_at, chips) & inside
            even, odd = jnp.where(y_rising, none, at(0, 0)), jnp.where(y_rising, at(1, 2), none)
        row = jnp.concatenate([jnp.where(lane + start < tok, even, odd) for start in range(0, two, width)], axis=1)
        return jnp.where(inside, (row - 1.0) * 1e30, -1e30)

    blocks = []
    for line in range(3):
        for slot in range(2 + sides):
            at = line * (1 + sides) + max(slot - 1, 0)
            blocks.append((line, slot, at, pl.ds(tok if slot == 1 else 0, tok), pl.ds(len(blocks) * tok, tok)))

    top = jnp.full((8, two), -1e30, f32)
    for line, slot, at, rows, kept in blocks:
        scores = dot(sources[at][0, rows, :], qs[...], ROWS_T) * scale + bias(line, slot)
        s_ref[kept, :] = scores
        top = jnp.maximum(top, jnp.max(scores.reshape(tok // 8, 8, two), axis=0))
    top = jnp.max(top, axis=0, keepdims=True)
    total = jnp.zeros((8, two), f32)
    for _, _, _, _, kept in blocks:
        weights = jnp.exp(s_ref[kept, :] - top)
        s_ref[kept, :] = weights
        total = total + jnp.sum(weights.reshape(tok // 8, 8, two), axis=0)
    share = 1.0 / jnp.sum(total, axis=0, keepdims=True)

    dq = jnp.zeros((two, width), f32)
    for _, _, at, rows, kept in blocks:
        probs = s_ref[kept, :] * share
        grads = dot(sources[at][1, rows, :], gs[...], ROWS_T)
        low = (probs * (grads - delta) * scale).astype(bf16)
        results[at][0, rows, :] = dot(low, qs[...]).astype(bf16)
        results[at][1, rows, :] = dot(probs.astype(bf16), gs[...]).astype(bf16)
        dq = dq + dot(low, sources[at][0, rows, :], COLS_T)
    dq_ref[...] = dq.astype(bf16)


def sum_kernel(tok, chips, heights, sides, *refs):
    count = 3 * (1 + sides)
    parts, (dq_ref, mine_ref, swap_ref) = refs[:count], refs[count:]
    y, c, z = place()

    def total(i, tile):
        value = jnp.zeros(mine_ref.shape[1:], jnp.float32)
        for line in range(3):
            inside = True
            if line:
                _, z_at = pair(z, line - 1)
                inside = within(z_at, heights)
            block = parts[line * (1 + sides)][i, tile_rows(tile, tok), :].astype(jnp.float32)
            value = value + (jnp.where(inside, block, 0.0) if line else block)
            for which in range(sides):
                y_rising, y_at = pair(y, which)
                halo = parts[line * (1 + sides) + 1 + which][i].astype(jnp.float32)
                value = value + jnp.where(((tile == 1) == y_rising) & within(y_at, chips) & inside, halo, 0.0)
        return value

    for i in range(2):
        mine_ref[i] = total(i, c)
        swap_ref[i] = total(i, 1 - c).astype(jnp.bfloat16)
    swap_ref[2] = dq_ref[tile_rows(1 - c, tok), :]


def final_kernel(tok, mine_ref, swap_ref, dq_ref, gq_ref, gk_ref, gv_ref):
    _, c, _ = place()
    gq_ref[0, 0, c, 0] = dq_ref[tile_rows(c, tok), :]
    gq_ref[0, 0, 1 - c, 0] = swap_ref[2]
    for i, ref in enumerate((gk_ref, gv_ref)):
        ref[0, 0, c, 0] = mine_ref[i].astype(jnp.bfloat16)
        ref[0, 0, 1 - c, 0] = swap_ref[i]


def body(queries, keys, values, grad_out, attn_out, window_mask):
    tok, width = queries.shape[-2:]
    scale = width ** -0.5
    times, heights = lax.axis_size("tm"), lax.axis_size("height")
    chips = times // 2
    sides = 1 if chips == 2 else 2
    bf16, f32 = jnp.bfloat16, jnp.float32

    def call(kernel, shapes, specs, scratch=()):
        return pl.pallas_call(
            kernel,
            out_shape=[jax.ShapeDtypeStruct(*shape) for shape in shapes],
            in_specs=list(specs),
            out_specs=[VMEM] * len(shapes),
            scratch_shapes=list(scratch),
            compiler_params=LIMIT,
        )

    def partner(index, which, size):
        if which is None:
            return index
        at = index + 1 if index % 2 == which else index - 1
        return at if 0 <= at < size else None

    def exchange(block, y_which, z_which):
        pairs = []
        for t in range(times):
            for z in range(heights):
                y_at, z_at = partner(t // 2, y_which, chips), partner(z, z_which, heights)
                at = t * heights + z
                pairs.append((at, at if y_at is None or z_at is None else (2 * y_at + t % 2) * heights + z_at))
        return lax.ppermute(block, ("tm", "height"), pairs)

    def swap_cores(block):
        return lax.ppermute(block, "tm", [(t, t ^ 1) for t in range(times)])

    def exchange_all(lines, halos):
        found = {(j, 0): exchange(lines[j], None, j - 1) for j in (1, 2)}
        for j in range(3):
            for which in range(sides):
                found[j, 1 + which] = exchange(halos[j][which], which, None if j == 0 else j - 1)
        return found

    packed = ((5 * tok + 16, width), bf16)
    own, other = call(
        functools.partial(pack_kernel, tok),
        [packed, packed],
        [HBM] * 6,
        [pltpu.SMEM(window_mask.shape, jnp.int32), pltpu.SemaphoreType.DMA((11,))],
    )(*(pltpu.with_memory_space_constraint(x, pltpu.HBM) for x in (keys, values, queries, grad_out, attn_out, window_mask)))
    par = swap_cores(other)
    line_shape, tile_shape = ((2, 2 * tok, width), bf16), ((2, tok, width), bf16)
    line, *borders = call(
        functools.partial(line_kernel, tok), [line_shape] + [tile_shape] * sides, [VMEM] * 2
    )(own, par)
    found = exchange_all([None, line, line], [borders] * 3)
    found[0, 0] = line
    order = [(j, k) for j in range(3) for k in range(1 + sides)]
    *columns, dq = call(
        functools.partial(main_kernel, tok, chips, heights, sides, scale),
        [line_shape if k == 0 else tile_shape for _, k in order] + [((2 * tok, width), bf16)],
        [VMEM] * (2 + len(order)),
        [
            pltpu.VMEM((2 * tok, width), bf16),
            pltpu.VMEM((2 * tok, width), bf16),
            pltpu.VMEM((3 * (2 + sides) * tok, 2 * tok), f32),
        ],
    )(own, par, *(found[at] for at in order))
    columns = dict(zip(order, columns))
    back = exchange_all(
        [columns[j, 0] for j in range(3)], [[columns[j, 1 + k] for k in range(sides)] for j in range(3)]
    )
    back[0, 0] = columns[0, 0]
    mine, leaving = call(
        functools.partial(sum_kernel, tok, chips, heights, sides),
        [((2, tok, width), f32), ((3, tok, width), bf16)],
        [VMEM] * (len(order) + 1),
    )(*(back[at] for at in order), dq)
    return call(
        functools.partial(final_kernel, tok),
        [(queries.shape, bf16)] * 3,
        [VMEM] * 3,
    )(mine, swap_cores(leaving), dq)


def solution(mesh):
    placed = P("tm", "height", "dp", None, None, None)
    return jax.shard_map(
        body,
        mesh=mesh,
        in_specs=(placed,) * 5 + (P("tm", "height", None, None),),
        out_specs=(placed,) * 3,
        check_vma=False,
    )
```

```python
import functools

import jax
import jax.numpy as jnp
from jax import lax
from jax.experimental import pallas as pl
from jax.experimental.pallas import tpu as pltpu
from jax.sharding import PartitionSpec as P

VMEM = pl.BlockSpec(memory_space=pltpu.VMEM)
HBM = pl.BlockSpec(memory_space=pltpu.HBM)
LIMIT = pltpu.CompilerParams(vmem_limit_bytes=32 * 1024 * 1024)
ROWS_T = (((1,), (1,)), ((), ()))
COLS_T = (((0,), (0,)), ((), ()))


def dot(a, b, dims=(((1,), (0,)), ((), ()))):
    return lax.dot_general(a, b, dims, preferred_element_type=jnp.float32)


def place():
    t = lax.axis_index("tm")
    return t // 2, t % 2, lax.axis_index("height")


def pair(index, which):
    rising = (index % 2) == (0 if which == 0 else 1)
    return rising, jnp.where(rising, index + 1, index - 1)


def within(index, size):
    return (index >= 0) & (index < size)


def tile_rows(index, tok):
    return pl.ds(pl.multiple_of(index * tok, tok), tok)


def pack_kernel(tok, k_ref, v_ref, q_ref, g_ref, o_ref, mask_ref, own_ref, other_ref, flags, sems):
    _, c, _ = place()
    copies = [pltpu.make_async_copy(mask_ref, flags, sems.at[10])]
    for i, ref in enumerate((k_ref, v_ref, q_ref, g_ref, o_ref)):
        rows = pl.ds(i * tok, tok)
        copies.append(pltpu.make_async_copy(ref.at[0, 0, 1 - c, 0], other_ref.at[rows, :], sems.at[2 * i]))
        copies.append(pltpu.make_async_copy(ref.at[0, 0, c, 0], own_ref.at[rows, :], sems.at[2 * i + 1]))
    for copy in copies:
        copy.start()
    copies[0].wait()
    row = lax.broadcasted_iota(jnp.int32, (16, own_ref.shape[1]), 0)
    spread = jnp.zeros(row.shape, jnp.float32)
    for i in range(9):
        on = (flags[0, 0, 0, 9 * (i // 3) + 3 * (i % 3) + 1] != 0).astype(jnp.float32)
        spread = jnp.where(row == i, on, spread)
    own_ref[pl.ds(5 * tok, 16), :] = spread.astype(jnp.bfloat16)
    other_ref[pl.ds(5 * tok, 16), :] = spread.astype(jnp.bfloat16)
    for copy in copies[1:]:
        copy.wait()


def line_kernel(tok, own_ref, par_ref, line_ref, *border_refs):
    y, c, _ = place()
    for i in range(2):
        rows = pl.ds(i * tok, tok)
        line_ref[i, tile_rows(c, tok), :] = own_ref[rows, :]
        line_ref[i, tile_rows(1 - c, tok), :] = par_ref[rows, :]
        for which, ref in enumerate(border_refs):
            rising, _ = pair(y, which)
            ref[i] = jnp.where((c == 1) == rising, own_ref[rows, :], par_ref[rows, :])


def main_kernel(tok, chips, heights, sides, scale, *refs):
    own_ref, par_ref = refs[:2]
    count = 3 * (1 + sides)
    sources, results = refs[2 : 2 + count], refs[2 + count : 2 + 2 * count]
    dq_ref, qs, gs, s_ref = refs[2 + 2 * count :]
    y, c, z = place()
    two = 2 * tok
    width = own_ref.shape[1]
    f32, bf16 = jnp.float32, jnp.bfloat16
    first = c == 0

    def by_tile(part):
        own, par = own_ref[pl.ds(part * tok, tok), :], par_ref[pl.ds(part * tok, tok), :]
        return own, par

    for part, ref in ((2, qs), (3, gs)):
        own, par = by_tile(part)
        ref[tile_rows(c, tok), :] = own
        ref[tile_rows(1 - c, tok), :] = par
    (g_own, g_par), (o_own, o_par) = by_tile(3), by_tile(4)
    p_own, p_par = g_own.astype(f32) * o_own.astype(f32), g_par.astype(f32) * o_par.astype(f32)
    product = jnp.concatenate([jnp.where(first, p_own, p_par), jnp.where(first, p_par, p_own)], axis=0)
    delta = jnp.sum(product.T, axis=0, keepdims=True)

    lane = lax.broadcasted_iota(jnp.int32, (1, width), 1)
    own_flags = own_ref[pl.ds(5 * tok, 16), :].astype(f32)
    par_flags = par_ref[pl.ds(5 * tok, 16), :].astype(f32)
    flags = jnp.where(first, own_flags, par_flags), jnp.where(first, par_flags, own_flags)
    none = jnp.zeros((1, width), f32)

    def bias(line, slot):
        inside = True
        if line:
            z_rising, z_at = pair(z, line - 1)
            inside = within(z_at, heights)

        def at(tile, dt):
            row = flags[tile]
            if line == 0:
                return row[3 * dt + 1 : 3 * dt + 2] if dt != 1 else none + 1.0
            return jnp.where(z_rising, row[3 * dt + 2 : 3 * dt + 3], row[3 * dt : 3 * dt + 1])

        if slot == 0:
            even, odd = at(0, 1), at(1, 0)
        elif slot == 1:
            even, odd = at(0, 2), at(1, 1)
        else:
            y_rising, y_at = pair(y, slot - 2)
            inside = within(y_at, chips) & inside
            even, odd = jnp.where(y_rising, none, at(0, 0)), jnp.where(y_rising, at(1, 2), none)
        row = jnp.concatenate([jnp.where(lane + start < tok, even, odd) for start in range(0, two, width)], axis=1)
        return jnp.where(inside, (row - 1.0) * 1e30, -1e30)

    blocks = []
    for line in range(3):
        for slot in range(2 + sides):
            at = line * (1 + sides) + max(slot - 1, 0)
            blocks.append((line, slot, at, pl.ds(tok if slot == 1 else 0, tok), pl.ds(len(blocks) * tok, tok)))

    top = jnp.full((8, two), -1e30, f32)
    for line, slot, at, rows, kept in blocks:
        scores = dot(sources[at][0, rows, :], qs[...], ROWS_T) * scale + bias(line, slot)
        s_ref[kept, :] = scores
        top = jnp.maximum(top, jnp.max(scores.reshape(tok // 8, 8, two), axis=0))
    top = jnp.max(top, axis=0, keepdims=True)
    total = jnp.zeros((8, two), f32)
    for _, _, _, _, kept in blocks:
        weights = jnp.exp(s_ref[kept, :] - top)
        s_ref[kept, :] = weights
        total = total + jnp.sum(weights.reshape(tok // 8, 8, two), axis=0)
    share = 1.0 / jnp.sum(total, axis=0, keepdims=True)

    dq = jnp.zeros((two, width), f32)
    for _, _, at, rows, kept in blocks:
        probs = s_ref[kept, :] * share
        grads = dot(sources[at][1, rows, :], gs[...], ROWS_T)
        low = (probs * (grads - delta) * scale).astype(bf16)
        results[at][0, rows, :] = dot(low, qs[...]).astype(bf16)
        results[at][1, rows, :] = dot(probs.astype(bf16), gs[...]).astype(bf16)
        dq = dq + dot(low, sources[at][0, rows, :], COLS_T)
    dq_ref[...] = dq.astype(bf16)


def sum_kernel(tok, chips, heights, sides, *refs):
    count = 3 * (1 + sides)
    parts, (dq_ref, mine_ref, swap_ref) = refs[:count], refs[count:]
    y, c, z = place()

    def total(i, tile):
        value = jnp.zeros(mine_ref.shape[1:], jnp.float32)
        for line in range(3):
            inside = True
            if line:
                _, z_at = pair(z, line - 1)
                inside = within(z_at, heights)
            block = parts[line * (1 + sides)][i, tile_rows(tile, tok), :].astype(jnp.float32)
            value = value + (jnp.where(inside, block, 0.0) if line else block)
            for which in range(sides):
                y_rising, y_at = pair(y, which)
                halo = parts[line * (1 + sides) + 1 + which][i].astype(jnp.float32)
                value = value + jnp.where(((tile == 1) == y_rising) & within(y_at, chips) & inside, halo, 0.0)
        return value

    for i in range(2):
        mine_ref[i] = total(i, c)
        swap_ref[i] = total(i, 1 - c).astype(jnp.bfloat16)
    swap_ref[2] = dq_ref[tile_rows(1 - c, tok), :]


def final_kernel(tok, mine_ref, swap_ref, dq_ref, gq_ref, gk_ref, gv_ref):
    _, c, _ = place()
    gq_ref[0, 0, c, 0] = dq_ref[tile_rows(c, tok), :]
    gq_ref[0, 0, 1 - c, 0] = swap_ref[2]
    for i, ref in enumerate((gk_ref, gv_ref)):
        ref[0, 0, c, 0] = mine_ref[i].astype(jnp.bfloat16)
        ref[0, 0, 1 - c, 0] = swap_ref[i]


def body(queries, keys, values, grad_out, attn_out, window_mask):
    tok, width = queries.shape[-2:]
    scale = width ** -0.5
    times, heights = lax.axis_size("tm"), lax.axis_size("height")
    chips = times // 2
    sides = 1 if chips == 2 else 2
    bf16, f32 = jnp.bfloat16, jnp.float32

    def call(kernel, shapes, specs, scratch=()):
        return pl.pallas_call(
            kernel,
            out_shape=[jax.ShapeDtypeStruct(*shape) for shape in shapes],
            in_specs=list(specs),
            out_specs=[VMEM] * len(shapes),
            scratch_shapes=list(scratch),
            compiler_params=LIMIT,
        )

    def partner(index, which, size):
        if which is None:
            return index
        at = index + 1 if index % 2 == which else index - 1
        return at if 0 <= at < size else None

    def exchange(block, y_which, z_which):
        pairs = []
        for t in range(times):
            for z in range(heights):
                y_at, z_at = partner(t // 2, y_which, chips), partner(z, z_which, heights)
                at = t * heights + z
                alone = y_at is None or z_at is None
                pairs.append((at, (t ^ 1) * heights + z if alone else (2 * y_at + t % 2) * heights + z_at))
        return lax.ppermute(block, ("tm", "height"), pairs)

    def swap_cores(block):
        return lax.ppermute(block, "tm", [(t, t ^ 1) for t in range(times)])

    def exchange_all(lines, halos):
        found = {(j, 0): exchange(lines[j], None, j - 1) for j in (1, 2)}
        for j in range(3):
            for which in range(sides):
                found[j, 1 + which] = exchange(halos[j][which], which, None if j == 0 else j - 1)
        return found

    packed = ((5 * tok + 16, width), bf16)
    arguments = (keys, values, queries, grad_out, attn_out, window_mask)
    own, other = call(
        functools.partial(pack_kernel, tok),
        [packed, packed],
        [HBM] * 6,
        [pltpu.SMEM(window_mask.shape, jnp.int32), pltpu.SemaphoreType.DMA((11,))],
    )(*(pltpu.with_memory_space_constraint(x, pltpu.HBM) for x in arguments))
    par = swap_cores(other)
    line_shape, tile_shape = ((2, 2 * tok, width), bf16), ((2, tok, width), bf16)
    line, *borders = call(
        functools.partial(line_kernel, tok), [line_shape] + [tile_shape] * sides, [VMEM] * 2
    )(own, par)
    found = exchange_all([None, line, line], [borders] * 3)
    found[0, 0] = line
    order = [(j, k) for j in range(3) for k in range(1 + sides)]
    *columns, dq = call(
        functools.partial(main_kernel, tok, chips, heights, sides, scale),
        [line_shape if k == 0 else tile_shape for _, k in order] + [((2 * tok, width), bf16)],
        [VMEM] * (2 + len(order)),
        [
            pltpu.VMEM((2 * tok, width), bf16),
            pltpu.VMEM((2 * tok, width), bf16),
            pltpu.VMEM((3 * (2 + sides) * tok, 2 * tok), f32),
        ],
    )(own, par, *(found[at] for at in order))
    columns = dict(zip(order, columns))
    back = exchange_all(
        [columns[j, 0] for j in range(3)], [[columns[j, 1 + k] for k in range(sides)] for j in range(3)]
    )
    back[0, 0] = columns[0, 0]
    mine, leaving = call(
        functools.partial(sum_kernel, tok, chips, heights, sides),
        [((2, tok, width), f32), ((3, tok, width), bf16)],
        [VMEM] * (len(order) + 1),
    )(*(back[at] for at in order), dq)
    return call(
        functools.partial(final_kernel, tok),
        [(queries.shape, bf16)] * 3,
        [VMEM] * 3,
    )(mine, swap_cores(leaving), dq)


def solution(mesh):
    placed = P("tm", "height", "dp", None, None, None)
    return jax.shard_map(
        body,
        mesh=mesh,
        in_specs=(placed,) * 5 + (P("tm", "height", None, None),),
        out_specs=(placed,) * 3,
        check_vma=False,
    )
```

```python
import functools

import jax
import jax.numpy as jnp
from jax import lax
from jax.experimental import pallas as pl
from jax.experimental.pallas import tpu as pltpu
from jax.sharding import PartitionSpec as P

VMEM = pl.BlockSpec(memory_space=pltpu.VMEM)
HBM = pl.BlockSpec(memory_space=pltpu.HBM)
LIMIT = pltpu.CompilerParams(vmem_limit_bytes=32 * 1024 * 1024)
ROWS_T = (((1,), (1,)), ((), ()))
COLS_T = (((0,), (0,)), ((), ()))


def dot(a, b, dims=(((1,), (0,)), ((), ()))):
    return lax.dot_general(a, b, dims, preferred_element_type=jnp.float32)


def place():
    t = lax.axis_index("tm")
    return t // 2, t % 2, lax.axis_index("height")


def pair(index, which):
    rising = (index % 2) == (0 if which == 0 else 1)
    return rising, jnp.where(rising, index + 1, index - 1)


def within(index, size):
    return (index >= 0) & (index < size)


def pack_kernel(tok, k_ref, v_ref, q_ref, g_ref, o_ref, mask_ref, kv_ref, rest_ref, other_ref, flags, sems):
    _, c, _ = place()
    copies = [pltpu.make_async_copy(mask_ref, flags, sems.at[10])]
    for i, ref in enumerate((k_ref, v_ref, q_ref, g_ref, o_ref)):
        own = kv_ref.at[i] if i < 2 else rest_ref.at[pl.ds((i - 2) * tok, tok), :]
        copies.append(pltpu.make_async_copy(ref.at[0, 0, c, 0], own, sems.at[2 * i + 1]))
        copies.append(
            pltpu.make_async_copy(ref.at[0, 0, 1 - c, 0], other_ref.at[pl.ds(i * tok, tok), :], sems.at[2 * i])
        )
    for copy in copies:
        copy.start()
    copies[0].wait()
    row = lax.broadcasted_iota(jnp.int32, (16, rest_ref.shape[1]), 0)
    spread = jnp.zeros(row.shape, jnp.float32)
    for i in range(9):
        on = (flags[0, 0, 0, 9 * (i // 3) + 3 * (i % 3) + 1] != 0).astype(jnp.float32)
        spread = jnp.where(row == i, on, spread)
    rest_ref[pl.ds(3 * tok, 16), :] = spread.astype(jnp.bfloat16)
    other_ref[pl.ds(5 * tok, 16), :] = spread.astype(jnp.bfloat16)
    for copy in copies[1:]:
        copy.wait()


def line_kernel(tok, kv_ref, par_ref, par_kv_ref, *border_refs):
    y, c, _ = place()
    for i in range(2):
        block = par_ref[pl.ds(i * tok, tok), :]
        par_kv_ref[i] = block
        for which, ref in enumerate(border_refs):
            rising, _ = pair(y, which)
            ref[i] = jnp.where((c == 1) == rising, kv_ref[i], block)


def main_kernel(tok, chips, heights, sides, scale, *refs):
    rest_ref, par_ref = refs[:2]
    slots = 2 + sides
    sources, refs = refs[2 : 2 + 3 * slots][::-1], refs[2 + 3 * slots :]
    count = 3 * (1 + sides)
    results, (dq_ref, qs, gs, s_ref) = refs[:count], refs[count:]
    y, c, z = place()
    two = 2 * tok
    width = rest_ref.shape[1]
    f32, bf16 = jnp.float32, jnp.bfloat16
    first = c == 0

    def both(part):
        return jnp.concatenate(
            [rest_ref[pl.ds(part * tok, tok), :], par_ref[pl.ds((part + 2) * tok, tok), :]], axis=0
        )

    qs[...], gs[...] = both(0), both(1)
    product = both(1).astype(f32) * both(2).astype(f32)
    delta = jnp.sum(product.T, axis=0, keepdims=True)

    lane = lax.broadcasted_iota(jnp.int32, (1, width), 1)
    own_flags = rest_ref[pl.ds(3 * tok, 16), :].astype(f32)
    par_flags = par_ref[pl.ds(5 * tok, 16), :].astype(f32)
    none = jnp.zeros((1, width), f32)

    def bias(line, slot):
        inside = True
        if line:
            z_rising, z_at = pair(z, line - 1)
            inside = within(z_at, heights)

        def at(flags, dt):
            if line == 0:
                return flags[3 * dt + 1 : 3 * dt + 2] if dt != 1 else none + 1.0
            return jnp.where(z_rising, flags[3 * dt + 2 : 3 * dt + 3], flags[3 * dt : 3 * dt + 1])

        if slot == 0:
            own, par = at(own_flags, 1), jnp.where(first, at(par_flags, 0), at(par_flags, 2))
        elif slot == 1:
            own, par = jnp.where(first, at(own_flags, 2), at(own_flags, 0)), at(par_flags, 1)
        else:
            rising, y_at = pair(y, slot - 2)
            inside = within(y_at, chips) & inside
            near = first != rising
            own = jnp.where(near, jnp.where(rising, at(own_flags, 2), at(own_flags, 0)), none)
            par = jnp.where(near, none, jnp.where(rising, at(par_flags, 2), at(par_flags, 0)))
        row = jnp.concatenate([jnp.where(lane + start < tok, own, par) for start in range(0, two, width)], axis=1)
        return jnp.where(inside, (row - 1.0) * 1e30, -1e30)

    blocks = [(line, slot, pl.ds((line * slots + slot) * tok, tok)) for line in range(3) for slot in range(slots)]
    top = jnp.full((8, two), -1e30, f32)
    for line, slot, kept in blocks:
        scores = dot(sources[line * slots + slot][0], qs[...], ROWS_T) * scale + bias(line, slot)
        s_ref[kept, :] = scores
        top = jnp.maximum(top, jnp.max(scores.reshape(tok // 8, 8, two), axis=0))
    top = jnp.max(top, axis=0, keepdims=True)
    total = jnp.zeros((8, two), f32)
    for _, _, kept in blocks:
        weights = jnp.exp(s_ref[kept, :] - top)
        s_ref[kept, :] = weights
        total = total + jnp.sum(weights.reshape(tok // 8, 8, two), axis=0)
    share = 1.0 / jnp.sum(total, axis=0, keepdims=True)

    dq = jnp.zeros((two, width), f32)
    for line, slot, kept in blocks:
        source = sources[line * slots + slot]
        probs = s_ref[kept, :] * share
        grads = dot(source[1], gs[...], ROWS_T)
        low = (probs * (grads - delta) * scale).astype(bf16)
        result = results[line * (1 + sides) + max(slot - 1, 0)]
        rows = pl.ds(tok if slot == 1 else 0, tok)
        result[0, rows, :] = dot(low, qs[...]).astype(bf16)
        result[1, rows, :] = dot(probs.astype(bf16), gs[...]).astype(bf16)
        dq = dq + dot(low, source[0], COLS_T)
    dq_ref[...] = dq.astype(bf16)


def sum_kernel(tok, chips, heights, sides, *refs):
    count = 3 * (1 + sides)
    parts, (dq_ref, mine_ref, swap_ref) = refs[:count], refs[count:]
    y, c, z = place()

    def total(i, own):
        value = jnp.zeros(mine_ref.shape[1:], jnp.float32)
        for line in range(3):
            inside = True
            if line:
                _, z_at = pair(z, line - 1)
                inside = within(z_at, heights)
            block = parts[line * (1 + sides)][i, pl.ds(0 if own else tok, tok), :].astype(jnp.float32)
            value = value + (jnp.where(inside, block, 0.0) if line else block)
            for which in range(sides):
                rising, y_at = pair(y, which)
                near = ((c == 1) == rising) if own else ((c == 0) == rising)
                halo = parts[line * (1 + sides) + 1 + which][i].astype(jnp.float32)
                value = value + jnp.where(near & within(y_at, chips) & inside, halo, 0.0)
        return value

    for i in range(2):
        mine_ref[i] = total(i, True)
        swap_ref[i] = total(i, False).astype(jnp.bfloat16)
    swap_ref[2] = dq_ref[pl.ds(tok, tok), :]


def final_kernel(tok, mine_ref, swap_ref, dq_ref, gq_ref, gk_ref, gv_ref):
    _, c, _ = place()
    gq_ref[0, 0, c, 0] = dq_ref[pl.ds(0, tok), :]
    gq_ref[0, 0, 1 - c, 0] = swap_ref[2]
    for i, ref in enumerate((gk_ref, gv_ref)):
        ref[0, 0, c, 0] = mine_ref[i].astype(jnp.bfloat16)
        ref[0, 0, 1 - c, 0] = swap_ref[i]


def body(queries, keys, values, grad_out, attn_out, window_mask):
    tok, width = queries.shape[-2:]
    scale = width ** -0.5
    times, heights = lax.axis_size("tm"), lax.axis_size("height")
    chips = times // 2
    sides = 1 if chips == 2 else 2
    bf16, f32 = jnp.bfloat16, jnp.float32

    def call(kernel, shapes, specs, scratch=()):
        return pl.pallas_call(
            kernel,
            out_shape=[jax.ShapeDtypeStruct(*shape) for shape in shapes],
            in_specs=list(specs),
            out_specs=[VMEM] * len(shapes),
            scratch_shapes=list(scratch),
            compiler_params=LIMIT,
        )

    def partner(index, which, size):
        if which is None:
            return index
        at = index + 1 if index % 2 == which else index - 1
        return at if 0 <= at < size else None

    def exchange(block, y_which, z_which):
        pairs = []
        for t in range(times):
            for z in range(heights):
                y_at, z_at = partner(t // 2, y_which, chips), partner(z, z_which, heights)
                at = t * heights + z
                alone = y_at is None or z_at is None
                pairs.append((at, (t ^ 1) * heights + z if alone else (2 * y_at + t % 2) * heights + z_at))
        return lax.ppermute(block, ("tm", "height"), pairs)

    def swap_cores(block):
        return lax.ppermute(block, "tm", [(t, t ^ 1) for t in range(times)])

    line_shape, tile_shape = ((2, 2 * tok, width), bf16), ((2, tok, width), bf16)
    arguments = (keys, values, queries, grad_out, attn_out, window_mask)
    kv, rest, other = call(
        functools.partial(pack_kernel, tok),
        [tile_shape, ((3 * tok + 16, width), bf16), ((5 * tok + 16, width), bf16)],
        [HBM] * 6,
        [pltpu.SMEM(window_mask.shape, jnp.int32), pltpu.SemaphoreType.DMA((11,))],
    )(*(pltpu.with_memory_space_constraint(x, pltpu.HBM) for x in arguments))
    found = {(0, 0): kv}
    for j in (1, 2):
        found[j, 0] = exchange(kv, None, j - 1)
    par = swap_cores(other)
    par_kv, *borders = call(
        functools.partial(line_kernel, tok), [tile_shape] * (1 + sides), [VMEM] * 2
    )(kv, par)
    found[0, 1] = par_kv
    for j in (1, 2):
        found[j, 1] = exchange(par_kv, None, j - 1)
    for j in (2, 1, 0):
        for which in range(sides):
            found[j, 2 + which] = exchange(borders[which], which, None if j == 0 else j - 1)
    order = [(j, k) for j in range(3) for k in range(2 + sides)]
    back_order = [(j, k) for j in range(3) for k in range(1 + sides)]
    *columns, dq = call(
        functools.partial(main_kernel, tok, chips, heights, sides, scale),
        [line_shape if k == 0 else tile_shape for _, k in back_order] + [((2 * tok, width), bf16)],
        [VMEM] * (2 + len(order)),
        [
            pltpu.VMEM((2 * tok, width), bf16),
            pltpu.VMEM((2 * tok, width), bf16),
            pltpu.VMEM((3 * (2 + sides) * tok, 2 * tok), f32),
        ],
    )(rest, par, *(found[at] for at in order[::-1]))
    back = []
    for (j, k), column in zip(back_order, columns):
        y_which, z_which = None if k == 0 else k - 1, None if j == 0 else j - 1
        back.append(column if j == k == 0 else exchange(column, y_which, z_which))
    mine, leaving = call(
        functools.partial(sum_kernel, tok, chips, heights, sides),
        [((2, tok, width), f32), ((3, tok, width), bf16)],
        [VMEM] * (len(back) + 1),
    )(*back, dq)
    return call(
        functools.partial(final_kernel, tok),
        [(queries.shape, bf16)] * 3,
        [VMEM] * 3,
    )(mine, swap_cores(leaving), dq)


def solution(mesh):
    placed = P("tm", "height", "dp", None, None, None)
    return jax.shard_map(
        body,
        mesh=mesh,
        in_specs=(placed,) * 5 + (P("tm", "height", None, None),),
        out_specs=(placed,) * 3,
        check_vma=False,
    )
```

```python
import functools

import jax
import jax.numpy as jnp
from jax import lax
from jax.experimental import pallas as pl
from jax.experimental.pallas import tpu as pltpu
from jax.sharding import PartitionSpec as P

VMEM = pl.BlockSpec(memory_space=pltpu.VMEM)
HBM = pl.BlockSpec(memory_space=pltpu.HBM)
LIMIT = pltpu.CompilerParams(vmem_limit_bytes=32 * 1024 * 1024)
ROWS_T = (((1,), (1,)), ((), ()))
COLS_T = (((0,), (0,)), ((), ()))


def dot(a, b, dims=(((1,), (0,)), ((), ()))):
    return lax.dot_general(a, b, dims, preferred_element_type=jnp.float32)


def place():
    t = lax.axis_index("tm")
    return t // 2, t % 2, lax.axis_index("height")


def pair(index, which):
    rising = (index % 2) == (0 if which == 0 else 1)
    return rising, jnp.where(rising, index + 1, index - 1)


def within(index, size):
    return (index >= 0) & (index < size)


def pack_kernel(tok, k_ref, v_ref, q_ref, g_ref, o_ref, mask_ref, kv_ref, rest_ref, other_ref, flags, sems):
    _, c, _ = place()
    copies = [pltpu.make_async_copy(mask_ref, flags, sems.at[10])]
    for i, ref in enumerate((k_ref, v_ref, q_ref, g_ref, o_ref)):
        own = kv_ref.at[i] if i < 2 else rest_ref.at[pl.ds((i - 2) * tok, tok), :]
        copies.append(pltpu.make_async_copy(ref.at[0, 0, c, 0], own, sems.at[2 * i + 1]))
        copies.append(
            pltpu.make_async_copy(ref.at[0, 0, 1 - c, 0], other_ref.at[pl.ds(i * tok, tok), :], sems.at[2 * i])
        )
    for copy in copies:
        copy.start()
    copies[0].wait()
    row = lax.broadcasted_iota(jnp.int32, (16, rest_ref.shape[1]), 0)
    spread = jnp.zeros(row.shape, jnp.float32)
    for i in range(9):
        on = (flags[0, 0, 0, 9 * (i // 3) + 3 * (i % 3) + 1] != 0).astype(jnp.float32)
        spread = jnp.where(row == i, on, spread)
    rest_ref[pl.ds(3 * tok, 16), :] = spread.astype(jnp.bfloat16)
    other_ref[pl.ds(5 * tok, 16), :] = spread.astype(jnp.bfloat16)
    for copy in copies[1:]:
        copy.wait()


def line_kernel(tok, kv_ref, par_ref, par_kv_ref, *border_refs):
    y, c, _ = place()
    for i in range(2):
        block = par_ref[pl.ds(i * tok, tok), :]
        par_kv_ref[i] = block
        for which, ref in enumerate(border_refs):
            rising, _ = pair(y, which)
            ref[i] = jnp.where((c == 1) == rising, kv_ref[i], block)


def slots_of(sides):
    halos = [(line, 2 + which) for line in (2, 1, 0) for which in range(sides)]
    return [(0, 0), (0, 1)], [(1, 0), (2, 0)] + halos, [(1, 1), (2, 1)]


def rows_at(index, tok):
    return pl.ds(index * tok, tok)


def score_block(source, qg, table, row, delta_row, scale):
    scores = dot(source[0], qg[0], ROWS_T) * scale + table[row : row + 1, :]
    return scores, dot(source[1], qg[1], ROWS_T) - table[delta_row : delta_row + 1, :]


def first_kernel(tok, chips, heights, sides, scale, kv_ref, par_kv_ref, rest_ref, par_ref, qg, table, s_ref, d_ref):
    y, c, z = place()
    two = 2 * tok
    width = rest_ref.shape[1]
    f32 = jnp.float32
    first = c == 0
    for part in range(2):
        qg[part, rows_at(0, tok), :] = rest_ref[rows_at(part, tok), :]
        qg[part, rows_at(1, tok), :] = par_ref[rows_at(part + 2, tok), :]
    out = jnp.concatenate([rest_ref[rows_at(2, tok), :], par_ref[rows_at(4, tok), :]], axis=0)
    delta = jnp.sum((qg[1].astype(f32) * out.astype(f32)).T, axis=0, keepdims=True)

    lane = lax.broadcasted_iota(jnp.int32, (1, width), 1)
    own_flags = rest_ref[pl.ds(3 * tok, 16), :].astype(f32)
    par_flags = par_ref[pl.ds(5 * tok, 16), :].astype(f32)
    none = jnp.zeros((1, width), f32)

    def bias(line, slot):
        inside = True
        if line:
            z_rising, z_at = pair(z, line - 1)
            inside = within(z_at, heights)

        def at(flags, dt):
            if line == 0:
                return flags[3 * dt + 1 : 3 * dt + 2] if dt != 1 else none + 1.0
            return jnp.where(z_rising, flags[3 * dt + 2 : 3 * dt + 3], flags[3 * dt : 3 * dt + 1])

        if slot == 0:
            own, par = at(own_flags, 1), jnp.where(first, at(par_flags, 0), at(par_flags, 2))
        elif slot == 1:
            own, par = jnp.where(first, at(own_flags, 2), at(own_flags, 0)), at(par_flags, 1)
        else:
            rising, y_at = pair(y, slot - 2)
            inside = within(y_at, chips) & inside
            near = first != rising
            own = jnp.where(near, jnp.where(rising, at(own_flags, 2), at(own_flags, 0)), none)
            par = jnp.where(near, none, jnp.where(rising, at(par_flags, 2), at(par_flags, 0)))
        row = jnp.concatenate([jnp.where(lane + start < tok, own, par) for start in range(0, two, width)], axis=1)
        return jnp.where(inside, (row - 1.0) * 1e30, -1e30)

    stages = slots_of(sides)
    lines = [bias(*at) for stage in stages for at in stage] + [delta]
    table[...] = jnp.concatenate(lines + [jnp.zeros((16 - len(lines), two), f32)], axis=0)
    for i, source in enumerate((kv_ref, par_kv_ref)):
        s_ref[rows_at(i, tok), :], d_ref[rows_at(i, tok), :] = score_block(source, qg, table, i, len(lines) - 1, scale)


def second_kernel(tok, delta_row, scale, qg, table, *refs):
    *sources, s_ref, d_ref = refs
    for i, source in enumerate(sources):
        rows = rows_at(i, tok)
        s_ref[rows, :], d_ref[rows, :] = score_block(source, qg, table, 2 + i, delta_row, scale)


def leave_kernel(tok, sides, scale, qg, table, s_own, s_ref, d_ref, last1, last2, *refs):
    _, early, late = slots_of(sides)
    count = 2 * (1 + sides) + sides
    results = dict(zip([(line, k) for line in range(3) for k in range(1 + sides) if line + k], refs[:count]))
    low_ref, lse_ref, w_ref, e_ref = refs[count:]
    two = 2 * tok
    f32, bf16 = jnp.float32, jnp.bfloat16
    slots = early + late
    delta_row = 2 + len(slots)
    eighths = (tok // 8, 8, two)

    late_grads = []
    for i, source in enumerate((last1, last2)):
        scores, grads = score_block(source, qg, table, 2 + len(early) + i, delta_row, scale)
        w_ref[rows_at(len(early) + i, tok), :] = scores
        e_ref[rows_at(i, tok), :] = grads

    def scores_at(i):
        return s_ref[rows_at(i, tok), :] if i < len(early) else w_ref[rows_at(i, tok), :]

    top = jnp.full((8, two), -1e30, f32)
    for i in range(len(slots)):
        top = jnp.maximum(top, jnp.max(scores_at(i).reshape(eighths), axis=0))
    for i in range(2):
        top = jnp.maximum(top, jnp.max(s_own[rows_at(i, tok), :].reshape(eighths), axis=0))
    top = jnp.max(top, axis=0, keepdims=True)
    total = jnp.zeros((8, two), f32)
    for i in range(2):
        total = total + jnp.sum(jnp.exp(s_own[rows_at(i, tok), :] - top).reshape(eighths), axis=0)
    for i in range(len(slots)):
        weights = jnp.exp(scores_at(i) - top)
        w_ref[rows_at(i, tok), :] = weights
        total = total + jnp.sum(weights.reshape(eighths), axis=0)
    total = jnp.sum(total, axis=0, keepdims=True)
    lse_ref[...] = jnp.broadcast_to(top + jnp.log(total), (8, two))
    share = 1.0 / total

    for i, (line, slot) in enumerate(slots):
        probs = w_ref[rows_at(i, tok), :] * share
        grads = d_ref[rows_at(i, tok), :] if i < len(early) else e_ref[rows_at(i - len(early), tok), :]
        low = (probs * grads * scale).astype(bf16)
        low_ref[rows_at(i, tok), :] = low
        result, rows = results[line, max(slot - 1, 0)], rows_at(1 if slot == 1 else 0, tok)
        result[0, rows, :] = dot(low, qg[0]).astype(bf16)
        result[1, rows, :] = dot(probs.astype(bf16), qg[1]).astype(bf16)


def stay_kernel(tok, scale, qg, s_own, d_own, lse_ref, low_ref, *refs):
    *sources, own_ref, dq_ref = refs
    bf16 = jnp.bfloat16
    dq = jnp.zeros(dq_ref.shape[::-1], jnp.float32)
    for i, source in enumerate(sources):
        if i < 2:
            rows = rows_at(i, tok)
            probs = jnp.exp(s_own[rows, :] - lse_ref[0:1, :])
            low = (probs * d_own[rows, :] * scale).astype(bf16)
            own_ref[0, rows, :] = dot(low, qg[0]).astype(bf16)
            own_ref[1, rows, :] = dot(probs.astype(bf16), qg[1]).astype(bf16)
        else:
            low = low_ref[rows_at(i - 2, tok), :]
        dq = dq + dot(source[0], low, COLS_T)
    dq_ref[...] = dq.T.astype(bf16)


def sum_kernel(tok, chips, heights, sides, *refs):
    count = 3 * (1 + sides)
    parts, (dq_ref, mine_ref, swap_ref) = refs[:count], refs[count:]
    y, c, z = place()

    def total(i, own):
        value = jnp.zeros(mine_ref.shape[1:], jnp.float32)
        for line in range(3):
            inside = True
            if line:
                _, z_at = pair(z, line - 1)
                inside = within(z_at, heights)
            block = parts[line * (1 + sides)][i, pl.ds(0 if own else tok, tok), :].astype(jnp.float32)
            value = value + (jnp.where(inside, block, 0.0) if line else block)
            for which in range(sides):
                rising, y_at = pair(y, which)
                near = ((c == 1) == rising) if own else ((c == 0) == rising)
                halo = parts[line * (1 + sides) + 1 + which][i].astype(jnp.float32)
                value = value + jnp.where(near & within(y_at, chips) & inside, halo, 0.0)
        return value

    for i in range(2):
        mine_ref[i] = total(i, True)
        swap_ref[i] = total(i, False).astype(jnp.bfloat16)
    swap_ref[2] = dq_ref[pl.ds(tok, tok), :]


def final_kernel(tok, mine_ref, swap_ref, dq_ref, gq_ref, gk_ref, gv_ref):
    _, c, _ = place()
    gq_ref[0, 0, c, 0] = dq_ref[pl.ds(0, tok), :]
    gq_ref[0, 0, 1 - c, 0] = swap_ref[2]
    for i, ref in enumerate((gk_ref, gv_ref)):
        ref[0, 0, c, 0] = mine_ref[i].astype(jnp.bfloat16)
        ref[0, 0, 1 - c, 0] = swap_ref[i]


def body(queries, keys, values, grad_out, attn_out, window_mask):
    tok, width = queries.shape[-2:]
    scale = width ** -0.5
    times, heights = lax.axis_size("tm"), lax.axis_size("height")
    chips = times // 2
    sides = 1 if chips == 2 else 2
    bf16, f32 = jnp.bfloat16, jnp.float32

    def call(kernel, shapes, specs, scratch=()):
        return pl.pallas_call(
            kernel,
            out_shape=[jax.ShapeDtypeStruct(*shape) for shape in shapes],
            in_specs=list(specs),
            out_specs=[VMEM] * len(shapes),
            scratch_shapes=list(scratch),
            compiler_params=LIMIT,
        )

    def partner(index, which, size):
        if which is None:
            return index
        at = index + 1 if index % 2 == which else index - 1
        return at if 0 <= at < size else None

    def exchange(block, y_which, z_which):
        pairs = []
        for t in range(times):
            for z in range(heights):
                y_at, z_at = partner(t // 2, y_which, chips), partner(z, z_which, heights)
                at = t * heights + z
                alone = y_at is None or z_at is None
                pairs.append((at, (t ^ 1) * heights + z if alone else (2 * y_at + t % 2) * heights + z_at))
        return lax.ppermute(block, ("tm", "height"), pairs)

    def swap_cores(block):
        return lax.ppermute(block, "tm", [(t, t ^ 1) for t in range(times)])

    line_shape, tile_shape = ((2, 2 * tok, width), bf16), ((2, tok, width), bf16)
    arguments = (keys, values, queries, grad_out, attn_out, window_mask)
    kv, rest, other = call(
        functools.partial(pack_kernel, tok),
        [tile_shape, ((3 * tok + 16, width), bf16), ((5 * tok + 16, width), bf16)],
        [HBM] * 6,
        [pltpu.SMEM(window_mask.shape, jnp.int32), pltpu.SemaphoreType.DMA((11,))],
    )(*(pltpu.with_memory_space_constraint(x, pltpu.HBM) for x in arguments))
    found = {(0, 0): kv}
    for j in (1, 2):
        found[j, 0] = exchange(kv, None, j - 1)
    par = swap_cores(other)
    par_kv, *borders = call(
        functools.partial(line_kernel, tok), [tile_shape] * (1 + sides), [VMEM] * 2
    )(kv, par)
    found[0, 1] = par_kv
    for j in (1, 2):
        found[j, 1] = exchange(par_kv, None, j - 1)
    for j in (2, 1, 0):
        for which in range(sides):
            found[j, 2 + which] = exchange(borders[which], which, None if j == 0 else j - 1)
    own_slots, early, late = slots_of(sides)
    two = 2 * tok

    def square(count):
        return ((count * tok, two), f32)

    qg, table, s_own, d_own = call(
        functools.partial(first_kernel, tok, chips, heights, sides, scale),
        [((2, two, width), bf16), ((16, two), f32), square(2), square(2)],
        [VMEM] * 4,
    )(kv, par_kv, rest, par)
    s_early, d_early = call(
        functools.partial(second_kernel, tok, 2 + len(early) + len(late), scale),
        [square(len(early)), square(len(early))],
        [VMEM] * (2 + len(early)),
    )(qg, table, *(found[at] for at in early))
    back_order = [(j, k) for j in range(3) for k in range(1 + sides) if j + k]
    leaving_count = len(early) + len(late)
    *columns, low, lse = call(
        functools.partial(leave_kernel, tok, sides, scale),
        [line_shape if k == 0 else tile_shape for _, k in back_order]
        + [((leaving_count * tok, two), bf16), ((8, two), f32)],
        [VMEM] * 7,
        [pltpu.VMEM(*square(leaving_count)), pltpu.VMEM(*square(2))],
    )(qg, table, s_own, s_early, d_early, *(found[at] for at in late))
    own, dq = call(
        functools.partial(stay_kernel, tok, scale),
        [line_shape, ((two, width), bf16)],
        [VMEM] * (7 + leaving_count),
    )(qg, s_own, d_own, lse, low, *(found[at] for at in own_slots + early + late))
    back = [own]
    for (j, k), column in zip(back_order, columns):
        back.append(exchange(column, None if k == 0 else k - 1, None if j == 0 else j - 1))
    mine, leaving = call(
        functools.partial(sum_kernel, tok, chips, heights, sides),
        [((2, tok, width), f32), ((3, tok, width), bf16)],
        [VMEM] * (len(back) + 1),
    )(*back, dq)
    return call(
        functools.partial(final_kernel, tok),
        [(queries.shape, bf16)] * 3,
        [VMEM] * 3,
    )(mine, swap_cores(leaving), dq)


def solution(mesh):
    placed = P("tm", "height", "dp", None, None, None)
    return jax.shard_map(
        body,
        mesh=mesh,
        in_specs=(placed,) * 5 + (P("tm", "height", None, None),),
        out_specs=(placed,) * 3,
        check_vma=False,
    )
```

```python
import functools

import jax
import jax.numpy as jnp
from jax import lax
from jax.experimental import pallas as pl
from jax.experimental.pallas import tpu as pltpu
from jax.sharding import PartitionSpec as P

VMEM = pl.BlockSpec(memory_space=pltpu.VMEM)
HBM = pl.BlockSpec(memory_space=pltpu.HBM)
LIMIT = pltpu.CompilerParams(vmem_limit_bytes=32 * 1024 * 1024)
ROWS_T = (((1,), (1,)), ((), ()))
COLS_T = (((0,), (0,)), ((), ()))


def dot(a, b, dims=(((1,), (0,)), ((), ()))):
    return lax.dot_general(a, b, dims, preferred_element_type=jnp.float32)


def place():
    t = lax.axis_index("tm")
    return t // 2, t % 2, lax.axis_index("height")


def pair(index, which):
    rising = (index % 2) == (0 if which == 0 else 1)
    return rising, jnp.where(rising, index + 1, index - 1)


def within(index, size):
    return (index >= 0) & (index < size)


def pack_kernel(tok, k_ref, v_ref, q_ref, g_ref, o_ref, mask_ref, kv_ref, rest_ref, other_ref, flags, sems):
    _, c, _ = place()
    copies = [pltpu.make_async_copy(mask_ref, flags, sems.at[10])]
    for i, ref in enumerate((k_ref, v_ref, q_ref, g_ref, o_ref)):
        own = kv_ref.at[i] if i < 2 else rest_ref.at[pl.ds((i - 2) * tok, tok), :]
        copies.append(pltpu.make_async_copy(ref.at[0, 0, c, 0], own, sems.at[2 * i + 1]))
        copies.append(
            pltpu.make_async_copy(ref.at[0, 0, 1 - c, 0], other_ref.at[pl.ds(i * tok, tok), :], sems.at[2 * i])
        )
    for copy in copies:
        copy.start()
    copies[0].wait()
    row = lax.broadcasted_iota(jnp.int32, (16, rest_ref.shape[1]), 0)
    spread = jnp.zeros(row.shape, jnp.float32)
    for i in range(9):
        on = (flags[0, 0, 0, 9 * (i // 3) + 3 * (i % 3) + 1] != 0).astype(jnp.float32)
        spread = jnp.where(row == i, on, spread)
    rest_ref[pl.ds(3 * tok, 16), :] = spread.astype(jnp.bfloat16)
    other_ref[pl.ds(5 * tok, 16), :] = spread.astype(jnp.bfloat16)
    for copy in copies[1:]:
        copy.wait()


def rows_at(index, tok):
    return pl.ds(index * tok, tok)


def border_is_own(y, c):
    rising, _ = pair(y, 0)
    return (c == 1) == rising


def pick(near, which, own, par):
    return jnp.where(near, own, par) if which == 0 else jnp.where(near, par, own)


def line_kernel(tok, rest_ref, par_ref, par_kv_ref, *border_refs):
    y, c, _ = place()
    near = border_is_own(y, c)
    for i in range(2):
        par_kv_ref[i] = par_ref[rows_at(i, tok), :]
    for which, ref in enumerate(border_refs):
        for part in range(2):
            rows = rows_at(part, tok)
            ref[rows, :] = pick(near, which, rest_ref[rows, :], par_ref[rows_at(part + 2, tok), :])
        ref[pl.ds(2 * tok, 16), :] = pick(
            near, which, rest_ref[pl.ds(3 * tok, 16), :], par_ref[pl.ds(5 * tok, 16), :]
        )


def line_place(z, line, heights):
    if line == 0:
        return True, lambda flags, dt: flags[3 * dt + 1 : 3 * dt + 2]
    rising, at = pair(z, line - 1)
    return within(at, heights), lambda flags, dt: jnp.where(
        rising, flags[3 * dt + 2 : 3 * dt + 3], flags[3 * dt : 3 * dt + 1]
    )


def lanes_of(tok, border, other):
    width = border.shape[1]
    lane = lax.broadcasted_iota(jnp.int32, (1, width), 1)
    return jnp.concatenate(
        [jnp.where(lane + start < tok, border, other) for start in range(0, 2 * tok, width)], axis=1
    )


def first_kernel(tok, heights, scale, kv_ref, par_kv_ref, rest_ref, par_ref, qg, table, s_ref, d_ref):
    y, c, z = place()
    two = 2 * tok
    f32 = jnp.float32
    first, near = c == 0, border_is_own(y, c)
    out = []
    for part in range(3):
        own, par = rest_ref[rows_at(part, tok), :], par_ref[rows_at(part + 2, tok), :]
        tiles = [pick(near, which, own, par) for which in range(2)]
        if part == 2:
            out = jnp.concatenate(tiles, axis=0)
        else:
            for which in range(2):
                qg[part, rows_at(which, tok), :] = tiles[which]
    delta = jnp.sum((qg[1].astype(f32) * out.astype(f32)).T, axis=0, keepdims=True)

    own_flags = rest_ref[pl.ds(3 * tok, 16), :].astype(f32)
    par_flags = par_ref[pl.ds(5 * tok, 16), :].astype(f32)
    lines = []
    for line in range(3):
        inside, at = line_place(z, line, heights)
        centre = jnp.ones_like(own_flags[0:1]) if line == 0 else None
        for slot in range(2):
            if slot == 0:
                own, par = at(own_flags, 1), jnp.where(first, at(par_flags, 0), at(par_flags, 2))
            else:
                own, par = jnp.where(first, at(own_flags, 2), at(own_flags, 0)), at(par_flags, 1)
            if line == 0:
                own, par = (centre, par) if slot == 0 else (own, centre)
            row = lanes_of(tok, pick(near, 0, own, par), pick(near, 1, own, par))
            lines.append(jnp.where(inside, (row - 1.0) * 1e30, -1e30))
    table[...] = jnp.concatenate(lines + [delta, jnp.zeros((1, two), f32)], axis=0)
    for i, source in enumerate((kv_ref, par_kv_ref)):
        rows = rows_at(i, tok)
        s_ref[rows, :] = dot(source[0], qg[0], ROWS_T) * scale + table[i : i + 1, :]
        d_ref[rows, :] = dot(source[1], qg[1], ROWS_T) - table[6:7, :]


def early_kernel(tok, scale, qg, table, one_ref, two_ref, s_ref, d_ref):
    for i, source in enumerate((one_ref, two_ref)):
        rows = rows_at(i, tok)
        s_ref[rows, :] = dot(source[0], qg[0], ROWS_T) * scale + table[2 + 2 * i : 3 + 2 * i, :]
        d_ref[rows, :] = dot(source[1], qg[1], ROWS_T) - table[6:7, :]


def foreign_rows(ref, part, which, tok):
    block = ref[rows_at(part, tok), :]
    return jnp.concatenate([block, jnp.zeros_like(block)] if which == 0 else [jnp.zeros_like(block), block], axis=0)


def score_kernel(tok, chips, heights, sides, scale, qg, table, s_own, s_early, *refs):
    keys, foreign, refs = refs[:6], refs[6 : 6 + sides], refs[6 + sides :]
    s_late, s_far, *notes = refs
    y, c, z = place()
    near = border_is_own(y, c)
    two = 2 * tok
    f32 = jnp.float32
    eighths = (tok // 8, 8, two)

    def summed(blocks):
        top = jnp.full((8, two), -1e30, f32)
        for ref, i in blocks:
            top = jnp.maximum(top, jnp.max(ref[rows_at(i, tok), :].reshape(eighths), axis=0))
        top = jnp.max(top, axis=0, keepdims=True)
        total = jnp.zeros((8, two), f32)
        for ref, i in blocks:
            total = total + jnp.sum(jnp.exp(ref[rows_at(i, tok), :] - top).reshape(eighths), axis=0)
        return [top, jnp.sum(total, axis=0, keepdims=True)]

    far = []
    for which in range(sides):
        rising, y_at = pair(y, which)
        flags = foreign[which][pl.ds(2 * tok, 16), :].astype(f32)
        queries = foreign_rows(foreign[which], 0, which, tok)
        for line in range(3):
            inside, at = line_place(z, line, heights)
            row = jnp.where(rising, at(flags, 0), at(flags, 2))
            none = jnp.zeros_like(row)
            row = lanes_of(tok, *((row, none) if which == 0 else (none, row)))
            bias = jnp.where(inside & within(y_at, chips), (row - 1.0) * 1e30, -1e30)
            border = pick(near, which, keys[2 * line][0], keys[2 * line + 1][0])
            s_far[rows_at(3 * which + line, tok), :] = dot(border, queries, ROWS_T) * scale + bias
        far.append(summed([(s_far, 3 * which + line) for line in range(3)]))
    for i in range(2):
        s_late[rows_at(i, tok), :] = dot(keys[3 + 2 * i][0], qg[0], ROWS_T) * scale + table[3 + 2 * i : 4 + 2 * i, :]
    mine = summed([(ref, i) for ref in (s_own, s_early, s_late) for i in range(2)])
    for which in range(sides):
        notes[which][...] = jnp.concatenate(mine + far[which] + [table[6:7, :], jnp.zeros((3, two), f32)], axis=0)


def late_kernel(tok, sides, qg, table, *refs):
    values, foreign, (d_late, d_far) = refs[:6], refs[6 : 6 + sides], refs[6 + sides :]
    y, c, _ = place()
    near = border_is_own(y, c)
    for i in range(2):
        d_late[rows_at(i, tok), :] = dot(values[3 + 2 * i][1], qg[1], ROWS_T) - table[6:7, :]
    for which in range(sides):
        grads = foreign_rows(foreign[which], 1, which, tok)
        for line in range(3):
            border = pick(near, which, values[2 * line][1], values[2 * line + 1][1])
            d_far[rows_at(3 * which + line, tok), :] = dot(border, grads, ROWS_T)


def column_sums(low, probs, qg, far):
    sums = [dot(low, qg[0]), dot(probs, qg[1])]
    for (far_low, far_probs, queries, grads), mine in far:
        sums[0] = sums[0] + jnp.where(mine, dot(far_low, queries), 0.0)
        sums[1] = sums[1] + jnp.where(mine, dot(far_probs, grads), 0.0)
    return sums


def leave_kernel(tok, chips, sides, scale, qg, s_early, d_early, s_late, d_late, s_far, d_far, *refs):
    sent, came, foreign = (refs[i * sides : (i + 1) * sides] for i in range(3))
    one_ref, two_ref, low_ref, low_far, lse_ref = refs[3 * sides :]
    y, c, _ = place()
    near = border_is_own(y, c)
    f32, bf16 = jnp.float32, jnp.bfloat16

    def joined(top, total, other_top, other_total):
        both = jnp.maximum(top, other_top)
        return both, total * jnp.exp(top - both) + other_total * jnp.exp(other_top - both)

    top, total = sent[0][0:1, :], sent[0][1:2, :]
    table = []
    for which in range(sides):
        _, y_at = pair(y, which)
        inside = within(y_at, chips)
        note = came[which]
        top, total = joined(
            top, total, jnp.where(inside, note[2:3, :], -1e30), jnp.where(inside, note[3:4, :], 0.0)
        )
        far_top, far_total = joined(note[0:1, :], note[1:2, :], sent[which][2:3, :], sent[which][3:4, :])
        table += [jnp.where(inside, far_top + jnp.log(far_total), 0.0), jnp.where(inside, note[4:5, :], 0.0)]
    lines = [top + jnp.log(total)] + table
    lse_ref[...] = jnp.concatenate(lines + [jnp.zeros((8 - len(lines), 2 * tok), f32)], axis=0)

    queries = [foreign_rows(ref, 0, which, tok) for which, ref in enumerate(foreign)]
    grads = [foreign_rows(ref, 1, which, tok) for which, ref in enumerate(foreign)]
    for line, result in ((1, one_ref), (2, two_ref)):
        far = []
        for which in range(sides):
            rows = rows_at(3 * which + line, tok)
            probs = jnp.exp(s_far[rows, :] - lse_ref[1 + 2 * which : 2 + 2 * which, :])
            low = (probs * (d_far[rows, :] - lse_ref[2 + 2 * which : 3 + 2 * which, :]) * scale).astype(bf16)
            low_far[rows_at(2 * which + line - 1, tok), :] = low
            far.append((low, probs.astype(bf16), queries[which], grads[which]))
        for slot, (s_ref, d_ref) in enumerate(((s_early, d_early), (s_late, d_late))):
            rows = rows_at(line - 1, tok)
            probs = jnp.exp(s_ref[rows, :] - lse_ref[0:1, :])
            low = (probs * d_ref[rows, :] * scale).astype(bf16)
            low_ref[rows_at(2 * (line - 1) + slot, tok), :] = low
            owns = [(far[which], near == ((slot == 0) == (which == 0))) for which in range(sides)]
            sums = column_sums(low, probs.astype(bf16), qg, owns)
            for i in range(2):
                result[i, rows_at(slot, tok), :] = sums[i].astype(bf16)


def stay_kernel(tok, sides, scale, qg, s_own, d_own, s_far, d_far, low_ref, low_far, lse_ref, *refs):
    keys, foreign, (own_ref, dq_ref, *back_refs) = refs[:6], refs[6 : 6 + sides], refs[6 + sides :]
    y, c, _ = place()
    near = border_is_own(y, c)
    bf16 = jnp.bfloat16
    far = []
    for which in range(sides):
        rows = rows_at(3 * which, tok)
        probs = jnp.exp(s_far[rows, :] - lse_ref[1 + 2 * which : 2 + 2 * which, :])
        low = (probs * (d_far[rows, :] - lse_ref[2 + 2 * which : 3 + 2 * which, :]) * scale).astype(bf16)
        parts = [foreign_rows(foreign[which], part, which, tok) for part in range(2)]
        far.append((low, probs.astype(bf16), *parts))
        dq = dot(pick(near, which, keys[0][0], keys[1][0]), low, COLS_T)
        for line in (1, 2):
            border = pick(near, which, keys[2 * line][0], keys[2 * line + 1][0])
            dq = dq + dot(border, low_far[rows_at(2 * which + line - 1, tok), :], COLS_T)
        back_refs[which][...] = dq.T[which * tok : (which + 1) * tok].astype(bf16)
    dq = jnp.zeros(dq_ref.shape[::-1], jnp.float32)
    for slot in range(2):
        rows = rows_at(slot, tok)
        probs = jnp.exp(s_own[rows, :] - lse_ref[0:1, :])
        low = (probs * d_own[rows, :] * scale).astype(bf16)
        owns = [(far[which], near == ((slot == 0) == (which == 0))) for which in range(sides)]
        sums = column_sums(low, probs.astype(bf16), qg, owns)
        for i in range(2):
            own_ref[i, rows, :] = sums[i].astype(bf16)
        dq = dq + dot(keys[slot][0], low, COLS_T)
    for i in range(4):
        dq = dq + dot(keys[2 + i][0], low_ref[rows_at(i, tok), :], COLS_T)
    dq_ref[...] = dq.T


def sum_kernel(tok, chips, heights, sides, own_ref, one_ref, two_ref, dq_ref, *refs):
    backs, (mine_ref, mine_q_ref, swap_ref) = refs[:sides], refs[sides:]
    y, c, z = place()
    near = border_is_own(y, c)
    f32, bf16 = jnp.float32, jnp.bfloat16
    for i in range(2):
        for slot in range(2):
            rows = rows_at(slot, tok)
            value = own_ref[i, rows, :].astype(f32)
            for line, ref in ((1, one_ref), (2, two_ref)):
                inside, _ = line_place(z, line, heights)
                value = value + jnp.where(inside, ref[i, rows, :].astype(f32), 0.0)
            if slot == 0:
                mine_ref[i] = value.astype(bf16)
            else:
                swap_ref[i] = value.astype(bf16)
    tiles = []
    for tile in range(2):
        value = dq_ref[rows_at(tile, tok), :]
        if tile < sides:
            _, y_at = pair(y, tile)
            value = value + jnp.where(within(y_at, chips), backs[tile][...].astype(f32), 0.0)
        tiles.append(value.astype(bf16))
    mine_q_ref[...] = jnp.where(near, tiles[0], tiles[1])
    swap_ref[2] = jnp.where(near, tiles[1], tiles[0])


def final_kernel(mine_ref, swap_ref, mine_q_ref, gq_ref, gk_ref, gv_ref):
    _, c, _ = place()
    gq_ref[0, 0, c, 0] = mine_q_ref[...]
    gq_ref[0, 0, 1 - c, 0] = swap_ref[2]
    for i, ref in enumerate((gk_ref, gv_ref)):
        ref[0, 0, c, 0] = mine_ref[i]
        ref[0, 0, 1 - c, 0] = swap_ref[i]


def body(queries, keys, values, grad_out, attn_out, window_mask):
    tok, width = queries.shape[-2:]
    scale = width ** -0.5
    times, heights = lax.axis_size("tm"), lax.axis_size("height")
    chips = times // 2
    sides = 1 if chips == 2 else 2
    bf16, f32 = jnp.bfloat16, jnp.float32

    def call(kernel, shapes, specs, scratch=()):
        return pl.pallas_call(
            kernel,
            out_shape=[jax.ShapeDtypeStruct(*shape) for shape in shapes],
            in_specs=list(specs),
            out_specs=[VMEM] * len(shapes),
            scratch_shapes=list(scratch),
            compiler_params=LIMIT,
        )

    def partner(index, which, size):
        if which is None:
            return index
        at = index + 1 if index % 2 == which else index - 1
        return at if 0 <= at < size else None

    def exchange(block, y_which, z_which):
        pairs = []
        for t in range(times):
            for z in range(heights):
                y_at, z_at = partner(t // 2, y_which, chips), partner(z, z_which, heights)
                at = t * heights + z
                alone = y_at is None or z_at is None
                pairs.append((at, (t ^ 1) * heights + z if alone else (2 * y_at + t % 2) * heights + z_at))
        return lax.ppermute(block, ("tm", "height"), pairs)

    def swap_cores(block):
        return lax.ppermute(block, "tm", [(t, t ^ 1) for t in range(times)])

    line_shape, tile_shape = ((2, 2 * tok, width), bf16), ((2, tok, width), bf16)
    arguments = (keys, values, queries, grad_out, attn_out, window_mask)
    kv, rest, other = call(
        functools.partial(pack_kernel, tok),
        [tile_shape, ((3 * tok + 16, width), bf16), ((5 * tok + 16, width), bf16)],
        [HBM] * 6,
        [pltpu.SMEM(window_mask.shape, jnp.int32), pltpu.SemaphoreType.DMA((11,))],
    )(*(pltpu.with_memory_space_constraint(x, pltpu.HBM) for x in arguments))
    early = [exchange(kv, None, which) for which in range(2)]
    par = swap_cores(other)
    border_shape, two = ((2 * tok + 16, width), bf16), 2 * tok
    par_kv, *borders = call(
        functools.partial(line_kernel, tok), [tile_shape] + [border_shape] * sides, [VMEM] * 2
    )(rest, par)
    foreign = [exchange(borders[which], which, None) for which in range(sides)]
    late = [exchange(par_kv, None, which) for which in range(2)]
    tiles = (kv, par_kv, early[0], late[0], early[1], late[1])

    def square(count, kind=f32):
        return ((count * tok, two), kind)

    qg, table, s_own, d_own = call(
        functools.partial(first_kernel, tok, heights, scale),
        [((2, two, width), bf16), ((8, two), f32), square(2), square(2)],
        [VMEM] * 4,
    )(kv, par_kv, rest, par)
    s_early, d_early = call(
        functools.partial(early_kernel, tok, scale), [square(2), square(2)], [VMEM] * 4
    )(qg, table, *early)
    s_late, s_far, *sent = call(
        functools.partial(score_kernel, tok, chips, heights, sides, scale),
        [square(2), square(3 * sides)] + [((8, two), f32)] * sides,
        [VMEM] * (10 + sides),
    )(qg, table, s_own, s_early, *tiles, *foreign)
    came = [exchange(sent[which], which, None) for which in range(sides)]
    d_late, d_far = call(
        functools.partial(late_kernel, tok, sides), [square(2), square(3 * sides)], [VMEM] * (8 + sides)
    )(qg, table, *tiles, *foreign)
    one, other_one, low, low_far, lse = call(
        functools.partial(leave_kernel, tok, chips, sides, scale),
        [line_shape, line_shape, square(4, bf16), square(2 * sides, bf16), ((8, two), f32)],
        [VMEM] * (7 + 3 * sides),
    )(qg, s_early, d_early, s_late, d_late, s_far, d_far, *sent, *came, *foreign)
    back = [exchange(block, None, which) for which, block in enumerate((one, other_one))]
    own, dq, *shares = call(
        functools.partial(stay_kernel, tok, sides, scale),
        [line_shape, ((two, width), f32)] + [((tok, width), bf16)] * sides,
        [VMEM] * (14 + sides),
    )(qg, s_own, d_own, s_far, d_far, low, low_far, lse, *tiles, *foreign)
    shares = [exchange(share, which, None) for which, share in enumerate(shares)]
    mine, mine_q, leaving = call(
        functools.partial(sum_kernel, tok, chips, heights, sides),
        [tile_shape, ((tok, width), bf16), ((3, tok, width), bf16)],
        [VMEM] * (4 + sides),
    )(own, *back, dq, *shares)
    return call(final_kernel, [(queries.shape, bf16)] * 3, [VMEM] * 3)(mine, swap_cores(leaving), mine_q)


def solution(mesh):
    placed = P("tm", "height", "dp", None, None, None)
    return jax.shard_map(
        body,
        mesh=mesh,
        in_specs=(placed,) * 5 + (P("tm", "height", None, None),),
        out_specs=(placed,) * 3,
        check_vma=False,
    )
```

```python
import functools

import jax
import jax.numpy as jnp
from jax import lax
from jax.experimental import pallas as pl
from jax.experimental.pallas import tpu as pltpu
from jax.sharding import PartitionSpec as P

VMEM = pl.BlockSpec(memory_space=pltpu.VMEM)
HBM = pl.BlockSpec(memory_space=pltpu.HBM)
LIMIT = pltpu.CompilerParams(vmem_limit_bytes=32 * 1024 * 1024)
ROWS_T = (((1,), (1,)), ((), ()))
COLS_T = (((0,), (0,)), ((), ()))


def dot(a, b, dims=(((1,), (0,)), ((), ()))):
    return lax.dot_general(a, b, dims, preferred_element_type=jnp.float32)


def place():
    t = lax.axis_index("tm")
    return t // 2, t % 2, lax.axis_index("height")


def pair(index, which):
    rising = (index % 2) == (0 if which == 0 else 1)
    return rising, jnp.where(rising, index + 1, index - 1)


def within(index, size):
    return (index >= 0) & (index < size)


def pack_kernel(tok, k_ref, v_ref, q_ref, g_ref, o_ref, mask_ref, kv_ref, rest_ref, other_ref, flags, sems):
    _, c, _ = place()
    copies = [pltpu.make_async_copy(mask_ref, flags, sems.at[10])]
    for i, ref in enumerate((k_ref, v_ref, q_ref, g_ref, o_ref)):
        own = (kv_ref if i < 2 else rest_ref).at[pl.ds((i if i < 2 else i - 2) * tok, tok), :]
        copies.append(pltpu.make_async_copy(ref.at[0, 0, c, 0], own, sems.at[2 * i + 1]))
        copies.append(
            pltpu.make_async_copy(ref.at[0, 0, 1 - c, 0], other_ref.at[pl.ds(i * tok, tok), :], sems.at[2 * i])
        )
    for copy in copies:
        copy.start()
    copies[0].wait()
    row = lax.broadcasted_iota(jnp.int32, (16, rest_ref.shape[1]), 0)
    spread = jnp.zeros(row.shape, jnp.float32)
    for i in range(9):
        on = (flags[0, 0, 0, 9 * (i // 3) + 3 * (i % 3) + 1] != 0).astype(jnp.float32)
        spread = jnp.where(row == i, on, spread)
    rest_ref[pl.ds(3 * tok, 16), :] = spread.astype(jnp.bfloat16)
    other_ref[pl.ds(5 * tok, 16), :] = spread.astype(jnp.bfloat16)
    for copy in copies[1:]:
        copy.wait()


def rows_at(index, tok):
    return pl.ds(index * tok, tok)


def border_is_own(y, c):
    rising, _ = pair(y, 0)
    return (c == 1) == rising


def pick(near, which, own, par):
    return jnp.where(near, own, par) if which == 0 else jnp.where(near, par, own)


def line_kernel(tok, rest_ref, par_ref, par_kv_ref, *border_refs):
    y, c, _ = place()
    near = border_is_own(y, c)
    for i in range(2):
        par_kv_ref[rows_at(i, tok), :] = par_ref[rows_at(i, tok), :]
    width = par_ref.shape[1]
    f32 = jnp.float32
    for which, ref in enumerate(border_refs):
        tiles = [pick(near, which, rest_ref[rows_at(i, tok), :], par_ref[rows_at(i + 2, tok), :]) for i in range(3)]
        ref[rows_at(0, tok), :], ref[rows_at(1, tok), :] = tiles[0], tiles[1]
        flags = pick(near, which, rest_ref[pl.ds(3 * tok, 16), :], par_ref[pl.ds(5 * tok, 16), :]).astype(f32)
        product, gap = tiles[1].astype(f32) * tiles[2].astype(f32), jnp.zeros((2 * width - tok, width), f32)
        product = jnp.concatenate([product, gap] if which == 0 else [gap, product], axis=0)
        left, lines = jnp.sum(product.T, axis=0, keepdims=True), [flags[0:9]]
        for _ in range(3):
            term = left.astype(jnp.bfloat16).astype(f32)
            left = left - term
            lines += [term[:, :width], term[:, width:]]
        ref[pl.ds(2 * tok, 16), :] = jnp.concatenate(lines + [jnp.zeros((1, width), f32)], axis=0).astype(jnp.bfloat16)


def foreign_delta(ref, which, tok):
    terms = ref[pl.ds(2 * tok, 16), :].astype(jnp.float32)
    one, two = (sum(terms[9 + 2 * i + half : 10 + 2 * i + half] for i in range(3)) for half in range(2))
    none = jnp.zeros_like(one)
    return jnp.concatenate([one, two, none] if which == 0 else [none, one, two], axis=1)


def line_place(z, line, heights):
    if line == 0:
        return True, lambda flags, dt: flags[3 * dt + 1 : 3 * dt + 2]
    rising, at = pair(z, line - 1)
    return within(at, heights), lambda flags, dt: jnp.where(
        rising, flags[3 * dt + 2 : 3 * dt + 3], flags[3 * dt : 3 * dt + 1]
    )


def lanes_of(tok, border, other):
    width = border.shape[1]
    lane = lax.broadcasted_iota(jnp.int32, (1, width), 1)
    return jnp.concatenate(
        [jnp.where(lane + start < tok, border, other) for start in range(0, 2 * tok, width)], axis=1
    )


def first_kernel(tok, heights, scale, kv_ref, par_kv_ref, rest_ref, par_ref, qg, table, s_ref, d_ref):
    y, c, z = place()
    two = 2 * tok
    f32 = jnp.float32
    first, near = c == 0, border_is_own(y, c)
    out = []
    for part in range(3):
        own, par = rest_ref[rows_at(part, tok), :], par_ref[rows_at(part + 2, tok), :]
        tiles = [pick(near, which, own, par) for which in range(2)]
        if part == 2:
            out = jnp.concatenate(tiles, axis=0)
        else:
            for which in range(2):
                qg[part, rows_at(which, tok), :] = tiles[which]
    delta = jnp.sum((qg[1].astype(f32) * out.astype(f32)).T, axis=0, keepdims=True)

    own_flags = rest_ref[pl.ds(3 * tok, 16), :].astype(f32)
    par_flags = par_ref[pl.ds(5 * tok, 16), :].astype(f32)
    lines = []
    for line in range(3):
        inside, at = line_place(z, line, heights)
        centre = jnp.ones_like(own_flags[0:1]) if line == 0 else None
        for slot in range(2):
            if slot == 0:
                own, par = at(own_flags, 1), jnp.where(first, at(par_flags, 0), at(par_flags, 2))
            else:
                own, par = jnp.where(first, at(own_flags, 2), at(own_flags, 0)), at(par_flags, 1)
            if line == 0:
                own, par = (centre, par) if slot == 0 else (own, centre)
            row = lanes_of(tok, pick(near, 0, own, par), pick(near, 1, own, par))
            lines.append(jnp.where(inside, (row - 1.0) * 1e30, -1e30))
    table[...] = jnp.concatenate(lines + [delta, jnp.zeros((1, two), f32)], axis=0)
    for i, source in enumerate((kv_ref, par_kv_ref)):
        rows = rows_at(i, tok)
        s_ref[rows, :] = dot(source[rows_at(0, tok), :], qg[0], ROWS_T) * scale + table[i : i + 1, :]
        d_ref[rows, :] = dot(source[rows_at(1, tok), :], qg[1], ROWS_T) - table[6:7, :]


def largest(tok, blocks):
    top = jnp.full((8, 2 * tok), -1e30, jnp.float32)
    for ref, i in blocks:
        top = jnp.maximum(top, jnp.max(ref[rows_at(i, tok), :].reshape(tok // 8, 8, 2 * tok), axis=0))
    return jnp.max(top, axis=0, keepdims=True)


def summed(tok, blocks, top):
    total = jnp.zeros((8, 2 * tok), jnp.float32)
    for ref, i in blocks:
        weights = jnp.exp(ref[rows_at(i, tok), :] - top)
        total = total + jnp.sum(weights.reshape(tok // 8, 8, 2 * tok), axis=0)
    return jnp.sum(total, axis=0, keepdims=True)


def early_kernel(tok, scale, qg, table, s_own, one_ref, two_ref, s_ref, d_ref, part_ref):
    for i, source in enumerate((one_ref, two_ref)):
        rows = rows_at(i, tok)
        s_ref[rows, :] = dot(source[rows_at(0, tok), :], qg[0], ROWS_T) * scale + table[2 + 2 * i : 3 + 2 * i, :]
        d_ref[rows, :] = dot(source[rows_at(1, tok), :], qg[1], ROWS_T) - table[6:7, :]
    blocks = [(ref, i) for ref in (s_own, s_ref) for i in range(2)]
    top = largest(tok, blocks)
    total = summed(tok, blocks, top)
    part_ref[...] = jnp.concatenate([top, total, jnp.zeros((6, 2 * tok), jnp.float32)], axis=0)


def foreign_rows(ref, part, which, tok):
    block = ref[rows_at(part, tok), :]
    return jnp.concatenate([block, jnp.zeros_like(block)] if which == 0 else [jnp.zeros_like(block), block], axis=0)


def score_kernel(tok, chips, heights, sides, scale, qg, table, part, *refs):
    keys, foreign, refs = refs[:6], refs[6 : 6 + sides], refs[6 + sides :]
    s_late, s_far, *notes = refs
    y, c, z = place()
    near = border_is_own(y, c)
    two = 2 * tok
    f32 = jnp.float32
    far = []
    for which in range(sides):
        rising, y_at = pair(y, which)
        flags = foreign[which][pl.ds(2 * tok, 16), :].astype(f32)
        queries = foreign_rows(foreign[which], 0, which, tok)
        for line in range(3):
            inside, at = line_place(z, line, heights)
            row = jnp.where(rising, at(flags, 0), at(flags, 2))
            none = jnp.zeros_like(row)
            row = lanes_of(tok, *((row, none) if which == 0 else (none, row)))
            bias = jnp.where(inside & within(y_at, chips), (row - 1.0) * 1e30, -1e30)
            border = pick(near, which, keys[2 * line][rows_at(0, tok), :], keys[2 * line + 1][rows_at(0, tok), :])
            s_far[rows_at(3 * which + line, tok), :] = dot(border, queries, ROWS_T) * scale + bias
        blocks = [(s_far, 3 * which + line) for line in range(3)]
        top = largest(tok, blocks)
        far.append([top, summed(tok, blocks, top)])
    for i in range(2):
        scores = dot(keys[3 + 2 * i][rows_at(0, tok), :], qg[0], ROWS_T) * scale
        s_late[rows_at(i, tok), :] = scores + table[3 + 2 * i : 4 + 2 * i, :]
    blocks = [(s_late, i) for i in range(2)]
    top = jnp.maximum(part[0:1, :], largest(tok, blocks))
    total = part[1:2, :] * jnp.exp(part[0:1, :] - top) + summed(tok, blocks, top)
    for which in range(sides):
        notes[which][...] = jnp.concatenate([top, total] + far[which] + [jnp.zeros((4, two), f32)], axis=0)


def middle_kernel(tok, sides, scale, qg, table, s_own, d_own, s_early, d_early, s_late, s_far, *refs):
    tiles, foreign, sent = refs[:6], refs[6 : 6 + sides], refs[6 + sides : 6 + 2 * sides]
    e_ref, ds_ref, e_far, ds_far, dq_ref, *far_dq = refs[6 + 2 * sides :]
    y, c, _ = place()
    near = border_is_own(y, c)
    f32, bf16 = jnp.float32, jnp.bfloat16
    dq = jnp.zeros(dq_ref.shape, f32)
    for line, scores in enumerate(((s_own, s_own), (s_early, s_late), (s_early, s_late))):
        for slot in range(2):
            i, at = 2 * line + slot, rows_at(max(line - 1, 0) if line else slot, tok)
            weights = jnp.exp(scores[slot][at, :] - sent[0][0:1, :])
            if line and slot:
                grads = dot(tiles[i][rows_at(1, tok), :], qg[1], ROWS_T) - table[6:7, :]
            else:
                grads = (d_early if line else d_own)[at, :]
            low = (weights * grads * scale).astype(bf16)
            e_ref[rows_at(i, tok), :] = weights.astype(bf16)
            ds_ref[rows_at(i, tok), :] = low
            dq = dq + dot(tiles[i][rows_at(0, tok), :], low, COLS_T)
    dq_ref[...] = dq
    for which in range(sides):
        far_g = foreign_rows(foreign[which], 1, which, tok)
        delta = foreign_delta(foreign[which], which, tok)
        dq = jnp.zeros(dq_ref.shape, f32)
        for line in range(3):
            rows = rows_at(3 * which + line, tok)
            own, par = tiles[2 * line], tiles[2 * line + 1]
            key, value = (pick(near, which, own[rows_at(i, tok), :], par[rows_at(i, tok), :]) for i in range(2))
            weights = jnp.exp(s_far[rows, :] - sent[which][2:3, :])
            low = (weights * (dot(value, far_g, ROWS_T) - delta) * scale).astype(bf16)
            e_far[rows, :] = weights.astype(bf16)
            ds_far[rows, :] = low
            dq = dq + dot(key, low, COLS_T)
        far_dq[which][...] = dq


def column_sums(tok, near, sides, line, slot, e_ref, ds_ref, e_far, ds_far, scaled, far_scaled):
    rows = rows_at(2 * line + slot, tok)
    sums = [dot(ds_ref[rows, :], scaled[0]), dot(e_ref[rows, :], scaled[1])]
    for which in range(sides):
        rows = rows_at(3 * which + line, tok)
        mine = near == ((slot == 0) == (which == 0))
        for i, ref in enumerate((ds_far, e_far)):
            sums[i] = sums[i] + jnp.where(mine, dot(ref[rows, :], far_scaled[which][i]), 0.0)
    return [part.astype(jnp.bfloat16) for part in sums]


def leave_kernel(tok, chips, sides, qg, e_ref, ds_ref, e_far, ds_far, *refs):
    far_dq, sent, came, foreign = (refs[i * sides : (i + 1) * sides] for i in range(4))
    one_ref, two_ref, scaled, factor_ref, *refs = refs[4 * sides :]
    shares, far_scaled = refs[:sides], refs[sides:]
    y, c, _ = place()
    near = border_is_own(y, c)
    bf16 = jnp.bfloat16
    width = qg.shape[2]

    def log_total(top, total, other_top, other_total):
        both = jnp.maximum(top, other_top)
        return both + jnp.log(total * jnp.exp(top - both) + other_total * jnp.exp(other_top - both))

    def times(block, factor):
        return (block.astype(jnp.float32) * jnp.broadcast_to(factor, (width, 2 * tok)).T).astype(bf16)

    top, total = sent[0][0:1, :], sent[0][1:2, :]
    lse = None
    for which in range(sides):
        _, y_at = pair(y, which)
        inside = within(y_at, chips)
        note = came[which]
        far_lse = log_total(note[0:1, :], note[1:2, :], sent[which][2:3, :], sent[which][3:4, :])
        factor = jnp.where(inside, jnp.exp(sent[which][2:3, :] - far_lse), 0.0)
        share = (far_dq[which][...] * factor).T
        shares[which][...] = share[which * tok : (which + 1) * tok].astype(bf16)
        for part in range(2):
            far_scaled[which][part] = times(foreign_rows(foreign[which], part, which, tok), factor)
        other = jnp.where(inside, note[2:3, :], -1e30), jnp.where(inside, note[3:4, :], 0.0)
        lse = log_total(top, total, *other) if which == 0 else log_total(lse, jnp.ones_like(lse), *other)
    factor = jnp.exp(top - lse)
    factor_ref[...] = jnp.broadcast_to(factor, factor_ref.shape)
    for part in range(2):
        scaled[part] = times(qg[part], factor)
    for line, result in ((1, one_ref), (2, two_ref)):
        for slot in range(2):
            sums = column_sums(tok, near, sides, line, slot, e_ref, ds_ref, e_far, ds_far, scaled, far_scaled)
            for i in range(2):
                result[i, rows_at(slot, tok), :] = sums[i]


def stay_kernel(tok, sides, e_ref, ds_ref, e_far, ds_far, scaled, factor_ref, raw_dq, *refs):
    far_scaled, (own_ref, dq_ref) = refs[:sides], refs[sides:]
    y, c, _ = place()
    near = border_is_own(y, c)
    for slot in range(2):
        sums = column_sums(tok, near, sides, 0, slot, e_ref, ds_ref, e_far, ds_far, scaled, far_scaled)
        for i in range(2):
            own_ref[i, rows_at(slot, tok), :] = sums[i]
    dq_ref[...] = (raw_dq[...] * factor_ref[0:1, :]).T


def sum_kernel(tok, chips, heights, sides, own_ref, one_ref, two_ref, dq_ref, *refs):
    backs, (mine_ref, mine_q_ref, swap_ref) = refs[:sides], refs[sides:]
    y, c, z = place()
    near = border_is_own(y, c)
    f32, bf16 = jnp.float32, jnp.bfloat16
    for i in range(2):
        for slot in range(2):
            rows = rows_at(slot, tok)
            value = own_ref[i, rows, :].astype(f32)
            for line, ref in ((1, one_ref), (2, two_ref)):
                inside, _ = line_place(z, line, heights)
                value = value + jnp.where(inside, ref[i, rows, :].astype(f32), 0.0)
            if slot == 0:
                mine_ref[i] = value.astype(bf16)
            else:
                swap_ref[i] = value.astype(bf16)
    tiles = []
    for tile in range(2):
        value = dq_ref[rows_at(tile, tok), :]
        if tile < sides:
            _, y_at = pair(y, tile)
            value = value + jnp.where(within(y_at, chips), backs[tile][...].astype(f32), 0.0)
        tiles.append(value.astype(bf16))
    mine_q_ref[...] = jnp.where(near, tiles[0], tiles[1])
    swap_ref[2] = jnp.where(near, tiles[1], tiles[0])


def final_kernel(mine_ref, swap_ref, mine_q_ref, gq_ref, gk_ref, gv_ref):
    _, c, _ = place()
    gq_ref[0, 0, c, 0] = mine_q_ref[...]
    gq_ref[0, 0, 1 - c, 0] = swap_ref[2]
    for i, ref in enumerate((gk_ref, gv_ref)):
        ref[0, 0, c, 0] = mine_ref[i]
        ref[0, 0, 1 - c, 0] = swap_ref[i]


def body(queries, keys, values, grad_out, attn_out, window_mask):
    tok, width = queries.shape[-2:]
    scale = width ** -0.5
    times, heights = lax.axis_size("tm"), lax.axis_size("height")
    chips = times // 2
    sides = 1 if chips == 2 else 2
    bf16, f32 = jnp.bfloat16, jnp.float32

    def call(kernel, shapes, specs, scratch=()):
        return pl.pallas_call(
            kernel,
            out_shape=[jax.ShapeDtypeStruct(*shape) for shape in shapes],
            in_specs=list(specs),
            out_specs=[VMEM] * len(shapes),
            scratch_shapes=list(scratch),
            compiler_params=LIMIT,
        )

    def partner(index, which, size):
        if which is None:
            return index
        at = index + 1 if index % 2 == which else index - 1
        return at if 0 <= at < size else None

    def exchange(block, y_which, z_which):
        pairs = []
        for t in range(times):
            for z in range(heights):
                y_at, z_at = partner(t // 2, y_which, chips), partner(z, z_which, heights)
                at = t * heights + z
                alone = y_at is None or z_at is None
                pairs.append((at, (t ^ 1) * heights + z if alone else (2 * y_at + t % 2) * heights + z_at))
        return lax.ppermute(block, ("tm", "height"), pairs)

    def swap_cores(block):
        return lax.ppermute(block, "tm", [(t, t ^ 1) for t in range(times)])

    line_shape, tile_shape = ((2, 2 * tok, width), bf16), ((2, tok, width), bf16)
    extra = 32
    arguments = (keys, values, queries, grad_out, attn_out, window_mask)
    kv, rest, other = call(
        functools.partial(pack_kernel, tok),
        [((2 * tok + extra, width), bf16), ((3 * tok + 16, width), bf16), ((5 * tok + 16, width), bf16)],
        [HBM] * 6,
        [pltpu.SMEM(window_mask.shape, jnp.int32), pltpu.SemaphoreType.DMA((11,))],
    )(*(pltpu.with_memory_space_constraint(x, pltpu.HBM) for x in arguments))
    early = [exchange(kv, None, which) for which in range(2)]
    par = swap_cores(other)
    border_shape, two = ((2 * tok + 16, width), bf16), 2 * tok
    par_kv, *borders = call(
        functools.partial(line_kernel, tok), [((2 * tok, width), bf16)] + [border_shape] * sides, [VMEM] * 2
    )(rest, par)
    foreign = [exchange(borders[which], which, None) for which in range(sides)]
    late = [exchange(par_kv, None, which) for which in range(2)]
    tiles = (kv, par_kv, early[0], late[0], early[1], late[1])
    pair_shape, note_shape, raw_shape = ((2, two, width), bf16), ((8, two), f32), ((width, two), f32)

    def square(count, kind=f32):
        return ((count * tok, two), kind)

    qg, table, s_own, d_own = call(
        functools.partial(first_kernel, tok, heights, scale),
        [pair_shape, note_shape, square(2), square(2)],
        [VMEM] * 4,
    )(kv, par_kv, rest, par)
    s_early, d_early, part = call(
        functools.partial(early_kernel, tok, scale), [square(2), square(2), note_shape], [VMEM] * 5
    )(qg, table, s_own, *early)
    s_late, s_far, *sent = call(
        functools.partial(score_kernel, tok, chips, heights, sides, scale),
        [square(2), square(3 * sides)] + [note_shape] * sides,
        [VMEM] * (9 + sides),
    )(qg, table, part, *tiles, *foreign)
    came = [exchange(sent[which], which, None) for which in range(sides)]
    e, ds, e_far, ds_far, raw_dq, *far_dq = call(
        functools.partial(middle_kernel, tok, sides, scale),
        [square(6, bf16)] * 2 + [square(3 * sides, bf16)] * 2 + [raw_shape] * (1 + sides),
        [VMEM] * (14 + 2 * sides),
    )(qg, table, s_own, d_own, s_early, d_early, s_late, s_far, *tiles, *foreign, *sent)
    one, other_one, scaled, factor, *rest_out = call(
        functools.partial(leave_kernel, tok, chips, sides),
        [line_shape, line_shape, pair_shape, note_shape] + [((tok, width), bf16)] * sides + [pair_shape] * sides,
        [VMEM] * (5 + 4 * sides),
    )(qg, e, ds, e_far, ds_far, *far_dq, *sent, *came, *foreign)
    shares, far_scaled = rest_out[:sides], rest_out[sides:]
    back = [exchange(block, None, which) for which, block in enumerate((one, other_one))]
    shares = [exchange(share, which, None) for which, share in enumerate(shares)]
    own, dq = call(
        functools.partial(stay_kernel, tok, sides),
        [line_shape, ((two, width), f32)],
        [VMEM] * (7 + sides),
    )(e, ds, e_far, ds_far, scaled, factor, raw_dq, *far_scaled)
    mine, mine_q, leaving = call(
        functools.partial(sum_kernel, tok, chips, heights, sides),
        [tile_shape, ((tok, width), bf16), ((3, tok, width), bf16)],
        [VMEM] * (4 + sides),
    )(own, *back, dq, *shares)
    return call(final_kernel, [(queries.shape, bf16)] * 3, [VMEM] * 3)(mine, swap_cores(leaving), mine_q)


def solution(mesh):
    placed = P("tm", "height", "dp", None, None, None)
    return jax.shard_map(
        body,
        mesh=mesh,
        in_specs=(placed,) * 5 + (P("tm", "height", None, None),),
        out_specs=(placed,) * 3,
        check_vma=False,
    )
```

```python
import functools

import jax
import jax.numpy as jnp
from jax import lax
from jax.experimental import pallas as pl
from jax.experimental.pallas import tpu as pltpu
from jax.sharding import PartitionSpec as P

VMEM = pl.BlockSpec(memory_space=pltpu.VMEM)
HBM = pl.BlockSpec(memory_space=pltpu.HBM)
LIMIT = pltpu.CompilerParams(vmem_limit_bytes=32 * 1024 * 1024)
ROWS_T = (((1,), (1,)), ((), ()))
COLS_T = (((0,), (0,)), ((), ()))


def dot(a, b, dims=(((1,), (0,)), ((), ()))):
    return lax.dot_general(a, b, dims, preferred_element_type=jnp.float32)


def place():
    t = lax.axis_index("tm")
    return t // 2, t % 2, lax.axis_index("height")


def pair(index, which):
    rising = (index % 2) == (0 if which == 0 else 1)
    return rising, jnp.where(rising, index + 1, index - 1)


def within(index, size):
    return (index >= 0) & (index < size)


def pack_kernel(tok, k_ref, v_ref, q_ref, g_ref, o_ref, mask_ref, kv_ref, rest_ref, other_ref, flags, sems):
    _, c, _ = place()
    copies = [pltpu.make_async_copy(mask_ref, flags, sems.at[10])]
    for i, ref in enumerate((k_ref, v_ref, q_ref, g_ref, o_ref)):
        own = (kv_ref if i < 2 else rest_ref).at[pl.ds((i if i < 2 else i - 2) * tok, tok), :]
        copies.append(pltpu.make_async_copy(ref.at[0, 0, c, 0], own, sems.at[2 * i + 1]))
        copies.append(
            pltpu.make_async_copy(ref.at[0, 0, 1 - c, 0], other_ref.at[pl.ds(i * tok, tok), :], sems.at[2 * i])
        )
    for copy in copies:
        copy.start()
    copies[0].wait()
    row = lax.broadcasted_iota(jnp.int32, (16, rest_ref.shape[1]), 0)
    spread = jnp.zeros(row.shape, jnp.float32)
    for i in range(9):
        on = (flags[0, 0, 0, 9 * (i // 3) + 3 * (i % 3) + 1] != 0).astype(jnp.float32)
        spread = jnp.where(row == i, on, spread)
    rest_ref[pl.ds(3 * tok, 16), :] = spread.astype(jnp.bfloat16)
    other_ref[pl.ds(5 * tok, 16), :] = spread.astype(jnp.bfloat16)
    for copy in copies[1:]:
        copy.wait()


def rows_at(index, tok):
    return pl.ds(index * tok, tok)


def border_is_own(y, c):
    rising, _ = pair(y, 0)
    return (c == 1) == rising


def pick(near, which, own, par):
    return jnp.where(near, own, par) if which == 0 else jnp.where(near, par, own)


def line_kernel(tok, rest_ref, par_ref, par_kv_ref, *border_refs):
    y, c, _ = place()
    near = border_is_own(y, c)
    for i in range(2):
        par_kv_ref[rows_at(i, tok), :] = par_ref[rows_at(i, tok), :]
    width = par_ref.shape[1]
    f32 = jnp.float32
    for which, ref in enumerate(border_refs):
        tiles = [pick(near, which, rest_ref[rows_at(i, tok), :], par_ref[rows_at(i + 2, tok), :]) for i in range(3)]
        ref[rows_at(0, tok), :], ref[rows_at(1, tok), :] = tiles[0], tiles[1]
        flags = pick(near, which, rest_ref[pl.ds(3 * tok, 16), :], par_ref[pl.ds(5 * tok, 16), :]).astype(f32)
        product, gap = tiles[1].astype(f32) * tiles[2].astype(f32), jnp.zeros((2 * width - tok, width), f32)
        product = jnp.concatenate([product, gap] if which == 0 else [gap, product], axis=0)
        left, lines = jnp.sum(product.T, axis=0, keepdims=True), [flags[0:9]]
        for _ in range(3):
            term = left.astype(jnp.bfloat16).astype(f32)
            left = left - term
            lines += [term[:, :width], term[:, width:]]
        ref[pl.ds(2 * tok, 16), :] = jnp.concatenate(lines + [jnp.zeros((1, width), f32)], axis=0).astype(jnp.bfloat16)


def foreign_delta(ref, tok):
    terms = ref[pl.ds(2 * tok, 16), :].astype(jnp.float32)
    return jnp.concatenate(
        [sum(terms[9 + 2 * i + half : 10 + 2 * i + half] for i in range(3)) for half in range(2)], axis=1
    )


def line_place(z, line, heights):
    if line == 0:
        return True, lambda flags, dt: flags[3 * dt + 1 : 3 * dt + 2]
    rising, at = pair(z, line - 1)
    return within(at, heights), lambda flags, dt: jnp.where(
        rising, flags[3 * dt + 2 : 3 * dt + 3], flags[3 * dt : 3 * dt + 1]
    )


def lanes_of(tok, border, other):
    width = border.shape[1]
    lane = lax.broadcasted_iota(jnp.int32, (1, width), 1)
    return jnp.concatenate(
        [jnp.where(lane + start < tok, border, other) for start in range(0, 2 * tok, width)], axis=1
    )


def first_kernel(tok, heights, scale, kv_ref, par_kv_ref, rest_ref, par_ref, qg, table, s_ref, d_ref):
    y, c, z = place()
    two = 2 * tok
    f32 = jnp.float32
    first, near = c == 0, border_is_own(y, c)
    out = []
    for part in range(3):
        own, par = rest_ref[rows_at(part, tok), :], par_ref[rows_at(part + 2, tok), :]
        tiles = [pick(near, which, own, par) for which in range(2)]
        if part == 2:
            out = jnp.concatenate(tiles, axis=0)
        else:
            for which in range(2):
                qg[part, rows_at(which, tok), :] = tiles[which]
    delta = jnp.sum((qg[1].astype(f32) * out.astype(f32)).T, axis=0, keepdims=True)

    own_flags = rest_ref[pl.ds(3 * tok, 16), :].astype(f32)
    par_flags = par_ref[pl.ds(5 * tok, 16), :].astype(f32)
    lines = []
    for line in range(3):
        inside, at = line_place(z, line, heights)
        centre = jnp.ones_like(own_flags[0:1]) if line == 0 else None
        for slot in range(2):
            if slot == 0:
                own, par = at(own_flags, 1), jnp.where(first, at(par_flags, 0), at(par_flags, 2))
            else:
                own, par = jnp.where(first, at(own_flags, 2), at(own_flags, 0)), at(par_flags, 1)
            if line == 0:
                own, par = (centre, par) if slot == 0 else (own, centre)
            row = lanes_of(tok, pick(near, 0, own, par), pick(near, 1, own, par))
            lines.append(jnp.where(inside, (row - 1.0) * 1e30, -1e30))
    table[...] = jnp.concatenate(lines + [delta, jnp.zeros((1, two), f32)], axis=0)
    for i, source in enumerate((kv_ref, par_kv_ref)):
        rows = rows_at(i, tok)
        s_ref[rows, :] = dot(source[rows_at(0, tok), :], qg[0], ROWS_T) * scale + table[i : i + 1, :]
        d_ref[rows, :] = dot(source[rows_at(1, tok), :], qg[1], ROWS_T) - table[6:7, :]


def largest(tok, blocks):
    lanes = blocks[0][0].shape[1]
    top = jnp.full((8, lanes), -1e30, jnp.float32)
    for ref, i in blocks:
        top = jnp.maximum(top, jnp.max(ref[rows_at(i, tok), :].reshape(tok // 8, 8, lanes), axis=0))
    return jnp.max(top, axis=0, keepdims=True)


def summed(tok, blocks, top):
    lanes = blocks[0][0].shape[1]
    total = jnp.zeros((8, lanes), jnp.float32)
    for ref, i in blocks:
        weights = jnp.exp(ref[rows_at(i, tok), :] - top)
        total = total + jnp.sum(weights.reshape(tok // 8, 8, lanes), axis=0)
    return jnp.sum(total, axis=0, keepdims=True)


def early_kernel(tok, scale, qg, table, s_own, one_ref, two_ref, s_ref, d_ref, part_ref):
    for i, source in enumerate((one_ref, two_ref)):
        rows = rows_at(i, tok)
        s_ref[rows, :] = dot(source[rows_at(0, tok), :], qg[0], ROWS_T) * scale + table[2 + 2 * i : 3 + 2 * i, :]
        d_ref[rows, :] = dot(source[rows_at(1, tok), :], qg[1], ROWS_T) - table[6:7, :]
    blocks = [(ref, i) for ref in (s_own, s_ref) for i in range(2)]
    top = largest(tok, blocks)
    total = summed(tok, blocks, top)
    part_ref[...] = jnp.concatenate([top, total, jnp.zeros((6, 2 * tok), jnp.float32)], axis=0)


def foreign_rows(ref, part, which, tok):
    block = ref[rows_at(part, tok), :]
    gap = jnp.zeros((2 * block.shape[1] - tok, block.shape[1]), block.dtype)
    return jnp.concatenate([block, gap] if which == 0 else [gap, block], axis=0)


def foreign_lanes(which, tok, width):
    return slice(0, 2 * width) if which == 0 else slice(2 * tok - 2 * width, 2 * tok)


def to_lanes(which, tok, row, fill):
    gap = jnp.full((1, 2 * tok - row.shape[1]), fill, jnp.float32)
    return jnp.concatenate([row, gap] if which == 0 else [gap, row], axis=1)


def score_kernel(tok, chips, heights, sides, scale, qg, table, part, *refs):
    keys, foreign, refs = refs[:6], refs[6 : 6 + sides], refs[6 + sides :]
    s_late, s_far, *notes = refs
    y, c, z = place()
    near = border_is_own(y, c)
    two = 2 * tok
    f32 = jnp.float32
    far = []
    for which in range(sides):
        rising, y_at = pair(y, which)
        flags = foreign[which][pl.ds(2 * tok, 16), :].astype(f32)
        queries = foreign_rows(foreign[which], 0, which, tok)
        for line in range(3):
            inside, at = line_place(z, line, heights)
            row = jnp.where(rising, at(flags, 0), at(flags, 2))
            lane = lax.broadcasted_iota(jnp.int32, row.shape, 1)
            width = row.shape[1]
            row = jnp.concatenate(
                [
                    jnp.where(lane + start < tok if which == 0 else lane + start >= 2 * width - tok, row, 0.0)
                    for start in (0, width)
                ],
                axis=1,
            )
            bias = jnp.where(inside & within(y_at, chips), (row - 1.0) * 1e30, -1e30)
            border = pick(near, which, keys[2 * line][rows_at(0, tok), :], keys[2 * line + 1][rows_at(0, tok), :])
            s_far[rows_at(3 * which + line, tok), :] = dot(border, queries, ROWS_T) * scale + bias
        blocks = [(s_far, 3 * which + line) for line in range(3)]
        top = largest(tok, blocks)
        far.append([to_lanes(which, tok, top, -1e30), to_lanes(which, tok, summed(tok, blocks, top), 0.0)])
    for i in range(2):
        scores = dot(keys[3 + 2 * i][rows_at(0, tok), :], qg[0], ROWS_T) * scale
        s_late[rows_at(i, tok), :] = scores + table[3 + 2 * i : 4 + 2 * i, :]
    blocks = [(s_late, i) for i in range(2)]
    top = jnp.maximum(part[0:1, :], largest(tok, blocks))
    total = part[1:2, :] * jnp.exp(part[0:1, :] - top) + summed(tok, blocks, top)
    for which in range(sides):
        notes[which][...] = jnp.concatenate([top, total] + far[which] + [jnp.zeros((4, two), f32)], axis=0)


def middle_kernel(tok, sides, scale, qg, table, s_own, d_own, s_early, d_early, s_late, s_far, *refs):
    tiles, foreign, sent = refs[:6], refs[6 : 6 + sides], refs[6 + sides : 6 + 2 * sides]
    e_ref, ds_ref, e_far, ds_far, dq_ref, *far_dq = refs[6 + 2 * sides :]
    y, c, _ = place()
    near = border_is_own(y, c)
    f32, bf16 = jnp.float32, jnp.bfloat16
    dq = jnp.zeros(dq_ref.shape, f32)
    for line, scores in enumerate(((s_own, s_own), (s_early, s_late), (s_early, s_late))):
        for slot in range(2):
            i, at = 2 * line + slot, rows_at(max(line - 1, 0) if line else slot, tok)
            weights = jnp.exp(scores[slot][at, :] - sent[0][0:1, :])
            if line and slot:
                grads = dot(tiles[i][rows_at(1, tok), :], qg[1], ROWS_T) - table[6:7, :]
            else:
                grads = (d_early if line else d_own)[at, :]
            low = (weights * grads * scale).astype(bf16)
            e_ref[rows_at(i, tok), :] = weights.astype(bf16)
            ds_ref[rows_at(i, tok), :] = low
            dq = dq + dot(tiles[i][rows_at(0, tok), :], low, COLS_T)
    dq_ref[...] = dq
    for which in range(sides):
        far_g = foreign_rows(foreign[which], 1, which, tok)
        delta = foreign_delta(foreign[which], tok)
        lanes = foreign_lanes(which, tok, qg.shape[2])
        dq = jnp.zeros(far_dq[which].shape, f32)
        for line in range(3):
            rows = rows_at(3 * which + line, tok)
            own, par = tiles[2 * line], tiles[2 * line + 1]
            key, value = (pick(near, which, own[rows_at(i, tok), :], par[rows_at(i, tok), :]) for i in range(2))
            weights = jnp.exp(s_far[rows, :] - sent[which][2:3, lanes])
            low = (weights * (dot(value, far_g, ROWS_T) - delta) * scale).astype(bf16)
            e_far[rows, :] = weights.astype(bf16)
            ds_far[rows, :] = low
            dq = dq + dot(key, low, COLS_T)
        far_dq[which][...] = dq


def column_sums(tok, near, sides, line, e_ref, ds_ref, e_far, ds_far, scaled, far_scaled):
    rows = [rows_at(2 * line + slot, tok) for slot in range(2)]
    sums = [[dot(ref[at, :], scaled[i]) for i, ref in enumerate((ds_ref, e_ref))] for at in rows]
    for which in range(sides):
        at = rows_at(3 * which + line, tok)
        for i, ref in enumerate((ds_far, e_far)):
            far = dot(ref[at, :], far_scaled[which][i])
            for slot in range(2):
                mine = near == ((slot == 0) == (which == 0))
                sums[slot][i] = sums[slot][i] + jnp.where(mine, far, 0.0)
    return [[part.astype(jnp.bfloat16) for part in pair] for pair in sums]


def leave_kernel(tok, chips, sides, qg, e_ref, ds_ref, e_far, ds_far, *refs):
    far_dq, sent, came, foreign = (refs[i * sides : (i + 1) * sides] for i in range(4))
    one_ref, two_ref, scaled, factor_ref, *refs = refs[4 * sides :]
    shares, far_scaled = refs[:sides], refs[sides:]
    y, c, _ = place()
    near = border_is_own(y, c)
    bf16 = jnp.bfloat16
    width = qg.shape[2]

    def log_total(top, total, other_top, other_total):
        both = jnp.maximum(top, other_top)
        return both + jnp.log(total * jnp.exp(top - both) + other_total * jnp.exp(other_top - both))

    def times(block, factor):
        return (block.astype(jnp.float32) * jnp.broadcast_to(factor, (width, factor.shape[1])).T).astype(bf16)

    top, total = sent[0][0:1, :], sent[0][1:2, :]
    lse = None
    for which in range(sides):
        _, y_at = pair(y, which)
        inside = within(y_at, chips)
        note = came[which]
        far_lse = log_total(note[0:1, :], note[1:2, :], sent[which][2:3, :], sent[which][3:4, :])
        lanes = foreign_lanes(which, tok, width)
        factor = jnp.where(inside, jnp.exp(sent[which][2:3, lanes] - far_lse[:, lanes]), 0.0)
        share = (far_dq[which][...] * factor).T
        shares[which][...] = (share[:tok] if which == 0 else share[2 * width - tok :]).astype(bf16)
        for part in range(2):
            far_scaled[which][part] = times(foreign_rows(foreign[which], part, which, tok), factor)
        other = jnp.where(inside, note[2:3, :], -1e30), jnp.where(inside, note[3:4, :], 0.0)
        lse = log_total(top, total, *other) if which == 0 else log_total(lse, jnp.ones_like(lse), *other)
    factor = jnp.exp(top - lse)
    factor_ref[...] = jnp.broadcast_to(factor, factor_ref.shape)
    for part in range(2):
        scaled[part] = times(qg[part], factor)
    for line, result in ((1, one_ref), (2, two_ref)):
        sums = column_sums(tok, near, sides, line, e_ref, ds_ref, e_far, ds_far, scaled, far_scaled)
        for slot in range(2):
            for i in range(2):
                result[i, rows_at(slot, tok), :] = sums[slot][i]


def stay_kernel(tok, sides, e_ref, ds_ref, e_far, ds_far, scaled, factor_ref, raw_dq, *refs):
    far_scaled, (own_ref, dq_ref) = refs[:sides], refs[sides:]
    y, c, _ = place()
    near = border_is_own(y, c)
    sums = column_sums(tok, near, sides, 0, e_ref, ds_ref, e_far, ds_far, scaled, far_scaled)
    for slot in range(2):
        for i in range(2):
            own_ref[i, rows_at(slot, tok), :] = sums[slot][i]
    dq_ref[...] = (raw_dq[...] * factor_ref[0:1, :]).T


def sum_kernel(tok, chips, heights, sides, own_ref, one_ref, two_ref, dq_ref, *refs):
    backs, (mine_ref, mine_q_ref, swap_ref) = refs[:sides], refs[sides:]
    y, c, z = place()
    near = border_is_own(y, c)
    f32, bf16 = jnp.float32, jnp.bfloat16
    for i in range(2):
        for slot in range(2):
            rows = rows_at(slot, tok)
            value = own_ref[i, rows, :].astype(f32)
            for line, ref in ((1, one_ref), (2, two_ref)):
                inside, _ = line_place(z, line, heights)
                value = value + jnp.where(inside, ref[i, rows, :].astype(f32), 0.0)
            if slot == 0:
                mine_ref[i] = value.astype(bf16)
            else:
                swap_ref[i] = value.astype(bf16)
    tiles = []
    for tile in range(2):
        value = dq_ref[rows_at(tile, tok), :]
        if tile < sides:
            _, y_at = pair(y, tile)
            value = value + jnp.where(within(y_at, chips), backs[tile][...].astype(f32), 0.0)
        tiles.append(value.astype(bf16))
    mine_q_ref[...] = jnp.where(near, tiles[0], tiles[1])
    swap_ref[2] = jnp.where(near, tiles[1], tiles[0])


def final_kernel(mine_ref, swap_ref, mine_q_ref, gq_ref, gk_ref, gv_ref):
    _, c, _ = place()
    gq_ref[0, 0, c, 0] = mine_q_ref[...]
    gq_ref[0, 0, 1 - c, 0] = swap_ref[2]
    for i, ref in enumerate((gk_ref, gv_ref)):
        ref[0, 0, c, 0] = mine_ref[i]
        ref[0, 0, 1 - c, 0] = swap_ref[i]


def body(queries, keys, values, grad_out, attn_out, window_mask):
    tok, width = queries.shape[-2:]
    scale = width ** -0.5
    times, heights = lax.axis_size("tm"), lax.axis_size("height")
    chips = times // 2
    sides = 1 if chips == 2 else 2
    bf16, f32 = jnp.bfloat16, jnp.float32

    def call(kernel, shapes, specs, scratch=()):
        return pl.pallas_call(
            kernel,
            out_shape=[jax.ShapeDtypeStruct(*shape) for shape in shapes],
            in_specs=list(specs),
            out_specs=[VMEM] * len(shapes),
            scratch_shapes=list(scratch),
            compiler_params=LIMIT,
        )

    def partner(index, which, size):
        if which is None:
            return index
        at = index + 1 if index % 2 == which else index - 1
        return at if 0 <= at < size else None

    def exchange(block, y_which, z_which):
        pairs = []
        for t in range(times):
            for z in range(heights):
                y_at, z_at = partner(t // 2, y_which, chips), partner(z, z_which, heights)
                at = t * heights + z
                alone = y_at is None or z_at is None
                pairs.append((at, (t ^ 1) * heights + z if alone else (2 * y_at + t % 2) * heights + z_at))
        return lax.ppermute(block, ("tm", "height"), pairs)

    def swap_cores(block):
        return lax.ppermute(block, "tm", [(t, t ^ 1) for t in range(times)])

    line_shape, tile_shape = ((2, 2 * tok, width), bf16), ((2, tok, width), bf16)
    extra = 48
    arguments = (keys, values, queries, grad_out, attn_out, window_mask)
    kv, rest, other = call(
        functools.partial(pack_kernel, tok),
        [((2 * tok + extra, width), bf16), ((3 * tok + 16, width), bf16), ((5 * tok + 16, width), bf16)],
        [HBM] * 6,
        [pltpu.SMEM(window_mask.shape, jnp.int32), pltpu.SemaphoreType.DMA((11,))],
    )(*(pltpu.with_memory_space_constraint(x, pltpu.HBM) for x in arguments))
    early = [exchange(kv, None, which) for which in range(2)]
    par = swap_cores(other)
    border_shape, two = ((2 * tok + 16, width), bf16), 2 * tok
    par_kv, *borders = call(
        functools.partial(line_kernel, tok), [((2 * tok + 32, width), bf16)] + [border_shape] * sides, [VMEM] * 2
    )(rest, par)
    foreign = [exchange(borders[which], which, None) for which in range(sides)]
    late = [exchange(par_kv, None, which) for which in range(2)]
    tiles = (kv, par_kv, early[0], late[0], early[1], late[1])
    pair_shape, note_shape, raw_shape = ((2, two, width), bf16), ((8, two), f32), ((width, two), f32)

    def square(count, kind=f32):
        return ((count * tok, two), kind)

    def far_square(kind=f32):
        return ((3 * sides * tok, 2 * width), kind)

    qg, table, s_own, d_own = call(
        functools.partial(first_kernel, tok, heights, scale),
        [pair_shape, note_shape, square(2), square(2)],
        [VMEM] * 4,
    )(kv, par_kv, rest, par)
    s_early, d_early, part = call(
        functools.partial(early_kernel, tok, scale), [square(2), square(2), note_shape], [VMEM] * 5
    )(qg, table, s_own, *early)
    s_late, s_far, *sent = call(
        functools.partial(score_kernel, tok, chips, heights, sides, scale),
        [square(2), far_square()] + [note_shape] * sides,
        [VMEM] * (9 + sides),
    )(qg, table, part, *tiles, *foreign)
    came = [exchange(sent[which], which, None) for which in range(sides)]
    e, ds, e_far, ds_far, raw_dq, *far_dq = call(
        functools.partial(middle_kernel, tok, sides, scale),
        [square(6, bf16)] * 2 + [far_square(bf16)] * 2 + [raw_shape] + [((width, 2 * width), f32)] * sides,
        [VMEM] * (14 + 2 * sides),
    )(qg, table, s_own, d_own, s_early, d_early, s_late, s_far, *tiles, *foreign, *sent)
    one, other_one, scaled, factor, *rest_out = call(
        functools.partial(leave_kernel, tok, chips, sides),
        [line_shape, line_shape, pair_shape, note_shape] + [((tok, width), bf16)] * sides + [((2, 2 * width, width), bf16)] * sides,
        [VMEM] * (5 + 4 * sides),
    )(qg, e, ds, e_far, ds_far, *far_dq, *sent, *came, *foreign)
    shares, far_scaled = rest_out[:sides], rest_out[sides:]
    back = [exchange(block, None, which) for which, block in enumerate((one, other_one))]
    shares = [exchange(share, which, None) for which, share in enumerate(shares)]
    own, dq = call(
        functools.partial(stay_kernel, tok, sides),
        [line_shape, ((two, width), f32)],
        [VMEM] * (7 + sides),
    )(e, ds, e_far, ds_far, scaled, factor, raw_dq, *far_scaled)
    mine, mine_q, leaving = call(
        functools.partial(sum_kernel, tok, chips, heights, sides),
        [tile_shape, ((tok, width), bf16), ((3, tok, width), bf16)],
        [VMEM] * (4 + sides),
    )(own, *back, dq, *shares)
    return call(final_kernel, [(queries.shape, bf16)] * 3, [VMEM] * 3)(mine, swap_cores(leaving), mine_q)


def solution(mesh):
    placed = P("tm", "height", "dp", None, None, None)
    return jax.shard_map(
        body,
        mesh=mesh,
        in_specs=(placed,) * 5 + (P("tm", "height", None, None),),
        out_specs=(placed,) * 3,
        check_vma=False,
    )
```

```python
import functools

import jax
import jax.numpy as jnp
from jax import lax
from jax.experimental import pallas as pl
from jax.experimental.pallas import tpu as pltpu
from jax.sharding import PartitionSpec as P

VMEM = pl.BlockSpec(memory_space=pltpu.VMEM)
HBM = pl.BlockSpec(memory_space=pltpu.HBM)
LIMIT = pltpu.CompilerParams(vmem_limit_bytes=32 * 1024 * 1024)
ROWS_T = (((1,), (1,)), ((), ()))
COLS_T = (((0,), (0,)), ((), ()))


def dot(a, b, dims=(((1,), (0,)), ((), ()))):
    return lax.dot_general(a, b, dims, preferred_element_type=jnp.float32)


LATE, EARLY = 0, 1


def place():
    t = lax.axis_index("tm")
    return t // 2, t % 2, lax.axis_index("height")


def head_at():
    y, c, z = place()
    return (c + y + z) % 2


def pair(index, which):
    rising = (index % 2) == (0 if which == 0 else 1)
    return rising, jnp.where(rising, index + 1, index - 1)


def within(index, size):
    return (index >= 0) & (index < size)


def pack_kernel(tok, k_ref, v_ref, q_ref, g_ref, o_ref, mask_ref, kv_ref, rest_ref, other_ref, flags, sems):
    head = head_at()
    copies = [pltpu.make_async_copy(mask_ref, flags, sems.at[10])]
    for i, ref in enumerate((k_ref, v_ref, q_ref, g_ref, o_ref)):
        own = (kv_ref if i < 2 else rest_ref).at[pl.ds((i if i < 2 else i - 2) * tok, tok), :]
        copies.append(pltpu.make_async_copy(ref.at[0, 0, head, 0], own, sems.at[2 * i + 1]))
        copies.append(
            pltpu.make_async_copy(ref.at[0, 0, 1 - head, 0], other_ref.at[pl.ds(i * tok, tok), :], sems.at[2 * i])
        )
    for copy in copies:
        copy.start()
    copies[0].wait()
    row = lax.broadcasted_iota(jnp.int32, (16, rest_ref.shape[1]), 0)
    spread = jnp.zeros(row.shape, jnp.float32)
    for i in range(9):
        on = (flags[0, 0, 0, 9 * (i // 3) + 3 * (i % 3) + 1] != 0).astype(jnp.float32)
        spread = jnp.where(row == i, on, spread)
    rest_ref[pl.ds(3 * tok, 16), :] = spread.astype(jnp.bfloat16)
    other_ref[pl.ds(5 * tok, 16), :] = spread.astype(jnp.bfloat16)
    for copy in copies[1:]:
        copy.wait()


def rows_at(index, tok):
    return pl.ds(index * tok, tok)


def border_is_own(y, c):
    rising, _ = pair(y, 0)
    return (c == 1) == rising


def pick(near, which, own, par):
    return jnp.where(near, own, par) if which == 0 else jnp.where(near, par, own)


def line_kernel(tok, rest_ref, par_ref, par_kv_ref, *border_refs):
    y, c, _ = place()
    near = border_is_own(y, c)
    for i in range(2):
        par_kv_ref[rows_at(i, tok), :] = par_ref[rows_at(i, tok), :]
    width = par_ref.shape[1]
    f32 = jnp.float32
    for which, ref in enumerate(border_refs):
        tiles = [pick(near, which, rest_ref[rows_at(i, tok), :], par_ref[rows_at(i + 2, tok), :]) for i in range(3)]
        ref[rows_at(0, tok), :], ref[rows_at(1, tok), :] = tiles[0], tiles[1]
        flags = pick(near, which, rest_ref[pl.ds(3 * tok, 16), :], par_ref[pl.ds(5 * tok, 16), :]).astype(f32)
        product, gap = tiles[1].astype(f32) * tiles[2].astype(f32), jnp.zeros((2 * width - tok, width), f32)
        product = jnp.concatenate([product, gap] if which == 0 else [gap, product], axis=0)
        left, lines = jnp.sum(product.T, axis=0, keepdims=True), [flags[0:9]]
        for _ in range(3):
            term = left.astype(jnp.bfloat16).astype(f32)
            left = left - term
            lines += [term[:, :width], term[:, width:]]
        ref[pl.ds(2 * tok, 16), :] = jnp.concatenate(lines + [jnp.zeros((1, width), f32)], axis=0).astype(jnp.bfloat16)


def foreign_delta(ref, tok):
    terms = ref[pl.ds(2 * tok, 16), :].astype(jnp.float32)
    return jnp.concatenate(
        [sum(terms[9 + 2 * i + half : 10 + 2 * i + half] for i in range(3)) for half in range(2)], axis=1
    )


def line_place(z, line, heights):
    if line == 0:
        return True, lambda flags, dt: flags[3 * dt + 1 : 3 * dt + 2]
    rising, at = pair(z, line - 1)
    return within(at, heights), lambda flags, dt: jnp.where(
        rising, flags[3 * dt + 2 : 3 * dt + 3], flags[3 * dt : 3 * dt + 1]
    )


def lanes_of(tok, border, other):
    width = border.shape[1]
    lane = lax.broadcasted_iota(jnp.int32, (1, width), 1)
    return jnp.concatenate(
        [jnp.where(lane + start < tok, border, other) for start in range(0, 2 * tok, width)], axis=1
    )


def first_kernel(tok, heights, scale, kv_ref, par_kv_ref, rest_ref, par_ref, qg, table, s_ref, d_ref):
    y, c, z = place()
    two = 2 * tok
    f32 = jnp.float32
    first, near = c == 0, border_is_own(y, c)
    out = []
    for part in range(3):
        own, par = rest_ref[rows_at(part, tok), :], par_ref[rows_at(part + 2, tok), :]
        tiles = [pick(near, which, own, par) for which in range(2)]
        if part == 2:
            out = jnp.concatenate(tiles, axis=0)
        else:
            for which in range(2):
                qg[part, rows_at(which, tok), :] = tiles[which]
    delta = jnp.sum((qg[1].astype(f32) * out.astype(f32)).T, axis=0, keepdims=True)

    own_flags = rest_ref[pl.ds(3 * tok, 16), :].astype(f32)
    par_flags = par_ref[pl.ds(5 * tok, 16), :].astype(f32)
    lines = []
    for line in range(3):
        inside, at = line_place(z, line, heights)
        centre = jnp.ones_like(own_flags[0:1]) if line == 0 else None
        for slot in range(2):
            if slot == 0:
                own, par = at(own_flags, 1), jnp.where(first, at(par_flags, 0), at(par_flags, 2))
            else:
                own, par = jnp.where(first, at(own_flags, 2), at(own_flags, 0)), at(par_flags, 1)
            if line == 0:
                own, par = (centre, par) if slot == 0 else (own, centre)
            row = lanes_of(tok, pick(near, 0, own, par), pick(near, 1, own, par))
            lines.append(jnp.where(inside, (row - 1.0) * 1e30, -1e30))
    table[...] = jnp.concatenate(lines + [delta, jnp.zeros((1, two), f32)], axis=0)
    for i, source in enumerate((kv_ref, par_kv_ref)):
        rows = rows_at(i, tok)
        s_ref[rows, :] = dot(source[rows_at(0, tok), :], qg[0], ROWS_T) * scale + table[i : i + 1, :]
        d_ref[rows, :] = dot(source[rows_at(1, tok), :], qg[1], ROWS_T) - table[6:7, :]


def largest(tok, blocks):
    lanes = blocks[0][0].shape[1]
    top = jnp.full((8, lanes), -1e30, jnp.float32)
    for ref, i in blocks:
        top = jnp.maximum(top, jnp.max(ref[rows_at(i, tok), :].reshape(tok // 8, 8, lanes), axis=0))
    return jnp.max(top, axis=0, keepdims=True)


def summed(tok, blocks, top):
    lanes = blocks[0][0].shape[1]
    total = jnp.zeros((8, lanes), jnp.float32)
    for ref, i in blocks:
        weights = jnp.exp(ref[rows_at(i, tok), :] - top)
        total = total + jnp.sum(weights.reshape(tok // 8, 8, lanes), axis=0)
    return jnp.sum(total, axis=0, keepdims=True)


def early_kernel(tok, scale, qg, table, s_own, one_ref, two_ref, s_ref, d_ref, part_ref):
    for i, source in enumerate((one_ref, two_ref)):
        rows = rows_at(i, tok)
        s_ref[rows, :] = dot(source[rows_at(0, tok), :], qg[0], ROWS_T) * scale + table[2 + 2 * i + EARLY : 3 + 2 * i + EARLY, :]
        d_ref[rows, :] = dot(source[rows_at(1, tok), :], qg[1], ROWS_T) - table[6:7, :]
    blocks = [(ref, i) for ref in (s_own, s_ref) for i in range(2)]
    top = largest(tok, blocks)
    total = summed(tok, blocks, top)
    part_ref[...] = jnp.concatenate([top, total, jnp.zeros((6, 2 * tok), jnp.float32)], axis=0)


def foreign_rows(ref, part, which, tok):
    block = ref[rows_at(part, tok), :]
    gap = jnp.zeros((2 * block.shape[1] - tok, block.shape[1]), block.dtype)
    return jnp.concatenate([block, gap] if which == 0 else [gap, block], axis=0)


def foreign_lanes(which, tok, width):
    return slice(0, 2 * width) if which == 0 else slice(2 * tok - 2 * width, 2 * tok)


def to_lanes(which, tok, row, fill):
    gap = jnp.full((1, 2 * tok - row.shape[1]), fill, jnp.float32)
    return jnp.concatenate([row, gap] if which == 0 else [gap, row], axis=1)


def score_kernel(tok, chips, heights, sides, scale, qg, table, part, *refs):
    keys, foreign, refs = refs[:6], refs[6 : 6 + sides], refs[6 + sides :]
    s_late, s_far, *notes = refs
    y, c, z = place()
    near = border_is_own(y, c)
    two = 2 * tok
    f32 = jnp.float32
    far = []
    for which in range(sides):
        rising, y_at = pair(y, which)
        flags = foreign[which][pl.ds(2 * tok, 16), :].astype(f32)
        queries = foreign_rows(foreign[which], 0, which, tok)
        for line in range(3):
            inside, at = line_place(z, line, heights)
            row = jnp.where(rising, at(flags, 0), at(flags, 2))
            lane = lax.broadcasted_iota(jnp.int32, row.shape, 1)
            width = row.shape[1]
            row = jnp.concatenate(
                [
                    jnp.where(lane + start < tok if which == 0 else lane + start >= 2 * width - tok, row, 0.0)
                    for start in (0, width)
                ],
                axis=1,
            )
            bias = jnp.where(inside & within(y_at, chips), (row - 1.0) * 1e30, -1e30)
            border = pick(near, which, keys[2 * line][rows_at(0, tok), :], keys[2 * line + 1][rows_at(0, tok), :])
            s_far[rows_at(3 * which + line, tok), :] = dot(border, queries, ROWS_T) * scale + bias
        blocks = [(s_far, 3 * which + line) for line in range(3)]
        top = largest(tok, blocks)
        far.append([to_lanes(which, tok, top, -1e30), to_lanes(which, tok, summed(tok, blocks, top), 0.0)])
    for i in range(2):
        at = 2 + 2 * i + LATE
        scores = dot(keys[at][rows_at(0, tok), :], qg[0], ROWS_T) * scale
        s_late[rows_at(i, tok), :] = scores + table[at : at + 1, :]
    blocks = [(s_late, i) for i in range(2)]
    top = jnp.maximum(part[0:1, :], largest(tok, blocks))
    total = part[1:2, :] * jnp.exp(part[0:1, :] - top) + summed(tok, blocks, top)
    for which in range(sides):
        notes[which][...] = jnp.concatenate([top, total] + far[which] + [jnp.zeros((4, two), f32)], axis=0)


def middle_kernel(tok, sides, scale, qg, table, s_own, d_own, s_early, d_early, s_late, s_far, *refs):
    tiles, foreign, sent = refs[:6], refs[6 : 6 + sides], refs[6 + sides : 6 + 2 * sides]
    e_ref, ds_ref, e_far, ds_far, dq_ref, *far_dq = refs[6 + 2 * sides :]
    y, c, _ = place()
    near = border_is_own(y, c)
    f32, bf16 = jnp.float32, jnp.bfloat16
    dq = jnp.zeros(dq_ref.shape, f32)
    for line in range(3):
        for slot in range(2):
            i, at = 2 * line + slot, rows_at(line - 1 if line else slot, tok)
            scores = s_own if line == 0 else s_early if slot == EARLY else s_late
            weights = jnp.exp(scores[at, :] - sent[0][0:1, :])
            if line and slot == LATE:
                grads = dot(tiles[i][rows_at(1, tok), :], qg[1], ROWS_T) - table[6:7, :]
            else:
                grads = (d_early if line else d_own)[at, :]
            low = (weights * grads * scale).astype(bf16)
            e_ref[rows_at(i, tok), :] = weights.astype(bf16)
            ds_ref[rows_at(i, tok), :] = low
            dq = dq + dot(tiles[i][rows_at(0, tok), :], low, COLS_T)
    dq_ref[...] = dq
    for which in range(sides):
        far_g = foreign_rows(foreign[which], 1, which, tok)
        delta = foreign_delta(foreign[which], tok)
        lanes = foreign_lanes(which, tok, qg.shape[2])
        dq = jnp.zeros(far_dq[which].shape, f32)
        for line in range(3):
            rows = rows_at(3 * which + line, tok)
            own, par = tiles[2 * line], tiles[2 * line + 1]
            key, value = (pick(near, which, own[rows_at(i, tok), :], par[rows_at(i, tok), :]) for i in range(2))
            weights = jnp.exp(s_far[rows, :] - sent[which][2:3, lanes])
            low = (weights * (dot(value, far_g, ROWS_T) - delta) * scale).astype(bf16)
            e_far[rows, :] = weights.astype(bf16)
            ds_far[rows, :] = low
            dq = dq + dot(key, low, COLS_T)
        far_dq[which][...] = dq


def column_sums(tok, near, sides, line, e_ref, ds_ref, e_far, ds_far, scaled, far_scaled):
    rows = [rows_at(2 * line + slot, tok) for slot in range(2)]
    sums = [[dot(ref[at, :], scaled[i]) for i, ref in enumerate((ds_ref, e_ref))] for at in rows]
    for which in range(sides):
        at = rows_at(3 * which + line, tok)
        for i, ref in enumerate((ds_far, e_far)):
            far = dot(ref[at, :], far_scaled[which][i])
            for slot in range(2):
                mine = near == ((slot == 0) == (which == 0))
                sums[slot][i] = sums[slot][i] + jnp.where(mine, far, 0.0)
    return [[part.astype(jnp.bfloat16) for part in pair] for pair in sums]


def leave_kernel(tok, chips, sides, qg, e_ref, ds_ref, e_far, ds_far, *refs):
    far_dq, sent, came, foreign = (refs[i * sides : (i + 1) * sides] for i in range(4))
    one_ref, two_ref, scaled, factor_ref, *refs = refs[4 * sides :]
    shares, far_scaled = refs[:sides], refs[sides:]
    y, c, _ = place()
    near = border_is_own(y, c)
    bf16 = jnp.bfloat16
    width = qg.shape[2]

    def log_total(top, total, other_top, other_total):
        both = jnp.maximum(top, other_top)
        return both + jnp.log(total * jnp.exp(top - both) + other_total * jnp.exp(other_top - both))

    def times(block, factor):
        return (block.astype(jnp.float32) * jnp.broadcast_to(factor, (width, factor.shape[1])).T).astype(bf16)

    top, total = sent[0][0:1, :], sent[0][1:2, :]
    lse = None
    for which in range(sides):
        _, y_at = pair(y, which)
        inside = within(y_at, chips)
        note = came[which]
        far_lse = log_total(note[0:1, :], note[1:2, :], sent[which][2:3, :], sent[which][3:4, :])
        lanes = foreign_lanes(which, tok, width)
        factor = jnp.where(inside, jnp.exp(sent[which][2:3, lanes] - far_lse[:, lanes]), 0.0)
        share = (far_dq[which][...] * factor).T
        shares[which][...] = (share[:tok] if which == 0 else share[2 * width - tok :]).astype(bf16)
        for part in range(2):
            far_scaled[which][part] = times(foreign_rows(foreign[which], part, which, tok), factor)
        other = jnp.where(inside, note[2:3, :], -1e30), jnp.where(inside, note[3:4, :], 0.0)
        lse = log_total(top, total, *other) if which == 0 else log_total(lse, jnp.ones_like(lse), *other)
    factor = jnp.exp(top - lse)
    factor_ref[...] = jnp.broadcast_to(factor, factor_ref.shape)
    for part in range(2):
        scaled[part] = times(qg[part], factor)
    for line, result in ((1, one_ref), (2, two_ref)):
        sums = column_sums(tok, near, sides, line, e_ref, ds_ref, e_far, ds_far, scaled, far_scaled)
        for slot in range(2):
            for i in range(2):
                result[i, rows_at(slot, tok), :] = sums[slot][i]


def stay_kernel(tok, sides, e_ref, ds_ref, e_far, ds_far, scaled, factor_ref, raw_dq, *refs):
    far_scaled, (own_ref, dq_ref) = refs[:sides], refs[sides:]
    y, c, _ = place()
    near = border_is_own(y, c)
    sums = column_sums(tok, near, sides, 0, e_ref, ds_ref, e_far, ds_far, scaled, far_scaled)
    for slot in range(2):
        for i in range(2):
            own_ref[i, rows_at(slot, tok), :] = sums[slot][i]
    dq_ref[...] = (raw_dq[...] * factor_ref[0:1, :]).T


def sum_kernel(tok, chips, heights, sides, own_ref, one_ref, two_ref, dq_ref, *refs):
    backs, (mine_ref, mine_q_ref, swap_ref) = refs[:sides], refs[sides:]
    y, c, z = place()
    near = border_is_own(y, c)
    f32, bf16 = jnp.float32, jnp.bfloat16
    for i in range(2):
        for slot in range(2):
            rows = rows_at(slot, tok)
            value = own_ref[i, rows, :].astype(f32)
            for line, ref in ((1, one_ref), (2, two_ref)):
                inside, _ = line_place(z, line, heights)
                value = value + jnp.where(inside, ref[i, rows_at(1 - slot, tok), :].astype(f32), 0.0)
            if slot == 0:
                mine_ref[i] = value.astype(bf16)
            else:
                swap_ref[i] = value.astype(bf16)
    tiles = []
    for tile in range(2):
        value = dq_ref[rows_at(tile, tok), :]
        if tile < sides:
            _, y_at = pair(y, tile)
            value = value + jnp.where(within(y_at, chips), backs[tile][...].astype(f32), 0.0)
        tiles.append(value.astype(bf16))
    mine_q_ref[...] = jnp.where(near, tiles[0], tiles[1])
    swap_ref[2] = jnp.where(near, tiles[1], tiles[0])


def final_kernel(mine_ref, swap_ref, mine_q_ref, gq_ref, gk_ref, gv_ref):
    head = head_at()
    gq_ref[0, 0, head, 0] = mine_q_ref[...]
    gq_ref[0, 0, 1 - head, 0] = swap_ref[2]
    for i, ref in enumerate((gk_ref, gv_ref)):
        ref[0, 0, head, 0] = mine_ref[i]
        ref[0, 0, 1 - head, 0] = swap_ref[i]


def body(queries, keys, values, grad_out, attn_out, window_mask):
    tok, width = queries.shape[-2:]
    scale = width ** -0.5
    times, heights = lax.axis_size("tm"), lax.axis_size("height")
    chips = times // 2
    sides = 1 if chips == 2 else 2
    bf16, f32 = jnp.bfloat16, jnp.float32

    def call(kernel, shapes, specs, scratch=()):
        return pl.pallas_call(
            kernel,
            out_shape=[jax.ShapeDtypeStruct(*shape) for shape in shapes],
            in_specs=list(specs),
            out_specs=[VMEM] * len(shapes),
            scratch_shapes=list(scratch),
            compiler_params=LIMIT,
        )

    def partner(index, which, size):
        if which is None:
            return index
        at = index + 1 if index % 2 == which else index - 1
        return at if 0 <= at < size else None

    def exchange(block, y_which, z_which):
        pairs = []
        for t in range(times):
            for z in range(heights):
                y_at, z_at = partner(t // 2, y_which, chips), partner(z, z_which, heights)
                at = t * heights + z
                alone = y_at is None or z_at is None
                pairs.append((at, (t ^ 1) * heights + z if alone else (2 * y_at + 1 - t % 2) * heights + z_at))
        return lax.ppermute(block, ("tm", "height"), pairs)

    def swap_cores(block):
        return lax.ppermute(block, "tm", [(t, t ^ 1) for t in range(times)])

    line_shape, tile_shape = ((2, 2 * tok, width), bf16), ((2, tok, width), bf16)
    extra = 48
    arguments = (keys, values, queries, grad_out, attn_out, window_mask)
    kv, rest, other = call(
        functools.partial(pack_kernel, tok),
        [((2 * tok + extra, width), bf16), ((3 * tok + 16, width), bf16), ((5 * tok + 16, width), bf16)],
        [HBM] * 6,
        [pltpu.SMEM(window_mask.shape, jnp.int32), pltpu.SemaphoreType.DMA((11,))],
    )(*(pltpu.with_memory_space_constraint(x, pltpu.HBM) for x in arguments))
    early = [exchange(kv, None, which) for which in range(2)]
    par = swap_cores(other)
    border_shape, two = ((2 * tok + 16, width), bf16), 2 * tok
    par_kv, *borders = call(
        functools.partial(line_kernel, tok), [((2 * tok + 32, width), bf16)] + [border_shape] * sides, [VMEM] * 2
    )(rest, par)
    foreign = [exchange(borders[which], which, None) for which in range(sides)]
    late = [exchange(par_kv, None, which) for which in range(2)]
    tiles = (kv, par_kv, late[0], early[0], late[1], early[1])
    pair_shape, note_shape, raw_shape = ((2, two, width), bf16), ((8, two), f32), ((width, two), f32)

    def square(count, kind=f32):
        return ((count * tok, two), kind)

    def far_square(kind=f32):
        return ((3 * sides * tok, 2 * width), kind)

    qg, table, s_own, d_own = call(
        functools.partial(first_kernel, tok, heights, scale),
        [pair_shape, note_shape, square(2), square(2)],
        [VMEM] * 4,
    )(kv, par_kv, rest, par)
    s_early, d_early, part = call(
        functools.partial(early_kernel, tok, scale), [square(2), square(2), note_shape], [VMEM] * 5
    )(qg, table, s_own, *early)
    s_late, s_far, *sent = call(
        functools.partial(score_kernel, tok, chips, heights, sides, scale),
        [square(2), far_square()] + [note_shape] * sides,
        [VMEM] * (9 + sides),
    )(qg, table, part, *tiles, *foreign)
    came = [exchange(sent[which], which, None) for which in range(sides)]
    e, ds, e_far, ds_far, raw_dq, *far_dq = call(
        functools.partial(middle_kernel, tok, sides, scale),
        [square(6, bf16)] * 2 + [far_square(bf16)] * 2 + [raw_shape] + [((width, 2 * width), f32)] * sides,
        [VMEM] * (14 + 2 * sides),
    )(qg, table, s_own, d_own, s_early, d_early, s_late, s_far, *tiles, *foreign, *sent)
    one, other_one, scaled, factor, *rest_out = call(
        functools.partial(leave_kernel, tok, chips, sides),
        [line_shape, line_shape, pair_shape, note_shape] + [((tok, width), bf16)] * sides + [((2, 2 * width, width), bf16)] * sides,
        [VMEM] * (5 + 4 * sides),
    )(qg, e, ds, e_far, ds_far, *far_dq, *sent, *came, *foreign)
    shares, far_scaled = rest_out[:sides], rest_out[sides:]
    back = [exchange(block, None, which) for which, block in enumerate((one, other_one))]
    shares = [exchange(share, which, None) for which, share in enumerate(shares)]
    own, dq = call(
        functools.partial(stay_kernel, tok, sides),
        [line_shape, ((two, width), f32)],
        [VMEM] * (7 + sides),
    )(e, ds, e_far, ds_far, scaled, factor, raw_dq, *far_scaled)
    mine, mine_q, leaving = call(
        functools.partial(sum_kernel, tok, chips, heights, sides),
        [tile_shape, ((tok, width), bf16), ((3, tok, width), bf16)],
        [VMEM] * (4 + sides),
    )(own, *back, dq, *shares)
    return call(final_kernel, [(queries.shape, bf16)] * 3, [VMEM] * 3)(mine, swap_cores(leaving), mine_q)


def solution(mesh):
    placed = P("tm", "height", "dp", None, None, None)
    return jax.shard_map(
        body,
        mesh=mesh,
        in_specs=(placed,) * 5 + (P("tm", "height", None, None),),
        out_specs=(placed,) * 3,
        check_vma=False,
    )
```

```python
import functools

import jax
import jax.numpy as jnp
from jax import lax
from jax.experimental import pallas as pl
from jax.experimental.pallas import tpu as pltpu
from jax.sharding import PartitionSpec as P

VMEM = pl.BlockSpec(memory_space=pltpu.VMEM)
HBM = pl.BlockSpec(memory_space=pltpu.HBM)
LIMIT = pltpu.CompilerParams(vmem_limit_bytes=32 * 1024 * 1024)
ROWS_T = (((1,), (1,)), ((), ()))
COLS_T = (((0,), (0,)), ((), ()))


def dot(a, b, dims=(((1,), (0,)), ((), ()))):
    return lax.dot_general(a, b, dims, preferred_element_type=jnp.float32)


LATE, EARLY = 0, 1


def place():
    t = lax.axis_index("tm")
    return t // 2, t % 2, lax.axis_index("height")


def head_at():
    y, c, z = place()
    return (c + y + z) % 2


def pair(index, which):
    rising = (index % 2) == (0 if which == 0 else 1)
    return rising, jnp.where(rising, index + 1, index - 1)


def within(index, size):
    return (index >= 0) & (index < size)


def pack_kernel(tok, k_ref, v_ref, q_ref, g_ref, o_ref, mask_ref, kv_ref, rest_ref, other_ref, flags, sems):
    head = head_at()
    copies = [pltpu.make_async_copy(mask_ref, flags, sems.at[10])]
    for i, ref in enumerate((k_ref, v_ref, q_ref, g_ref, o_ref)):
        own = (kv_ref if i < 2 else rest_ref).at[pl.ds((i if i < 2 else i - 2) * tok, tok), :]
        copies.append(pltpu.make_async_copy(ref.at[0, 0, head, 0], own, sems.at[2 * i + 1]))
        copies.append(
            pltpu.make_async_copy(ref.at[0, 0, 1 - head, 0], other_ref.at[pl.ds(i * tok, tok), :], sems.at[2 * i])
        )
    for copy in copies:
        copy.start()
    copies[0].wait()
    row = lax.broadcasted_iota(jnp.int32, (16, rest_ref.shape[1]), 0)
    spread = jnp.zeros(row.shape, jnp.float32)
    for i in range(9):
        on = (flags[0, 0, 0, 9 * (i // 3) + 3 * (i % 3) + 1] != 0).astype(jnp.float32)
        spread = jnp.where(row == i, on, spread)
    rest_ref[pl.ds(3 * tok, 16), :] = spread.astype(jnp.bfloat16)
    other_ref[pl.ds(5 * tok, 16), :] = spread.astype(jnp.bfloat16)
    for copy in copies[1:]:
        copy.wait()


def rows_at(index, tok):
    return pl.ds(index * tok, tok)


def border_is_own(y, c):
    rising, _ = pair(y, 0)
    return (c == 1) == rising


def pick(near, which, own, par):
    return jnp.where(near, own, par) if which == 0 else jnp.where(near, par, own)


def three_terms(row):
    terms = []
    for _ in range(3):
        terms.append(row.astype(jnp.bfloat16).astype(jnp.float32))
        row = row - terms[-1]
    return terms


def line_kernel(tok, rest_ref, par_ref, par_kv_ref, *border_refs):
    y, c, _ = place()
    near = border_is_own(y, c)
    for i in range(2):
        par_kv_ref[rows_at(i, tok), :] = par_ref[rows_at(i, tok), :]
    width = par_ref.shape[1]
    f32 = jnp.float32
    q, g, o = (
        [pick(near, which, rest_ref[rows_at(i, tok), :], par_ref[rows_at(i + 2, tok), :]) for which in range(2)]
        for i in range(3)
    )
    own_flags, par_flags = rest_ref[pl.ds(3 * tok, 16), :].astype(f32), par_ref[pl.ds(5 * tok, 16), :].astype(f32)
    flags = [pick(near, which, own_flags, par_flags)[0:9] for which in range(2)]
    product = jnp.concatenate(g, axis=0).astype(f32) * jnp.concatenate(o, axis=0).astype(f32)
    terms = [
        [term[:, start : start + width] for start in range(0, 2 * tok, width)]
        for term in three_terms(jnp.sum(product.T, axis=0, keepdims=True))
    ]
    for which, ref in enumerate(border_refs):
        ref[rows_at(0, tok), :], ref[rows_at(1, tok), :] = q[which], g[which]
        part = slice(0, 2) if which == 0 else slice(len(terms[0]) - 2, None)
        lines = [flags[which]] + [row for term in terms for row in term[part]] + [jnp.zeros((1, width), f32)]
        ref[pl.ds(2 * tok, 16), :] = jnp.concatenate(lines, axis=0).astype(jnp.bfloat16)
    lines = flags + [row for term in terms for row in term] + [jnp.zeros((5, width), f32)]
    par_kv_ref[pl.ds(2 * tok, 32), :] = jnp.concatenate(lines, axis=0).astype(jnp.bfloat16)


def foreign_delta(ref, tok):
    terms = ref[pl.ds(2 * tok, 16), :].astype(jnp.float32)
    return jnp.concatenate(
        [sum(terms[9 + 2 * i + half : 10 + 2 * i + half] for i in range(3)) for half in range(2)], axis=1
    )


def line_place(z, line, heights):
    if line == 0:
        return True, lambda flags, dt: flags[3 * dt + 1 : 3 * dt + 2]
    rising, at = pair(z, line - 1)
    return within(at, heights), lambda flags, dt: jnp.where(
        rising, flags[3 * dt + 2 : 3 * dt + 3], flags[3 * dt : 3 * dt + 1]
    )


def lanes_of(tok, border, other):
    width = border.shape[1]
    lane = lax.broadcasted_iota(jnp.int32, (1, width), 1)
    return jnp.concatenate(
        [jnp.where(lane + start < tok, border, other) for start in range(0, 2 * tok, width)], axis=1
    )


def flag_row(tok, slot, at, own_flags, par_flags, own_query):
    y, c, _ = place()
    first, near = c == 0, border_is_own(y, c)
    if slot == 0:
        own, par = at(own_flags, 1), jnp.where(first, at(par_flags, 0), at(par_flags, 2))
    else:
        own, par = jnp.where(first, at(own_flags, 2), at(own_flags, 0)), at(par_flags, 1)
    if own_query:
        centre = jnp.ones_like(own)
        own, par = (centre, par) if slot == 0 else (own, centre)
    return lanes_of(tok, pick(near, 0, own, par), pick(near, 1, own, par))


def first_kernel(tok, heights, scale, kv_ref, par_kv_ref, rest_ref, par_ref, q_all, g_all, table, s_ref, d_ref):
    qg = (q_all, g_all)
    y, c, z = place()
    two = 2 * tok
    width = rest_ref.shape[1]
    f32 = jnp.float32
    near = border_is_own(y, c)
    out = []
    for part in range(3):
        own, par = rest_ref[rows_at(part, tok), :], par_ref[rows_at(part + 2, tok), :]
        tiles = [pick(near, which, own, par) for which in range(2)]
        if part == 2:
            out = jnp.concatenate(tiles, axis=0)
        else:
            for which in range(2):
                qg[part][rows_at(which, tok), :] = tiles[which]
    delta = jnp.sum((qg[1][...].astype(f32) * out.astype(f32)).T, axis=0, keepdims=True)

    own_flags = rest_ref[pl.ds(3 * tok, 16), :].astype(f32)
    par_flags = par_ref[pl.ds(5 * tok, 16), :].astype(f32)
    lines = []
    for line in range(3):
        inside, at = line_place(z, line, heights)
        for slot in range(2):
            row = flag_row(tok, slot, at, own_flags, par_flags, line == 0)
            lines.append(jnp.where(inside, (row - 1.0) * 1e30, -1e30))
    table[...] = jnp.concatenate(lines + [delta, jnp.zeros((1, two), f32)], axis=0)
    for i, source in enumerate((kv_ref, par_kv_ref)):
        rows = rows_at(i, tok)
        s_ref[rows, :] = dot(source[rows_at(0, tok), :], qg[0][...], ROWS_T) * scale + table[i : i + 1, :]
        d_ref[rows, :] = dot(source[rows_at(1, tok), :], qg[1][...], ROWS_T) - table[6:7, :]


def largest(tok, blocks):
    lanes = blocks[0][0].shape[1]
    top = jnp.full((8, lanes), -1e30, jnp.float32)
    for ref, i in blocks:
        top = jnp.maximum(top, jnp.max(ref[rows_at(i, tok), :].reshape(tok // 8, 8, lanes), axis=0))
    return jnp.max(top, axis=0, keepdims=True)


def summed(tok, blocks, top):
    lanes = blocks[0][0].shape[1]
    total = jnp.zeros((8, lanes), jnp.float32)
    for ref, i in blocks:
        weights = jnp.exp(ref[rows_at(i, tok), :] - top)
        total = total + jnp.sum(weights.reshape(tok // 8, 8, lanes), axis=0)
    return jnp.sum(total, axis=0, keepdims=True)


def early_kernel(tok, scale, q_all, g_all, table, s_own, one_ref, two_ref, s_ref, d_ref, part_ref):
    qg = (q_all, g_all)
    for i, source in enumerate((one_ref, two_ref)):
        rows = rows_at(i, tok)
        s_ref[rows, :] = dot(source[rows_at(0, tok), :], qg[0][...], ROWS_T) * scale + table[2 + 2 * i + EARLY : 3 + 2 * i + EARLY, :]
        d_ref[rows, :] = dot(source[rows_at(1, tok), :], qg[1][...], ROWS_T) - table[6:7, :]
    blocks = [(ref, i) for ref in (s_own, s_ref) for i in range(2)]
    top = largest(tok, blocks)
    total = summed(tok, blocks, top)
    part_ref[...] = jnp.concatenate([top, total, jnp.zeros((6, 2 * tok), jnp.float32)], axis=0)


def foreign_rows(ref, part, which, tok):
    block = ref[rows_at(part, tok), :]
    gap = jnp.zeros((2 * block.shape[1] - tok, block.shape[1]), block.dtype)
    return jnp.concatenate([block, gap] if which == 0 else [gap, block], axis=0)


def foreign_lanes(which, tok, width):
    return slice(0, 2 * width) if which == 0 else slice(2 * tok - 2 * width, 2 * tok)


def far_row(tok, which, row):
    lane, width = lax.broadcasted_iota(jnp.int32, row.shape, 1), row.shape[1]
    return jnp.concatenate(
        [
            jnp.where(lane + start < tok if which == 0 else lane + start >= 2 * width - tok, row, 0.0)
            for start in (0, width)
        ],
        axis=1,
    )


def to_lanes(which, tok, row, fill):
    gap = jnp.full((1, 2 * tok - row.shape[1]), fill, jnp.float32)
    return jnp.concatenate([row, gap] if which == 0 else [gap, row], axis=1)


def score_kernel(tok, chips, heights, sides, scale, q_all, g_all, table, part, *refs):
    qg = (q_all, g_all)
    keys, foreign, refs = refs[:6], refs[6 : 6 + sides], refs[6 + sides :]
    s_late, s_far, *notes = refs
    y, c, z = place()
    near = border_is_own(y, c)
    two = 2 * tok
    f32 = jnp.float32
    far = []
    for which in range(sides):
        rising, y_at = pair(y, which)
        flags = foreign[which][pl.ds(2 * tok, 16), :].astype(f32)
        queries = foreign_rows(foreign[which], 0, which, tok)
        for line in range(3):
            inside, at = line_place(z, line, heights)
            row = far_row(tok, which, jnp.where(rising, at(flags, 0), at(flags, 2)))
            bias = jnp.where(inside & within(y_at, chips), (row - 1.0) * 1e30, -1e30)
            border = pick(near, which, keys[2 * line][rows_at(0, tok), :], keys[2 * line + 1][rows_at(0, tok), :])
            s_far[rows_at(3 * which + line, tok), :] = dot(border, queries, ROWS_T) * scale + bias
        blocks = [(s_far, 3 * which + line) for line in range(3)]
        top = largest(tok, blocks)
        far.append([to_lanes(which, tok, top, -1e30), to_lanes(which, tok, summed(tok, blocks, top), 0.0)])
    for i in range(2):
        at = 2 + 2 * i + LATE
        scores = dot(keys[at][rows_at(0, tok), :], qg[0][...], ROWS_T) * scale
        s_late[rows_at(i, tok), :] = scores + table[at : at + 1, :]
    blocks = [(s_late, i) for i in range(2)]
    top = jnp.maximum(part[0:1, :], largest(tok, blocks))
    total = part[1:2, :] * jnp.exp(part[0:1, :] - top) + summed(tok, blocks, top)
    for which in range(sides):
        notes[which][...] = jnp.concatenate([top, total] + far[which] + [jnp.zeros((4, two), f32)], axis=0)


def middle_kernel(tok, sides, scale, q_all, g_all, table, s_own, d_own, s_early, d_early, s_late, s_far, *refs):
    qg = (q_all, g_all)
    tiles, foreign, sent = refs[:6], refs[6 : 6 + sides], refs[6 + sides : 6 + 2 * sides]
    e_ref, ds_ref, e_far, ds_far, dq_ref, *far_dq = refs[6 + 2 * sides :]
    y, c, _ = place()
    near = border_is_own(y, c)
    f32, bf16 = jnp.float32, jnp.bfloat16
    dq = jnp.zeros(dq_ref.shape, f32)
    for line in range(3):
        for slot in range(2):
            i, at = 2 * line + slot, rows_at(line - 1 if line else slot, tok)
            scores = s_own if line == 0 else s_early if slot == EARLY else s_late
            weights = jnp.exp(scores[at, :] - sent[0][0:1, :])
            if line and slot == LATE:
                grads = dot(tiles[i][rows_at(1, tok), :], qg[1][...], ROWS_T) - table[6:7, :]
            else:
                grads = (d_early if line else d_own)[at, :]
            low = (weights * grads * scale).astype(bf16)
            if line == 0:
                e_ref[rows_at(i, tok), :] = weights.astype(bf16)
                ds_ref[rows_at(i, tok), :] = low
            dq = dq + dot(tiles[i][rows_at(0, tok), :], low, COLS_T)
    dq_ref[...] = dq
    for which in range(sides):
        far_g = foreign_rows(foreign[which], 1, which, tok)
        delta = foreign_delta(foreign[which], tok)
        lanes = foreign_lanes(which, tok, qg[0].shape[1])
        dq = jnp.zeros(far_dq[which].shape, f32)
        for line in range(3):
            rows = rows_at(3 * which + line, tok)
            own, par = tiles[2 * line], tiles[2 * line + 1]
            key, value = (pick(near, which, own[rows_at(i, tok), :], par[rows_at(i, tok), :]) for i in range(2))
            weights = jnp.exp(s_far[rows, :] - sent[which][2:3, lanes])
            low = (weights * (dot(value, far_g, ROWS_T) - delta) * scale).astype(bf16)
            if line == 0:
                e_far[rows_at(which, tok), :] = weights.astype(bf16)
                ds_far[rows_at(which, tok), :] = low
            dq = dq + dot(key, low, COLS_T)
        far_dq[which][...] = dq


def total_kernel(tok, chips, sides, *refs):
    far_dq, sent, came = (refs[i * sides : (i + 1) * sides] for i in range(3))
    note_ref, *shares = refs[3 * sides :]
    y, _, _ = place()
    width = far_dq[0].shape[0]

    def log_total(top, total, other_top, other_total):
        both = jnp.maximum(top, other_top)
        return both + jnp.log(total * jnp.exp(top - both) + other_total * jnp.exp(other_top - both))

    lse, far_rows = None, []
    for which in range(sides):
        _, y_at = pair(y, which)
        inside = within(y_at, chips)
        note = came[which]
        far_lse = log_total(note[0:1, :], note[1:2, :], sent[which][2:3, :], sent[which][3:4, :])
        far_lse = jnp.where(inside, far_lse, 0.0)
        far_rows.append(far_lse)
        lanes = foreign_lanes(which, tok, width)
        factor = jnp.where(inside, jnp.exp(sent[which][2:3, lanes] - far_lse[:, lanes]), 0.0)
        share = (far_dq[which][...] * factor).T
        shares[which][...] = (share[:tok] if which == 0 else share[2 * width - tok :]).astype(jnp.bfloat16)
        other = jnp.where(inside, note[2:3, :], -1e30), jnp.where(inside, note[3:4, :], 0.0)
        if which == 0:
            lse = log_total(sent[0][0:1, :], sent[0][1:2, :], *other)
        else:
            lse = log_total(lse, jnp.ones_like(lse), *other)
    rows = [lse] + far_rows
    note_ref[...] = jnp.concatenate(rows + [jnp.zeros((8 - len(rows), 2 * tok), jnp.float32)], axis=0)


def line_query_kernel(tok, chips, heights, sides, scale, kv_ref, par_kv_ref, *refs):
    queries, grads_in, extras = refs[:2], refs[2:4], refs[4:6]
    foreign, outs = refs[6 : 6 + 2 * sides], refs[6 + 2 * sides :]
    e_ref, ds_ref, e_far, ds_far, top_ref = outs
    y, c, z = place()
    near = border_is_own(y, c)
    two = 2 * tok
    width = kv_ref.shape[1]
    f32, bf16 = jnp.float32, jnp.bfloat16
    tops, far_tops = [], []
    tiles = (kv_ref, par_kv_ref)
    for line in (1, 2):
        rising, z_at = pair(z, line - 1)
        inside = within(z_at, heights)

        def at(flags, dt):
            return jnp.where(rising, flags[3 * dt : 3 * dt + 1], flags[3 * dt + 2 : 3 * dt + 3])

        rows = extras[line - 1][pl.ds(2 * tok, 32), :].astype(f32)
        own_flags, par_flags = (pick(near, which, rows[0:9], rows[9:18]) for which in range(2))
        delta = [sum(rows[18 + 3 * i + part : 19 + 3 * i + part] for i in range(3)) for part in range(two // width)]
        delta = jnp.concatenate(delta, axis=1)
        line_q, line_g = queries[line - 1][...], grads_in[line - 1][...]
        scores = []
        for slot in range(2):
            row = flag_row(tok, slot, at, own_flags, par_flags, False)
            bias = jnp.where(inside, (row - 1.0) * 1e30, -1e30)
            scores.append(dot(tiles[slot][rows_at(0, tok), :], line_q, ROWS_T) * scale + bias)
        top = jnp.maximum(*(jnp.max(block, axis=0, keepdims=True) for block in scores))
        tops.append(top)
        for slot in range(2):
            weights = jnp.exp(scores[slot] - top)
            grads = dot(tiles[slot][rows_at(1, tok), :], line_g, ROWS_T) - delta
            kept = rows_at(2 * (line - 1) + slot, tok)
            e_ref[kept, :] = weights.astype(bf16)
            ds_ref[kept, :] = (weights * grads * scale).astype(bf16)
        for which in range(sides):
            ref = foreign[2 * which + line - 1]
            y_rising, y_at = pair(y, which)
            flags = ref[pl.ds(2 * tok, 16), :].astype(f32)
            row = far_row(tok, which, jnp.where(y_rising, at(flags, 0), at(flags, 2)))
            bias = jnp.where(inside & within(y_at, chips), (row - 1.0) * 1e30, -1e30)
            key, value = (pick(near, which, *(tile[rows_at(i, tok), :] for tile in tiles)) for i in range(2))
            far_q, far_g = (foreign_rows(ref, part, which, tok) for part in range(2))
            block = dot(key, far_q, ROWS_T) * scale + bias
            top = jnp.max(block, axis=0, keepdims=True)
            far_tops.append(to_lanes(which, tok, top, -1e30))
            weights = jnp.exp(block - top)
            grads = dot(value, far_g, ROWS_T) - foreign_delta(ref, tok)
            kept = rows_at(2 * which + line - 1, tok)
            e_far[kept, :] = weights.astype(bf16)
            ds_far[kept, :] = (weights * grads * scale).astype(bf16)
    top_ref[...] = jnp.concatenate(tops + far_tops + [jnp.zeros((6 - 2 * sides, two), f32)], axis=0)


def times(block, factor):
    column = jnp.broadcast_to(factor, (block.shape[1], factor.shape[1])).T
    return (block.astype(jnp.float32) * column).astype(jnp.bfloat16)


def key_sums(tok, near, line, e_ref, ds_ref, scaled, far):
    rows = [rows_at(2 * line + slot, tok) for slot in range(2)]
    sums = [[dot(ref[at, :], scaled[i]) for i, ref in enumerate((ds_ref, e_ref))] for at in rows]
    for which, (e_far, ds_far, at, far_scaled) in enumerate(far):
        for i, ref in enumerate((ds_far, e_far)):
            block = dot(ref[at, :], far_scaled[i])
            for slot in range(2):
                sums[slot][i] = sums[slot][i] + jnp.where(near == ((slot == 0) == (which == 0)), block, 0.0)
    return sums


def stay_kernel(tok, chips, sides, q_all, g_all, e_ref, ds_ref, e_far, ds_far, raw_dq, note, *refs):
    qg = (q_all, g_all)
    sent, foreign, (own_ref, dq_ref) = refs[:sides], refs[sides : 2 * sides], refs[2 * sides :]
    y, c, _ = place()
    near = border_is_own(y, c)
    width = qg[0].shape[1]
    factor = jnp.exp(sent[0][0:1, :] - note[0:1, :])
    dq_ref[...] = (raw_dq[...] * factor).T
    far = []
    for which in range(sides):
        _, y_at = pair(y, which)
        lanes = foreign_lanes(which, tok, width)
        far_factor = jnp.exp(sent[which][2:3, lanes] - note[1 + which : 2 + which, lanes])
        far_factor = jnp.where(within(y_at, chips), far_factor, 0.0)
        scaled = [times(foreign_rows(foreign[which], part, which, tok), far_factor) for part in range(2)]
        far.append((e_far, ds_far, rows_at(which, tok), scaled))
    sums = key_sums(tok, near, 0, e_ref, ds_ref, [times(qg[part][...], factor) for part in range(2)], far)
    for slot in range(2):
        for i in range(2):
            own_ref[i, rows_at(slot, tok), :] = sums[slot][i]


def leave_kernel(tok, chips, sides, own_ref, dq_ref, e_ref, ds_ref, e_far, ds_far, top_ref, *refs):
    queries, refs = (refs[0:2], refs[2:4]), refs[4:]
    foreign, notes, backs = refs[: 2 * sides], refs[2 * sides : 2 + 2 * sides], refs[2 + 2 * sides : 2 + 3 * sides]
    mine_ref, mine_q_ref, swap_ref = refs[2 + 3 * sides :]
    y, c, _ = place()
    near = border_is_own(y, c)
    f32, bf16 = jnp.float32, jnp.bfloat16
    width = dq_ref.shape[1]
    sums = [[own_ref[i, rows_at(slot, tok), :] for i in range(2)] for slot in range(2)]
    for line in (1, 2):
        note = notes[line - 1]
        factor = jnp.exp(top_ref[line - 1 : line, :] - note[0:1, :])
        scaled = [times(queries[part][line - 1][...], factor) for part in range(2)]
        far = []
        for which in range(sides):
            lanes = foreign_lanes(which, tok, width)
            at = 2 + sides * (line - 1) + which
            far_factor = jnp.exp(top_ref[at : at + 1, lanes] - note[1 + which : 2 + which, lanes])
            rows = [foreign_rows(foreign[2 * which + line - 1], part, which, tok) for part in range(2)]
            far.append(
                (e_far, ds_far, rows_at(2 * which + line - 1, tok), [times(block, far_factor) for block in rows])
            )
        more = key_sums(tok, near, line - 1, e_ref, ds_ref, scaled, far)
        sums = [[sums[slot][i] + more[slot][i] for i in range(2)] for slot in range(2)]
    for i in range(2):
        mine_ref[i], swap_ref[i] = sums[0][i].astype(bf16), sums[1][i].astype(bf16)
    tiles = []
    for tile in range(2):
        value = dq_ref[rows_at(tile, tok), :]
        if tile < sides:
            _, y_at = pair(y, tile)
            value = value + jnp.where(within(y_at, chips), backs[tile][...].astype(f32), 0.0)
        tiles.append(value.astype(bf16))
    mine_q_ref[...] = jnp.where(near, tiles[0], tiles[1])
    swap_ref[2] = jnp.where(near, tiles[1], tiles[0])


def final_kernel(mine_ref, swap_ref, mine_q_ref, gq_ref, gk_ref, gv_ref):
    head = head_at()
    gq_ref[0, 0, head, 0] = mine_q_ref[...]
    gq_ref[0, 0, 1 - head, 0] = swap_ref[2]
    for i, ref in enumerate((gk_ref, gv_ref)):
        ref[0, 0, head, 0] = mine_ref[i]
        ref[0, 0, 1 - head, 0] = swap_ref[i]


def body(queries, keys, values, grad_out, attn_out, window_mask):
    tok, width = queries.shape[-2:]
    scale = width ** -0.5
    times, heights = lax.axis_size("tm"), lax.axis_size("height")
    chips = times // 2
    sides = 1 if chips == 2 else 2
    bf16, f32 = jnp.bfloat16, jnp.float32

    def call(kernel, shapes, specs, scratch=()):
        return pl.pallas_call(
            kernel,
            out_shape=[jax.ShapeDtypeStruct(*shape) for shape in shapes],
            in_specs=list(specs),
            out_specs=[VMEM] * len(shapes),
            scratch_shapes=list(scratch),
            compiler_params=LIMIT,
        )

    def partner(index, which, size):
        if which is None:
            return index
        at = index + 1 if index % 2 == which else index - 1
        return at if 0 <= at < size else None

    def exchange(block, y_which, z_which):
        pairs = []
        for t in range(times):
            for z in range(heights):
                y_at, z_at = partner(t // 2, y_which, chips), partner(z, z_which, heights)
                at = t * heights + z
                alone = y_at is None or z_at is None
                pairs.append((at, (t ^ 1) * heights + z if alone else (2 * y_at + 1 - t % 2) * heights + z_at))
        return lax.ppermute(block, ("tm", "height"), pairs)

    def swap_cores(block):
        return lax.ppermute(block, "tm", [(t, t ^ 1) for t in range(times)])

    line_shape, tile_shape = ((2, 2 * tok, width), bf16), ((2, tok, width), bf16)
    extra = 48
    arguments = (keys, values, queries, grad_out, attn_out, window_mask)
    kv, rest, other = call(
        functools.partial(pack_kernel, tok),
        [((2 * tok + extra, width), bf16), ((3 * tok + 16, width), bf16), ((5 * tok + 16, width), bf16)],
        [HBM] * 6,
        [pltpu.SMEM(window_mask.shape, jnp.int32), pltpu.SemaphoreType.DMA((11,))],
    )(*(pltpu.with_memory_space_constraint(x, pltpu.HBM) for x in arguments))
    early = [exchange(kv, None, which) for which in range(2)]
    par = swap_cores(other)
    border_shape, two = ((2 * tok + 16, width), bf16), 2 * tok
    par_kv, *borders = call(
        functools.partial(line_kernel, tok), [((2 * tok + 32, width), bf16)] + [border_shape] * sides, [VMEM] * 2
    )(rest, par)
    foreign = [exchange(borders[which], which, None) for which in range(sides)]
    late = [exchange(par_kv, None, which) for which in range(2)]
    tiles = (kv, par_kv, late[0], early[0], late[1], early[1])
    note_shape, raw_shape = ((8, two), f32), ((width, two), f32)

    def square(count, kind=f32):
        return ((count * tok, two), kind)

    def far_square(kind=f32):
        return ((3 * sides * tok, 2 * width), kind)

    q_all, g_all, table, s_own, d_own = call(
        functools.partial(first_kernel, tok, heights, scale),
        [((two, width), bf16)] * 2 + [note_shape, square(2), square(2)],
        [VMEM] * 4,
    )(kv, par_kv, rest, par)
    qg = (q_all, g_all)
    queries_in = [exchange(block, None, which) for block in qg for which in range(2)]
    foreign_in = [exchange(block, None, which) for block in foreign for which in range(2)]
    s_early, d_early, part = call(
        functools.partial(early_kernel, tok, scale), [square(2), square(2), note_shape], [VMEM] * 6
    )(*qg, table, s_own, *early)
    s_late, s_far, *sent = call(
        functools.partial(score_kernel, tok, chips, heights, sides, scale),
        [square(2), far_square()] + [note_shape] * sides,
        [VMEM] * (10 + sides),
    )(*qg, table, part, *tiles, *foreign)
    came = [exchange(sent[which], which, None) for which in range(sides)]
    far_tile = ((sides * tok, 2 * width), bf16)
    e, ds, e_far, ds_far, raw_dq, *far_dq = call(
        functools.partial(middle_kernel, tok, sides, scale),
        [square(2, bf16)] * 2 + [far_tile] * 2 + [raw_shape] + [((width, 2 * width), f32)] * sides,
        [VMEM] * (15 + 2 * sides),
    )(*qg, table, s_own, d_own, s_early, d_early, s_late, s_far, *tiles, *foreign, *sent)
    note, *shares = call(
        functools.partial(total_kernel, tok, chips, sides),
        [note_shape] + [((tok, width), bf16)] * sides,
        [VMEM] * (3 * sides),
    )(*far_dq, *sent, *came)
    notes = [exchange(note, None, which) for which in range(2)]
    shares = [exchange(share, which, None) for which, share in enumerate(shares)]
    far_pair = ((2 * sides * tok, 2 * width), bf16)
    line_terms = call(
        functools.partial(line_query_kernel, tok, chips, heights, sides, scale),
        [square(4, bf16)] * 2 + [far_pair] * 2 + [note_shape],
        [VMEM] * (8 + 2 * sides),
    )(kv, par_kv, *queries_in, *late, *foreign_in)
    own, dq = call(
        functools.partial(stay_kernel, tok, chips, sides),
        [((2, two, width), f32), ((two, width), f32)],
        [VMEM] * (8 + 2 * sides),
    )(*qg, e, ds, e_far, ds_far, raw_dq, note, *sent, *foreign)
    mine, mine_q, leaving = call(
        functools.partial(leave_kernel, tok, chips, sides),
        [tile_shape, ((tok, width), bf16), ((3, tok, width), bf16)],
        [VMEM] * (13 + 3 * sides),
    )(own, dq, *line_terms, *queries_in, *foreign_in, *notes, *shares)
    return call(final_kernel, [(queries.shape, bf16)] * 3, [VMEM] * 3)(mine, swap_cores(leaving), mine_q)


def solution(mesh):
    placed = P("tm", "height", "dp", None, None, None)
    return jax.shard_map(
        body,
        mesh=mesh,
        in_specs=(placed,) * 5 + (P("tm", "height", None, None),),
        out_specs=(placed,) * 3,
        check_vma=False,
    )
```

```python
import functools

import jax
import jax.numpy as jnp
from jax import lax
from jax.experimental import pallas as pl
from jax.experimental.pallas import tpu as pltpu
from jax.sharding import PartitionSpec as P

VMEM = pl.BlockSpec(memory_space=pltpu.VMEM)
HBM = pl.BlockSpec(memory_space=pltpu.HBM)
LIMIT = pltpu.CompilerParams(vmem_limit_bytes=32 * 1024 * 1024)
ROWS_T = (((1,), (1,)), ((), ()))
COLS_T = (((0,), (0,)), ((), ()))


def dot(a, b, dims=(((1,), (0,)), ((), ()))):
    return lax.dot_general(a, b, dims, preferred_element_type=jnp.float32)


LATE, EARLY = 0, 1


def place():
    t = lax.axis_index("tm")
    return t // 2, t % 2, lax.axis_index("height")


def head_at():
    y, c, z = place()
    return (c + y + z) % 2


def pair(index, which):
    rising = (index % 2) == (0 if which == 0 else 1)
    return rising, jnp.where(rising, index + 1, index - 1)


def within(index, size):
    return (index >= 0) & (index < size)


def pack_kernel(tok, k_ref, v_ref, q_ref, g_ref, o_ref, mask_ref, kv_ref, rest_ref, other_ref, flags, sems):
    head = head_at()
    copies = [pltpu.make_async_copy(mask_ref, flags, sems.at[10])]
    for i, ref in enumerate((k_ref, v_ref, q_ref, g_ref, o_ref)):
        own = (kv_ref if i < 2 else rest_ref).at[pl.ds((i if i < 2 else i - 2) * tok, tok), :]
        copies.append(pltpu.make_async_copy(ref.at[0, 0, head, 0], own, sems.at[2 * i + 1]))
        copies.append(
            pltpu.make_async_copy(ref.at[0, 0, 1 - head, 0], other_ref.at[pl.ds(i * tok, tok), :], sems.at[2 * i])
        )
    for copy in copies:
        copy.start()
    copies[0].wait()
    row = lax.broadcasted_iota(jnp.int32, (16, rest_ref.shape[1]), 0)
    spread = jnp.zeros(row.shape, jnp.float32)
    for i in range(9):
        on = (flags[0, 0, 0, 9 * (i // 3) + 3 * (i % 3) + 1] != 0).astype(jnp.float32)
        spread = jnp.where(row == i, on, spread)
    rest_ref[pl.ds(3 * tok, 16), :] = spread.astype(jnp.bfloat16)
    other_ref[pl.ds(5 * tok, 16), :] = spread.astype(jnp.bfloat16)
    for copy in copies[1:]:
        copy.wait()


def rows_at(index, tok):
    return pl.ds(index * tok, tok)


def border_is_own(y, c):
    rising, _ = pair(y, 0)
    return (c == 1) == rising


def pick(near, which, own, par):
    return jnp.where(near, own, par) if which == 0 else jnp.where(near, par, own)


def three_terms(row):
    terms = []
    for _ in range(3):
        terms.append(row.astype(jnp.bfloat16).astype(jnp.float32))
        row = row - terms[-1]
    return terms


def line_kernel(tok, rest_ref, par_ref, par_kv_ref, *border_refs):
    y, c, _ = place()
    near = border_is_own(y, c)
    for i in range(2):
        par_kv_ref[rows_at(i, tok), :] = par_ref[rows_at(i, tok), :]
    width = par_ref.shape[1]
    f32 = jnp.float32
    q, g, o = (
        [pick(near, which, rest_ref[rows_at(i, tok), :], par_ref[rows_at(i + 2, tok), :]) for which in range(2)]
        for i in range(3)
    )
    own_flags, par_flags = rest_ref[pl.ds(3 * tok, 16), :].astype(f32), par_ref[pl.ds(5 * tok, 16), :].astype(f32)
    flags = [pick(near, which, own_flags, par_flags)[0:9] for which in range(2)]
    product = jnp.concatenate(g, axis=0).astype(f32) * jnp.concatenate(o, axis=0).astype(f32)
    terms = [
        [term[:, start : start + width] for start in range(0, 2 * tok, width)]
        for term in three_terms(jnp.sum(product.T, axis=0, keepdims=True))
    ]
    for which, ref in enumerate(border_refs):
        ref[rows_at(0, tok), :], ref[rows_at(1, tok), :] = q[which], g[which]
        part = slice(0, 2) if which == 0 else slice(len(terms[0]) - 2, None)
        lines = [flags[which]] + [row for term in terms for row in term[part]] + [jnp.zeros((1, width), f32)]
        ref[pl.ds(2 * tok, 16), :] = jnp.concatenate(lines, axis=0).astype(jnp.bfloat16)
    lines = flags + [row for term in terms for row in term] + [jnp.zeros((5, width), f32)]
    par_kv_ref[pl.ds(2 * tok, 32), :] = jnp.concatenate(lines, axis=0).astype(jnp.bfloat16)


def foreign_delta(ref, tok):
    terms = ref[pl.ds(2 * tok, 16), :].astype(jnp.float32)
    return jnp.concatenate(
        [sum(terms[9 + 2 * i + half : 10 + 2 * i + half] for i in range(3)) for half in range(2)], axis=1
    )


def line_place(z, line, heights):
    if line == 0:
        return True, lambda flags, dt: flags[3 * dt + 1 : 3 * dt + 2]
    rising, at = pair(z, line - 1)
    return within(at, heights), lambda flags, dt: jnp.where(
        rising, flags[3 * dt + 2 : 3 * dt + 3], flags[3 * dt : 3 * dt + 1]
    )


def lanes_of(tok, border, other):
    width = border.shape[1]
    lane = lax.broadcasted_iota(jnp.int32, (1, width), 1)
    return jnp.concatenate(
        [jnp.where(lane + start < tok, border, other) for start in range(0, 2 * tok, width)], axis=1
    )


def flag_row(tok, slot, at, own_flags, par_flags, own_query):
    y, c, _ = place()
    first, near = c == 0, border_is_own(y, c)
    if slot == 0:
        own, par = at(own_flags, 1), jnp.where(first, at(par_flags, 0), at(par_flags, 2))
    else:
        own, par = jnp.where(first, at(own_flags, 2), at(own_flags, 0)), at(par_flags, 1)
    if own_query:
        centre = jnp.ones_like(own)
        own, par = (centre, par) if slot == 0 else (own, centre)
    return lanes_of(tok, pick(near, 0, own, par), pick(near, 1, own, par))


def first_kernel(tok, heights, scale, kv_ref, par_kv_ref, rest_ref, par_ref, q_all, g_all, table, s_ref, d_ref):
    qg = (q_all, g_all)
    y, c, z = place()
    two = 2 * tok
    width = rest_ref.shape[1]
    f32 = jnp.float32
    near = border_is_own(y, c)
    out = []
    for part in range(3):
        own, par = rest_ref[rows_at(part, tok), :], par_ref[rows_at(part + 2, tok), :]
        tiles = [pick(near, which, own, par) for which in range(2)]
        if part == 2:
            out = jnp.concatenate(tiles, axis=0)
        else:
            for which in range(2):
                qg[part][rows_at(which, tok), :] = tiles[which]
    delta = jnp.sum((qg[1][...].astype(f32) * out.astype(f32)).T, axis=0, keepdims=True)

    own_flags = rest_ref[pl.ds(3 * tok, 16), :].astype(f32)
    par_flags = par_ref[pl.ds(5 * tok, 16), :].astype(f32)
    lines = []
    for line in range(3):
        inside, at = line_place(z, line, heights)
        for slot in range(2):
            row = flag_row(tok, slot, at, own_flags, par_flags, line == 0)
            lines.append(jnp.where(inside, (row - 1.0) * 1e30, -1e30))
    table[...] = jnp.concatenate(lines + [delta, jnp.zeros((1, two), f32)], axis=0)
    for i, source in enumerate((kv_ref, par_kv_ref)):
        rows = rows_at(i, tok)
        s_ref[rows, :] = dot(source[rows_at(0, tok), :], qg[0][...], ROWS_T) * scale + table[i : i + 1, :]
        d_ref[rows, :] = dot(source[rows_at(1, tok), :], qg[1][...], ROWS_T) - table[6:7, :]


def largest(tok, blocks):
    lanes = blocks[0][0].shape[1]
    top = jnp.full((8, lanes), -1e30, jnp.float32)
    for ref, i in blocks:
        top = jnp.maximum(top, jnp.max(ref[rows_at(i, tok), :].reshape(tok // 8, 8, lanes), axis=0))
    return jnp.max(top, axis=0, keepdims=True)


def summed(tok, blocks, top):
    lanes = blocks[0][0].shape[1]
    total = jnp.zeros((8, lanes), jnp.float32)
    for ref, i in blocks:
        weights = jnp.exp(ref[rows_at(i, tok), :] - top)
        total = total + jnp.sum(weights.reshape(tok // 8, 8, lanes), axis=0)
    return jnp.sum(total, axis=0, keepdims=True)


def early_kernel(tok, scale, q_all, g_all, table, s_own, one_ref, two_ref, s_ref, d_ref, part_ref):
    qg = (q_all, g_all)
    for i, source in enumerate((one_ref, two_ref)):
        rows = rows_at(i, tok)
        s_ref[rows, :] = dot(source[rows_at(0, tok), :], qg[0][...], ROWS_T) * scale + table[2 + 2 * i + EARLY : 3 + 2 * i + EARLY, :]
        d_ref[rows, :] = dot(source[rows_at(1, tok), :], qg[1][...], ROWS_T) - table[6:7, :]
    blocks = [(ref, i) for ref in (s_own, s_ref) for i in range(2)]
    top = largest(tok, blocks)
    total = summed(tok, blocks, top)
    part_ref[...] = jnp.concatenate([top, total, jnp.zeros((6, 2 * tok), jnp.float32)], axis=0)


def foreign_rows(ref, part, which, tok):
    block = ref[rows_at(part, tok), :]
    gap = jnp.zeros((2 * block.shape[1] - tok, block.shape[1]), block.dtype)
    return jnp.concatenate([block, gap] if which == 0 else [gap, block], axis=0)


def foreign_lanes(which, tok, width):
    return slice(0, 2 * width) if which == 0 else slice(2 * tok - 2 * width, 2 * tok)


def far_row(tok, which, row):
    lane, width = lax.broadcasted_iota(jnp.int32, row.shape, 1), row.shape[1]
    return jnp.concatenate(
        [
            jnp.where(lane + start < tok if which == 0 else lane + start >= 2 * width - tok, row, 0.0)
            for start in (0, width)
        ],
        axis=1,
    )


def to_lanes(which, tok, row, fill):
    gap = jnp.full((1, 2 * tok - row.shape[1]), fill, jnp.float32)
    return jnp.concatenate([row, gap] if which == 0 else [gap, row], axis=1)


def score_kernel(tok, chips, heights, sides, scale, q_all, g_all, table, part, *refs):
    qg = (q_all, g_all)
    keys, foreign, refs = refs[:6], refs[6 : 6 + sides], refs[6 + sides :]
    s_late, s_far, *notes = refs
    y, c, z = place()
    near = border_is_own(y, c)
    two = 2 * tok
    f32 = jnp.float32
    far = []
    for which in range(sides):
        rising, y_at = pair(y, which)
        flags = foreign[which][pl.ds(2 * tok, 16), :].astype(f32)
        queries = foreign_rows(foreign[which], 0, which, tok)
        for line in range(3):
            inside, at = line_place(z, line, heights)
            row = far_row(tok, which, jnp.where(rising, at(flags, 0), at(flags, 2)))
            bias = jnp.where(inside & within(y_at, chips), (row - 1.0) * 1e30, -1e30)
            border = pick(near, which, keys[2 * line][rows_at(0, tok), :], keys[2 * line + 1][rows_at(0, tok), :])
            s_far[rows_at(3 * which + line, tok), :] = dot(border, queries, ROWS_T) * scale + bias
        blocks = [(s_far, 3 * which + line) for line in range(3)]
        top = largest(tok, blocks)
        far.append([to_lanes(which, tok, top, -1e30), to_lanes(which, tok, summed(tok, blocks, top), 0.0)])
    for i in range(2):
        at = 2 + 2 * i + LATE
        scores = dot(keys[at][rows_at(0, tok), :], qg[0][...], ROWS_T) * scale
        s_late[rows_at(i, tok), :] = scores + table[at : at + 1, :]
    blocks = [(s_late, i) for i in range(2)]
    top = jnp.maximum(part[0:1, :], largest(tok, blocks))
    total = part[1:2, :] * jnp.exp(part[0:1, :] - top) + summed(tok, blocks, top)
    for which in range(sides):
        notes[which][...] = jnp.concatenate([top, total] + far[which] + [jnp.zeros((4, two), f32)], axis=0)


def middle_kernel(tok, sides, scale, q_all, g_all, table, s_own, d_own, s_early, d_early, s_late, s_far, *refs):
    qg = (q_all, g_all)
    tiles, foreign, sent = refs[:6], refs[6 : 6 + sides], refs[6 + sides : 6 + 2 * sides]
    e_ref, ds_ref, e_far, ds_far, dq_ref, *far_dq = refs[6 + 2 * sides :]
    y, c, _ = place()
    near = border_is_own(y, c)
    f32, bf16 = jnp.float32, jnp.bfloat16
    dq = jnp.zeros(dq_ref.shape, f32)
    for line in range(3):
        for slot in range(2):
            i, at = 2 * line + slot, rows_at(line - 1 if line else slot, tok)
            scores = s_own if line == 0 else s_early if slot == EARLY else s_late
            weights = jnp.exp(scores[at, :] - sent[0][0:1, :])
            if line and slot == LATE:
                grads = dot(tiles[i][rows_at(1, tok), :], qg[1][...], ROWS_T) - table[6:7, :]
            else:
                grads = (d_early if line else d_own)[at, :]
            low = (weights * grads * scale).astype(bf16)
            if line == 0:
                e_ref[rows_at(i, tok), :] = weights.astype(bf16)
                ds_ref[rows_at(i, tok), :] = low
            dq = dq + dot(tiles[i][rows_at(0, tok), :], low, COLS_T)
    dq_ref[...] = dq
    for which in range(sides):
        far_g = foreign_rows(foreign[which], 1, which, tok)
        delta = foreign_delta(foreign[which], tok)
        lanes = foreign_lanes(which, tok, qg[0].shape[1])
        dq = jnp.zeros(far_dq[which].shape, f32)
        for line in range(3):
            rows = rows_at(3 * which + line, tok)
            own, par = tiles[2 * line], tiles[2 * line + 1]
            key, value = (pick(near, which, own[rows_at(i, tok), :], par[rows_at(i, tok), :]) for i in range(2))
            weights = jnp.exp(s_far[rows, :] - sent[which][2:3, lanes])
            low = (weights * (dot(value, far_g, ROWS_T) - delta) * scale).astype(bf16)
            if line == 0:
                e_far[rows_at(which, tok), :] = weights.astype(bf16)
                ds_far[rows_at(which, tok), :] = low
            dq = dq + dot(key, low, COLS_T)
        far_dq[which][...] = dq


def message_kernel(tok, q_all, g_all, *refs):
    *foreign, out_ref = refs
    out_ref[pl.ds(0, 2 * tok), :] = q_all[...]
    out_ref[pl.ds(2 * tok, 2 * tok), :] = g_all[...]
    for which, ref in enumerate(foreign):
        far_part(out_ref, which, tok)[...] = ref[pl.ds(0, 2 * tok + 16), :]


def far_part(ref, which, tok):
    return ref.at[pl.ds(4 * tok + which * (2 * tok + 16), 2 * tok + 16), :]


def total_kernel(tok, chips, sides, *refs):
    sent, came, note_ref = refs[:sides], refs[sides : 2 * sides], refs[2 * sides]
    y, _, _ = place()

    def log_total(top, total, other_top, other_total):
        both = jnp.maximum(top, other_top)
        return both + jnp.log(total * jnp.exp(top - both) + other_total * jnp.exp(other_top - both))

    lse, far_rows = None, []
    for which in range(sides):
        _, y_at = pair(y, which)
        inside = within(y_at, chips)
        note = came[which]
        far_lse = log_total(note[0:1, :], note[1:2, :], sent[which][2:3, :], sent[which][3:4, :])
        far_rows.append(jnp.where(inside, far_lse, 0.0))
        other = jnp.where(inside, note[2:3, :], -1e30), jnp.where(inside, note[3:4, :], 0.0)
        if which == 0:
            lse = log_total(sent[0][0:1, :], sent[0][1:2, :], *other)
        else:
            lse = log_total(lse, jnp.ones_like(lse), *other)
    rows = [lse] + far_rows
    note_ref[...] = jnp.concatenate(rows + [jnp.zeros((8 - len(rows), 2 * tok), jnp.float32)], axis=0)


def share_kernel(tok, chips, sides, note, *refs):
    far_dq, sent, shares = (refs[i * sides : (i + 1) * sides] for i in range(3))
    y, _, _ = place()
    width = far_dq[0].shape[0]
    for which in range(sides):
        _, y_at = pair(y, which)
        lanes = foreign_lanes(which, tok, width)
        factor = jnp.exp(sent[which][2:3, lanes] - note[1 + which : 2 + which, lanes])
        share = (far_dq[which][...] * jnp.where(within(y_at, chips), factor, 0.0)).T
        shares[which][...] = (share[:tok] if which == 0 else share[2 * width - tok :]).astype(jnp.bfloat16)


def line_query_kernel(tok, chips, heights, sides, scale, kv_ref, par_kv_ref, *refs):
    queries, extras, outs = refs[:2], refs[2:4], refs[4:]
    e_ref, ds_ref, e_far, ds_far, top_ref = outs
    y, c, z = place()
    near = border_is_own(y, c)
    two = 2 * tok
    width = kv_ref.shape[1]
    f32, bf16 = jnp.float32, jnp.bfloat16
    tops, far_tops = [], []
    tiles = (kv_ref, par_kv_ref)
    for line in (1, 2):
        rising, z_at = pair(z, line - 1)
        inside = within(z_at, heights)

        def at(flags, dt):
            return jnp.where(rising, flags[3 * dt : 3 * dt + 1], flags[3 * dt + 2 : 3 * dt + 3])

        rows = extras[line - 1][pl.ds(2 * tok, 32), :].astype(f32)
        own_flags, par_flags = (pick(near, which, rows[0:9], rows[9:18]) for which in range(2))
        delta = [sum(rows[18 + 3 * i + part : 19 + 3 * i + part] for i in range(3)) for part in range(two // width)]
        delta = jnp.concatenate(delta, axis=1)
        line_q, line_g = (queries[line - 1][pl.ds(part * two, two), :] for part in range(2))
        scores = []
        for slot in range(2):
            row = flag_row(tok, slot, at, own_flags, par_flags, False)
            bias = jnp.where(inside, (row - 1.0) * 1e30, -1e30)
            scores.append(dot(tiles[slot][rows_at(0, tok), :], line_q, ROWS_T) * scale + bias)
        top = jnp.maximum(*(jnp.max(block, axis=0, keepdims=True) for block in scores))
        tops.append(top)
        for slot in range(2):
            weights = jnp.exp(scores[slot] - top)
            grads = dot(tiles[slot][rows_at(1, tok), :], line_g, ROWS_T) - delta
            kept = rows_at(2 * (line - 1) + slot, tok)
            e_ref[kept, :] = weights.astype(bf16)
            ds_ref[kept, :] = (weights * grads * scale).astype(bf16)
        for which in range(sides):
            ref = far_part(queries[line - 1], which, tok)
            y_rising, y_at = pair(y, which)
            flags = ref[pl.ds(2 * tok, 16), :].astype(f32)
            row = far_row(tok, which, jnp.where(y_rising, at(flags, 0), at(flags, 2)))
            bias = jnp.where(inside & within(y_at, chips), (row - 1.0) * 1e30, -1e30)
            key, value = (pick(near, which, *(tile[rows_at(i, tok), :] for tile in tiles)) for i in range(2))
            far_q, far_g = (foreign_rows(ref, part, which, tok) for part in range(2))
            block = dot(key, far_q, ROWS_T) * scale + bias
            top = jnp.max(block, axis=0, keepdims=True)
            far_tops.append(to_lanes(which, tok, top, -1e30))
            weights = jnp.exp(block - top)
            grads = dot(value, far_g, ROWS_T) - foreign_delta(ref, tok)
            kept = rows_at(2 * which + line - 1, tok)
            e_far[kept, :] = weights.astype(bf16)
            ds_far[kept, :] = (weights * grads * scale).astype(bf16)
    top_ref[...] = jnp.concatenate(tops + far_tops + [jnp.zeros((6 - 2 * sides, two), f32)], axis=0)


def times(block, factor):
    column = jnp.broadcast_to(factor, (block.shape[1], factor.shape[1])).T
    return (block.astype(jnp.float32) * column).astype(jnp.bfloat16)


def key_sums(tok, near, line, e_ref, ds_ref, scaled, far):
    rows = [rows_at(2 * line + slot, tok) for slot in range(2)]
    sums = [[dot(ref[at, :], scaled[i]) for i, ref in enumerate((ds_ref, e_ref))] for at in rows]
    for which, (e_far, ds_far, at, far_scaled) in enumerate(far):
        for i, ref in enumerate((ds_far, e_far)):
            block = dot(ref[at, :], far_scaled[i])
            for slot in range(2):
                sums[slot][i] = sums[slot][i] + jnp.where(near == ((slot == 0) == (which == 0)), block, 0.0)
    return sums


def stay_kernel(tok, chips, sides, q_all, g_all, e_ref, ds_ref, e_far, ds_far, raw_dq, note, *refs):
    qg = (q_all, g_all)
    sent, foreign, (own_ref, dq_ref) = refs[:sides], refs[sides : 2 * sides], refs[2 * sides :]
    y, c, _ = place()
    near = border_is_own(y, c)
    width = qg[0].shape[1]
    factor = jnp.exp(sent[0][0:1, :] - note[0:1, :])
    dq_ref[...] = (raw_dq[...] * factor).T
    far = []
    for which in range(sides):
        _, y_at = pair(y, which)
        lanes = foreign_lanes(which, tok, width)
        far_factor = jnp.exp(sent[which][2:3, lanes] - note[1 + which : 2 + which, lanes])
        far_factor = jnp.where(within(y_at, chips), far_factor, 0.0)
        scaled = [times(foreign_rows(foreign[which], part, which, tok), far_factor) for part in range(2)]
        far.append((e_far, ds_far, rows_at(which, tok), scaled))
    sums = key_sums(tok, near, 0, e_ref, ds_ref, [times(qg[part][...], factor) for part in range(2)], far)
    for slot in range(2):
        for i in range(2):
            own_ref[i, rows_at(slot, tok), :] = sums[slot][i]


def leave_kernel(tok, chips, sides, own_ref, dq_ref, e_ref, ds_ref, e_far, ds_far, top_ref, *refs):
    queries, notes, backs = refs[:2], refs[2:4], refs[4 : 4 + sides]
    mine_ref, mine_q_ref, swap_ref = refs[4 + sides :]
    y, c, _ = place()
    near = border_is_own(y, c)
    f32, bf16 = jnp.float32, jnp.bfloat16
    width = dq_ref.shape[1]
    sums = [[own_ref[i, rows_at(slot, tok), :] for i in range(2)] for slot in range(2)]
    for line in (1, 2):
        note = notes[line - 1]
        factor = jnp.exp(top_ref[line - 1 : line, :] - note[0:1, :])
        scaled = [times(queries[line - 1][pl.ds(part * 2 * tok, 2 * tok), :], factor) for part in range(2)]
        far = []
        for which in range(sides):
            lanes = foreign_lanes(which, tok, width)
            at = 2 + sides * (line - 1) + which
            far_factor = jnp.exp(top_ref[at : at + 1, lanes] - note[1 + which : 2 + which, lanes])
            rows = [foreign_rows(far_part(queries[line - 1], which, tok), part, which, tok) for part in range(2)]
            far.append(
                (e_far, ds_far, rows_at(2 * which + line - 1, tok), [times(block, far_factor) for block in rows])
            )
        more = key_sums(tok, near, line - 1, e_ref, ds_ref, scaled, far)
        sums = [[sums[slot][i] + more[slot][i] for i in range(2)] for slot in range(2)]
    for i in range(2):
        mine_ref[i], swap_ref[i] = sums[0][i].astype(bf16), sums[1][i].astype(bf16)
    tiles = []
    for tile in range(2):
        value = dq_ref[rows_at(tile, tok), :]
        if tile < sides:
            _, y_at = pair(y, tile)
            value = value + jnp.where(within(y_at, chips), backs[tile][...].astype(f32), 0.0)
        tiles.append(value.astype(bf16))
    mine_q_ref[...] = jnp.where(near, tiles[0], tiles[1])
    swap_ref[2] = jnp.where(near, tiles[1], tiles[0])


def final_kernel(mine_ref, swap_ref, mine_q_ref, gq_ref, gk_ref, gv_ref):
    head = head_at()
    gq_ref[0, 0, head, 0] = mine_q_ref[...]
    gq_ref[0, 0, 1 - head, 0] = swap_ref[2]
    for i, ref in enumerate((gk_ref, gv_ref)):
        ref[0, 0, head, 0] = mine_ref[i]
        ref[0, 0, 1 - head, 0] = swap_ref[i]


def body(queries, keys, values, grad_out, attn_out, window_mask):
    tok, width = queries.shape[-2:]
    scale = width ** -0.5
    times, heights = lax.axis_size("tm"), lax.axis_size("height")
    chips = times // 2
    sides = 1 if chips == 2 else 2
    bf16, f32 = jnp.bfloat16, jnp.float32

    def call(kernel, shapes, specs, scratch=(), cost=0):
        return pl.pallas_call(
            kernel,
            out_shape=[jax.ShapeDtypeStruct(*shape) for shape in shapes],
            in_specs=list(specs),
            out_specs=[VMEM] * len(shapes),
            scratch_shapes=list(scratch),
            compiler_params=LIMIT,
            cost_estimate=pl.CostEstimate(flops=cost * 10**9, bytes_accessed=0, transcendentals=0) if cost else None,
        )

    def partner(index, which, size):
        if which is None:
            return index
        at = index + 1 if index % 2 == which else index - 1
        return at if 0 <= at < size else None

    def exchange(block, y_which, z_which):
        pairs = []
        for t in range(times):
            for z in range(heights):
                y_at, z_at = partner(t // 2, y_which, chips), partner(z, z_which, heights)
                at = t * heights + z
                alone = y_at is None or z_at is None
                pairs.append((at, (t ^ 1) * heights + z if alone else (2 * y_at + 1 - t % 2) * heights + z_at))
        return lax.ppermute(block, ("tm", "height"), pairs)

    def swap_cores(block):
        return lax.ppermute(block, "tm", [(t, t ^ 1) for t in range(times)])

    line_shape, tile_shape = ((2, 2 * tok, width), bf16), ((2, tok, width), bf16)
    extra = 64
    arguments = (keys, values, queries, grad_out, attn_out, window_mask)
    kv, rest, other = call(
        functools.partial(pack_kernel, tok),
        [((2 * tok + extra, width), bf16), ((3 * tok + 16, width), bf16), ((5 * tok + 16, width), bf16)],
        [HBM] * 6,
        [pltpu.SMEM(window_mask.shape, jnp.int32), pltpu.SemaphoreType.DMA((11,))],
    )(*(pltpu.with_memory_space_constraint(x, pltpu.HBM) for x in arguments))
    early = [exchange(kv, None, which) for which in range(2)]
    par = swap_cores(other)
    border_shape, two = ((2 * tok + 48, width), bf16), 2 * tok
    par_kv, *borders = call(
        functools.partial(line_kernel, tok), [((2 * tok + 32, width), bf16)] + [border_shape] * sides, [VMEM] * 2
    )(rest, par)
    foreign = [exchange(borders[which], which, None) for which in range(sides)]
    late = [exchange(par_kv, None, which) for which in range(2)]
    tiles = (kv, par_kv, late[0], early[0], late[1], early[1])
    note_shape, raw_shape = ((8, two), f32), ((width, two), f32)

    def square(count, kind=f32):
        return ((count * tok, two), kind)

    def far_square(kind=f32):
        return ((3 * sides * tok, 2 * width), kind)

    q_all, g_all, table, s_own, d_own = call(
        functools.partial(first_kernel, tok, heights, scale),
        [((two, width), bf16)] * 2 + [note_shape, square(2), square(2)],
        [VMEM] * 4,
    )(kv, par_kv, rest, par)
    qg = (q_all, g_all)
    (message,) = call(
        functools.partial(message_kernel, tok),
        [((4 * tok + sides * (2 * tok + 16), width), bf16)],
        [VMEM] * (2 + sides),
    )(*qg, *foreign)
    queries_in = [exchange(message, None, which) for which in range(2)]
    s_early, d_early, part = call(
        functools.partial(early_kernel, tok, scale), [square(2), square(2), note_shape], [VMEM] * 6, cost=20
    )(*qg, table, s_own, *early)
    s_late, s_far, *sent = call(
        functools.partial(score_kernel, tok, chips, heights, sides, scale),
        [square(2), far_square()] + [note_shape] * sides,
        [VMEM] * (10 + sides),
    )(*qg, table, part, *tiles, *foreign)
    came = [exchange(sent[which], which, None) for which in range(sides)]
    far_tile = ((sides * tok, 2 * width), bf16)
    e, ds, e_far, ds_far, raw_dq, *far_dq = call(
        functools.partial(middle_kernel, tok, sides, scale),
        [square(2, bf16)] * 2 + [far_tile] * 2 + [raw_shape] + [((width, 2 * width), f32)] * sides,
        [VMEM] * (15 + 2 * sides),
        cost=20,
    )(*qg, table, s_own, d_own, s_early, d_early, s_late, s_far, *tiles, *foreign, *sent)
    (note,) = call(functools.partial(total_kernel, tok, chips, sides), [note_shape], [VMEM] * (2 * sides))(*sent, *came)
    shares = call(
        functools.partial(share_kernel, tok, chips, sides), [((tok, width), bf16)] * sides, [VMEM] * (1 + 2 * sides)
    )(note, *far_dq, *sent)
    notes = [exchange(note, None, which) for which in range(2)]
    shares = [exchange(share, which, None) for which, share in enumerate(shares)]
    far_pair = ((2 * sides * tok, 2 * width), bf16)
    line_terms = call(
        functools.partial(line_query_kernel, tok, chips, heights, sides, scale),
        [square(4, bf16)] * 2 + [far_pair] * 2 + [note_shape],
        [VMEM] * 6,
        cost=20,
    )(kv, par_kv, *queries_in, *late)
    own, dq = call(
        functools.partial(stay_kernel, tok, chips, sides),
        [((2, two, width), f32), ((two, width), f32)],
        [VMEM] * (8 + 2 * sides),
    )(*qg, e, ds, e_far, ds_far, raw_dq, note, *sent, *foreign)
    mine, mine_q, leaving = call(
        functools.partial(leave_kernel, tok, chips, sides),
        [tile_shape, ((tok, width), bf16), ((3, tok, width), bf16)],
        [VMEM] * (11 + sides),
    )(own, dq, *line_terms, *queries_in, *notes, *shares)
    return call(final_kernel, [(queries.shape, bf16)] * 3, [VMEM] * 3)(mine, swap_cores(leaving), mine_q)


def solution(mesh):
    placed = P("tm", "height", "dp", None, None, None)
    return jax.shard_map(
        body,
        mesh=mesh,
        in_specs=(placed,) * 5 + (P("tm", "height", None, None),),
        out_specs=(placed,) * 3,
        check_vma=False,
    )
```

```python
import functools

import jax
import jax.numpy as jnp
from jax import lax
from jax.experimental import pallas as pl
from jax.experimental.pallas import tpu as pltpu
from jax.sharding import PartitionSpec as P

VMEM = pl.BlockSpec(memory_space=pltpu.VMEM)
HBM = pl.BlockSpec(memory_space=pltpu.HBM)
LIMIT = pltpu.CompilerParams(vmem_limit_bytes=32 * 1024 * 1024)
ROWS_T = (((1,), (1,)), ((), ()))
COLS_T = (((0,), (0,)), ((), ()))


def dot(a, b, dims=(((1,), (0,)), ((), ()))):
    return lax.dot_general(a, b, dims, preferred_element_type=jnp.float32)


LATE, EARLY = 0, 1


def place():
    t = lax.axis_index("tm")
    return t // 2, t % 2, lax.axis_index("height")


def head_at():
    y, c, z = place()
    return (c + y + z) % 2


def pair(index, which):
    rising = (index % 2) == (0 if which == 0 else 1)
    return rising, jnp.where(rising, index + 1, index - 1)


def within(index, size):
    return (index >= 0) & (index < size)


def pack_kernel(tok, k_ref, v_ref, q_ref, g_ref, o_ref, mask_ref, kv_ref, rest_ref, other_ref, flags, sems):
    head = head_at()
    copies = [pltpu.make_async_copy(mask_ref, flags, sems.at[10])]
    for i, ref in enumerate((k_ref, v_ref, q_ref, g_ref, o_ref)):
        own = (kv_ref if i < 2 else rest_ref).at[pl.ds((i if i < 2 else i - 2) * tok, tok), :]
        copies.append(pltpu.make_async_copy(ref.at[0, 0, head, 0], own, sems.at[2 * i + 1]))
        copies.append(
            pltpu.make_async_copy(ref.at[0, 0, 1 - head, 0], other_ref.at[pl.ds(i * tok, tok), :], sems.at[2 * i])
        )
    for copy in copies:
        copy.start()
    copies[0].wait()
    row = lax.broadcasted_iota(jnp.int32, (16, rest_ref.shape[1]), 0)
    spread = jnp.zeros(row.shape, jnp.float32)
    for i in range(9):
        on = (flags[0, 0, 0, 9 * (i // 3) + 3 * (i % 3) + 1] != 0).astype(jnp.float32)
        spread = jnp.where(row == i, on, spread)
    rest_ref[pl.ds(3 * tok, 16), :] = spread.astype(jnp.bfloat16)
    other_ref[pl.ds(5 * tok, 16), :] = spread.astype(jnp.bfloat16)
    for copy in copies[1:]:
        copy.wait()


def rows_at(index, tok):
    return pl.ds(index * tok, tok)


def border_is_own(y, c):
    rising, _ = pair(y, 0)
    return (c == 1) == rising


def pick(near, which, own, par):
    return jnp.where(near, own, par) if which == 0 else jnp.where(near, par, own)


def three_terms(row):
    terms = []
    for _ in range(3):
        terms.append(row.astype(jnp.bfloat16).astype(jnp.float32))
        row = row - terms[-1]
    return terms


def line_kernel(tok, rest_ref, par_ref, par_kv_ref, *border_refs):
    y, c, _ = place()
    near = border_is_own(y, c)
    for i in range(2):
        par_kv_ref[rows_at(i, tok), :] = par_ref[rows_at(i, tok), :]
    width = par_ref.shape[1]
    f32 = jnp.float32
    q, g, o = (
        [pick(near, which, rest_ref[rows_at(i, tok), :], par_ref[rows_at(i + 2, tok), :]) for which in range(2)]
        for i in range(3)
    )
    own_flags, par_flags = rest_ref[pl.ds(3 * tok, 16), :].astype(f32), par_ref[pl.ds(5 * tok, 16), :].astype(f32)
    flags = [pick(near, which, own_flags, par_flags)[0:9] for which in range(2)]
    product = jnp.concatenate(g, axis=0).astype(f32) * jnp.concatenate(o, axis=0).astype(f32)
    terms = [
        [term[:, start : start + width] for start in range(0, 2 * tok, width)]
        for term in three_terms(jnp.sum(product.T, axis=0, keepdims=True))
    ]
    for which, ref in enumerate(border_refs):
        ref[rows_at(0, tok), :], ref[rows_at(1, tok), :] = q[which], g[which]
        part = slice(0, 2) if which == 0 else slice(len(terms[0]) - 2, None)
        lines = [flags[which]] + [row for term in terms for row in term[part]] + [jnp.zeros((1, width), f32)]
        ref[pl.ds(2 * tok, 16), :] = jnp.concatenate(lines, axis=0).astype(jnp.bfloat16)
    lines = flags + [row for term in terms for row in term] + [jnp.zeros((5, width), f32)]
    par_kv_ref[pl.ds(2 * tok, 32), :] = jnp.concatenate(lines, axis=0).astype(jnp.bfloat16)


def foreign_delta(ref, tok):
    terms = ref[pl.ds(2 * tok, 16), :].astype(jnp.float32)
    return jnp.concatenate(
        [sum(terms[9 + 2 * i + half : 10 + 2 * i + half] for i in range(3)) for half in range(2)], axis=1
    )


def line_place(z, line, heights):
    if line == 0:
        return True, lambda flags, dt: flags[3 * dt + 1 : 3 * dt + 2]
    rising, at = pair(z, 2 - line)
    return within(at, heights), lambda flags, dt: jnp.where(
        rising, flags[3 * dt + 2 : 3 * dt + 3], flags[3 * dt : 3 * dt + 1]
    )


def lanes_of(tok, border, other):
    width = border.shape[1]
    lane = lax.broadcasted_iota(jnp.int32, (1, width), 1)
    return jnp.concatenate(
        [jnp.where(lane + start < tok, border, other) for start in range(0, 2 * tok, width)], axis=1
    )


def flag_row(tok, slot, at, own_flags, par_flags, own_query):
    y, c, _ = place()
    first, near = c == 0, border_is_own(y, c)
    if slot == 0:
        own, par = at(own_flags, 1), jnp.where(first, at(par_flags, 0), at(par_flags, 2))
    else:
        own, par = jnp.where(first, at(own_flags, 2), at(own_flags, 0)), at(par_flags, 1)
    if own_query:
        centre = jnp.ones_like(own)
        own, par = (centre, par) if slot == 0 else (own, centre)
    return lanes_of(tok, pick(near, 0, own, par), pick(near, 1, own, par))


def first_kernel(tok, heights, scale, kv_ref, par_kv_ref, rest_ref, par_ref, q_all, g_all, table, s_ref, d_ref):
    qg = (q_all, g_all)
    y, c, z = place()
    two = 2 * tok
    width = rest_ref.shape[1]
    f32 = jnp.float32
    near = border_is_own(y, c)
    out = []
    for part in range(3):
        own, par = rest_ref[rows_at(part, tok), :], par_ref[rows_at(part + 2, tok), :]
        tiles = [pick(near, which, own, par) for which in range(2)]
        if part == 2:
            out = jnp.concatenate(tiles, axis=0)
        else:
            for which in range(2):
                qg[part][rows_at(which, tok), :] = tiles[which]
    delta = jnp.sum((qg[1][...].astype(f32) * out.astype(f32)).T, axis=0, keepdims=True)

    own_flags = rest_ref[pl.ds(3 * tok, 16), :].astype(f32)
    par_flags = par_ref[pl.ds(5 * tok, 16), :].astype(f32)
    lines = []
    for line in range(3):
        inside, at = line_place(z, line, heights)
        for slot in range(2):
            row = flag_row(tok, slot, at, own_flags, par_flags, line == 0)
            lines.append(jnp.where(inside, (row - 1.0) * 1e30, -1e30))
    table[...] = jnp.concatenate(lines + [delta, jnp.zeros((1, two), f32)], axis=0)
    for i, source in enumerate((kv_ref, par_kv_ref)):
        rows = rows_at(i, tok)
        s_ref[rows, :] = dot(source[rows_at(0, tok), :], qg[0][...], ROWS_T) * scale + table[i : i + 1, :]
        d_ref[rows, :] = dot(source[rows_at(1, tok), :], qg[1][...], ROWS_T) - table[6:7, :]


def largest(tok, blocks):
    lanes = blocks[0][0].shape[1]
    top = jnp.full((8, lanes), -1e30, jnp.float32)
    for ref, i in blocks:
        top = jnp.maximum(top, jnp.max(ref[rows_at(i, tok), :].reshape(tok // 8, 8, lanes), axis=0))
    return jnp.max(top, axis=0, keepdims=True)


def summed(tok, blocks, top):
    lanes = blocks[0][0].shape[1]
    total = jnp.zeros((8, lanes), jnp.float32)
    for ref, i in blocks:
        weights = jnp.exp(ref[rows_at(i, tok), :] - top)
        total = total + jnp.sum(weights.reshape(tok // 8, 8, lanes), axis=0)
    return jnp.sum(total, axis=0, keepdims=True)


def early_kernel(tok, scale, q_all, g_all, table, s_own, one_ref, two_ref, s_ref, d_ref, part_ref):
    qg = (q_all, g_all)
    for i, source in enumerate((one_ref, two_ref)):
        rows = rows_at(i, tok)
        s_ref[rows, :] = dot(source[rows_at(0, tok), :], qg[0][...], ROWS_T) * scale + table[2 + 2 * i + EARLY : 3 + 2 * i + EARLY, :]
        d_ref[rows, :] = dot(source[rows_at(1, tok), :], qg[1][...], ROWS_T) - table[6:7, :]
    blocks = [(ref, i) for ref in (s_own, s_ref) for i in range(2)]
    top = largest(tok, blocks)
    total = summed(tok, blocks, top)
    part_ref[...] = jnp.concatenate([top, total, jnp.zeros((6, 2 * tok), jnp.float32)], axis=0)


def foreign_rows(ref, part, which, tok):
    block = ref[rows_at(part, tok), :]
    gap = jnp.zeros((2 * block.shape[1] - tok, block.shape[1]), block.dtype)
    return jnp.concatenate([block, gap] if which == 0 else [gap, block], axis=0)


def foreign_lanes(which, tok, width):
    return slice(0, 2 * width) if which == 0 else slice(2 * tok - 2 * width, 2 * tok)


def far_row(tok, which, row):
    lane, width = lax.broadcasted_iota(jnp.int32, row.shape, 1), row.shape[1]
    return jnp.concatenate(
        [
            jnp.where(lane + start < tok if which == 0 else lane + start >= 2 * width - tok, row, 0.0)
            for start in (0, width)
        ],
        axis=1,
    )


def to_lanes(which, tok, row, fill):
    gap = jnp.full((1, 2 * tok - row.shape[1]), fill, jnp.float32)
    return jnp.concatenate([row, gap] if which == 0 else [gap, row], axis=1)


def score_kernel(tok, chips, heights, sides, scale, q_all, g_all, table, part, *refs):
    qg = (q_all, g_all)
    foreign, keys, refs = refs[:sides], refs[sides : 6 + sides], refs[6 + sides :]
    s_late, s_far, *notes = refs
    y, c, z = place()
    near = border_is_own(y, c)
    two = 2 * tok
    f32 = jnp.float32
    far = []
    for which in range(sides):
        rising, y_at = pair(y, which)
        flags = foreign[which][pl.ds(2 * tok, 16), :].astype(f32)
        queries = foreign_rows(foreign[which], 0, which, tok)
        for line in range(3):
            inside, at = line_place(z, line, heights)
            row = far_row(tok, which, jnp.where(rising, at(flags, 0), at(flags, 2)))
            bias = jnp.where(inside & within(y_at, chips), (row - 1.0) * 1e30, -1e30)
            border = pick(near, which, keys[2 * line][rows_at(0, tok), :], keys[2 * line + 1][rows_at(0, tok), :])
            s_far[rows_at(3 * which + line, tok), :] = dot(border, queries, ROWS_T) * scale + bias
        blocks = [(s_far, 3 * which + line) for line in range(3)]
        top = largest(tok, blocks)
        far.append([to_lanes(which, tok, top, -1e30), to_lanes(which, tok, summed(tok, blocks, top), 0.0)])
    for i in range(2):
        at = 2 + 2 * i + LATE
        scores = dot(keys[at][rows_at(0, tok), :], qg[0][...], ROWS_T) * scale
        s_late[rows_at(i, tok), :] = scores + table[at : at + 1, :]
    blocks = [(s_late, i) for i in range(2)]
    top = jnp.maximum(part[0:1, :], largest(tok, blocks))
    total = part[1:2, :] * jnp.exp(part[0:1, :] - top) + summed(tok, blocks, top)
    for which in range(sides):
        notes[which][...] = jnp.concatenate([top, total] + far[which] + [jnp.zeros((4, two), f32)], axis=0)


def middle_kernel(tok, sides, scale, q_all, g_all, table, s_own, d_own, s_early, d_early, s_late, s_far, *refs):
    qg = (q_all, g_all)
    tiles, foreign, sent = refs[:6], refs[6 : 6 + sides], refs[6 + sides : 6 + 2 * sides]
    e_ref, ds_ref, e_far, ds_far, dq_ref, *far_dq = refs[6 + 2 * sides :]
    y, c, _ = place()
    near = border_is_own(y, c)
    f32, bf16 = jnp.float32, jnp.bfloat16
    dq = jnp.zeros(dq_ref.shape, f32)
    for line in range(3):
        for slot in range(2):
            i, at = 2 * line + slot, rows_at(line - 1 if line else slot, tok)
            scores = s_own if line == 0 else s_early if slot == EARLY else s_late
            weights = jnp.exp(scores[at, :] - sent[0][0:1, :])
            if line and slot == LATE:
                grads = dot(tiles[i][rows_at(1, tok), :], qg[1][...], ROWS_T) - table[6:7, :]
            else:
                grads = (d_early if line else d_own)[at, :]
            low = (weights * grads * scale).astype(bf16)
            if line == 0:
                e_ref[rows_at(i, tok), :] = weights.astype(bf16)
                ds_ref[rows_at(i, tok), :] = low
            dq = dq + dot(tiles[i][rows_at(0, tok), :], low, COLS_T)
    dq_ref[...] = dq
    for which in range(sides):
        far_g = foreign_rows(foreign[which], 1, which, tok)
        delta = foreign_delta(foreign[which], tok)
        lanes = foreign_lanes(which, tok, qg[0].shape[1])
        dq = jnp.zeros(far_dq[which].shape, f32)
        for line in range(3):
            rows = rows_at(3 * which + line, tok)
            own, par = tiles[2 * line], tiles[2 * line + 1]
            key, value = (pick(near, which, own[rows_at(i, tok), :], par[rows_at(i, tok), :]) for i in range(2))
            weights = jnp.exp(s_far[rows, :] - sent[which][2:3, lanes])
            low = (weights * (dot(value, far_g, ROWS_T) - delta) * scale).astype(bf16)
            if line == 0:
                e_far[rows_at(which, tok), :] = weights.astype(bf16)
                ds_far[rows_at(which, tok), :] = low
            dq = dq + dot(key, low, COLS_T)
        far_dq[which][...] = dq


def message_kernel(tok, q_all, g_all, *refs):
    *foreign, out_ref = refs
    out_ref[pl.ds(0, 2 * tok), :] = q_all[...]
    out_ref[pl.ds(2 * tok, 2 * tok), :] = g_all[...]
    for which, ref in enumerate(foreign):
        far_part(out_ref, which, tok)[...] = ref[pl.ds(0, 2 * tok + 16), :]


def far_part(ref, which, tok):
    return ref.at[pl.ds(4 * tok + which * (2 * tok + 16), 2 * tok + 16), :]


def total_kernel(tok, chips, sides, *refs):
    sent, came, note_ref = refs[:sides], refs[sides : 2 * sides], refs[2 * sides]
    y, _, _ = place()

    def log_total(top, total, other_top, other_total):
        both = jnp.maximum(top, other_top)
        return both + jnp.log(total * jnp.exp(top - both) + other_total * jnp.exp(other_top - both))

    lse, far_rows = None, []
    for which in range(sides):
        _, y_at = pair(y, which)
        inside = within(y_at, chips)
        note = came[which]
        far_lse = log_total(note[0:1, :], note[1:2, :], sent[which][2:3, :], sent[which][3:4, :])
        far_rows.append(jnp.where(inside, far_lse, 0.0))
        other = jnp.where(inside, note[2:3, :], -1e30), jnp.where(inside, note[3:4, :], 0.0)
        if which == 0:
            lse = log_total(sent[0][0:1, :], sent[0][1:2, :], *other)
        else:
            lse = log_total(lse, jnp.ones_like(lse), *other)
    rows = [lse] + far_rows
    note_ref[...] = jnp.concatenate(rows + [jnp.zeros((8 - len(rows), 2 * tok), jnp.float32)], axis=0)


def share_kernel(tok, chips, sides, note, *refs):
    far_dq, sent, shares = (refs[i * sides : (i + 1) * sides] for i in range(3))
    y, _, _ = place()
    width = far_dq[0].shape[0]
    for which in range(sides):
        _, y_at = pair(y, which)
        lanes = foreign_lanes(which, tok, width)
        factor = jnp.exp(sent[which][2:3, lanes] - note[1 + which : 2 + which, lanes])
        share = (far_dq[which][...] * jnp.where(within(y_at, chips), factor, 0.0)).T
        shares[which][...] = (share[:tok] if which == 0 else share[2 * width - tok :]).astype(jnp.bfloat16)


def line_query_kernel(tok, chips, heights, sides, scale, kv_ref, par_kv_ref, *refs):
    queries, extras, outs = refs[:2], refs[2:4], refs[4:]
    e_ref, ds_ref, e_far, ds_far, top_ref = outs
    y, c, z = place()
    near = border_is_own(y, c)
    two = 2 * tok
    width = kv_ref.shape[1]
    f32, bf16 = jnp.float32, jnp.bfloat16
    tops, far_tops = [], []
    tiles = (kv_ref, par_kv_ref)
    for line in (1, 2):
        rising, z_at = pair(z, 2 - line)
        inside = within(z_at, heights)

        def at(flags, dt):
            return jnp.where(rising, flags[3 * dt : 3 * dt + 1], flags[3 * dt + 2 : 3 * dt + 3])

        rows = extras[line - 1][pl.ds(2 * tok, 32), :].astype(f32)
        own_flags, par_flags = (pick(near, which, rows[0:9], rows[9:18]) for which in range(2))
        delta = [sum(rows[18 + 3 * i + part : 19 + 3 * i + part] for i in range(3)) for part in range(two // width)]
        delta = jnp.concatenate(delta, axis=1)
        line_q, line_g = (queries[line - 1][pl.ds(part * two, two), :] for part in range(2))
        scores = []
        for slot in range(2):
            row = flag_row(tok, slot, at, own_flags, par_flags, False)
            bias = jnp.where(inside, (row - 1.0) * 1e30, -1e30)
            scores.append(dot(tiles[slot][rows_at(0, tok), :], line_q, ROWS_T) * scale + bias)
        top = jnp.maximum(*(jnp.max(block, axis=0, keepdims=True) for block in scores))
        tops.append(top)
        for slot in range(2):
            weights = jnp.exp(scores[slot] - top)
            grads = dot(tiles[slot][rows_at(1, tok), :], line_g, ROWS_T) - delta
            kept = rows_at(2 * (line - 1) + slot, tok)
            e_ref[kept, :] = weights.astype(bf16)
            ds_ref[kept, :] = (weights * grads * scale).astype(bf16)
        for which in range(sides):
            ref = far_part(queries[line - 1], which, tok)
            y_rising, y_at = pair(y, which)
            flags = ref[pl.ds(2 * tok, 16), :].astype(f32)
            row = far_row(tok, which, jnp.where(y_rising, at(flags, 0), at(flags, 2)))
            bias = jnp.where(inside & within(y_at, chips), (row - 1.0) * 1e30, -1e30)
            key, value = (pick(near, which, *(tile[rows_at(i, tok), :] for tile in tiles)) for i in range(2))
            far_q, far_g = (foreign_rows(ref, part, which, tok) for part in range(2))
            block = dot(key, far_q, ROWS_T) * scale + bias
            top = jnp.max(block, axis=0, keepdims=True)
            far_tops.append(to_lanes(which, tok, top, -1e30))
            weights = jnp.exp(block - top)
            grads = dot(value, far_g, ROWS_T) - foreign_delta(ref, tok)
            kept = rows_at(2 * which + line - 1, tok)
            e_far[kept, :] = weights.astype(bf16)
            ds_far[kept, :] = (weights * grads * scale).astype(bf16)
    top_ref[...] = jnp.concatenate(tops + far_tops + [jnp.zeros((6 - 2 * sides, two), f32)], axis=0)


def times(block, factor):
    column = jnp.broadcast_to(factor, (block.shape[1], factor.shape[1])).T
    return (block.astype(jnp.float32) * column).astype(jnp.bfloat16)


def key_sums(tok, near, line, e_ref, ds_ref, scaled, far):
    rows = [rows_at(2 * line + slot, tok) for slot in range(2)]
    sums = [[dot(ref[at, :], scaled[i]) for i, ref in enumerate((ds_ref, e_ref))] for at in rows]
    for which, (e_far, ds_far, at, far_scaled) in enumerate(far):
        for i, ref in enumerate((ds_far, e_far)):
            block = dot(ref[at, :], far_scaled[i])
            for slot in range(2):
                sums[slot][i] = sums[slot][i] + jnp.where(near == ((slot == 0) == (which == 0)), block, 0.0)
    return sums


def stay_kernel(tok, chips, sides, q_all, g_all, e_ref, ds_ref, e_far, ds_far, raw_dq, note, *refs):
    qg = (q_all, g_all)
    sent, foreign, (own_ref, dq_ref) = refs[:sides], refs[sides : 2 * sides], refs[2 * sides :]
    y, c, _ = place()
    near = border_is_own(y, c)
    width = qg[0].shape[1]
    factor = jnp.exp(sent[0][0:1, :] - note[0:1, :])
    dq_ref[...] = (raw_dq[...] * factor).T
    far = []
    for which in range(sides):
        _, y_at = pair(y, which)
        lanes = foreign_lanes(which, tok, width)
        far_factor = jnp.exp(sent[which][2:3, lanes] - note[1 + which : 2 + which, lanes])
        far_factor = jnp.where(within(y_at, chips), far_factor, 0.0)
        scaled = [times(foreign_rows(foreign[which], part, which, tok), far_factor) for part in range(2)]
        far.append((e_far, ds_far, rows_at(which, tok), scaled))
    sums = key_sums(tok, near, 0, e_ref, ds_ref, [times(qg[part][...], factor) for part in range(2)], far)
    for slot in range(2):
        for i in range(2):
            own_ref[i, rows_at(slot, tok), :] = sums[slot][i]


def leave_kernel(tok, chips, sides, own_ref, dq_ref, e_ref, ds_ref, e_far, ds_far, top_ref, *refs):
    queries, notes, backs = refs[:2], refs[2:4], refs[4 : 4 + sides]
    mine_ref, mine_q_ref, swap_ref = refs[4 + sides :]
    y, c, _ = place()
    near = border_is_own(y, c)
    f32, bf16 = jnp.float32, jnp.bfloat16
    width = dq_ref.shape[1]
    sums = [[own_ref[i, rows_at(slot, tok), :] for i in range(2)] for slot in range(2)]
    for line in (1, 2):
        note = notes[line - 1]
        factor = jnp.exp(top_ref[line - 1 : line, :] - note[0:1, :])
        scaled = [times(queries[line - 1][pl.ds(part * 2 * tok, 2 * tok), :], factor) for part in range(2)]
        far = []
        for which in range(sides):
            lanes = foreign_lanes(which, tok, width)
            at = 2 + sides * (line - 1) + which
            far_factor = jnp.exp(top_ref[at : at + 1, lanes] - note[1 + which : 2 + which, lanes])
            rows = [foreign_rows(far_part(queries[line - 1], which, tok), part, which, tok) for part in range(2)]
            far.append(
                (e_far, ds_far, rows_at(2 * which + line - 1, tok), [times(block, far_factor) for block in rows])
            )
        more = key_sums(tok, near, line - 1, e_ref, ds_ref, scaled, far)
        sums = [[sums[slot][i] + more[slot][i] for i in range(2)] for slot in range(2)]
    for i in range(2):
        mine_ref[i], swap_ref[i] = sums[0][i].astype(bf16), sums[1][i].astype(bf16)
    tiles = []
    for tile in range(2):
        value = dq_ref[rows_at(tile, tok), :]
        if tile < sides:
            _, y_at = pair(y, tile)
            value = value + jnp.where(within(y_at, chips), backs[tile][...].astype(f32), 0.0)
        tiles.append(value.astype(bf16))
    mine_q_ref[...] = jnp.where(near, tiles[0], tiles[1])
    swap_ref[2] = jnp.where(near, tiles[1], tiles[0])


def final_kernel(mine_ref, swap_ref, mine_q_ref, gq_ref, gk_ref, gv_ref):
    head = head_at()
    gq_ref[0, 0, head, 0] = mine_q_ref[...]
    gq_ref[0, 0, 1 - head, 0] = swap_ref[2]
    for i, ref in enumerate((gk_ref, gv_ref)):
        ref[0, 0, head, 0] = mine_ref[i]
        ref[0, 0, 1 - head, 0] = swap_ref[i]


def body(queries, keys, values, grad_out, attn_out, window_mask):
    tok, width = queries.shape[-2:]
    scale = width ** -0.5
    times, heights = lax.axis_size("tm"), lax.axis_size("height")
    chips = times // 2
    sides = 1 if chips == 2 else 2
    bf16, f32 = jnp.bfloat16, jnp.float32

    def call(kernel, shapes, specs, scratch=(), cost=0):
        return pl.pallas_call(
            kernel,
            out_shape=[jax.ShapeDtypeStruct(*shape) for shape in shapes],
            in_specs=list(specs),
            out_specs=[VMEM] * len(shapes),
            scratch_shapes=list(scratch),
            compiler_params=LIMIT,
            cost_estimate=pl.CostEstimate(flops=cost * 10**9, bytes_accessed=0, transcendentals=0) if cost else None,
        )

    def partner(index, which, size):
        if which is None:
            return index
        at = index + 1 if index % 2 == which else index - 1
        return at if 0 <= at < size else None

    def exchange(block, y_which, z_which):
        pairs = []
        for t in range(times):
            for z in range(heights):
                y_at, z_at = partner(t // 2, y_which, chips), partner(z, z_which, heights)
                at = t * heights + z
                alone = y_at is None or z_at is None
                pairs.append((at, (t ^ 1) * heights + z if alone else (2 * y_at + 1 - t % 2) * heights + z_at))
        return lax.ppermute(block, ("tm", "height"), pairs)

    def swap_cores(block):
        return lax.ppermute(block, "tm", [(t, t ^ 1) for t in range(times)])

    line_shape, tile_shape = ((2, 2 * tok, width), bf16), ((2, tok, width), bf16)
    extra = 64
    arguments = (keys, values, queries, grad_out, attn_out, window_mask)
    kv, rest, other = call(
        functools.partial(pack_kernel, tok),
        [((2 * tok + extra, width), bf16), ((3 * tok + 16, width), bf16), ((5 * tok + 16, width), bf16)],
        [HBM] * 6,
        [pltpu.SMEM(window_mask.shape, jnp.int32), pltpu.SemaphoreType.DMA((11,))],
    )(*(pltpu.with_memory_space_constraint(x, pltpu.HBM) for x in arguments))
    early = [exchange(kv, None, which) for which in (1, 0)]
    par = swap_cores(other)
    border_shape, two = ((2 * tok + 48, width), bf16), 2 * tok
    par_kv, *borders = call(
        functools.partial(line_kernel, tok), [((2 * tok + 32, width), bf16)] + [border_shape] * sides, [VMEM] * 2
    )(rest, par)
    foreign = [exchange(borders[which], which, None) for which in range(sides)]
    late = [exchange(par_kv, None, which) for which in (1, 0)]
    tiles = (kv, par_kv, late[0], early[0], late[1], early[1])
    note_shape, raw_shape = ((8, two), f32), ((width, two), f32)

    def square(count, kind=f32):
        return ((count * tok, two), kind)

    def far_square(kind=f32):
        return ((3 * sides * tok, 2 * width), kind)

    q_all, g_all, table, s_own, d_own = call(
        functools.partial(first_kernel, tok, heights, scale),
        [((two, width), bf16)] * 2 + [note_shape, square(2), square(2)],
        [VMEM] * 4,
    )(kv, par_kv, rest, par)
    qg = (q_all, g_all)
    (message,) = call(
        functools.partial(message_kernel, tok),
        [((4 * tok + sides * (2 * tok + 16), width), bf16)],
        [VMEM] * (2 + sides),
    )(*qg, *foreign)
    queries_in = [exchange(message, None, which) for which in (1, 0)]
    s_early, d_early, part = call(
        functools.partial(early_kernel, tok, scale), [square(2), square(2), note_shape], [VMEM] * 6
    )(*qg, table, s_own, *early)
    s_late, s_far, *sent = call(
        functools.partial(score_kernel, tok, chips, heights, sides, scale),
        [square(2), far_square()] + [note_shape] * sides,
        [VMEM] * (10 + sides),
    )(*qg, table, part, *foreign, *tiles)
    came = [exchange(sent[which], which, None) for which in range(sides)]
    far_tile = ((sides * tok, 2 * width), bf16)
    e, ds, e_far, ds_far, raw_dq, *far_dq = call(
        functools.partial(middle_kernel, tok, sides, scale),
        [square(2, bf16)] * 2 + [far_tile] * 2 + [raw_shape] + [((width, 2 * width), f32)] * sides,
        [VMEM] * (15 + 2 * sides),
        cost=20,
    )(*qg, table, s_own, d_own, s_early, d_early, s_late, s_far, *tiles, *foreign, *sent)
    (note,) = call(functools.partial(total_kernel, tok, chips, sides), [note_shape], [VMEM] * (2 * sides))(*sent, *came)
    shares = call(
        functools.partial(share_kernel, tok, chips, sides), [((tok, width), bf16)] * sides, [VMEM] * (1 + 2 * sides)
    )(note, *far_dq, *sent)
    notes = [exchange(note, None, which) for which in (1, 0)]
    shares = [exchange(share, which, None) for which, share in enumerate(shares)]
    far_pair = ((2 * sides * tok, 2 * width), bf16)
    line_terms = call(
        functools.partial(line_query_kernel, tok, chips, heights, sides, scale),
        [square(4, bf16)] * 2 + [far_pair] * 2 + [note_shape],
        [VMEM] * 6,
        cost=20,
    )(kv, par_kv, *queries_in, *late)
    own, dq = call(
        functools.partial(stay_kernel, tok, chips, sides),
        [((2, two, width), f32), ((two, width), f32)],
        [VMEM] * (8 + 2 * sides),
    )(*qg, e, ds, e_far, ds_far, raw_dq, note, *sent, *foreign)
    mine, mine_q, leaving = call(
        functools.partial(leave_kernel, tok, chips, sides),
        [tile_shape, ((tok, width), bf16), ((3, tok, width), bf16)],
        [VMEM] * (11 + sides),
    )(own, dq, *line_terms, *queries_in, *notes, *shares)
    return call(final_kernel, [(queries.shape, bf16)] * 3, [VMEM] * 3)(mine, swap_cores(leaving), mine_q)


def solution(mesh):
    placed = P("tm", "height", "dp", None, None, None)
    return jax.shard_map(
        body,
        mesh=mesh,
        in_specs=(placed,) * 5 + (P("tm", "height", None, None),),
        out_specs=(placed,) * 3,
        check_vma=False,
    )
```

```python
import functools

import jax
import jax.numpy as jnp
from jax import lax
from jax.experimental import pallas as pl
from jax.experimental.pallas import tpu as pltpu
from jax.sharding import PartitionSpec as P

VMEM = pl.BlockSpec(memory_space=pltpu.VMEM)
HBM = pl.BlockSpec(memory_space=pltpu.HBM)
LIMIT = pltpu.CompilerParams(vmem_limit_bytes=32 * 1024 * 1024)
ROWS_T = (((1,), (1,)), ((), ()))
COLS_T = (((0,), (0,)), ((), ()))


def dot(a, b, dims=(((1,), (0,)), ((), ()))):
    return lax.dot_general(a, b, dims, preferred_element_type=jnp.float32)


LATE, EARLY = 0, 1


def place():
    t = lax.axis_index("tm")
    return t // 2, t % 2, lax.axis_index("height")


def head_at():
    y, c, z = place()
    return (c + y + z) % 2


def pair(index, which):
    rising = (index % 2) == (0 if which == 0 else 1)
    return rising, jnp.where(rising, index + 1, index - 1)


def within(index, size):
    return (index >= 0) & (index < size)


def pack_kernel(tok, k_ref, v_ref, q_ref, g_ref, o_ref, mask_ref, kv_ref, rest_ref, other_ref, flags, sems):
    head = head_at()
    copies = [pltpu.make_async_copy(mask_ref, flags, sems.at[10])]
    for i, ref in enumerate((k_ref, v_ref, q_ref, g_ref, o_ref)):
        own = (kv_ref if i < 2 else rest_ref).at[pl.ds((i if i < 2 else i - 2) * tok, tok), :]
        copies.append(pltpu.make_async_copy(ref.at[0, 0, head, 0], own, sems.at[2 * i + 1]))
        copies.append(
            pltpu.make_async_copy(ref.at[0, 0, 1 - head, 0], other_ref.at[pl.ds(i * tok, tok), :], sems.at[2 * i])
        )
    for copy in copies:
        copy.start()
    copies[0].wait()
    row = lax.broadcasted_iota(jnp.int32, (16, rest_ref.shape[1]), 0)
    spread = jnp.zeros(row.shape, jnp.float32)
    for i in range(9):
        on = (flags[0, 0, 0, 9 * (i // 3) + 3 * (i % 3) + 1] != 0).astype(jnp.float32)
        spread = jnp.where(row == i, on, spread)
    rest_ref[pl.ds(3 * tok, 16), :] = spread.astype(jnp.bfloat16)
    other_ref[pl.ds(5 * tok, 16), :] = spread.astype(jnp.bfloat16)
    for copy in copies[1:]:
        copy.wait()


def rows_at(index, tok):
    return pl.ds(index * tok, tok)


def border_is_own(y, c):
    rising, _ = pair(y, 0)
    return (c == 1) == rising


def pick(near, which, own, par):
    return jnp.where(near, own, par) if which == 0 else jnp.where(near, par, own)


def three_terms(row):
    terms = []
    for _ in range(3):
        terms.append(row.astype(jnp.bfloat16).astype(jnp.float32))
        row = row - terms[-1]
    return terms


def line_kernel(tok, rest_ref, par_ref, par_kv_ref, *border_refs):
    y, c, _ = place()
    near = border_is_own(y, c)
    for i in range(2):
        par_kv_ref[rows_at(i, tok), :] = par_ref[rows_at(i, tok), :]
    width = par_ref.shape[1]
    f32 = jnp.float32
    q, g, o = (
        [pick(near, which, rest_ref[rows_at(i, tok), :], par_ref[rows_at(i + 2, tok), :]) for which in range(2)]
        for i in range(3)
    )
    own_flags, par_flags = rest_ref[pl.ds(3 * tok, 16), :].astype(f32), par_ref[pl.ds(5 * tok, 16), :].astype(f32)
    flags = [pick(near, which, own_flags, par_flags)[0:9] for which in range(2)]
    product = jnp.concatenate(g, axis=0).astype(f32) * jnp.concatenate(o, axis=0).astype(f32)
    terms = [
        [term[:, start : start + width] for start in range(0, 2 * tok, width)]
        for term in three_terms(jnp.sum(product.T, axis=0, keepdims=True))
    ]
    for which, ref in enumerate(border_refs):
        ref[rows_at(0, tok), :], ref[rows_at(1, tok), :] = q[which], g[which]
        part = slice(0, 2) if which == 0 else slice(len(terms[0]) - 2, None)
        lines = [flags[which]] + [row for term in terms for row in term[part]] + [jnp.zeros((1, width), f32)]
        ref[pl.ds(2 * tok, 16), :] = jnp.concatenate(lines, axis=0).astype(jnp.bfloat16)
    lines = flags + [row for term in terms for row in term] + [jnp.zeros((5, width), f32)]
    par_kv_ref[pl.ds(2 * tok, 32), :] = jnp.concatenate(lines, axis=0).astype(jnp.bfloat16)


def foreign_delta(ref, tok):
    terms = ref[pl.ds(2 * tok, 16), :].astype(jnp.float32)
    return jnp.concatenate(
        [sum(terms[9 + 2 * i + half : 10 + 2 * i + half] for i in range(3)) for half in range(2)], axis=1
    )


def line_place(z, line, heights):
    if line == 0:
        return True, lambda flags, dt: flags[3 * dt + 1 : 3 * dt + 2]
    rising, at = pair(z, 2 - line)
    return within(at, heights), lambda flags, dt: jnp.where(
        rising, flags[3 * dt + 2 : 3 * dt + 3], flags[3 * dt : 3 * dt + 1]
    )


def lanes_of(tok, border, other):
    width = border.shape[1]
    lane = lax.broadcasted_iota(jnp.int32, (1, width), 1)
    return jnp.concatenate(
        [jnp.where(lane + start < tok, border, other) for start in range(0, 2 * tok, width)], axis=1
    )


def flag_row(tok, slot, at, own_flags, par_flags, own_query):
    y, c, _ = place()
    first, near = c == 0, border_is_own(y, c)
    if slot == 0:
        own, par = at(own_flags, 1), jnp.where(first, at(par_flags, 0), at(par_flags, 2))
    else:
        own, par = jnp.where(first, at(own_flags, 2), at(own_flags, 0)), at(par_flags, 1)
    if own_query:
        centre = jnp.ones_like(own)
        own, par = (centre, par) if slot == 0 else (own, centre)
    return lanes_of(tok, pick(near, 0, own, par), pick(near, 1, own, par))


def first_kernel(tok, heights, scale, kv_ref, par_kv_ref, rest_ref, par_ref, q_all, g_all, table, s_ref, d_ref):
    qg = (q_all, g_all)
    y, c, z = place()
    two = 2 * tok
    width = rest_ref.shape[1]
    f32 = jnp.float32
    near = border_is_own(y, c)
    out = []
    for part in range(3):
        own, par = rest_ref[rows_at(part, tok), :], par_ref[rows_at(part + 2, tok), :]
        tiles = [pick(near, which, own, par) for which in range(2)]
        if part == 2:
            out = jnp.concatenate(tiles, axis=0)
        else:
            for which in range(2):
                qg[part][rows_at(which, tok), :] = tiles[which]
    delta = jnp.sum((qg[1][...].astype(f32) * out.astype(f32)).T, axis=0, keepdims=True)

    own_flags = rest_ref[pl.ds(3 * tok, 16), :].astype(f32)
    par_flags = par_ref[pl.ds(5 * tok, 16), :].astype(f32)
    lines = []
    for line in range(3):
        inside, at = line_place(z, line, heights)
        for slot in range(2):
            row = flag_row(tok, slot, at, own_flags, par_flags, line == 0)
            lines.append(jnp.where(inside, (row - 1.0) * 1e30, -1e30))
    table[...] = jnp.concatenate(lines + [delta, jnp.zeros((1, two), f32)], axis=0)
    for i, source in enumerate((kv_ref, par_kv_ref)):
        rows = rows_at(i, tok)
        s_ref[rows, :] = dot(source[rows_at(0, tok), :], qg[0][...], ROWS_T) * scale + table[i : i + 1, :]
        d_ref[rows, :] = dot(source[rows_at(1, tok), :], qg[1][...], ROWS_T) - table[6:7, :]


def largest(tok, blocks):
    lanes = blocks[0][0].shape[1]
    top = jnp.full((8, lanes), -1e30, jnp.float32)
    for ref, i in blocks:
        top = jnp.maximum(top, jnp.max(ref[rows_at(i, tok), :].reshape(tok // 8, 8, lanes), axis=0))
    return jnp.max(top, axis=0, keepdims=True)


def summed(tok, blocks, top):
    lanes = blocks[0][0].shape[1]
    total = jnp.zeros((8, lanes), jnp.float32)
    for ref, i in blocks:
        weights = jnp.exp(ref[rows_at(i, tok), :] - top)
        total = total + jnp.sum(weights.reshape(tok // 8, 8, lanes), axis=0)
    return jnp.sum(total, axis=0, keepdims=True)


def early_kernel(tok, scale, q_all, g_all, table, s_own, one_ref, two_ref, s_ref, d_ref, part_ref):
    qg = (q_all, g_all)
    for i, source in enumerate((one_ref, two_ref)):
        rows = rows_at(i, tok)
        s_ref[rows, :] = dot(source[rows_at(0, tok), :], qg[0][...], ROWS_T) * scale + table[2 + 2 * i + EARLY : 3 + 2 * i + EARLY, :]
        d_ref[rows, :] = dot(source[rows_at(1, tok), :], qg[1][...], ROWS_T) - table[6:7, :]
    blocks = [(ref, i) for ref in (s_own, s_ref) for i in range(2)]
    top = largest(tok, blocks)
    total = summed(tok, blocks, top)
    part_ref[...] = jnp.concatenate([top, total, jnp.zeros((6, 2 * tok), jnp.float32)], axis=0)


def foreign_rows(ref, part, which, tok):
    block = ref[rows_at(part, tok), :]
    gap = jnp.zeros((2 * block.shape[1] - tok, block.shape[1]), block.dtype)
    return jnp.concatenate([block, gap] if which == 0 else [gap, block], axis=0)


def foreign_lanes(which, tok, width):
    return slice(0, 2 * width) if which == 0 else slice(2 * tok - 2 * width, 2 * tok)


def far_row(tok, which, row):
    lane, width = lax.broadcasted_iota(jnp.int32, row.shape, 1), row.shape[1]
    return jnp.concatenate(
        [
            jnp.where(lane + start < tok if which == 0 else lane + start >= 2 * width - tok, row, 0.0)
            for start in (0, width)
        ],
        axis=1,
    )


def to_lanes(which, tok, row, fill):
    gap = jnp.full((1, 2 * tok - row.shape[1]), fill, jnp.float32)
    return jnp.concatenate([row, gap] if which == 0 else [gap, row], axis=1)


def score_kernel(tok, chips, heights, sides, scale, q_all, g_all, table, part, *refs):
    qg = (q_all, g_all)
    foreign, keys, refs = refs[:sides], refs[sides : 6 + sides], refs[6 + sides :]
    s_late, s_far, *notes = refs
    y, c, z = place()
    near = border_is_own(y, c)
    two = 2 * tok
    f32 = jnp.float32
    far = []
    for which in range(sides):
        rising, y_at = pair(y, which)
        flags = foreign[which][pl.ds(2 * tok, 16), :].astype(f32)
        queries = foreign_rows(foreign[which], 0, which, tok)
        for line in range(3):
            inside, at = line_place(z, line, heights)
            row = far_row(tok, which, jnp.where(rising, at(flags, 0), at(flags, 2)))
            bias = jnp.where(inside & within(y_at, chips), (row - 1.0) * 1e30, -1e30)
            border = pick(near, which, keys[2 * line][rows_at(0, tok), :], keys[2 * line + 1][rows_at(0, tok), :])
            s_far[rows_at(3 * which + line, tok), :] = dot(border, queries, ROWS_T) * scale + bias
        blocks = [(s_far, 3 * which + line) for line in range(3)]
        top = largest(tok, blocks)
        far.append([to_lanes(which, tok, top, -1e30), to_lanes(which, tok, summed(tok, blocks, top), 0.0)])
    for i in range(2):
        at = 2 + 2 * i + LATE
        scores = dot(keys[at][rows_at(0, tok), :], qg[0][...], ROWS_T) * scale
        s_late[rows_at(i, tok), :] = scores + table[at : at + 1, :]
    blocks = [(s_late, i) for i in range(2)]
    top = jnp.maximum(part[0:1, :], largest(tok, blocks))
    total = part[1:2, :] * jnp.exp(part[0:1, :] - top) + summed(tok, blocks, top)
    for which in range(sides):
        notes[which][...] = jnp.concatenate([top, total] + far[which] + [jnp.zeros((4, two), f32)], axis=0)


def middle_kernel(tok, heights, sides, scale, q_all, g_all, table, s_own, d_own, s_early, d_early, s_late, s_far, *refs):
    qg = (q_all, g_all)
    tiles, foreign, sent = refs[:6], refs[6 : 6 + sides], refs[6 + sides : 6 + 2 * sides]
    e_ref, ds_ref, e_far, ds_far, dq_ref, *refs = refs[6 + 2 * sides :]
    shares, far_dq = refs[:sides], refs[sides:]
    y, c, z = place()
    near = border_is_own(y, c)
    bf16 = jnp.bfloat16

    def add(ref, line, value):
        ref[...] = value if line == 0 else ref[...] + value

    def work(line):
        dq = 0.0
        for slot in range(2):
            i, at = 2 * line + slot, rows_at(line - 1 if line else slot, tok)
            scores = s_own if line == 0 else s_early if slot == EARLY else s_late
            weights = jnp.exp(scores[at, :] - sent[0][0:1, :])
            if line and slot == LATE:
                grads = dot(tiles[i][rows_at(1, tok), :], qg[1][...], ROWS_T) - table[6:7, :]
            else:
                grads = (d_early if line else d_own)[at, :]
            low = (weights * grads * scale).astype(bf16)
            if line == 0:
                e_ref[rows_at(i, tok), :] = weights.astype(bf16)
                ds_ref[rows_at(i, tok), :] = low
            dq = dq + dot(tiles[i][rows_at(0, tok), :], low, COLS_T)
        add(dq_ref, line, dq)
        for which in range(sides):
            far_g = foreign_rows(foreign[which], 1, which, tok)
            delta = foreign_delta(foreign[which], tok)
            lanes = foreign_lanes(which, tok, qg[0].shape[1])
            rows = rows_at(3 * which + line, tok)
            own, par = tiles[2 * line], tiles[2 * line + 1]
            key, value = (pick(near, which, own[rows_at(i, tok), :], par[rows_at(i, tok), :]) for i in range(2))
            weights = jnp.exp(s_far[rows, :] - sent[which][2:3, lanes])
            low = (weights * (dot(value, far_g, ROWS_T) - delta) * scale).astype(bf16)
            if line == 0:
                e_far[rows_at(which, tok), :] = weights.astype(bf16)
                ds_far[rows_at(which, tok), :] = low
            add(far_dq[which], line, dot(key, low, COLS_T))

    for line in range(3):
        if line == 0:
            work(line)
        else:
            pl.when(line_place(z, line, heights)[0])(functools.partial(work, line))
    for which in range(sides):
        shares[which][...] = border_rows(which, tok, far_dq[which][...].T).astype(bf16)


def border_rows(which, tok, block):
    return block[:tok] if which == 0 else block[block.shape[0] - tok :]


def message_kernel(tok, q_all, g_all, *refs):
    *foreign, out_ref = refs
    out_ref[pl.ds(0, 2 * tok), :] = q_all[...]
    out_ref[pl.ds(2 * tok, 2 * tok), :] = g_all[...]
    for which, ref in enumerate(foreign):
        far_part(out_ref, which, tok)[...] = ref[pl.ds(0, 2 * tok + 16), :]


def far_part(ref, which, tok):
    return ref.at[pl.ds(4 * tok + which * (2 * tok + 16), 2 * tok + 16), :]


def total_kernel(tok, chips, sides, *refs):
    sent, came, note_ref = refs[:sides], refs[sides : 2 * sides], refs[2 * sides]
    y, _, _ = place()

    def log_total(top, total, other_top, other_total):
        both = jnp.maximum(top, other_top)
        return both + jnp.log(total * jnp.exp(top - both) + other_total * jnp.exp(other_top - both))

    lse, far_rows = None, []
    for which in range(sides):
        _, y_at = pair(y, which)
        inside = within(y_at, chips)
        note = came[which]
        far_lse = log_total(note[0:1, :], note[1:2, :], sent[which][2:3, :], sent[which][3:4, :])
        far_rows.append(jnp.where(inside, far_lse, 0.0))
        other = jnp.where(inside, note[2:3, :], -1e30), jnp.where(inside, note[3:4, :], 0.0)
        if which == 0:
            lse = log_total(sent[0][0:1, :], sent[0][1:2, :], *other)
        else:
            lse = log_total(lse, jnp.ones_like(lse), *other)
    rows = [lse] + far_rows
    note_ref[...] = jnp.concatenate(rows + [jnp.zeros((8 - len(rows), 2 * tok), jnp.float32)], axis=0)


def line_query_kernel(tok, chips, heights, sides, scale, kv_ref, par_kv_ref, *refs):
    queries, extras, outs = refs[:2], refs[2:4], refs[4:]
    e_ref, ds_ref, e_far, ds_far, top_ref = outs
    y, c, z = place()
    near = border_is_own(y, c)
    two = 2 * tok
    width = kv_ref.shape[1]
    f32, bf16 = jnp.float32, jnp.bfloat16
    tiles = (kv_ref, par_kv_ref)

    def work(line):
        rising, _ = pair(z, 2 - line)

        def at(flags, dt):
            return jnp.where(rising, flags[3 * dt : 3 * dt + 1], flags[3 * dt + 2 : 3 * dt + 3])

        rows = extras[line - 1][pl.ds(2 * tok, 32), :].astype(f32)
        own_flags, par_flags = (pick(near, which, rows[0:9], rows[9:18]) for which in range(2))
        delta = [sum(rows[18 + 3 * i + part : 19 + 3 * i + part] for i in range(3)) for part in range(two // width)]
        delta = jnp.concatenate(delta, axis=1)
        line_q, line_g = (queries[line - 1][pl.ds(part * two, two), :] for part in range(2))
        scores = []
        for slot in range(2):
            row = flag_row(tok, slot, at, own_flags, par_flags, False)
            scores.append(dot(tiles[slot][rows_at(0, tok), :], line_q, ROWS_T) * scale + (row - 1.0) * 1e30)
        tops = [jnp.maximum(*(jnp.max(block, axis=0, keepdims=True) for block in scores))]
        for slot in range(2):
            weights = jnp.exp(scores[slot] - tops[0])
            grads = dot(tiles[slot][rows_at(1, tok), :], line_g, ROWS_T) - delta
            kept = rows_at(2 * (line - 1) + slot, tok)
            e_ref[kept, :] = weights.astype(bf16)
            ds_ref[kept, :] = (weights * grads * scale).astype(bf16)
        for which in range(sides):
            ref = far_part(queries[line - 1], which, tok)
            y_rising, y_at = pair(y, which)
            flags = ref[pl.ds(2 * tok, 16), :].astype(f32)
            row = far_row(tok, which, jnp.where(y_rising, at(flags, 0), at(flags, 2)))
            bias = jnp.where(within(y_at, chips), (row - 1.0) * 1e30, -1e30)
            key, value = (pick(near, which, *(tile[rows_at(i, tok), :] for tile in tiles)) for i in range(2))
            far_q, far_g = (foreign_rows(ref, part, which, tok) for part in range(2))
            block = dot(key, far_q, ROWS_T) * scale + bias
            top = jnp.max(block, axis=0, keepdims=True)
            tops.append(to_lanes(which, tok, top, -1e30))
            weights = jnp.exp(block - top)
            grads = dot(value, far_g, ROWS_T) - foreign_delta(ref, tok)
            kept = rows_at(2 * which + line - 1, tok)
            e_far[kept, :] = weights.astype(bf16)
            ds_far[kept, :] = (weights * grads * scale).astype(bf16)
        gap = jnp.zeros((7 - sides, two), f32)
        top_ref[pl.ds(8 * (line - 1), 8), :] = jnp.concatenate(tops + [gap], axis=0)

    for line in (1, 2):
        pl.when(line_place(z, line, heights)[0])(functools.partial(work, line))


def times(block, factor):
    column = jnp.broadcast_to(factor, (block.shape[1], factor.shape[1])).T
    return (block.astype(jnp.float32) * column).astype(jnp.bfloat16)


def key_sums(tok, near, line, e_ref, ds_ref, scaled, far):
    rows = [rows_at(2 * line + slot, tok) for slot in range(2)]
    sums = [[dot(ref[at, :], scaled[i]) for i, ref in enumerate((ds_ref, e_ref))] for at in rows]
    for which, (e_far, ds_far, at, far_scaled) in enumerate(far):
        for i, ref in enumerate((ds_far, e_far)):
            block = dot(ref[at, :], far_scaled[i])
            for slot in range(2):
                sums[slot][i] = sums[slot][i] + jnp.where(near == ((slot == 0) == (which == 0)), block, 0.0)
    return sums


def stay_kernel(tok, chips, sides, q_all, g_all, e_ref, ds_ref, e_far, ds_far, raw_dq, note, *refs):
    qg = (q_all, g_all)
    sent, foreign, (own_ref, dq_ref) = refs[:sides], refs[sides : 2 * sides], refs[2 * sides :]
    y, c, _ = place()
    near = border_is_own(y, c)
    width = qg[0].shape[1]
    factor = jnp.exp(sent[0][0:1, :] - note[0:1, :])
    dq_ref[...] = (raw_dq[...] * factor).T
    far = []
    for which in range(sides):
        _, y_at = pair(y, which)
        lanes = foreign_lanes(which, tok, width)
        far_factor = jnp.exp(sent[which][2:3, lanes] - note[1 + which : 2 + which, lanes])
        far_factor = jnp.where(within(y_at, chips), far_factor, 0.0)
        scaled = [times(foreign_rows(foreign[which], part, which, tok), far_factor) for part in range(2)]
        far.append((e_far, ds_far, rows_at(which, tok), scaled))
    sums = key_sums(tok, near, 0, e_ref, ds_ref, [times(qg[part][...], factor) for part in range(2)], far)
    for slot in range(2):
        for i in range(2):
            own_ref[i, rows_at(slot, tok), :] = sums[slot][i]


def leave_kernel(tok, chips, heights, sides, own_ref, dq_ref, note, e_ref, ds_ref, e_far, ds_far, top_ref, *refs):
    queries, notes, refs = refs[:2], refs[2:4], refs[4:]
    came, backs, (mine_ref, mine_q_ref, swap_ref, sums) = refs[:sides], refs[sides : 2 * sides], refs[2 * sides :]
    y, c, z = place()
    near = border_is_own(y, c)
    f32, bf16 = jnp.float32, jnp.bfloat16
    width = dq_ref.shape[1]
    sums[...] = own_ref[...]

    def work(line):
        factor = jnp.exp(top_ref[8 * line - 8 : 8 * line - 7, :] - notes[line - 1][0:1, :])
        scaled = [times(queries[line - 1][pl.ds(part * 2 * tok, 2 * tok), :], factor) for part in range(2)]
        far = []
        for which in range(sides):
            lanes, at = foreign_lanes(which, tok, width), 8 * line - 7 + which
            far_factor = jnp.exp(top_ref[at : at + 1, lanes] - notes[line - 1][1 + which : 2 + which, lanes])
            rows = [foreign_rows(far_part(queries[line - 1], which, tok), part, which, tok) for part in range(2)]
            far.append(
                (e_far, ds_far, rows_at(2 * which + line - 1, tok), [times(block, far_factor) for block in rows])
            )
        more = key_sums(tok, near, line - 1, e_ref, ds_ref, scaled, far)
        for slot in range(2):
            for i in range(2):
                sums[i, rows_at(slot, tok), :] += more[slot][i]

    for line in (1, 2):
        pl.when(line_place(z, line, heights)[0])(functools.partial(work, line))
    for i in range(2):
        mine_ref[i], swap_ref[i] = sums[i, rows_at(0, tok), :].astype(bf16), sums[i, rows_at(1, tok), :].astype(bf16)
    tiles = []
    for tile in range(2):
        value = dq_ref[rows_at(tile, tok), :]
        if tile < sides:
            _, y_at = pair(y, tile)
            lanes = foreign_lanes(tile, tok, width)
            factor = jnp.exp(came[tile][2:3, lanes] - note[0:1, lanes])
            column = border_rows(tile, tok, jnp.broadcast_to(factor, (width, 2 * width)).T)
            value = value + jnp.where(within(y_at, chips), backs[tile][...].astype(f32) * column, 0.0)
        tiles.append(value.astype(bf16))
    mine_q_ref[...] = jnp.where(near, tiles[0], tiles[1])
    swap_ref[2] = jnp.where(near, tiles[1], tiles[0])


def final_kernel(mine_ref, swap_ref, mine_q_ref, gq_ref, gk_ref, gv_ref):
    head = head_at()
    gq_ref[0, 0, head, 0] = mine_q_ref[...]
    gq_ref[0, 0, 1 - head, 0] = swap_ref[2]
    for i, ref in enumerate((gk_ref, gv_ref)):
        ref[0, 0, head, 0] = mine_ref[i]
        ref[0, 0, 1 - head, 0] = swap_ref[i]


def body(queries, keys, values, grad_out, attn_out, window_mask):
    tok, width = queries.shape[-2:]
    scale = width ** -0.5
    times, heights = lax.axis_size("tm"), lax.axis_size("height")
    chips = times // 2
    sides = 1 if chips == 2 else 2
    bf16, f32 = jnp.bfloat16, jnp.float32

    def call(kernel, shapes, specs, scratch=(), cost=0):
        return pl.pallas_call(
            kernel,
            out_shape=[jax.ShapeDtypeStruct(*shape) for shape in shapes],
            in_specs=list(specs),
            out_specs=[VMEM] * len(shapes),
            scratch_shapes=list(scratch),
            compiler_params=LIMIT,
            cost_estimate=pl.CostEstimate(flops=cost * 10**9, bytes_accessed=0, transcendentals=0) if cost else None,
        )

    def partner(index, which, size):
        if which is None:
            return index
        at = index + 1 if index % 2 == which else index - 1
        return at if 0 <= at < size else None

    def exchange(block, y_which, z_which):
        pairs = []
        for t in range(times):
            for z in range(heights):
                y_at, z_at = partner(t // 2, y_which, chips), partner(z, z_which, heights)
                at = t * heights + z
                alone = y_at is None or z_at is None
                pairs.append((at, (t ^ 1) * heights + z if alone else (2 * y_at + 1 - t % 2) * heights + z_at))
        return lax.ppermute(block, ("tm", "height"), pairs)

    def swap_cores(block):
        return lax.ppermute(block, "tm", [(t, t ^ 1) for t in range(times)])

    line_shape, tile_shape = ((2, 2 * tok, width), bf16), ((2, tok, width), bf16)
    extra = 64
    arguments = (keys, values, queries, grad_out, attn_out, window_mask)
    kv, rest, other = call(
        functools.partial(pack_kernel, tok),
        [((2 * tok + extra, width), bf16), ((3 * tok + 16, width), bf16), ((5 * tok + 16, width), bf16)],
        [HBM] * 6,
        [pltpu.SMEM(window_mask.shape, jnp.int32), pltpu.SemaphoreType.DMA((11,))],
    )(*(pltpu.with_memory_space_constraint(x, pltpu.HBM) for x in arguments))
    early = [exchange(kv, None, which) for which in (1, 0)]
    par = swap_cores(other)
    border_shape, two = ((2 * tok + 48, width), bf16), 2 * tok
    par_kv, *borders = call(
        functools.partial(line_kernel, tok), [((2 * tok + 32, width), bf16)] + [border_shape] * sides, [VMEM] * 2
    )(rest, par)
    foreign = [exchange(borders[which], which, None) for which in range(sides)]
    late = [exchange(par_kv, None, which) for which in (1, 0)]
    tiles = (kv, par_kv, late[0], early[0], late[1], early[1])
    note_shape, raw_shape = ((8, two), f32), ((width, two), f32)

    def square(count, kind=f32):
        return ((count * tok, two), kind)

    def far_square(kind=f32):
        return ((3 * sides * tok, 2 * width), kind)

    q_all, g_all, table, s_own, d_own = call(
        functools.partial(first_kernel, tok, heights, scale),
        [((two, width), bf16)] * 2 + [note_shape, square(2), square(2)],
        [VMEM] * 4,
    )(kv, par_kv, rest, par)
    qg = (q_all, g_all)
    (message,) = call(
        functools.partial(message_kernel, tok),
        [((4 * tok + sides * (2 * tok + 16), width), bf16)],
        [VMEM] * (2 + sides),
    )(*qg, *foreign)
    queries_in = [exchange(message, None, which) for which in (1, 0)]
    s_early, d_early, part = call(
        functools.partial(early_kernel, tok, scale), [square(2), square(2), note_shape], [VMEM] * 6
    )(*qg, table, s_own, *early)
    s_late, s_far, *sent = call(
        functools.partial(score_kernel, tok, chips, heights, sides, scale),
        [square(2), far_square()] + [note_shape] * sides,
        [VMEM] * (10 + sides),
    )(*qg, table, part, *foreign, *tiles)
    came = [exchange(sent[which], which, None) for which in range(sides)]
    far_tile = ((sides * tok, 2 * width), bf16)
    e, ds, e_far, ds_far, raw_dq, *shares = call(
        functools.partial(middle_kernel, tok, heights, sides, scale),
        [square(2, bf16)] * 2 + [far_tile] * 2 + [raw_shape] + [((tok, width), bf16)] * sides,
        [VMEM] * (15 + 2 * sides),
        [pltpu.VMEM((width, 2 * width), f32)] * sides,
        cost=20,
    )(*qg, table, s_own, d_own, s_early, d_early, s_late, s_far, *tiles, *foreign, *sent)
    (note,) = call(functools.partial(total_kernel, tok, chips, sides), [note_shape], [VMEM] * (2 * sides))(*sent, *came)
    notes = [exchange(note, None, which) for which in (1, 0)]
    shares = [exchange(share, which, None) for which, share in enumerate(shares)]
    far_pair = ((2 * sides * tok, 2 * width), bf16)
    line_terms = call(
        functools.partial(line_query_kernel, tok, chips, heights, sides, scale),
        [square(4, bf16)] * 2 + [far_pair] * 2 + [((16, two), f32)],
        [VMEM] * 6,
        cost=20,
    )(kv, par_kv, *queries_in, *late)
    own, dq = call(
        functools.partial(stay_kernel, tok, chips, sides),
        [((2, two, width), f32), ((two, width), f32)],
        [VMEM] * (8 + 2 * sides),
    )(*qg, e, ds, e_far, ds_far, raw_dq, note, *sent, *foreign)
    mine, mine_q, leaving = call(
        functools.partial(leave_kernel, tok, chips, heights, sides),
        [tile_shape, ((tok, width), bf16), ((3, tok, width), bf16)],
        [VMEM] * (12 + 2 * sides),
        [pltpu.VMEM((2, two, width), f32)],
    )(own, dq, note, *line_terms, *queries_in, *notes, *came, *shares)
    return call(final_kernel, [(queries.shape, bf16)] * 3, [VMEM] * 3)(mine, swap_cores(leaving), mine_q)


def solution(mesh):
    placed = P("tm", "height", "dp", None, None, None)
    return jax.shard_map(
        body,
        mesh=mesh,
        in_specs=(placed,) * 5 + (P("tm", "height", None, None),),
        out_specs=(placed,) * 3,
        check_vma=False,
    )
```

```python
import functools

import jax
import jax.numpy as jnp
from jax import lax
from jax.experimental import pallas as pl
from jax.experimental.pallas import tpu as pltpu
from jax.sharding import PartitionSpec as P

VMEM = pl.BlockSpec(memory_space=pltpu.VMEM)
HBM = pl.BlockSpec(memory_space=pltpu.HBM)
LIMIT = pltpu.CompilerParams(vmem_limit_bytes=32 * 1024 * 1024)
ROWS_T = (((1,), (1,)), ((), ()))
COLS_T = (((0,), (0,)), ((), ()))


def dot(a, b, dims=(((1,), (0,)), ((), ()))):
    return lax.dot_general(a, b, dims, preferred_element_type=jnp.float32)


LATE, EARLY = 0, 1


def place():
    t = lax.axis_index("tm")
    return t // 2, t % 2, lax.axis_index("height")


def head_at():
    y, c, z = place()
    return (c + y + z) % 2


def pair(index, which):
    rising = (index % 2) == (0 if which == 0 else 1)
    return rising, jnp.where(rising, index + 1, index - 1)


def within(index, size):
    return (index >= 0) & (index < size)


def pack_kernel(tok, k_ref, v_ref, q_ref, g_ref, o_ref, mask_ref, kv_ref, rest_ref, other_ref, flags, sems):
    head = head_at()
    copies = [pltpu.make_async_copy(mask_ref, flags, sems.at[10])]
    for i, ref in enumerate((k_ref, v_ref, q_ref, g_ref, o_ref)):
        own = (kv_ref if i < 2 else rest_ref).at[pl.ds((i if i < 2 else i - 2) * tok, tok), :]
        copies.append(pltpu.make_async_copy(ref.at[0, 0, head, 0], own, sems.at[2 * i + 1]))
        copies.append(
            pltpu.make_async_copy(ref.at[0, 0, 1 - head, 0], other_ref.at[pl.ds(i * tok, tok), :], sems.at[2 * i])
        )
    for copy in copies:
        copy.start()
    copies[0].wait()
    row = lax.broadcasted_iota(jnp.int32, (16, rest_ref.shape[1]), 0)
    spread = jnp.zeros(row.shape, jnp.float32)
    for i in range(9):
        on = (flags[0, 0, 0, 9 * (i // 3) + 3 * (i % 3) + 1] != 0).astype(jnp.float32)
        spread = jnp.where(row == i, on, spread)
    rest_ref[pl.ds(3 * tok, 16), :] = spread.astype(jnp.bfloat16)
    other_ref[pl.ds(5 * tok, 16), :] = spread.astype(jnp.bfloat16)
    for copy in copies[1:]:
        copy.wait()


def rows_at(index, tok):
    return pl.ds(index * tok, tok)


def border_is_own(y, c):
    rising, _ = pair(y, 0)
    return (c == 1) == rising


def pick(near, which, own, par):
    return jnp.where(near, own, par) if which == 0 else jnp.where(near, par, own)


def three_terms(row):
    terms = []
    for _ in range(3):
        terms.append(row.astype(jnp.bfloat16).astype(jnp.float32))
        row = row - terms[-1]
    return terms


def line_kernel(tok, rest_ref, par_ref, par_kv_ref, *border_refs):
    y, c, _ = place()
    near = border_is_own(y, c)
    for i in range(2):
        par_kv_ref[rows_at(i, tok), :] = par_ref[rows_at(i, tok), :]
    width = par_ref.shape[1]
    f32 = jnp.float32
    q, g, o = (
        [pick(near, which, rest_ref[rows_at(i, tok), :], par_ref[rows_at(i + 2, tok), :]) for which in range(2)]
        for i in range(3)
    )
    own_flags, par_flags = rest_ref[pl.ds(3 * tok, 16), :].astype(f32), par_ref[pl.ds(5 * tok, 16), :].astype(f32)
    flags = [pick(near, which, own_flags, par_flags)[0:9] for which in range(2)]
    product = jnp.concatenate(g, axis=0).astype(f32) * jnp.concatenate(o, axis=0).astype(f32)
    terms = [
        [term[:, start : start + width] for start in range(0, 2 * tok, width)]
        for term in three_terms(jnp.sum(product.T, axis=0, keepdims=True))
    ]
    for which, ref in enumerate(border_refs):
        ref[rows_at(0, tok), :], ref[rows_at(1, tok), :] = q[which], g[which]
        part = slice(0, 2) if which == 0 else slice(len(terms[0]) - 2, None)
        lines = [flags[which]] + [row for term in terms for row in term[part]] + [jnp.zeros((1, width), f32)]
        ref[pl.ds(2 * tok, 16), :] = jnp.concatenate(lines, axis=0).astype(jnp.bfloat16)
    lines = flags + [row for term in terms for row in term] + [jnp.zeros((5, width), f32)]
    par_kv_ref[pl.ds(2 * tok, 32), :] = jnp.concatenate(lines, axis=0).astype(jnp.bfloat16)


def foreign_delta(ref, tok):
    terms = ref[pl.ds(2 * tok, 16), :].astype(jnp.float32)
    return jnp.concatenate(
        [sum(terms[9 + 2 * i + half : 10 + 2 * i + half] for i in range(3)) for half in range(2)], axis=1
    )


def line_place(z, line, heights):
    if line == 0:
        return True, lambda flags, dt: flags[3 * dt + 1 : 3 * dt + 2]
    rising, at = pair(z, 2 - line)
    return within(at, heights), lambda flags, dt: jnp.where(
        rising, flags[3 * dt + 2 : 3 * dt + 3], flags[3 * dt : 3 * dt + 1]
    )


def lanes_of(tok, border, other):
    width = border.shape[1]
    lane = lax.broadcasted_iota(jnp.int32, (1, width), 1)
    return jnp.concatenate(
        [jnp.where(lane + start < tok, border, other) for start in range(0, 2 * tok, width)], axis=1
    )


def flag_row(tok, slot, at, own_flags, par_flags, own_query):
    y, c, _ = place()
    first, near = c == 0, border_is_own(y, c)
    if slot == 0:
        own, par = at(own_flags, 1), jnp.where(first, at(par_flags, 0), at(par_flags, 2))
    else:
        own, par = jnp.where(first, at(own_flags, 2), at(own_flags, 0)), at(par_flags, 1)
    if own_query:
        centre = jnp.ones_like(own)
        own, par = (centre, par) if slot == 0 else (own, centre)
    return lanes_of(tok, pick(near, 0, own, par), pick(near, 1, own, par))


def first_kernel(tok, heights, scale, kv_ref, par_kv_ref, rest_ref, par_ref, q_all, g_all, table, s_ref, d_ref):
    qg = (q_all, g_all)
    y, c, z = place()
    two = 2 * tok
    width = rest_ref.shape[1]
    f32 = jnp.float32
    near = border_is_own(y, c)
    out = []
    for part in range(3):
        own, par = rest_ref[rows_at(part, tok), :], par_ref[rows_at(part + 2, tok), :]
        tiles = [pick(near, which, own, par) for which in range(2)]
        if part == 2:
            out = jnp.concatenate(tiles, axis=0)
        else:
            for which in range(2):
                qg[part][rows_at(which, tok), :] = tiles[which]
    delta = jnp.sum((qg[1][...].astype(f32) * out.astype(f32)).T, axis=0, keepdims=True)

    own_flags = rest_ref[pl.ds(3 * tok, 16), :].astype(f32)
    par_flags = par_ref[pl.ds(5 * tok, 16), :].astype(f32)
    lines = []
    for line in range(3):
        inside, at = line_place(z, line, heights)
        for slot in range(2):
            row = flag_row(tok, slot, at, own_flags, par_flags, line == 0)
            lines.append(jnp.where(inside, (row - 1.0) * 1e30, -1e30))
    table[...] = jnp.concatenate(lines + [delta, jnp.zeros((1, two), f32)], axis=0)
    for i, source in enumerate((kv_ref, par_kv_ref)):
        rows = rows_at(i, tok)
        s_ref[rows, :] = dot(source[rows_at(0, tok), :], qg[0][...], ROWS_T) * scale + table[i : i + 1, :]
        d_ref[rows, :] = dot(source[rows_at(1, tok), :], qg[1][...], ROWS_T) - table[6:7, :]


def largest(tok, blocks):
    lanes = blocks[0][0].shape[1]
    top = jnp.full((8, lanes), -1e30, jnp.float32)
    for ref, i in blocks:
        top = jnp.maximum(top, jnp.max(ref[rows_at(i, tok), :].reshape(tok // 8, 8, lanes), axis=0))
    return jnp.max(top, axis=0, keepdims=True)


def summed(tok, blocks, top):
    lanes = blocks[0][0].shape[1]
    total = jnp.zeros((8, lanes), jnp.float32)
    for ref, i in blocks:
        weights = jnp.exp(ref[rows_at(i, tok), :] - top)
        total = total + jnp.sum(weights.reshape(tok // 8, 8, lanes), axis=0)
    return jnp.sum(total, axis=0, keepdims=True)


def early_kernel(tok, scale, q_all, g_all, table, s_own, one_ref, two_ref, s_ref, d_ref, part_ref):
    qg = (q_all, g_all)
    for i, source in enumerate((one_ref, two_ref)):
        rows = rows_at(i, tok)
        s_ref[rows, :] = dot(source[rows_at(0, tok), :], qg[0][...], ROWS_T) * scale + table[2 + 2 * i + EARLY : 3 + 2 * i + EARLY, :]
        d_ref[rows, :] = dot(source[rows_at(1, tok), :], qg[1][...], ROWS_T) - table[6:7, :]
    blocks = [(ref, i) for ref in (s_own, s_ref) for i in range(2)]
    top = largest(tok, blocks)
    total = summed(tok, blocks, top)
    part_ref[...] = jnp.concatenate([top, total, jnp.zeros((6, 2 * tok), jnp.float32)], axis=0)


def foreign_rows(ref, part, which, tok):
    block = ref[rows_at(part, tok), :]
    gap = jnp.zeros((2 * block.shape[1] - tok, block.shape[1]), block.dtype)
    return jnp.concatenate([block, gap] if which == 0 else [gap, block], axis=0)


def foreign_lanes(which, tok, width):
    return slice(0, 2 * width) if which == 0 else slice(2 * tok - 2 * width, 2 * tok)


def far_row(tok, which, row):
    lane, width = lax.broadcasted_iota(jnp.int32, row.shape, 1), row.shape[1]
    return jnp.concatenate(
        [
            jnp.where(lane + start < tok if which == 0 else lane + start >= 2 * width - tok, row, 0.0)
            for start in (0, width)
        ],
        axis=1,
    )


def to_lanes(which, tok, row, fill):
    gap = jnp.full((1, 2 * tok - row.shape[1]), fill, jnp.float32)
    return jnp.concatenate([row, gap] if which == 0 else [gap, row], axis=1)


def score_kernel(tok, chips, heights, sides, scale, q_all, g_all, table, part, *refs):
    qg = (q_all, g_all)
    foreign, keys, refs = refs[:sides], refs[sides : 6 + sides], refs[6 + sides :]
    s_late, s_far, *notes = refs
    y, c, z = place()
    near = border_is_own(y, c)
    two = 2 * tok
    f32 = jnp.float32
    far = []
    for which in range(sides):
        rising, y_at = pair(y, which)
        flags = foreign[which][pl.ds(2 * tok, 16), :].astype(f32)
        queries = foreign_rows(foreign[which], 0, which, tok)
        for line in range(3):
            inside, at = line_place(z, line, heights)
            row = far_row(tok, which, jnp.where(rising, at(flags, 0), at(flags, 2)))
            bias = jnp.where(inside & within(y_at, chips), (row - 1.0) * 1e30, -1e30)
            border = pick(near, which, keys[2 * line][rows_at(0, tok), :], keys[2 * line + 1][rows_at(0, tok), :])
            s_far[rows_at(3 * which + line, tok), :] = dot(border, queries, ROWS_T) * scale + bias
        blocks = [(s_far, 3 * which + line) for line in range(3)]
        top = largest(tok, blocks)
        far.append([to_lanes(which, tok, top, -1e30), to_lanes(which, tok, summed(tok, blocks, top), 0.0)])
    for i in range(2):
        at = 2 + 2 * i + LATE
        scores = dot(keys[at][rows_at(0, tok), :], qg[0][...], ROWS_T) * scale
        s_late[rows_at(i, tok), :] = scores + table[at : at + 1, :]
    blocks = [(s_late, i) for i in range(2)]
    top = jnp.maximum(part[0:1, :], largest(tok, blocks))
    total = part[1:2, :] * jnp.exp(part[0:1, :] - top) + summed(tok, blocks, top)
    for which in range(sides):
        notes[which][...] = jnp.concatenate([top, total] + far[which] + [jnp.zeros((4, two), f32)], axis=0)


def middle_kernel(tok, sides, scale, q_all, g_all, table, s_own, d_own, s_early, d_early, s_late, s_far, *refs):
    qg = (q_all, g_all)
    tiles, foreign, sent = refs[:6], refs[6 : 6 + sides], refs[6 + sides : 6 + 2 * sides]
    e_ref, ds_ref, e_far, ds_far, dq_ref, *shares = refs[6 + 2 * sides :]
    y, c, _ = place()
    near = border_is_own(y, c)
    bf16 = jnp.bfloat16

    total, far_total = 0.0, [0.0] * sides
    for line in range(3):
        dq = 0.0
        for slot in range(2):
            i, at = 2 * line + slot, rows_at(line - 1 if line else slot, tok)
            scores = s_own if line == 0 else s_early if slot == EARLY else s_late
            weights = jnp.exp(scores[at, :] - sent[0][0:1, :])
            if line and slot == LATE:
                grads = dot(tiles[i][rows_at(1, tok), :], qg[1][...], ROWS_T) - table[6:7, :]
            else:
                grads = (d_early if line else d_own)[at, :]
            low = (weights * grads * scale).astype(bf16)
            if line == 0:
                e_ref[rows_at(i, tok), :] = weights.astype(bf16)
                ds_ref[rows_at(i, tok), :] = low
            dq = dq + dot(tiles[i][rows_at(0, tok), :], low, COLS_T)
        total = total + dq
        for which in range(sides):
            far_g = foreign_rows(foreign[which], 1, which, tok)
            delta = foreign_delta(foreign[which], tok)
            lanes = foreign_lanes(which, tok, qg[0].shape[1])
            rows = rows_at(3 * which + line, tok)
            own, par = tiles[2 * line], tiles[2 * line + 1]
            key, value = (pick(near, which, own[rows_at(i, tok), :], par[rows_at(i, tok), :]) for i in range(2))
            weights = jnp.exp(s_far[rows, :] - sent[which][2:3, lanes])
            low = (weights * (dot(value, far_g, ROWS_T) - delta) * scale).astype(bf16)
            if line == 0:
                e_far[rows_at(which, tok), :] = weights.astype(bf16)
                ds_far[rows_at(which, tok), :] = low
            far_total[which] = far_total[which] + dot(key, low, COLS_T)

    dq_ref[...] = total
    for which in range(sides):
        shares[which][...] = border_rows(which, tok, far_total[which].T).astype(bf16)


def border_rows(which, tok, block):
    return block[:tok] if which == 0 else block[block.shape[0] - tok :]


def message_kernel(tok, q_all, g_all, *refs):
    *foreign, out_ref = refs
    out_ref[pl.ds(0, 2 * tok), :] = q_all[...]
    out_ref[pl.ds(2 * tok, 2 * tok), :] = g_all[...]
    for which, ref in enumerate(foreign):
        far_part(out_ref, which, tok)[...] = ref[pl.ds(0, 2 * tok + 16), :]


def far_part(ref, which, tok):
    return ref.at[pl.ds(4 * tok + which * (2 * tok + 16), 2 * tok + 16), :]


def total_kernel(tok, chips, sides, *refs):
    sent, came, note_ref = refs[:sides], refs[sides : 2 * sides], refs[2 * sides]
    y, _, _ = place()

    def log_total(top, total, other_top, other_total):
        both = jnp.maximum(top, other_top)
        return both + jnp.log(total * jnp.exp(top - both) + other_total * jnp.exp(other_top - both))

    lse, far_rows = None, []
    for which in range(sides):
        _, y_at = pair(y, which)
        inside = within(y_at, chips)
        note = came[which]
        far_lse = log_total(note[0:1, :], note[1:2, :], sent[which][2:3, :], sent[which][3:4, :])
        far_rows.append(jnp.where(inside, far_lse, 0.0))
        other = jnp.where(inside, note[2:3, :], -1e30), jnp.where(inside, note[3:4, :], 0.0)
        if which == 0:
            lse = log_total(sent[0][0:1, :], sent[0][1:2, :], *other)
        else:
            lse = log_total(lse, jnp.ones_like(lse), *other)
    rows = [lse] + far_rows
    note_ref[...] = jnp.concatenate(rows + [jnp.zeros((8 - len(rows), 2 * tok), jnp.float32)], axis=0)


def line_query_kernel(tok, chips, heights, sides, scale, line, kv_ref, par_kv_ref, message, extras, *outs):
    e_ref, ds_ref, e_far, ds_far, top_ref = outs[-5:]
    y, c, z = place()
    near = border_is_own(y, c)
    two = 2 * tok
    width = kv_ref.shape[1]
    f32, bf16 = jnp.float32, jnp.bfloat16
    tiles = (kv_ref, par_kv_ref)

    def work():
        rising, _ = pair(z, 2 - line)

        def at(flags, dt):
            return jnp.where(rising, flags[3 * dt : 3 * dt + 1], flags[3 * dt + 2 : 3 * dt + 3])

        rows = extras[pl.ds(2 * tok, 32), :].astype(f32)
        own_flags, par_flags = (pick(near, which, rows[0:9], rows[9:18]) for which in range(2))
        delta = [sum(rows[18 + 3 * i + part : 19 + 3 * i + part] for i in range(3)) for part in range(two // width)]
        delta = jnp.concatenate(delta, axis=1)
        line_q, line_g = (message[pl.ds(part * two, two), :] for part in range(2))
        scores = []
        for slot in range(2):
            row = flag_row(tok, slot, at, own_flags, par_flags, False)
            scores.append(dot(tiles[slot][rows_at(0, tok), :], line_q, ROWS_T) * scale + (row - 1.0) * 1e30)
        tops = [jnp.maximum(*(jnp.max(block, axis=0, keepdims=True) for block in scores))]
        for slot in range(2):
            weights = jnp.exp(scores[slot] - tops[0])
            grads = dot(tiles[slot][rows_at(1, tok), :], line_g, ROWS_T) - delta
            kept = rows_at(slot, tok)
            e_ref[kept, :] = weights.astype(bf16)
            ds_ref[kept, :] = (weights * grads * scale).astype(bf16)
        for which in range(sides):
            ref = far_part(message, which, tok)
            y_rising, y_at = pair(y, which)
            flags = ref[pl.ds(2 * tok, 16), :].astype(f32)
            row = far_row(tok, which, jnp.where(y_rising, at(flags, 0), at(flags, 2)))
            bias = jnp.where(within(y_at, chips), (row - 1.0) * 1e30, -1e30)
            key, value = (pick(near, which, *(tile[rows_at(i, tok), :] for tile in tiles)) for i in range(2))
            far_q, far_g = (foreign_rows(ref, part, which, tok) for part in range(2))
            block = dot(key, far_q, ROWS_T) * scale + bias
            top = jnp.max(block, axis=0, keepdims=True)
            tops.append(to_lanes(which, tok, top, -1e30))
            weights = jnp.exp(block - top)
            grads = dot(value, far_g, ROWS_T) - foreign_delta(ref, tok)
            kept = rows_at(which, tok)
            e_far[kept, :] = weights.astype(bf16)
            ds_far[kept, :] = (weights * grads * scale).astype(bf16)
        top_ref[...] = jnp.concatenate(tops + [jnp.zeros((7 - sides, two), f32)], axis=0)

    pl.when(line_place(z, line, heights)[0])(work)


def times(block, factor):
    column = jnp.broadcast_to(factor, (block.shape[1], factor.shape[1])).T
    return (block.astype(jnp.float32) * column).astype(jnp.bfloat16)


def key_sums(tok, near, line, e_ref, ds_ref, scaled, far):
    rows = [rows_at(2 * line + slot, tok) for slot in range(2)]
    sums = [[dot(ref[at, :], scaled[i]) for i, ref in enumerate((ds_ref, e_ref))] for at in rows]
    for which, (e_far, ds_far, at, far_scaled) in enumerate(far):
        for i, ref in enumerate((ds_far, e_far)):
            block = dot(ref[at, :], far_scaled[i])
            for slot in range(2):
                sums[slot][i] = sums[slot][i] + jnp.where(near == ((slot == 0) == (which == 0)), block, 0.0)
    return sums


def stay_kernel(tok, chips, sides, q_all, g_all, e_ref, ds_ref, e_far, ds_far, raw_dq, note, *refs):
    qg = (q_all, g_all)
    sent, foreign, (own_ref, dq_ref) = refs[:sides], refs[sides : 2 * sides], refs[2 * sides :]
    y, c, _ = place()
    near = border_is_own(y, c)
    width = qg[0].shape[1]
    factor = jnp.exp(sent[0][0:1, :] - note[0:1, :])
    dq_ref[...] = (raw_dq[...] * factor).T
    far = []
    for which in range(sides):
        _, y_at = pair(y, which)
        lanes = foreign_lanes(which, tok, width)
        far_factor = jnp.exp(sent[which][2:3, lanes] - note[1 + which : 2 + which, lanes])
        far_factor = jnp.where(within(y_at, chips), far_factor, 0.0)
        scaled = [times(foreign_rows(foreign[which], part, which, tok), far_factor) for part in range(2)]
        far.append((e_far, ds_far, rows_at(which, tok), scaled))
    sums = key_sums(tok, near, 0, e_ref, ds_ref, [times(qg[part][...], factor) for part in range(2)], far)
    for slot in range(2):
        for i in range(2):
            own_ref[i, rows_at(slot, tok), :] = sums[slot][i]


def line_sums(tok, heights, sides, line, sums, message, note, e_ref, ds_ref, e_far, ds_far, top_ref):
    y, c, z = place()
    near = border_is_own(y, c)

    def work():
        factor = jnp.exp(top_ref[0:1, :] - note[0:1, :])
        scaled = [times(message[pl.ds(part * 2 * tok, 2 * tok), :], factor) for part in range(2)]
        far = []
        for which in range(sides):
            lanes, at = foreign_lanes(which, tok, message.shape[1]), 1 + which
            far_factor = jnp.exp(top_ref[at : at + 1, lanes] - note[at : at + 1, lanes])
            rows = [foreign_rows(far_part(message, which, tok), part, which, tok) for part in range(2)]
            far.append((e_far, ds_far, rows_at(which, tok), [times(block, far_factor) for block in rows]))
        more = key_sums(tok, near, 0, e_ref, ds_ref, scaled, far)
        for slot in range(2):
            for i in range(2):
                sums[i, rows_at(slot, tok), :] += more[slot][i]

    pl.when(line_place(z, line, heights)[0])(work)


def join_kernel(tok, heights, sides, line, own_ref, message, note, *refs):
    *terms, sums = refs
    sums[...] = own_ref[...]
    line_sums(tok, heights, sides, line, sums, message, note, *terms)


def leave_kernel(tok, chips, heights, sides, line, own_ref, dq_ref, note, message, note_in, *refs):
    terms, refs = refs[:5], refs[5:]
    came, backs, (mine_ref, mine_q_ref, swap_ref, sums) = refs[:sides], refs[sides : 2 * sides], refs[2 * sides :]
    y, c, _ = place()
    near = border_is_own(y, c)
    f32, bf16 = jnp.float32, jnp.bfloat16
    width = dq_ref.shape[1]
    sums[...] = own_ref[...]
    line_sums(tok, heights, sides, line, sums, message, note_in, *terms)
    for i in range(2):
        mine_ref[i], swap_ref[i] = sums[i, rows_at(0, tok), :].astype(bf16), sums[i, rows_at(1, tok), :].astype(bf16)
    tiles = []
    for tile in range(2):
        value = dq_ref[rows_at(tile, tok), :]
        if tile < sides:
            _, y_at = pair(y, tile)
            lanes = foreign_lanes(tile, tok, width)
            factor = jnp.exp(came[tile][2:3, lanes] - note[0:1, lanes])
            column = border_rows(tile, tok, jnp.broadcast_to(factor, (width, 2 * width)).T)
            value = value + jnp.where(within(y_at, chips), backs[tile][...].astype(f32) * column, 0.0)
        tiles.append(value.astype(bf16))
    mine_q_ref[...] = jnp.where(near, tiles[0], tiles[1])
    swap_ref[2] = jnp.where(near, tiles[1], tiles[0])


def final_kernel(mine_ref, swap_ref, mine_q_ref, gq_ref, gk_ref, gv_ref):
    head = head_at()
    gq_ref[0, 0, head, 0] = mine_q_ref[...]
    gq_ref[0, 0, 1 - head, 0] = swap_ref[2]
    for i, ref in enumerate((gk_ref, gv_ref)):
        ref[0, 0, head, 0] = mine_ref[i]
        ref[0, 0, 1 - head, 0] = swap_ref[i]


def body(queries, keys, values, grad_out, attn_out, window_mask):
    tok, width = queries.shape[-2:]
    scale = width ** -0.5
    times, heights = lax.axis_size("tm"), lax.axis_size("height")
    chips = times // 2
    sides = 1 if chips == 2 else 2
    bf16, f32 = jnp.bfloat16, jnp.float32

    def call(kernel, shapes, specs, scratch=(), cost=0):
        return pl.pallas_call(
            kernel,
            out_shape=[jax.ShapeDtypeStruct(*shape) for shape in shapes],
            in_specs=list(specs),
            out_specs=[VMEM] * len(shapes),
            scratch_shapes=list(scratch),
            compiler_params=LIMIT,
            cost_estimate=pl.CostEstimate(flops=cost * 10**9, bytes_accessed=0, transcendentals=0) if cost else None,
        )

    def partner(index, which, size):
        if which is None:
            return index
        at = index + 1 if index % 2 == which else index - 1
        return at if 0 <= at < size else None

    def exchange(block, y_which, z_which):
        pairs = []
        for t in range(times):
            for z in range(heights):
                y_at, z_at = partner(t // 2, y_which, chips), partner(z, z_which, heights)
                at = t * heights + z
                alone = y_at is None or z_at is None
                pairs.append((at, (t ^ 1) * heights + z if alone else (2 * y_at + 1 - t % 2) * heights + z_at))
        return lax.ppermute(block, ("tm", "height"), pairs)

    def swap_cores(block):
        return lax.ppermute(block, "tm", [(t, t ^ 1) for t in range(times)])

    line_shape, tile_shape = ((2, 2 * tok, width), bf16), ((2, tok, width), bf16)
    extra = 64
    arguments = (keys, values, queries, grad_out, attn_out, window_mask)
    kv, rest, other = call(
        functools.partial(pack_kernel, tok),
        [((2 * tok + extra, width), bf16), ((3 * tok + 16, width), bf16), ((5 * tok + 16, width), bf16)],
        [HBM] * 6,
        [pltpu.SMEM(window_mask.shape, jnp.int32), pltpu.SemaphoreType.DMA((11,))],
    )(*(pltpu.with_memory_space_constraint(x, pltpu.HBM) for x in arguments))
    early = [exchange(kv, None, which) for which in (1, 0)]
    par = swap_cores(other)
    border_shape, two = ((2 * tok + 48, width), bf16), 2 * tok
    par_kv, *borders = call(
        functools.partial(line_kernel, tok), [((2 * tok + 32, width), bf16)] + [border_shape] * sides, [VMEM] * 2
    )(rest, par)
    foreign = [exchange(borders[which], which, None) for which in range(sides)]
    late = [exchange(par_kv, None, which) for which in (1, 0)]
    tiles = (kv, par_kv, late[0], early[0], late[1], early[1])
    note_shape, raw_shape = ((8, two), f32), ((width, two), f32)

    def square(count, kind=f32):
        return ((count * tok, two), kind)

    def far_square(kind=f32):
        return ((3 * sides * tok, 2 * width), kind)

    q_all, g_all, table, s_own, d_own = call(
        functools.partial(first_kernel, tok, heights, scale),
        [((two, width), bf16)] * 2 + [note_shape, square(2), square(2)],
        [VMEM] * 4,
    )(kv, par_kv, rest, par)
    qg = (q_all, g_all)
    (message,) = call(
        functools.partial(message_kernel, tok),
        [((4 * tok + sides * (2 * tok + 16), width), bf16)],
        [VMEM] * (2 + sides),
    )(*qg, *foreign)
    queries_in = [exchange(message, None, which) for which in (1, 0)]
    s_early, d_early, part = call(
        functools.partial(early_kernel, tok, scale), [square(2), square(2), note_shape], [VMEM] * 6
    )(*qg, table, s_own, *early)
    s_late, s_far, *sent = call(
        functools.partial(score_kernel, tok, chips, heights, sides, scale),
        [square(2), far_square()] + [note_shape] * sides,
        [VMEM] * (10 + sides),
    )(*qg, table, part, *foreign, *tiles)
    came = [exchange(sent[which], which, None) for which in range(sides)]
    far_tile = ((sides * tok, 2 * width), bf16)
    e, ds, e_far, ds_far, raw_dq, *shares = call(
        functools.partial(middle_kernel, tok, sides, scale),
        [square(2, bf16)] * 2 + [far_tile] * 2 + [raw_shape] + [((tok, width), bf16)] * sides,
        [VMEM] * (15 + 2 * sides),
        cost=20,
    )(*qg, table, s_own, d_own, s_early, d_early, s_late, s_far, *tiles, *foreign, *sent)
    (note,) = call(functools.partial(total_kernel, tok, chips, sides), [note_shape], [VMEM] * (2 * sides))(*sent, *came)
    notes = [exchange(note, None, which) for which in (1, 0)]
    shares = [exchange(share, which, None) for which, share in enumerate(shares)]
    sums_shape = ((2, two, width), f32)

    def line_terms(line, *earlier):
        return call(
            functools.partial(line_query_kernel, tok, chips, heights, sides, scale, line),
            [square(2, bf16)] * 2 + [far_tile] * 2 + [note_shape],
            [VMEM] * (4 + len(earlier)),
            cost=20,
        )(kv, par_kv, queries_in[line - 1], late[line - 1], *earlier)

    own, dq = call(
        functools.partial(stay_kernel, tok, chips, sides),
        [sums_shape, ((two, width), f32)],
        [VMEM] * (8 + 2 * sides),
    )(*qg, e, ds, e_far, ds_far, raw_dq, note, *sent, *foreign)
    (joined,) = call(
        functools.partial(join_kernel, tok, heights, sides, 2), [sums_shape], [VMEM] * 8
    )(own, queries_in[1], notes[1], *line_terms(2))
    mine, mine_q, leaving = call(
        functools.partial(leave_kernel, tok, chips, heights, sides, 1),
        [tile_shape, ((tok, width), bf16), ((3, tok, width), bf16)],
        [VMEM] * (10 + 2 * sides),
        [pltpu.VMEM(*sums_shape)],
    )(joined, dq, note, queries_in[0], notes[0], *line_terms(1, joined), *came, *shares)
    return call(final_kernel, [(queries.shape, bf16)] * 3, [VMEM] * 3)(mine, swap_cores(leaving), mine_q)


def solution(mesh):
    placed = P("tm", "height", "dp", None, None, None)
    return jax.shard_map(
        body,
        mesh=mesh,
        in_specs=(placed,) * 5 + (P("tm", "height", None, None),),
        out_specs=(placed,) * 3,
        check_vma=False,
    )
```

```python
import functools

import jax
import jax.numpy as jnp
from jax import lax
from jax.experimental import pallas as pl
from jax.experimental.pallas import tpu as pltpu
from jax.sharding import PartitionSpec as P

VMEM = pl.BlockSpec(memory_space=pltpu.VMEM)
HBM = pl.BlockSpec(memory_space=pltpu.HBM)
LIMIT = pltpu.CompilerParams(vmem_limit_bytes=32 * 1024 * 1024)
ROWS_T = (((1,), (1,)), ((), ()))
COLS_T = (((0,), (0,)), ((), ()))


def dot(a, b, dims=(((1,), (0,)), ((), ()))):
    return lax.dot_general(a, b, dims, preferred_element_type=jnp.float32)


LATE, EARLY = 0, 1


def place():
    t = lax.axis_index("tm")
    return t // 2, t % 2, lax.axis_index("height")


def head_at():
    y, c, z = place()
    return (c + y + z) % 2


def pair(index, which):
    rising = (index % 2) == (0 if which == 0 else 1)
    return rising, jnp.where(rising, index + 1, index - 1)


def within(index, size):
    return (index >= 0) & (index < size)


def pack_kernel(tok, k_ref, v_ref, q_ref, g_ref, o_ref, mask_ref, kv_ref, rest_ref, other_ref, flags, sems):
    head = head_at()
    copies = [pltpu.make_async_copy(mask_ref, flags, sems.at[10])]
    for i, ref in enumerate((k_ref, v_ref, q_ref, g_ref, o_ref)):
        own = (kv_ref if i < 2 else rest_ref).at[pl.ds((i if i < 2 else i - 2) * tok, tok), :]
        copies.append(pltpu.make_async_copy(ref.at[0, 0, head, 0], own, sems.at[2 * i + 1]))
        copies.append(
            pltpu.make_async_copy(ref.at[0, 0, 1 - head, 0], other_ref.at[pl.ds(i * tok, tok), :], sems.at[2 * i])
        )
    for copy in copies:
        copy.start()
    copies[0].wait()
    row = lax.broadcasted_iota(jnp.int32, (16, rest_ref.shape[1]), 0)
    spread = jnp.zeros(row.shape, jnp.float32)
    for i in range(9):
        on = (flags[0, 0, 0, 9 * (i // 3) + 3 * (i % 3) + 1] != 0).astype(jnp.float32)
        spread = jnp.where(row == i, on, spread)
    rest_ref[pl.ds(3 * tok, 16), :] = spread.astype(jnp.bfloat16)
    other_ref[pl.ds(5 * tok, 16), :] = spread.astype(jnp.bfloat16)
    for copy in copies[1:]:
        copy.wait()


def rows_at(index, tok):
    return pl.ds(index * tok, tok)


def border_is_own(y, c):
    rising, _ = pair(y, 0)
    return (c == 1) == rising


def pick(near, which, own, par):
    return jnp.where(near, own, par) if which == 0 else jnp.where(near, par, own)


def three_terms(row):
    terms = []
    for _ in range(3):
        terms.append(row.astype(jnp.bfloat16).astype(jnp.float32))
        row = row - terms[-1]
    return terms


def line_kernel(tok, rest_ref, par_ref, par_kv_ref, *border_refs):
    y, c, _ = place()
    near = border_is_own(y, c)
    for i in range(2):
        par_kv_ref[rows_at(i, tok), :] = par_ref[rows_at(i, tok), :]
    width = par_ref.shape[1]
    f32 = jnp.float32
    q, g, o = (
        [pick(near, which, rest_ref[rows_at(i, tok), :], par_ref[rows_at(i + 2, tok), :]) for which in range(2)]
        for i in range(3)
    )
    own_flags, par_flags = rest_ref[pl.ds(3 * tok, 16), :].astype(f32), par_ref[pl.ds(5 * tok, 16), :].astype(f32)
    flags = [pick(near, which, own_flags, par_flags)[0:9] for which in range(2)]
    product = jnp.concatenate(g, axis=0).astype(f32) * jnp.concatenate(o, axis=0).astype(f32)
    terms = [
        [term[:, start : start + width] for start in range(0, 2 * tok, width)]
        for term in three_terms(jnp.sum(product.T, axis=0, keepdims=True))
    ]
    for which, ref in enumerate(border_refs):
        ref[rows_at(0, tok), :], ref[rows_at(1, tok), :] = q[which], g[which]
        part = slice(0, 2) if which == 0 else slice(len(terms[0]) - 2, None)
        lines = [flags[which]] + [row for term in terms for row in term[part]] + [jnp.zeros((1, width), f32)]
        ref[pl.ds(2 * tok, 16), :] = jnp.concatenate(lines, axis=0).astype(jnp.bfloat16)
    lines = flags + [row for term in terms for row in term] + [jnp.zeros((5, width), f32)]
    par_kv_ref[pl.ds(2 * tok, 32), :] = jnp.concatenate(lines, axis=0).astype(jnp.bfloat16)


def foreign_delta(ref, tok):
    terms = ref[pl.ds(2 * tok, 16), :].astype(jnp.float32)
    return jnp.concatenate(
        [sum(terms[9 + 2 * i + half : 10 + 2 * i + half] for i in range(3)) for half in range(2)], axis=1
    )


def line_place(z, line, heights):
    if line == 0:
        return True, lambda flags, dt: flags[3 * dt + 1 : 3 * dt + 2]
    rising, at = pair(z, 2 - line)
    return within(at, heights), lambda flags, dt: jnp.where(
        rising, flags[3 * dt + 2 : 3 * dt + 3], flags[3 * dt : 3 * dt + 1]
    )


def lanes_of(tok, border, other):
    width = border.shape[1]
    lane = lax.broadcasted_iota(jnp.int32, (1, width), 1)
    return jnp.concatenate(
        [jnp.where(lane + start < tok, border, other) for start in range(0, 2 * tok, width)], axis=1
    )


def flag_row(tok, slot, at, own_flags, par_flags, own_query):
    y, c, _ = place()
    first, near = c == 0, border_is_own(y, c)
    if slot == 0:
        own, par = at(own_flags, 1), jnp.where(first, at(par_flags, 0), at(par_flags, 2))
    else:
        own, par = jnp.where(first, at(own_flags, 2), at(own_flags, 0)), at(par_flags, 1)
    if own_query:
        centre = jnp.ones_like(own)
        own, par = (centre, par) if slot == 0 else (own, centre)
    return lanes_of(tok, pick(near, 0, own, par), pick(near, 1, own, par))


def first_kernel(tok, heights, scale, kv_ref, par_kv_ref, rest_ref, par_ref, q_all, g_all, table, s_ref, d_ref):
    qg = (q_all, g_all)
    y, c, z = place()
    two = 2 * tok
    width = rest_ref.shape[1]
    f32 = jnp.float32
    near = border_is_own(y, c)
    out = []
    for part in range(3):
        own, par = rest_ref[rows_at(part, tok), :], par_ref[rows_at(part + 2, tok), :]
        tiles = [pick(near, which, own, par) for which in range(2)]
        if part == 2:
            out = jnp.concatenate(tiles, axis=0)
        else:
            for which in range(2):
                qg[part][rows_at(which, tok), :] = tiles[which]
    delta = jnp.sum((qg[1][...].astype(f32) * out.astype(f32)).T, axis=0, keepdims=True)

    own_flags = rest_ref[pl.ds(3 * tok, 16), :].astype(f32)
    par_flags = par_ref[pl.ds(5 * tok, 16), :].astype(f32)
    lines = []
    for line in range(3):
        inside, at = line_place(z, line, heights)
        for slot in range(2):
            row = flag_row(tok, slot, at, own_flags, par_flags, line == 0)
            lines.append(jnp.where(inside, (row - 1.0) * 1e30, -1e30))
    table[...] = jnp.concatenate(lines + [delta, jnp.zeros((1, two), f32)], axis=0)
    for i, source in enumerate((kv_ref, par_kv_ref)):
        rows = rows_at(i, tok)
        s_ref[rows, :] = dot(source[rows_at(0, tok), :], qg[0][...], ROWS_T) * scale + table[i : i + 1, :]
        d_ref[rows, :] = dot(source[rows_at(1, tok), :], qg[1][...], ROWS_T) - table[6:7, :]


def largest(tok, blocks):
    lanes = blocks[0][0].shape[1]
    top = jnp.full((8, lanes), -1e30, jnp.float32)
    for ref, i in blocks:
        top = jnp.maximum(top, jnp.max(ref[rows_at(i, tok), :].reshape(tok // 8, 8, lanes), axis=0))
    return jnp.max(top, axis=0, keepdims=True)


def summed(tok, blocks, top):
    lanes = blocks[0][0].shape[1]
    total = jnp.zeros((8, lanes), jnp.float32)
    for ref, i in blocks:
        weights = jnp.exp(ref[rows_at(i, tok), :] - top)
        total = total + jnp.sum(weights.reshape(tok // 8, 8, lanes), axis=0)
    return jnp.sum(total, axis=0, keepdims=True)


def early_kernel(tok, scale, q_all, g_all, table, s_own, one_ref, two_ref, s_ref, d_ref, part_ref):
    qg = (q_all, g_all)
    for i, source in enumerate((one_ref, two_ref)):
        rows = rows_at(i, tok)
        s_ref[rows, :] = dot(source[rows_at(0, tok), :], qg[0][...], ROWS_T) * scale + table[2 + 2 * i + EARLY : 3 + 2 * i + EARLY, :]
        d_ref[rows, :] = dot(source[rows_at(1, tok), :], qg[1][...], ROWS_T) - table[6:7, :]
    blocks = [(ref, i) for ref in (s_own, s_ref) for i in range(2)]
    top = largest(tok, blocks)
    total = summed(tok, blocks, top)
    part_ref[...] = jnp.concatenate([top, total, jnp.zeros((6, 2 * tok), jnp.float32)], axis=0)


def foreign_rows(ref, part, which, tok):
    block = ref[rows_at(part, tok), :]
    gap = jnp.zeros((2 * block.shape[1] - tok, block.shape[1]), block.dtype)
    return jnp.concatenate([block, gap] if which == 0 else [gap, block], axis=0)


def foreign_lanes(which, tok, width):
    return slice(0, 2 * width) if which == 0 else slice(2 * tok - 2 * width, 2 * tok)


def far_row(tok, which, row):
    lane, width = lax.broadcasted_iota(jnp.int32, row.shape, 1), row.shape[1]
    return jnp.concatenate(
        [
            jnp.where(lane + start < tok if which == 0 else lane + start >= 2 * width - tok, row, 0.0)
            for start in (0, width)
        ],
        axis=1,
    )


def to_lanes(which, tok, row, fill):
    gap = jnp.full((1, 2 * tok - row.shape[1]), fill, jnp.float32)
    return jnp.concatenate([row, gap] if which == 0 else [gap, row], axis=1)


def score_kernel(tok, chips, heights, sides, scale, q_all, g_all, table, part, *refs):
    qg = (q_all, g_all)
    foreign, keys, refs = refs[:sides], refs[sides : 6 + sides], refs[6 + sides :]
    s_late, s_far, *notes = refs
    y, c, z = place()
    near = border_is_own(y, c)
    two = 2 * tok
    f32 = jnp.float32
    far = []
    for which in range(sides):
        rising, y_at = pair(y, which)
        flags = foreign[which][pl.ds(2 * tok, 16), :].astype(f32)
        queries = foreign_rows(foreign[which], 0, which, tok)
        for line in range(3):
            inside, at = line_place(z, line, heights)
            row = far_row(tok, which, jnp.where(rising, at(flags, 0), at(flags, 2)))
            bias = jnp.where(inside & within(y_at, chips), (row - 1.0) * 1e30, -1e30)
            border = pick(near, which, keys[2 * line][rows_at(0, tok), :], keys[2 * line + 1][rows_at(0, tok), :])
            s_far[rows_at(3 * which + line, tok), :] = dot(border, queries, ROWS_T) * scale + bias
        blocks = [(s_far, 3 * which + line) for line in range(3)]
        top = largest(tok, blocks)
        far.append([to_lanes(which, tok, top, -1e30), to_lanes(which, tok, summed(tok, blocks, top), 0.0)])
    for i in range(2):
        at = 2 + 2 * i + LATE
        scores = dot(keys[at][rows_at(0, tok), :], qg[0][...], ROWS_T) * scale
        s_late[rows_at(i, tok), :] = scores + table[at : at + 1, :]
    blocks = [(s_late, i) for i in range(2)]
    top = jnp.maximum(part[0:1, :], largest(tok, blocks))
    total = part[1:2, :] * jnp.exp(part[0:1, :] - top) + summed(tok, blocks, top)
    for which in range(sides):
        notes[which][...] = jnp.concatenate([top, total] + far[which] + [jnp.zeros((4, two), f32)], axis=0)


def middle_kernel(tok, sides, scale, q_all, g_all, table, s_own, d_own, s_early, d_early, s_late, s_far, *refs):
    qg = (q_all, g_all)
    tiles, foreign, sent = refs[:6], refs[6 : 6 + sides], refs[6 + sides : 6 + 2 * sides]
    e_ref, ds_ref, e_far, ds_far, dq_ref, *shares = refs[6 + 2 * sides :]
    y, c, _ = place()
    near = border_is_own(y, c)
    bf16 = jnp.bfloat16

    total, far_total = 0.0, [0.0] * sides
    for line in range(3):
        dq = 0.0
        for slot in range(2):
            i, at = 2 * line + slot, rows_at(line - 1 if line else slot, tok)
            scores = s_own if line == 0 else s_early if slot == EARLY else s_late
            weights = jnp.exp(scores[at, :] - sent[0][0:1, :])
            if line and slot == LATE:
                grads = dot(tiles[i][rows_at(1, tok), :], qg[1][...], ROWS_T) - table[6:7, :]
            else:
                grads = (d_early if line else d_own)[at, :]
            low = (weights * grads * scale).astype(bf16)
            if line == 0:
                e_ref[rows_at(i, tok), :] = weights.astype(bf16)
                ds_ref[rows_at(i, tok), :] = low
            dq = dq + dot(tiles[i][rows_at(0, tok), :], low, COLS_T)
        total = total + dq
        for which in range(sides):
            far_g = foreign_rows(foreign[which], 1, which, tok)
            delta = foreign_delta(foreign[which], tok)
            lanes = foreign_lanes(which, tok, qg[0].shape[1])
            rows = rows_at(3 * which + line, tok)
            own, par = tiles[2 * line], tiles[2 * line + 1]
            key, value = (pick(near, which, own[rows_at(i, tok), :], par[rows_at(i, tok), :]) for i in range(2))
            weights = jnp.exp(s_far[rows, :] - sent[which][2:3, lanes])
            low = (weights * (dot(value, far_g, ROWS_T) - delta) * scale).astype(bf16)
            if line == 0:
                e_far[rows_at(which, tok), :] = weights.astype(bf16)
                ds_far[rows_at(which, tok), :] = low
            far_total[which] = far_total[which] + dot(key, low, COLS_T)

    dq_ref[...] = total
    for which in range(sides):
        shares[which][...] = border_rows(which, tok, far_total[which].T).astype(bf16)


def border_rows(which, tok, block):
    return block[:tok] if which == 0 else block[block.shape[0] - tok :]


def message_kernel(tok, q_all, g_all, *refs):
    *foreign, out_ref = refs
    out_ref[pl.ds(0, 2 * tok), :] = q_all[...]
    out_ref[pl.ds(2 * tok, 2 * tok), :] = g_all[...]
    for which, ref in enumerate(foreign):
        far_part(out_ref, which, tok)[...] = ref[pl.ds(0, 2 * tok + 16), :]


def far_part(ref, which, tok):
    return ref.at[pl.ds(4 * tok + which * (2 * tok + 16), 2 * tok + 16), :]


def total_kernel(tok, chips, sides, *refs):
    sent, came, note_ref = refs[:sides], refs[sides : 2 * sides], refs[2 * sides]
    y, _, _ = place()

    def log_total(top, total, other_top, other_total):
        both = jnp.maximum(top, other_top)
        return both + jnp.log(total * jnp.exp(top - both) + other_total * jnp.exp(other_top - both))

    lse, far_rows = None, []
    for which in range(sides):
        _, y_at = pair(y, which)
        inside = within(y_at, chips)
        note = came[which]
        far_lse = log_total(note[0:1, :], note[1:2, :], sent[which][2:3, :], sent[which][3:4, :])
        far_rows.append(jnp.where(inside, far_lse, 0.0))
        other = jnp.where(inside, note[2:3, :], -1e30), jnp.where(inside, note[3:4, :], 0.0)
        if which == 0:
            lse = log_total(sent[0][0:1, :], sent[0][1:2, :], *other)
        else:
            lse = log_total(lse, jnp.ones_like(lse), *other)
    rows = [lse] + far_rows
    note_ref[...] = jnp.concatenate(rows + [jnp.zeros((8 - len(rows), 2 * tok), jnp.float32)], axis=0)


def line_query_kernel(tok, chips, heights, sides, scale, line, kv_ref, par_kv_ref, message, extras, *outs):
    e_ref, ds_ref, e_far, ds_far, top_ref = outs[-5:]
    y, c, z = place()
    near = border_is_own(y, c)
    two = 2 * tok
    width = kv_ref.shape[1]
    f32, bf16 = jnp.float32, jnp.bfloat16
    tiles = (kv_ref, par_kv_ref)

    def work():
        rising, _ = pair(z, 2 - line)

        def at(flags, dt):
            return jnp.where(rising, flags[3 * dt : 3 * dt + 1], flags[3 * dt + 2 : 3 * dt + 3])

        rows = extras[pl.ds(2 * tok, 32), :].astype(f32)
        own_flags, par_flags = (pick(near, which, rows[0:9], rows[9:18]) for which in range(2))
        delta = [sum(rows[18 + 3 * i + part : 19 + 3 * i + part] for i in range(3)) for part in range(two // width)]
        delta = jnp.concatenate(delta, axis=1)
        line_q, line_g = (message[pl.ds(part * two, two), :] for part in range(2))
        scores = []
        for slot in range(2):
            row = flag_row(tok, slot, at, own_flags, par_flags, False)
            scores.append(dot(tiles[slot][rows_at(0, tok), :], line_q, ROWS_T) * scale + (row - 1.0) * 1e30)
        tops = [jnp.maximum(*(jnp.max(block, axis=0, keepdims=True) for block in scores))]
        for slot in range(2):
            weights = jnp.exp(scores[slot] - tops[0])
            grads = dot(tiles[slot][rows_at(1, tok), :], line_g, ROWS_T) - delta
            kept = rows_at(slot, tok)
            e_ref[kept, :] = weights.astype(bf16)
            ds_ref[kept, :] = (weights * grads * scale).astype(bf16)
        for which in range(sides):
            ref = far_part(message, which, tok)
            y_rising, y_at = pair(y, which)
            flags = ref[pl.ds(2 * tok, 16), :].astype(f32)
            row = far_row(tok, which, jnp.where(y_rising, at(flags, 0), at(flags, 2)))
            bias = jnp.where(within(y_at, chips), (row - 1.0) * 1e30, -1e30)
            key, value = (pick(near, which, *(tile[rows_at(i, tok), :] for tile in tiles)) for i in range(2))
            far_q, far_g = (foreign_rows(ref, part, which, tok) for part in range(2))
            block = dot(key, far_q, ROWS_T) * scale + bias
            top = jnp.max(block, axis=0, keepdims=True)
            tops.append(to_lanes(which, tok, top, -1e30))
            weights = jnp.exp(block - top)
            grads = dot(value, far_g, ROWS_T) - foreign_delta(ref, tok)
            kept = rows_at(which, tok)
            e_far[kept, :] = weights.astype(bf16)
            ds_far[kept, :] = (weights * grads * scale).astype(bf16)
        top_ref[...] = jnp.concatenate(tops + [jnp.zeros((7 - sides, two), f32)], axis=0)

    pl.when(line_place(z, line, heights)[0])(work)


def times(block, factor):
    column = jnp.broadcast_to(factor, (block.shape[1], factor.shape[1])).T
    return (block.astype(jnp.float32) * column).astype(jnp.bfloat16)


def key_sums(tok, near, line, e_ref, ds_ref, scaled, far):
    rows = [rows_at(2 * line + slot, tok) for slot in range(2)]
    sums = [[dot(ref[at, :], scaled[i]) for i, ref in enumerate((ds_ref, e_ref))] for at in rows]
    for which, (e_far, ds_far, at, far_scaled) in enumerate(far):
        for i, ref in enumerate((ds_far, e_far)):
            block = dot(ref[at, :], far_scaled[i])
            for slot in range(2):
                sums[slot][i] = sums[slot][i] + jnp.where(near == ((slot == 0) == (which == 0)), block, 0.0)
    return sums


def stay_kernel(tok, chips, sides, q_all, g_all, e_ref, ds_ref, e_far, ds_far, raw_dq, note, *refs):
    qg = (q_all, g_all)
    sent, foreign, (own_ref, dq_ref) = refs[:sides], refs[sides : 2 * sides], refs[2 * sides :]
    y, c, _ = place()
    near = border_is_own(y, c)
    width = qg[0].shape[1]
    factor = jnp.exp(sent[0][0:1, :] - note[0:1, :])
    dq_ref[...] = (raw_dq[...] * factor).T
    far = []
    for which in range(sides):
        _, y_at = pair(y, which)
        lanes = foreign_lanes(which, tok, width)
        far_factor = jnp.exp(sent[which][2:3, lanes] - note[1 + which : 2 + which, lanes])
        far_factor = jnp.where(within(y_at, chips), far_factor, 0.0)
        scaled = [times(foreign_rows(foreign[which], part, which, tok), far_factor) for part in range(2)]
        far.append((e_far, ds_far, rows_at(which, tok), scaled))
    sums = key_sums(tok, near, 0, e_ref, ds_ref, [times(qg[part][...], factor) for part in range(2)], far)
    for slot in range(2):
        for i in range(2):
            own_ref[i, rows_at(slot, tok), :] = sums[slot][i]


def line_sums(tok, heights, sides, line, sums, message, note, e_ref, ds_ref, e_far, ds_far, top_ref):
    y, c, z = place()
    near = border_is_own(y, c)

    def work():
        factor = jnp.exp(top_ref[0:1, :] - note[0:1, :])
        scaled = [times(message[pl.ds(part * 2 * tok, 2 * tok), :], factor) for part in range(2)]
        far = []
        for which in range(sides):
            lanes, at = foreign_lanes(which, tok, message.shape[1]), 1 + which
            far_factor = jnp.exp(top_ref[at : at + 1, lanes] - note[at : at + 1, lanes])
            rows = [foreign_rows(far_part(message, which, tok), part, which, tok) for part in range(2)]
            far.append((e_far, ds_far, rows_at(which, tok), [times(block, far_factor) for block in rows]))
        more = key_sums(tok, near, 0, e_ref, ds_ref, scaled, far)
        for slot in range(2):
            for i in range(2):
                sums[i, rows_at(slot, tok), :] += more[slot][i]

    pl.when(line_place(z, line, heights)[0])(work)


def join_kernel(tok, heights, sides, line, own_ref, message, note, *refs):
    *terms, sums = refs
    sums[...] = own_ref[...]
    line_sums(tok, heights, sides, line, sums, message, note, *terms)


def leave_kernel(tok, chips, heights, sides, line, own_ref, dq_ref, note, message, note_in, *refs):
    terms, refs = refs[:5], refs[5:]
    came, backs, (mine_ref, mine_q_ref, swap_ref, sums) = refs[:sides], refs[sides : 2 * sides], refs[2 * sides :]
    y, c, _ = place()
    near = border_is_own(y, c)
    f32, bf16 = jnp.float32, jnp.bfloat16
    width = dq_ref.shape[1]
    sums[...] = own_ref[...]
    line_sums(tok, heights, sides, line, sums, message, note_in, *terms)
    for i in range(2):
        mine_ref[i], swap_ref[i] = sums[i, rows_at(0, tok), :].astype(bf16), sums[i, rows_at(1, tok), :].astype(bf16)
    tiles = []
    for tile in range(2):
        value = dq_ref[rows_at(tile, tok), :]
        if tile < sides:
            _, y_at = pair(y, tile)
            lanes = foreign_lanes(tile, tok, width)
            factor = jnp.exp(came[tile][2:3, lanes] - note[0:1, lanes])
            column = border_rows(tile, tok, jnp.broadcast_to(factor, (width, 2 * width)).T)
            value = value + jnp.where(within(y_at, chips), backs[tile][...].astype(f32) * column, 0.0)
        tiles.append(value.astype(bf16))
    mine_q_ref[...] = jnp.where(near, tiles[0], tiles[1])
    swap_ref[2] = jnp.where(near, tiles[1], tiles[0])


def final_kernel(mine_ref, swap_ref, mine_q_ref, gq_ref, gk_ref, gv_ref, sems):
    head = head_at()
    blocks = [(mine_q_ref, head, gq_ref), (swap_ref.at[2], 1 - head, gq_ref)]
    for i, ref in enumerate((gk_ref, gv_ref)):
        blocks += [(mine_ref.at[i], head, ref), (swap_ref.at[i], 1 - head, ref)]
    copies = [
        pltpu.make_async_copy(block, ref.at[0, 0, at, 0], sems.at[i]) for i, (block, at, ref) in enumerate(blocks)
    ]
    for copy in copies:
        copy.start()
    for copy in copies:
        copy.wait()


def body(queries, keys, values, grad_out, attn_out, window_mask):
    tok, width = queries.shape[-2:]
    scale = width ** -0.5
    times, heights = lax.axis_size("tm"), lax.axis_size("height")
    chips = times // 2
    sides = 1 if chips == 2 else 2
    bf16, f32 = jnp.bfloat16, jnp.float32

    def call(kernel, shapes, specs, scratch=(), cost=0):
        return pl.pallas_call(
            kernel,
            out_shape=[jax.ShapeDtypeStruct(*shape) for shape in shapes],
            in_specs=list(specs),
            out_specs=[VMEM] * len(shapes),
            scratch_shapes=list(scratch),
            compiler_params=LIMIT,
            cost_estimate=pl.CostEstimate(flops=cost * 10**9, bytes_accessed=0, transcendentals=0) if cost else None,
        )

    def partner(index, which, size):
        if which is None:
            return index
        at = index + 1 if index % 2 == which else index - 1
        return at if 0 <= at < size else None

    def exchange(block, y_which, z_which):
        pairs = []
        for t in range(times):
            for z in range(heights):
                y_at, z_at = partner(t // 2, y_which, chips), partner(z, z_which, heights)
                at = t * heights + z
                alone = y_at is None or z_at is None
                pairs.append((at, (t ^ 1) * heights + z if alone else (2 * y_at + 1 - t % 2) * heights + z_at))
        return lax.ppermute(block, ("tm", "height"), pairs)

    def swap_cores(block):
        return lax.ppermute(block, "tm", [(t, t ^ 1) for t in range(times)])

    line_shape, tile_shape = ((2, 2 * tok, width), bf16), ((2, tok, width), bf16)
    extra = 64
    arguments = (keys, values, queries, grad_out, attn_out, window_mask)
    kv, rest, other = call(
        functools.partial(pack_kernel, tok),
        [((2 * tok + extra, width), bf16), ((3 * tok + 16, width), bf16), ((5 * tok + 16, width), bf16)],
        [HBM] * 6,
        [pltpu.SMEM(window_mask.shape, jnp.int32), pltpu.SemaphoreType.DMA((11,))],
    )(*(pltpu.with_memory_space_constraint(x, pltpu.HBM) for x in arguments))
    early = [exchange(kv, None, which) for which in (1, 0)]
    par = swap_cores(other)
    border_shape, two = ((2 * tok + 48, width), bf16), 2 * tok
    par_kv, *borders = call(
        functools.partial(line_kernel, tok), [((2 * tok + 32, width), bf16)] + [border_shape] * sides, [VMEM] * 2
    )(rest, par)
    foreign = [exchange(borders[which], which, None) for which in range(sides)]
    late = [exchange(par_kv, None, which) for which in (1, 0)]
    tiles = (kv, par_kv, late[0], early[0], late[1], early[1])
    note_shape, raw_shape = ((8, two), f32), ((width, two), f32)

    def square(count, kind=f32):
        return ((count * tok, two), kind)

    def far_square(kind=f32):
        return ((3 * sides * tok, 2 * width), kind)

    q_all, g_all, table, s_own, d_own = call(
        functools.partial(first_kernel, tok, heights, scale),
        [((two, width), bf16)] * 2 + [note_shape, square(2), square(2)],
        [VMEM] * 4,
    )(kv, par_kv, rest, par)
    qg = (q_all, g_all)
    (message,) = call(
        functools.partial(message_kernel, tok),
        [((4 * tok + sides * (2 * tok + 16), width), bf16)],
        [VMEM] * (2 + sides),
    )(*qg, *foreign)
    queries_in = [exchange(message, None, which) for which in (1, 0)]
    s_early, d_early, part = call(
        functools.partial(early_kernel, tok, scale), [square(2), square(2), note_shape], [VMEM] * 6
    )(*qg, table, s_own, *early)
    s_late, s_far, *sent = call(
        functools.partial(score_kernel, tok, chips, heights, sides, scale),
        [square(2), far_square()] + [note_shape] * sides,
        [VMEM] * (10 + sides),
    )(*qg, table, part, *foreign, *tiles)
    came = [exchange(sent[which], which, None) for which in range(sides)]
    far_tile = ((sides * tok, 2 * width), bf16)
    e, ds, e_far, ds_far, raw_dq, *shares = call(
        functools.partial(middle_kernel, tok, sides, scale),
        [square(2, bf16)] * 2 + [far_tile] * 2 + [raw_shape] + [((tok, width), bf16)] * sides,
        [VMEM] * (15 + 2 * sides),
        cost=20,
    )(*qg, table, s_own, d_own, s_early, d_early, s_late, s_far, *tiles, *foreign, *sent)
    (note,) = call(functools.partial(total_kernel, tok, chips, sides), [note_shape], [VMEM] * (2 * sides))(*sent, *came)
    notes = [exchange(note, None, which) for which in (1, 0)]
    shares = [exchange(share, which, None) for which, share in enumerate(shares)]
    sums_shape = ((2, two, width), f32)

    def line_terms(line, *earlier):
        return call(
            functools.partial(line_query_kernel, tok, chips, heights, sides, scale, line),
            [square(2, bf16)] * 2 + [far_tile] * 2 + [note_shape],
            [VMEM] * (4 + len(earlier)),
            cost=20,
        )(kv, par_kv, queries_in[line - 1], late[line - 1], *earlier)

    own, dq = call(
        functools.partial(stay_kernel, tok, chips, sides),
        [sums_shape, ((two, width), f32)],
        [VMEM] * (8 + 2 * sides),
    )(*qg, e, ds, e_far, ds_far, raw_dq, note, *sent, *foreign)
    (joined,) = call(
        functools.partial(join_kernel, tok, heights, sides, 2), [sums_shape], [VMEM] * 8
    )(own, queries_in[1], notes[1], *line_terms(2))
    mine, mine_q, leaving = call(
        functools.partial(leave_kernel, tok, chips, heights, sides, 1),
        [tile_shape, ((tok, width), bf16), ((3, tok, width), bf16)],
        [VMEM] * (10 + 2 * sides),
        [pltpu.VMEM(*sums_shape)],
    )(joined, dq, note, queries_in[0], notes[0], *line_terms(1, joined), *came, *shares)
    return pl.pallas_call(
        final_kernel,
        out_shape=[jax.ShapeDtypeStruct(queries.shape, bf16)] * 3,
        in_specs=[VMEM] * 3,
        out_specs=[HBM] * 3,
        scratch_shapes=[pltpu.SemaphoreType.DMA((6,))],
        compiler_params=LIMIT,
    )(mine, swap_cores(leaving), mine_q)


def solution(mesh):
    placed = P("tm", "height", "dp", None, None, None)
    return jax.shard_map(
        body,
        mesh=mesh,
        in_specs=(placed,) * 5 + (P("tm", "height", None, None),),
        out_specs=(placed,) * 3,
        check_vma=False,
    )
```

```python
import functools

import jax
import jax.numpy as jnp
from jax import lax
from jax.experimental import pallas as pl
from jax.experimental.pallas import tpu as pltpu
from jax.sharding import PartitionSpec as P

VMEM = pl.BlockSpec(memory_space=pltpu.VMEM)
HBM = pl.BlockSpec(memory_space=pltpu.HBM)
LIMIT = pltpu.CompilerParams(vmem_limit_bytes=32 * 1024 * 1024)
ROWS_T = (((1,), (1,)), ((), ()))
COLS_T = (((0,), (0,)), ((), ()))


def dot(a, b, dims=(((1,), (0,)), ((), ()))):
    return lax.dot_general(a, b, dims, preferred_element_type=jnp.float32)


LATE, EARLY = 0, 1


def place():
    t = lax.axis_index("tm")
    return t // 2, t % 2, lax.axis_index("height")


def head_at():
    y, c, z = place()
    return (c + y + z) % 2


def pair(index, which):
    rising = (index % 2) == (0 if which == 0 else 1)
    return rising, jnp.where(rising, index + 1, index - 1)


def within(index, size):
    return (index >= 0) & (index < size)


def pack_kernel(tok, k_ref, v_ref, q_ref, g_ref, o_ref, mask_ref, kv_ref, rest_ref, other_ref, flags, sems):
    head = head_at()
    copies = [pltpu.make_async_copy(mask_ref, flags, sems.at[10])]
    for i, ref in enumerate((k_ref, v_ref, q_ref, g_ref, o_ref)):
        own = (kv_ref if i < 2 else rest_ref).at[pl.ds((i if i < 2 else i - 2) * tok, tok), :]
        copies.append(pltpu.make_async_copy(ref.at[0, 0, head, 0], own, sems.at[2 * i + 1]))
        copies.append(
            pltpu.make_async_copy(ref.at[0, 0, 1 - head, 0], other_ref.at[pl.ds(i * tok, tok), :], sems.at[2 * i])
        )
    for copy in copies:
        copy.start()
    copies[0].wait()
    row = lax.broadcasted_iota(jnp.int32, (16, rest_ref.shape[1]), 0)
    spread = jnp.zeros(row.shape, jnp.float32)
    for i in range(9):
        on = (flags[0, 0, 0, 9 * (i // 3) + 3 * (i % 3) + 1] != 0).astype(jnp.float32)
        spread = jnp.where(row == i, on, spread)
    rest_ref[pl.ds(3 * tok, 16), :] = spread.astype(jnp.bfloat16)
    other_ref[pl.ds(5 * tok, 16), :] = spread.astype(jnp.bfloat16)
    for copy in copies[1:]:
        copy.wait()


def rows_at(index, tok):
    return pl.ds(index * tok, tok)


def border_is_own(y, c):
    rising, _ = pair(y, 0)
    return (c == 1) == rising


def pick(near, which, own, par):
    return jnp.where(near, own, par) if which == 0 else jnp.where(near, par, own)


def three_terms(row):
    terms = []
    for _ in range(3):
        terms.append(row.astype(jnp.bfloat16).astype(jnp.float32))
        row = row - terms[-1]
    return terms


def line_kernel(tok, rest_ref, par_ref, par_kv_ref, *border_refs):
    y, c, _ = place()
    near = border_is_own(y, c)
    for i in range(2):
        par_kv_ref[rows_at(i, tok), :] = par_ref[rows_at(i, tok), :]
    width = par_ref.shape[1]
    f32 = jnp.float32
    q, g, o = (
        [pick(near, which, rest_ref[rows_at(i, tok), :], par_ref[rows_at(i + 2, tok), :]) for which in range(2)]
        for i in range(3)
    )
    own_flags, par_flags = rest_ref[pl.ds(3 * tok, 16), :].astype(f32), par_ref[pl.ds(5 * tok, 16), :].astype(f32)
    flags = [pick(near, which, own_flags, par_flags)[0:9] for which in range(2)]
    product = jnp.concatenate(g, axis=0).astype(f32) * jnp.concatenate(o, axis=0).astype(f32)
    terms = [
        [term[:, start : start + width] for start in range(0, 2 * tok, width)]
        for term in three_terms(jnp.sum(product.T, axis=0, keepdims=True))
    ]
    for which, ref in enumerate(border_refs):
        ref[rows_at(0, tok), :], ref[rows_at(1, tok), :] = q[which], g[which]
        part = slice(0, 2) if which == 0 else slice(len(terms[0]) - 2, None)
        lines = [flags[which]] + [row for term in terms for row in term[part]] + [jnp.zeros((1, width), f32)]
        ref[pl.ds(2 * tok, 16), :] = jnp.concatenate(lines, axis=0).astype(jnp.bfloat16)
    lines = flags + [row for term in terms for row in term] + [jnp.zeros((5, width), f32)]
    par_kv_ref[pl.ds(2 * tok, 32), :] = jnp.concatenate(lines, axis=0).astype(jnp.bfloat16)


def foreign_delta(ref, tok):
    terms = ref[pl.ds(2 * tok, 16), :].astype(jnp.float32)
    return jnp.concatenate(
        [sum(terms[9 + 2 * i + half : 10 + 2 * i + half] for i in range(3)) for half in range(2)], axis=1
    )


def line_place(z, line, heights):
    if line == 0:
        return True, lambda flags, dt: flags[3 * dt + 1 : 3 * dt + 2]
    rising, at = pair(z, 2 - line)
    return within(at, heights), lambda flags, dt: jnp.where(
        rising, flags[3 * dt + 2 : 3 * dt + 3], flags[3 * dt : 3 * dt + 1]
    )


def lanes_of(tok, border, other):
    width = border.shape[1]
    lane = lax.broadcasted_iota(jnp.int32, (1, width), 1)
    return jnp.concatenate(
        [jnp.where(lane + start < tok, border, other) for start in range(0, 2 * tok, width)], axis=1
    )


def flag_row(tok, slot, at, own_flags, par_flags, own_query):
    y, c, _ = place()
    first, near = c == 0, border_is_own(y, c)
    if slot == 0:
        own, par = at(own_flags, 1), jnp.where(first, at(par_flags, 0), at(par_flags, 2))
    else:
        own, par = jnp.where(first, at(own_flags, 2), at(own_flags, 0)), at(par_flags, 1)
    if own_query:
        centre = jnp.ones_like(own)
        own, par = (centre, par) if slot == 0 else (own, centre)
    return lanes_of(tok, pick(near, 0, own, par), pick(near, 1, own, par))


def first_kernel(tok, heights, scale, kv_ref, par_kv_ref, rest_ref, par_ref, q_all, g_all, table, s_ref, d_ref):
    qg = (q_all, g_all)
    y, c, z = place()
    two = 2 * tok
    width = rest_ref.shape[1]
    f32 = jnp.float32
    near = border_is_own(y, c)
    out = []
    for part in range(3):
        own, par = rest_ref[rows_at(part, tok), :], par_ref[rows_at(part + 2, tok), :]
        tiles = [pick(near, which, own, par) for which in range(2)]
        if part == 2:
            out = jnp.concatenate(tiles, axis=0)
        else:
            for which in range(2):
                qg[part][rows_at(which, tok), :] = tiles[which]
    delta = jnp.sum((qg[1][...].astype(f32) * out.astype(f32)).T, axis=0, keepdims=True)

    own_flags = rest_ref[pl.ds(3 * tok, 16), :].astype(f32)
    par_flags = par_ref[pl.ds(5 * tok, 16), :].astype(f32)
    lines = []
    for line in range(3):
        inside, at = line_place(z, line, heights)
        for slot in range(2):
            row = flag_row(tok, slot, at, own_flags, par_flags, line == 0)
            lines.append(jnp.where(inside, (row - 1.0) * 1e30, -1e30))
    table[...] = jnp.concatenate(lines + [delta, jnp.zeros((1, two), f32)], axis=0)
    for i, source in enumerate((kv_ref, par_kv_ref)):
        rows = rows_at(i, tok)
        s_ref[rows, :] = dot(source[rows_at(0, tok), :], qg[0][...], ROWS_T) * scale + table[i : i + 1, :]
        d_ref[rows, :] = dot(source[rows_at(1, tok), :], qg[1][...], ROWS_T) - table[6:7, :]


def largest(tok, blocks):
    lanes = blocks[0][0].shape[1]
    top = jnp.full((8, lanes), -1e30, jnp.float32)
    for ref, i in blocks:
        top = jnp.maximum(top, jnp.max(ref[rows_at(i, tok), :].reshape(tok // 8, 8, lanes), axis=0))
    return jnp.max(top, axis=0, keepdims=True)


def summed(tok, blocks, top):
    lanes = blocks[0][0].shape[1]
    total = jnp.zeros((8, lanes), jnp.float32)
    for ref, i in blocks:
        weights = jnp.exp(ref[rows_at(i, tok), :] - top)
        total = total + jnp.sum(weights.reshape(tok // 8, 8, lanes), axis=0)
    return jnp.sum(total, axis=0, keepdims=True)


def early_kernel(tok, scale, q_all, g_all, table, s_own, one_ref, two_ref, s_ref, d_ref, part_ref):
    qg = (q_all, g_all)
    for i, source in enumerate((one_ref, two_ref)):
        rows = rows_at(i, tok)
        s_ref[rows, :] = dot(source[rows_at(0, tok), :], qg[0][...], ROWS_T) * scale + table[2 + 2 * i + EARLY : 3 + 2 * i + EARLY, :]
        d_ref[rows, :] = dot(source[rows_at(1, tok), :], qg[1][...], ROWS_T) - table[6:7, :]
    blocks = [(ref, i) for ref in (s_own, s_ref) for i in range(2)]
    top = largest(tok, blocks)
    total = summed(tok, blocks, top)
    part_ref[...] = jnp.concatenate([top, total, jnp.zeros((6, 2 * tok), jnp.float32)], axis=0)


def foreign_rows(ref, part, which, tok):
    block = ref[rows_at(part, tok), :]
    gap = jnp.zeros((2 * block.shape[1] - tok, block.shape[1]), block.dtype)
    return jnp.concatenate([block, gap] if which == 0 else [gap, block], axis=0)


def foreign_lanes(which, tok, width):
    return slice(0, 2 * width) if which == 0 else slice(2 * tok - 2 * width, 2 * tok)


def far_row(tok, which, row):
    lane, width = lax.broadcasted_iota(jnp.int32, row.shape, 1), row.shape[1]
    return jnp.concatenate(
        [
            jnp.where(lane + start < tok if which == 0 else lane + start >= 2 * width - tok, row, 0.0)
            for start in (0, width)
        ],
        axis=1,
    )


def to_lanes(which, tok, row, fill):
    gap = jnp.full((1, 2 * tok - row.shape[1]), fill, jnp.float32)
    return jnp.concatenate([row, gap] if which == 0 else [gap, row], axis=1)


def score_kernel(tok, chips, heights, sides, scale, q_all, g_all, table, part, *refs):
    qg = (q_all, g_all)
    foreign, keys, refs = refs[:sides], refs[sides : 6 + sides], refs[6 + sides :]
    s_late, s_far, *notes = refs
    y, c, z = place()
    near = border_is_own(y, c)
    two = 2 * tok
    f32 = jnp.float32
    far = []
    for which in range(sides):
        rising, y_at = pair(y, which)
        flags = foreign[which][pl.ds(2 * tok, 16), :].astype(f32)
        queries = foreign_rows(foreign[which], 0, which, tok)
        for line in range(3):
            inside, at = line_place(z, line, heights)
            row = far_row(tok, which, jnp.where(rising, at(flags, 0), at(flags, 2)))
            bias = jnp.where(inside & within(y_at, chips), (row - 1.0) * 1e30, -1e30)
            border = pick(near, which, keys[2 * line][rows_at(0, tok), :], keys[2 * line + 1][rows_at(0, tok), :])
            s_far[rows_at(3 * which + line, tok), :] = dot(border, queries, ROWS_T) * scale + bias
        blocks = [(s_far, 3 * which + line) for line in range(3)]
        top = largest(tok, blocks)
        far.append([to_lanes(which, tok, top, -1e30), to_lanes(which, tok, summed(tok, blocks, top), 0.0)])
    for i in range(2):
        at = 2 + 2 * i + LATE
        scores = dot(keys[at][rows_at(0, tok), :], qg[0][...], ROWS_T) * scale
        s_late[rows_at(i, tok), :] = scores + table[at : at + 1, :]
    blocks = [(s_late, i) for i in range(2)]
    top = jnp.maximum(part[0:1, :], largest(tok, blocks))
    total = part[1:2, :] * jnp.exp(part[0:1, :] - top) + summed(tok, blocks, top)
    for which in range(sides):
        notes[which][...] = jnp.concatenate([top, total] + far[which] + [jnp.zeros((4, two), f32)], axis=0)


def middle_kernel(tok, sides, scale, q_all, g_all, table, s_own, d_own, s_early, d_early, s_late, s_far, *refs):
    qg = (q_all, g_all)
    tiles, foreign, sent = refs[:6], refs[6 : 6 + sides], refs[6 + sides : 6 + 2 * sides]
    e_ref, ds_ref, e_far, ds_far, dq_ref, *shares = refs[6 + 2 * sides :]
    y, c, _ = place()
    near = border_is_own(y, c)
    bf16 = jnp.bfloat16

    total, far_total = 0.0, [0.0] * sides
    for line in range(3):
        dq = 0.0
        for slot in range(2):
            i, at = 2 * line + slot, rows_at(line - 1 if line else slot, tok)
            scores = s_own if line == 0 else s_early if slot == EARLY else s_late
            weights = jnp.exp(scores[at, :] - sent[0][0:1, :])
            if line and slot == LATE:
                grads = dot(tiles[i][rows_at(1, tok), :], qg[1][...], ROWS_T) - table[6:7, :]
            else:
                grads = (d_early if line else d_own)[at, :]
            low = (weights * grads * scale).astype(bf16)
            if line == 0:
                e_ref[rows_at(i, tok), :] = weights.astype(bf16)
                ds_ref[rows_at(i, tok), :] = low
            dq = dq + dot(tiles[i][rows_at(0, tok), :], low, COLS_T)
        total = total + dq
        for which in range(sides):
            far_g = foreign_rows(foreign[which], 1, which, tok)
            delta = foreign_delta(foreign[which], tok)
            lanes = foreign_lanes(which, tok, qg[0].shape[1])
            rows = rows_at(3 * which + line, tok)
            own, par = tiles[2 * line], tiles[2 * line + 1]
            key, value = (pick(near, which, own[rows_at(i, tok), :], par[rows_at(i, tok), :]) for i in range(2))
            weights = jnp.exp(s_far[rows, :] - sent[which][2:3, lanes])
            low = (weights * (dot(value, far_g, ROWS_T) - delta) * scale).astype(bf16)
            if line == 0:
                e_far[rows_at(which, tok), :] = weights.astype(bf16)
                ds_far[rows_at(which, tok), :] = low
            far_total[which] = far_total[which] + dot(key, low, COLS_T)

    dq_ref[...] = total
    for which in range(sides):
        shares[which][...] = border_rows(which, tok, far_total[which].T).astype(bf16)


def border_rows(which, tok, block):
    return block[:tok] if which == 0 else block[block.shape[0] - tok :]


def message_kernel(tok, q_all, g_all, *refs):
    *foreign, out_ref = refs
    out_ref[pl.ds(0, 2 * tok), :] = q_all[...]
    out_ref[pl.ds(2 * tok, 2 * tok), :] = g_all[...]
    for which, ref in enumerate(foreign):
        far_part(out_ref, which, tok)[...] = ref[pl.ds(0, 2 * tok + 16), :]


def far_part(ref, which, tok):
    return ref.at[pl.ds(4 * tok + which * (2 * tok + 16), 2 * tok + 16), :]


def total_kernel(tok, chips, sides, *refs):
    sent, came, note_ref = refs[:sides], refs[sides : 2 * sides], refs[2 * sides]
    y, _, _ = place()

    def log_total(top, total, other_top, other_total):
        both = jnp.maximum(top, other_top)
        return both + jnp.log(total * jnp.exp(top - both) + other_total * jnp.exp(other_top - both))

    lse, far_rows = None, []
    for which in range(sides):
        _, y_at = pair(y, which)
        inside = within(y_at, chips)
        note = came[which]
        far_lse = log_total(note[0:1, :], note[1:2, :], sent[which][2:3, :], sent[which][3:4, :])
        far_rows.append(jnp.where(inside, far_lse, 0.0))
        other = jnp.where(inside, note[2:3, :], -1e30), jnp.where(inside, note[3:4, :], 0.0)
        if which == 0:
            lse = log_total(sent[0][0:1, :], sent[0][1:2, :], *other)
        else:
            lse = log_total(lse, jnp.ones_like(lse), *other)
    rows = [lse] + far_rows
    note_ref[...] = jnp.concatenate(rows + [jnp.zeros((8 - len(rows), 2 * tok), jnp.float32)], axis=0)


def line_query_kernel(tok, chips, heights, sides, scale, line, kv_ref, par_kv_ref, message, extras, *outs):
    e_ref, ds_ref, e_far, ds_far, top_ref = outs[-5:]
    y, c, z = place()
    near = border_is_own(y, c)
    two = 2 * tok
    width = kv_ref.shape[1]
    f32, bf16 = jnp.float32, jnp.bfloat16
    tiles = (kv_ref, par_kv_ref)

    def work():
        rising, _ = pair(z, 2 - line)

        def at(flags, dt):
            return jnp.where(rising, flags[3 * dt : 3 * dt + 1], flags[3 * dt + 2 : 3 * dt + 3])

        rows = extras[pl.ds(2 * tok, 32), :].astype(f32)
        own_flags, par_flags = (pick(near, which, rows[0:9], rows[9:18]) for which in range(2))
        delta = [sum(rows[18 + 3 * i + part : 19 + 3 * i + part] for i in range(3)) for part in range(two // width)]
        delta = jnp.concatenate(delta, axis=1)
        line_q, line_g = (message[pl.ds(part * two, two), :] for part in range(2))
        scores = []
        for slot in range(2):
            row = flag_row(tok, slot, at, own_flags, par_flags, False)
            scores.append(dot(tiles[slot][rows_at(0, tok), :], line_q, ROWS_T) * scale + (row - 1.0) * 1e30)
        tops = [jnp.maximum(*(jnp.max(block, axis=0, keepdims=True) for block in scores))]
        for slot in range(2):
            weights = jnp.exp(scores[slot] - tops[0])
            grads = dot(tiles[slot][rows_at(1, tok), :], line_g, ROWS_T) - delta
            kept = rows_at(slot, tok)
            e_ref[kept, :] = weights.astype(bf16)
            ds_ref[kept, :] = (weights * grads * scale).astype(bf16)
        for which in range(sides):
            ref = far_part(message, which, tok)
            y_rising, y_at = pair(y, which)
            flags = ref[pl.ds(2 * tok, 16), :].astype(f32)
            row = far_row(tok, which, jnp.where(y_rising, at(flags, 0), at(flags, 2)))
            bias = jnp.where(within(y_at, chips), (row - 1.0) * 1e30, -1e30)
            key, value = (pick(near, which, *(tile[rows_at(i, tok), :] for tile in tiles)) for i in range(2))
            far_q, far_g = (foreign_rows(ref, part, which, tok) for part in range(2))
            block = dot(key, far_q, ROWS_T) * scale + bias
            top = jnp.max(block, axis=0, keepdims=True)
            tops.append(to_lanes(which, tok, top, -1e30))
            weights = jnp.exp(block - top)
            grads = dot(value, far_g, ROWS_T) - foreign_delta(ref, tok)
            kept = rows_at(which, tok)
            e_far[kept, :] = weights.astype(bf16)
            ds_far[kept, :] = (weights * grads * scale).astype(bf16)
        top_ref[...] = jnp.concatenate(tops + [jnp.zeros((7 - sides, two), f32)], axis=0)

    pl.when(line_place(z, line, heights)[0])(work)


def times(block, factor):
    column = jnp.broadcast_to(factor, (block.shape[1], factor.shape[1])).T
    return (block.astype(jnp.float32) * column).astype(jnp.bfloat16)


def key_sums(tok, near, line, e_ref, ds_ref, scaled, far, slots=(0, 1)):
    rows = [rows_at(2 * line + slot, tok) for slot in slots]
    sums = [[dot(ref[at, :], scaled[i]) for i, ref in enumerate((ds_ref, e_ref))] for at in rows]
    for which, (e_far, ds_far, at, far_scaled) in enumerate(far):
        for i, ref in enumerate((ds_far, e_far)):
            block = dot(ref[at, :], far_scaled[i])
            for at_slot, slot in enumerate(slots):
                mine = near == ((slot == 0) == (which == 0))
                sums[at_slot][i] = sums[at_slot][i] + jnp.where(mine, block, 0.0)
    return sums


def stay_kernel(tok, chips, sides, q_all, g_all, e_ref, ds_ref, e_far, ds_far, raw_dq, note, *refs):
    qg = (q_all, g_all)
    sent, foreign, (own_ref, dq_ref) = refs[:sides], refs[sides : 2 * sides], refs[2 * sides :]
    y, c, _ = place()
    near = border_is_own(y, c)
    width = qg[0].shape[1]
    factor = jnp.exp(sent[0][0:1, :] - note[0:1, :])
    dq_ref[...] = (raw_dq[...] * factor).T
    far = []
    for which in range(sides):
        _, y_at = pair(y, which)
        lanes = foreign_lanes(which, tok, width)
        far_factor = jnp.exp(sent[which][2:3, lanes] - note[1 + which : 2 + which, lanes])
        far_factor = jnp.where(within(y_at, chips), far_factor, 0.0)
        scaled = [times(foreign_rows(foreign[which], part, which, tok), far_factor) for part in range(2)]
        far.append((e_far, ds_far, rows_at(which, tok), scaled))
    sums = key_sums(tok, near, 0, e_ref, ds_ref, [times(qg[part][...], factor) for part in range(2)], far)
    for slot in range(2):
        for i in range(2):
            own_ref[i, rows_at(slot, tok), :] = sums[slot][i]


def line_sums(tok, heights, sides, line, slot, sums, message, note, e_ref, ds_ref, e_far, ds_far, top_ref):
    y, c, z = place()
    near = border_is_own(y, c)

    def work():
        factor = jnp.exp(top_ref[0:1, :] - note[0:1, :])
        scaled = [times(message[pl.ds(part * 2 * tok, 2 * tok), :], factor) for part in range(2)]
        far = []
        for which in range(sides):
            lanes, at = foreign_lanes(which, tok, message.shape[1]), 1 + which
            far_factor = jnp.exp(top_ref[at : at + 1, lanes] - note[at : at + 1, lanes])
            rows = [foreign_rows(far_part(message, which, tok), part, which, tok) for part in range(2)]
            far.append((e_far, ds_far, rows_at(which, tok), [times(block, far_factor) for block in rows]))
        more = key_sums(tok, near, 0, e_ref, ds_ref, scaled, far, (slot,))
        for i in range(2):
            sums[i] += more[0][i]

    pl.when(line_place(z, line, heights)[0])(work)


def join_kernel(tok, heights, sides, line, own_ref, message, note, *refs):
    *terms, sums = refs
    sums[...] = own_ref[:, rows_at(1, tok), :]
    line_sums(tok, heights, sides, line, 1, sums, message, note, *terms)


def own_kernel(tok, heights, sides, own_ref, *refs):
    *refs, mine_ref, sums = refs
    sums[...] = own_ref[:, rows_at(0, tok), :]
    for i, line in enumerate((2, 1)):
        line_sums(tok, heights, sides, line, 0, sums, *refs[7 * i : 7 * i + 7])
    mine_ref[...] = sums[...].astype(jnp.bfloat16)


def leave_kernel(tok, chips, heights, sides, line, own_ref, dq_ref, note, message, note_in, *refs):
    terms, refs = refs[:5], refs[5:]
    came, backs, (mine_q_ref, swap_ref, sums) = refs[:sides], refs[sides : 2 * sides], refs[2 * sides :]
    y, c, _ = place()
    near = border_is_own(y, c)
    f32, bf16 = jnp.float32, jnp.bfloat16
    width = dq_ref.shape[1]
    sums[...] = own_ref[...]
    line_sums(tok, heights, sides, line, 1, sums, message, note_in, *terms)
    for i in range(2):
        swap_ref[i] = sums[i].astype(bf16)
    tiles = []
    for tile in range(2):
        value = dq_ref[rows_at(tile, tok), :]
        if tile < sides:
            _, y_at = pair(y, tile)
            lanes = foreign_lanes(tile, tok, width)
            factor = jnp.exp(came[tile][2:3, lanes] - note[0:1, lanes])
            column = border_rows(tile, tok, jnp.broadcast_to(factor, (width, 2 * width)).T)
            value = value + jnp.where(within(y_at, chips), backs[tile][...].astype(f32) * column, 0.0)
        tiles.append(value.astype(bf16))
    mine_q_ref[...] = jnp.where(near, tiles[0], tiles[1])
    swap_ref[2] = jnp.where(near, tiles[1], tiles[0])


def final_kernel(mine_ref, swap_ref, mine_q_ref, gq_ref, gk_ref, gv_ref):
    head = head_at()
    gq_ref[0, 0, head, 0] = mine_q_ref[...]
    gq_ref[0, 0, 1 - head, 0] = swap_ref[2]
    for i, ref in enumerate((gk_ref, gv_ref)):
        ref[0, 0, head, 0] = mine_ref[i]
        ref[0, 0, 1 - head, 0] = swap_ref[i]


def body(queries, keys, values, grad_out, attn_out, window_mask):
    tok, width = queries.shape[-2:]
    scale = width ** -0.5
    times, heights = lax.axis_size("tm"), lax.axis_size("height")
    chips = times // 2
    sides = 1 if chips == 2 else 2
    bf16, f32 = jnp.bfloat16, jnp.float32

    def call(kernel, shapes, specs, scratch=(), cost=0):
        return pl.pallas_call(
            kernel,
            out_shape=[jax.ShapeDtypeStruct(*shape) for shape in shapes],
            in_specs=list(specs),
            out_specs=[VMEM] * len(shapes),
            scratch_shapes=list(scratch),
            compiler_params=LIMIT,
            cost_estimate=pl.CostEstimate(flops=cost * 10**9, bytes_accessed=0, transcendentals=0) if cost else None,
        )

    def partner(index, which, size):
        if which is None:
            return index
        at = index + 1 if index % 2 == which else index - 1
        return at if 0 <= at < size else None

    def exchange(block, y_which, z_which):
        pairs = []
        for t in range(times):
            for z in range(heights):
                y_at, z_at = partner(t // 2, y_which, chips), partner(z, z_which, heights)
                at = t * heights + z
                alone = y_at is None or z_at is None
                pairs.append((at, (t ^ 1) * heights + z if alone else (2 * y_at + 1 - t % 2) * heights + z_at))
        return lax.ppermute(block, ("tm", "height"), pairs)

    def swap_cores(block):
        return lax.ppermute(block, "tm", [(t, t ^ 1) for t in range(times)])

    line_shape, tile_shape = ((2, 2 * tok, width), bf16), ((2, tok, width), bf16)
    extra = 64
    arguments = (keys, values, queries, grad_out, attn_out, window_mask)
    kv, rest, other = call(
        functools.partial(pack_kernel, tok),
        [((2 * tok + extra, width), bf16), ((3 * tok + 16, width), bf16), ((5 * tok + 16, width), bf16)],
        [HBM] * 6,
        [pltpu.SMEM(window_mask.shape, jnp.int32), pltpu.SemaphoreType.DMA((11,))],
    )(*(pltpu.with_memory_space_constraint(x, pltpu.HBM) for x in arguments))
    early = [exchange(kv, None, which) for which in (1, 0)]
    par = swap_cores(other)
    border_shape, two = ((2 * tok + 48, width), bf16), 2 * tok
    par_kv, *borders = call(
        functools.partial(line_kernel, tok), [((2 * tok + 32, width), bf16)] + [border_shape] * sides, [VMEM] * 2
    )(rest, par)
    foreign = [exchange(borders[which], which, None) for which in range(sides)]
    late = [exchange(par_kv, None, which) for which in (1, 0)]
    tiles = (kv, par_kv, late[0], early[0], late[1], early[1])
    note_shape, raw_shape = ((8, two), f32), ((width, two), f32)

    def square(count, kind=f32):
        return ((count * tok, two), kind)

    def far_square(kind=f32):
        return ((3 * sides * tok, 2 * width), kind)

    q_all, g_all, table, s_own, d_own = call(
        functools.partial(first_kernel, tok, heights, scale),
        [((two, width), bf16)] * 2 + [note_shape, square(2), square(2)],
        [VMEM] * 4,
    )(kv, par_kv, rest, par)
    qg = (q_all, g_all)
    (message,) = call(
        functools.partial(message_kernel, tok),
        [((4 * tok + sides * (2 * tok + 16), width), bf16)],
        [VMEM] * (2 + sides),
    )(*qg, *foreign)
    queries_in = [exchange(message, None, which) for which in (1, 0)]
    s_early, d_early, part = call(
        functools.partial(early_kernel, tok, scale), [square(2), square(2), note_shape], [VMEM] * 6
    )(*qg, table, s_own, *early)
    s_late, s_far, *sent = call(
        functools.partial(score_kernel, tok, chips, heights, sides, scale),
        [square(2), far_square()] + [note_shape] * sides,
        [VMEM] * (10 + sides),
    )(*qg, table, part, *foreign, *tiles)
    came = [exchange(sent[which], which, None) for which in range(sides)]
    far_tile = ((sides * tok, 2 * width), bf16)
    e, ds, e_far, ds_far, raw_dq, *shares = call(
        functools.partial(middle_kernel, tok, sides, scale),
        [square(2, bf16)] * 2 + [far_tile] * 2 + [raw_shape] + [((tok, width), bf16)] * sides,
        [VMEM] * (15 + 2 * sides),
        cost=20,
    )(*qg, table, s_own, d_own, s_early, d_early, s_late, s_far, *tiles, *foreign, *sent)
    (note,) = call(functools.partial(total_kernel, tok, chips, sides), [note_shape], [VMEM] * (2 * sides))(*sent, *came)
    notes = [exchange(note, None, which) for which in (1, 0)]
    shares = [exchange(share, which, None) for which, share in enumerate(shares)]
    sums_shape = ((2, two, width), f32)

    def line_terms(line, *earlier):
        return call(
            functools.partial(line_query_kernel, tok, chips, heights, sides, scale, line),
            [square(2, bf16)] * 2 + [far_tile] * 2 + [note_shape],
            [VMEM] * (4 + len(earlier)),
            cost=20,
        )(kv, par_kv, queries_in[line - 1], late[line - 1], *earlier)

    own, dq = call(
        functools.partial(stay_kernel, tok, chips, sides),
        [sums_shape, ((two, width), f32)],
        [VMEM] * (8 + 2 * sides),
    )(*qg, e, ds, e_far, ds_far, raw_dq, note, *sent, *foreign)
    part_shape = ((2, tok, width), f32)
    even_terms = line_terms(2)
    (joined,) = call(
        functools.partial(join_kernel, tok, heights, sides, 2), [part_shape], [VMEM] * 8
    )(own, queries_in[1], notes[1], *even_terms)
    odd_terms = line_terms(1, joined)
    mine_q, leaving = call(
        functools.partial(leave_kernel, tok, chips, heights, sides, 1),
        [((tok, width), bf16), ((3, tok, width), bf16)],
        [VMEM] * (10 + 2 * sides),
        [pltpu.VMEM(*part_shape)],
    )(joined, dq, note, queries_in[0], notes[0], *odd_terms, *came, *shares)
    (mine,) = call(
        functools.partial(own_kernel, tok, heights, sides),
        [tile_shape],
        [VMEM] * 15,
        [pltpu.VMEM(*part_shape)],
        cost=20,
    )(own, queries_in[1], notes[1], *even_terms, queries_in[0], notes[0], *odd_terms)
    return call(final_kernel, [(queries.shape, bf16)] * 3, [VMEM] * 3)(mine, swap_cores(leaving), mine_q)


def solution(mesh):
    placed = P("tm", "height", "dp", None, None, None)
    return jax.shard_map(
        body,
        mesh=mesh,
        in_specs=(placed,) * 5 + (P("tm", "height", None, None),),
        out_specs=(placed,) * 3,
        check_vma=False,
    )
```

```python
import functools

import jax
import jax.numpy as jnp
from jax import lax
from jax.experimental import pallas as pl
from jax.experimental.pallas import tpu as pltpu
from jax.sharding import PartitionSpec as P

VMEM = pl.BlockSpec(memory_space=pltpu.VMEM)
HBM = pl.BlockSpec(memory_space=pltpu.HBM)
LIMIT = pltpu.CompilerParams(vmem_limit_bytes=32 * 1024 * 1024)
ROWS_T = (((1,), (1,)), ((), ()))
COLS_T = (((0,), (0,)), ((), ()))


def dot(a, b, dims=(((1,), (0,)), ((), ()))):
    return lax.dot_general(a, b, dims, preferred_element_type=jnp.float32)


LATE, EARLY = 0, 1


def place():
    t = lax.axis_index("tm")
    return t // 2, t % 2, lax.axis_index("height")


def head_at():
    y, c, z = place()
    return (c + y + z) % 2


def pair(index, which):
    rising = (index % 2) == (0 if which == 0 else 1)
    return rising, jnp.where(rising, index + 1, index - 1)


def within(index, size):
    return (index >= 0) & (index < size)


def pack_kernel(tok, k_ref, v_ref, q_ref, g_ref, o_ref, mask_ref, kv_ref, rest_ref, other_ref, flags, sems):
    head = head_at()
    copies = [pltpu.make_async_copy(mask_ref, flags, sems.at[10])]
    for i, ref in enumerate((k_ref, v_ref, q_ref, g_ref, o_ref)):
        own = (kv_ref if i < 2 else rest_ref).at[pl.ds((i if i < 2 else i - 2) * tok, tok), :]
        copies.append(pltpu.make_async_copy(ref.at[0, 0, head, 0], own, sems.at[2 * i + 1]))
        copies.append(
            pltpu.make_async_copy(ref.at[0, 0, 1 - head, 0], other_ref.at[pl.ds(i * tok, tok), :], sems.at[2 * i])
        )
    for copy in copies:
        copy.start()
    copies[0].wait()
    row = lax.broadcasted_iota(jnp.int32, (16, rest_ref.shape[1]), 0)
    spread = jnp.zeros(row.shape, jnp.float32)
    for i in range(9):
        on = (flags[0, 0, 0, 9 * (i // 3) + 3 * (i % 3) + 1] != 0).astype(jnp.float32)
        spread = jnp.where(row == i, on, spread)
    rest_ref[pl.ds(3 * tok, 16), :] = spread.astype(jnp.bfloat16)
    other_ref[pl.ds(5 * tok, 16), :] = spread.astype(jnp.bfloat16)
    for copy in copies[1:]:
        copy.wait()


def rows_at(index, tok):
    return pl.ds(index * tok, tok)


def border_is_own(y, c):
    rising, _ = pair(y, 0)
    return (c == 1) == rising


def pick(near, which, own, par):
    return jnp.where(near, own, par) if which == 0 else jnp.where(near, par, own)


def three_terms(row):
    terms = []
    for _ in range(3):
        terms.append(row.astype(jnp.bfloat16).astype(jnp.float32))
        row = row - terms[-1]
    return terms


def line_kernel(tok, rest_ref, par_ref, par_kv_ref, *border_refs):
    y, c, _ = place()
    near = border_is_own(y, c)
    for i in range(2):
        par_kv_ref[rows_at(i, tok), :] = par_ref[rows_at(i, tok), :]
    width = par_ref.shape[1]
    f32 = jnp.float32
    q, g, o = (
        [pick(near, which, rest_ref[rows_at(i, tok), :], par_ref[rows_at(i + 2, tok), :]) for which in range(2)]
        for i in range(3)
    )
    own_flags, par_flags = rest_ref[pl.ds(3 * tok, 16), :].astype(f32), par_ref[pl.ds(5 * tok, 16), :].astype(f32)
    flags = [pick(near, which, own_flags, par_flags)[0:9] for which in range(2)]
    product = jnp.concatenate(g, axis=0).astype(f32) * jnp.concatenate(o, axis=0).astype(f32)
    terms = [
        [term[:, start : start + width] for start in range(0, 2 * tok, width)]
        for term in three_terms(jnp.sum(product.T, axis=0, keepdims=True))
    ]
    for which, ref in enumerate(border_refs):
        ref[rows_at(0, tok), :], ref[rows_at(1, tok), :] = q[which], g[which]
        part = slice(0, 2) if which == 0 else slice(len(terms[0]) - 2, None)
        lines = [flags[which]] + [row for term in terms for row in term[part]] + [jnp.zeros((1, width), f32)]
        ref[pl.ds(2 * tok, 16), :] = jnp.concatenate(lines, axis=0).astype(jnp.bfloat16)
    lines = flags + [row for term in terms for row in term] + [jnp.zeros((5, width), f32)]
    par_kv_ref[pl.ds(2 * tok, 32), :] = jnp.concatenate(lines, axis=0).astype(jnp.bfloat16)


def foreign_delta(ref, tok):
    terms = ref[pl.ds(2 * tok, 16), :].astype(jnp.float32)
    return jnp.concatenate(
        [sum(terms[9 + 2 * i + half : 10 + 2 * i + half] for i in range(3)) for half in range(2)], axis=1
    )


def line_place(z, line, heights):
    if line == 0:
        return True, lambda flags, dt: flags[3 * dt + 1 : 3 * dt + 2]
    rising, at = pair(z, 2 - line)
    return within(at, heights), lambda flags, dt: jnp.where(
        rising, flags[3 * dt + 2 : 3 * dt + 3], flags[3 * dt : 3 * dt + 1]
    )


def lanes_of(tok, border, other):
    width = border.shape[1]
    lane = lax.broadcasted_iota(jnp.int32, (1, width), 1)
    return jnp.concatenate(
        [jnp.where(lane + start < tok, border, other) for start in range(0, 2 * tok, width)], axis=1
    )


def flag_row(tok, slot, at, own_flags, par_flags, own_query):
    y, c, _ = place()
    first, near = c == 0, border_is_own(y, c)
    if slot == 0:
        own, par = at(own_flags, 1), jnp.where(first, at(par_flags, 0), at(par_flags, 2))
    else:
        own, par = jnp.where(first, at(own_flags, 2), at(own_flags, 0)), at(par_flags, 1)
    if own_query:
        centre = jnp.ones_like(own)
        own, par = (centre, par) if slot == 0 else (own, centre)
    return lanes_of(tok, pick(near, 0, own, par), pick(near, 1, own, par))


def first_kernel(tok, heights, scale, kv_ref, par_kv_ref, rest_ref, par_ref, q_all, g_all, table, s_ref, d_ref):
    qg = (q_all, g_all)
    y, c, z = place()
    two = 2 * tok
    width = rest_ref.shape[1]
    f32 = jnp.float32
    near = border_is_own(y, c)
    out = []
    for part in range(3):
        own, par = rest_ref[rows_at(part, tok), :], par_ref[rows_at(part + 2, tok), :]
        tiles = [pick(near, which, own, par) for which in range(2)]
        if part == 2:
            out = jnp.concatenate(tiles, axis=0)
        else:
            for which in range(2):
                qg[part][rows_at(which, tok), :] = tiles[which]
    delta = jnp.sum((qg[1][...].astype(f32) * out.astype(f32)).T, axis=0, keepdims=True)

    own_flags = rest_ref[pl.ds(3 * tok, 16), :].astype(f32)
    par_flags = par_ref[pl.ds(5 * tok, 16), :].astype(f32)
    lines = []
    for line in range(3):
        inside, at = line_place(z, line, heights)
        for slot in range(2):
            row = flag_row(tok, slot, at, own_flags, par_flags, line == 0)
            lines.append(jnp.where(inside, (row - 1.0) * 1e30, -1e30))
    table[...] = jnp.concatenate(lines + [delta, jnp.zeros((1, two), f32)], axis=0)
    for i, source in enumerate((kv_ref, par_kv_ref)):
        rows = rows_at(i, tok)
        s_ref[rows, :] = dot(source[rows_at(0, tok), :], qg[0][...], ROWS_T) * scale + table[i : i + 1, :]
        d_ref[rows, :] = dot(source[rows_at(1, tok), :], qg[1][...], ROWS_T) - table[6:7, :]


def largest(tok, blocks):
    lanes = blocks[0][0].shape[1]
    top = jnp.full((8, lanes), -1e30, jnp.float32)
    for ref, i in blocks:
        top = jnp.maximum(top, jnp.max(ref[rows_at(i, tok), :].reshape(tok // 8, 8, lanes), axis=0))
    return jnp.max(top, axis=0, keepdims=True)


def summed(tok, blocks, top):
    lanes = blocks[0][0].shape[1]
    total = jnp.zeros((8, lanes), jnp.float32)
    for ref, i in blocks:
        weights = jnp.exp(ref[rows_at(i, tok), :] - top)
        total = total + jnp.sum(weights.reshape(tok // 8, 8, lanes), axis=0)
    return jnp.sum(total, axis=0, keepdims=True)


def early_kernel(tok, scale, q_all, g_all, table, s_own, one_ref, two_ref, _, s_ref, d_ref, part_ref):
    qg = (q_all, g_all)
    for i, source in enumerate((one_ref, two_ref)):
        rows = rows_at(i, tok)
        s_ref[rows, :] = dot(source[rows_at(0, tok), :], qg[0][...], ROWS_T) * scale + table[2 + 2 * i + EARLY : 3 + 2 * i + EARLY, :]
        d_ref[rows, :] = dot(source[rows_at(1, tok), :], qg[1][...], ROWS_T) - table[6:7, :]
    blocks = [(ref, i) for ref in (s_own, s_ref) for i in range(2)]
    top = largest(tok, blocks)
    total = summed(tok, blocks, top)
    part_ref[...] = jnp.concatenate([top, total, jnp.zeros((6, 2 * tok), jnp.float32)], axis=0)


def foreign_rows(ref, part, which, tok):
    block = ref[rows_at(part, tok), :]
    gap = jnp.zeros((2 * block.shape[1] - tok, block.shape[1]), block.dtype)
    return jnp.concatenate([block, gap] if which == 0 else [gap, block], axis=0)


def foreign_lanes(which, tok, width):
    return slice(0, 2 * width) if which == 0 else slice(2 * tok - 2 * width, 2 * tok)


def far_row(tok, which, row):
    lane, width = lax.broadcasted_iota(jnp.int32, row.shape, 1), row.shape[1]
    return jnp.concatenate(
        [
            jnp.where(lane + start < tok if which == 0 else lane + start >= 2 * width - tok, row, 0.0)
            for start in (0, width)
        ],
        axis=1,
    )


def to_lanes(which, tok, row, fill):
    gap = jnp.full((1, 2 * tok - row.shape[1]), fill, jnp.float32)
    return jnp.concatenate([row, gap] if which == 0 else [gap, row], axis=1)


def score_kernel(tok, chips, heights, sides, scale, q_all, g_all, table, part, *refs):
    qg = (q_all, g_all)
    foreign, keys, refs = refs[:sides], refs[sides : 6 + sides], refs[6 + sides :]
    s_late, s_far, *notes = refs
    y, c, z = place()
    near = border_is_own(y, c)
    two = 2 * tok
    f32 = jnp.float32
    far = []
    for which in range(sides):
        rising, y_at = pair(y, which)
        flags = foreign[which][pl.ds(2 * tok, 16), :].astype(f32)
        queries = foreign_rows(foreign[which], 0, which, tok)
        for line in range(3):
            inside, at = line_place(z, line, heights)
            row = far_row(tok, which, jnp.where(rising, at(flags, 0), at(flags, 2)))
            bias = jnp.where(inside & within(y_at, chips), (row - 1.0) * 1e30, -1e30)
            border = pick(near, which, keys[2 * line][rows_at(0, tok), :], keys[2 * line + 1][rows_at(0, tok), :])
            s_far[rows_at(3 * which + line, tok), :] = dot(border, queries, ROWS_T) * scale + bias
        blocks = [(s_far, 3 * which + line) for line in range(3)]
        top = largest(tok, blocks)
        far.append([to_lanes(which, tok, top, -1e30), to_lanes(which, tok, summed(tok, blocks, top), 0.0)])
    for i in range(2):
        at = 2 + 2 * i + LATE
        scores = dot(keys[at][rows_at(0, tok), :], qg[0][...], ROWS_T) * scale
        s_late[rows_at(i, tok), :] = scores + table[at : at + 1, :]
    blocks = [(s_late, i) for i in range(2)]
    top = jnp.maximum(part[0:1, :], largest(tok, blocks))
    total = part[1:2, :] * jnp.exp(part[0:1, :] - top) + summed(tok, blocks, top)
    for which in range(sides):
        notes[which][...] = jnp.concatenate([top, total] + far[which] + [jnp.zeros((4, two), f32)], axis=0)


def middle_kernel(tok, sides, scale, q_all, g_all, table, s_own, d_own, s_early, d_early, s_late, s_far, *refs):
    qg = (q_all, g_all)
    tiles, foreign, sent = refs[:6], refs[6 : 6 + sides], refs[6 + sides : 6 + 2 * sides]
    e_ref, ds_ref, e_far, ds_far, dq_ref, *shares = refs[6 + 2 * sides :]
    y, c, _ = place()
    near = border_is_own(y, c)
    bf16 = jnp.bfloat16

    total, far_total = 0.0, [0.0] * sides
    for line in range(3):
        dq = 0.0
        for slot in range(2):
            i, at = 2 * line + slot, rows_at(line - 1 if line else slot, tok)
            scores = s_own if line == 0 else s_early if slot == EARLY else s_late
            weights = jnp.exp(scores[at, :] - sent[0][0:1, :])
            if line and slot == LATE:
                grads = dot(tiles[i][rows_at(1, tok), :], qg[1][...], ROWS_T) - table[6:7, :]
            else:
                grads = (d_early if line else d_own)[at, :]
            low = (weights * grads * scale).astype(bf16)
            if line == 0:
                e_ref[rows_at(i, tok), :] = weights.astype(bf16)
                ds_ref[rows_at(i, tok), :] = low
            dq = dq + dot(tiles[i][rows_at(0, tok), :], low, COLS_T)
        total = total + dq
        for which in range(sides):
            far_g = foreign_rows(foreign[which], 1, which, tok)
            delta = foreign_delta(foreign[which], tok)
            lanes = foreign_lanes(which, tok, qg[0].shape[1])
            rows = rows_at(3 * which + line, tok)
            own, par = tiles[2 * line], tiles[2 * line + 1]
            key, value = (pick(near, which, own[rows_at(i, tok), :], par[rows_at(i, tok), :]) for i in range(2))
            weights = jnp.exp(s_far[rows, :] - sent[which][2:3, lanes])
            low = (weights * (dot(value, far_g, ROWS_T) - delta) * scale).astype(bf16)
            if line == 0:
                e_far[rows_at(which, tok), :] = weights.astype(bf16)
                ds_far[rows_at(which, tok), :] = low
            far_total[which] = far_total[which] + dot(key, low, COLS_T)

    dq_ref[...] = total
    for which in range(sides):
        shares[which][...] = border_rows(which, tok, far_total[which].T).astype(bf16)


def border_rows(which, tok, block):
    return block[:tok] if which == 0 else block[block.shape[0] - tok :]


def message_kernel(tok, q_all, g_all, *refs):
    *foreign, out_ref = refs
    out_ref[pl.ds(0, 2 * tok), :] = q_all[...]
    out_ref[pl.ds(2 * tok, 2 * tok), :] = g_all[...]
    for which, ref in enumerate(foreign):
        far_part(out_ref, which, tok)[...] = ref[pl.ds(0, 2 * tok + 16), :]


def far_part(ref, which, tok):
    return ref.at[pl.ds(4 * tok + which * (2 * tok + 16), 2 * tok + 16), :]


def total_kernel(tok, chips, sides, *refs):
    sent, came, note_ref = refs[:sides], refs[sides : 2 * sides], refs[2 * sides]
    y, _, _ = place()

    def log_total(top, total, other_top, other_total):
        both = jnp.maximum(top, other_top)
        return both + jnp.log(total * jnp.exp(top - both) + other_total * jnp.exp(other_top - both))

    lse, far_rows = None, []
    for which in range(sides):
        _, y_at = pair(y, which)
        inside = within(y_at, chips)
        note = came[which]
        far_lse = log_total(note[0:1, :], note[1:2, :], sent[which][2:3, :], sent[which][3:4, :])
        far_rows.append(jnp.where(inside, far_lse, 0.0))
        other = jnp.where(inside, note[2:3, :], -1e30), jnp.where(inside, note[3:4, :], 0.0)
        if which == 0:
            lse = log_total(sent[0][0:1, :], sent[0][1:2, :], *other)
        else:
            lse = log_total(lse, jnp.ones_like(lse), *other)
    rows = [lse] + far_rows
    note_ref[...] = jnp.concatenate(rows + [jnp.zeros((8 - len(rows), 2 * tok), jnp.float32)], axis=0)


def line_query_kernel(tok, chips, heights, sides, scale, line, kv_ref, par_kv_ref, message, extras, *outs):
    e_ref, ds_ref, e_far, ds_far, top_ref = outs[-5:]
    y, c, z = place()
    near = border_is_own(y, c)
    two = 2 * tok
    width = kv_ref.shape[1]
    f32, bf16 = jnp.float32, jnp.bfloat16
    tiles = (kv_ref, par_kv_ref)

    def work():
        rising, _ = pair(z, 2 - line)

        def at(flags, dt):
            return jnp.where(rising, flags[3 * dt : 3 * dt + 1], flags[3 * dt + 2 : 3 * dt + 3])

        rows = extras[pl.ds(2 * tok, 32), :].astype(f32)
        own_flags, par_flags = (pick(near, which, rows[0:9], rows[9:18]) for which in range(2))
        delta = [sum(rows[18 + 3 * i + part : 19 + 3 * i + part] for i in range(3)) for part in range(two // width)]
        delta = jnp.concatenate(delta, axis=1)
        line_q, line_g = (message[pl.ds(part * two, two), :] for part in range(2))
        scores = []
        for slot in range(2):
            row = flag_row(tok, slot, at, own_flags, par_flags, False)
            scores.append(dot(tiles[slot][rows_at(0, tok), :], line_q, ROWS_T) * scale + (row - 1.0) * 1e30)
        tops = [jnp.maximum(*(jnp.max(block, axis=0, keepdims=True) for block in scores))]
        for slot in range(2):
            weights = jnp.exp(scores[slot] - tops[0])
            grads = dot(tiles[slot][rows_at(1, tok), :], line_g, ROWS_T) - delta
            kept = rows_at(slot, tok)
            e_ref[kept, :] = weights.astype(bf16)
            ds_ref[kept, :] = (weights * grads * scale).astype(bf16)
        for which in range(sides):
            ref = far_part(message, which, tok)
            y_rising, y_at = pair(y, which)
            flags = ref[pl.ds(2 * tok, 16), :].astype(f32)
            row = far_row(tok, which, jnp.where(y_rising, at(flags, 0), at(flags, 2)))
            bias = jnp.where(within(y_at, chips), (row - 1.0) * 1e30, -1e30)
            key, value = (pick(near, which, *(tile[rows_at(i, tok), :] for tile in tiles)) for i in range(2))
            far_q, far_g = (foreign_rows(ref, part, which, tok) for part in range(2))
            block = dot(key, far_q, ROWS_T) * scale + bias
            top = jnp.max(block, axis=0, keepdims=True)
            tops.append(to_lanes(which, tok, top, -1e30))
            weights = jnp.exp(block - top)
            grads = dot(value, far_g, ROWS_T) - foreign_delta(ref, tok)
            kept = rows_at(which, tok)
            e_far[kept, :] = weights.astype(bf16)
            ds_far[kept, :] = (weights * grads * scale).astype(bf16)
        top_ref[...] = jnp.concatenate(tops + [jnp.zeros((7 - sides, two), f32)], axis=0)

    pl.when(line_place(z, line, heights)[0])(work)


def times(block, factor):
    column = jnp.broadcast_to(factor, (block.shape[1], factor.shape[1])).T
    return (block.astype(jnp.float32) * column).astype(jnp.bfloat16)


def key_sums(tok, near, line, e_ref, ds_ref, scaled, far, slots=(0, 1)):
    rows = [rows_at(2 * line + slot, tok) for slot in slots]
    sums = [[dot(ref[at, :], scaled[i]) for i, ref in enumerate((ds_ref, e_ref))] for at in rows]
    for which, (e_far, ds_far, at, far_scaled) in enumerate(far):
        for i, ref in enumerate((ds_far, e_far)):
            block = dot(ref[at, :], far_scaled[i])
            for at_slot, slot in enumerate(slots):
                mine = near == ((slot == 0) == (which == 0))
                sums[at_slot][i] = sums[at_slot][i] + jnp.where(mine, block, 0.0)
    return sums


def stay_kernel(tok, chips, sides, q_all, g_all, e_ref, ds_ref, e_far, ds_far, raw_dq, note, *refs):
    qg = (q_all, g_all)
    sent, foreign, (own_ref, dq_ref) = refs[:sides], refs[sides : 2 * sides], refs[2 * sides :]
    y, c, _ = place()
    near = border_is_own(y, c)
    width = qg[0].shape[1]
    factor = jnp.exp(sent[0][0:1, :] - note[0:1, :])
    dq_ref[...] = (raw_dq[...] * factor).T
    far = []
    for which in range(sides):
        _, y_at = pair(y, which)
        lanes = foreign_lanes(which, tok, width)
        far_factor = jnp.exp(sent[which][2:3, lanes] - note[1 + which : 2 + which, lanes])
        far_factor = jnp.where(within(y_at, chips), far_factor, 0.0)
        scaled = [times(foreign_rows(foreign[which], part, which, tok), far_factor) for part in range(2)]
        far.append((e_far, ds_far, rows_at(which, tok), scaled))
    sums = key_sums(tok, near, 0, e_ref, ds_ref, [times(qg[part][...], factor) for part in range(2)], far)
    for slot in range(2):
        for i in range(2):
            own_ref[i, rows_at(slot, tok), :] = sums[slot][i]


def line_sums(tok, heights, sides, line, slot, sums, message, note, e_ref, ds_ref, e_far, ds_far, top_ref):
    y, c, z = place()
    near = border_is_own(y, c)

    def work():
        factor = jnp.exp(top_ref[0:1, :] - note[0:1, :])
        scaled = [times(message[pl.ds(part * 2 * tok, 2 * tok), :], factor) for part in range(2)]
        far = []
        for which in range(sides):
            lanes, at = foreign_lanes(which, tok, message.shape[1]), 1 + which
            far_factor = jnp.exp(top_ref[at : at + 1, lanes] - note[at : at + 1, lanes])
            rows = [foreign_rows(far_part(message, which, tok), part, which, tok) for part in range(2)]
            far.append((e_far, ds_far, rows_at(which, tok), [times(block, far_factor) for block in rows]))
        more = key_sums(tok, near, 0, e_ref, ds_ref, scaled, far, (slot,))
        for i in range(2):
            sums[i] += more[0][i]

    pl.when(line_place(z, line, heights)[0])(work)


def join_kernel(tok, heights, sides, line, own_ref, message, note, *refs):
    *terms, sums = refs
    sums[...] = own_ref[:, rows_at(1, tok), :]
    line_sums(tok, heights, sides, line, 1, sums, message, note, *terms)


def own_kernel(tok, heights, sides, own_ref, *refs):
    *refs, mine_ref, sums = refs
    sums[...] = own_ref[:, rows_at(0, tok), :]
    for i, line in enumerate((2, 1)):
        line_sums(tok, heights, sides, line, 0, sums, *refs[7 * i : 7 * i + 7])
    mine_ref[...] = sums[...].astype(jnp.bfloat16)


def leave_kernel(tok, chips, heights, sides, line, own_ref, dq_ref, note, message, note_in, *refs):
    terms, refs = refs[:5], refs[5:]
    came, backs, (mine_q_ref, swap_ref, sums) = refs[:sides], refs[sides : 2 * sides], refs[2 * sides :]
    y, c, _ = place()
    near = border_is_own(y, c)
    f32, bf16 = jnp.float32, jnp.bfloat16
    width = dq_ref.shape[1]
    sums[...] = own_ref[...]
    line_sums(tok, heights, sides, line, 1, sums, message, note_in, *terms)
    for i in range(2):
        swap_ref[i] = sums[i].astype(bf16)
    tiles = []
    for tile in range(2):
        value = dq_ref[rows_at(tile, tok), :]
        if tile < sides:
            _, y_at = pair(y, tile)
            lanes = foreign_lanes(tile, tok, width)
            factor = jnp.exp(came[tile][2:3, lanes] - note[0:1, lanes])
            column = border_rows(tile, tok, jnp.broadcast_to(factor, (width, 2 * width)).T)
            value = value + jnp.where(within(y_at, chips), backs[tile][...].astype(f32) * column, 0.0)
        tiles.append(value.astype(bf16))
    mine_q_ref[...] = jnp.where(near, tiles[0], tiles[1])
    swap_ref[2] = jnp.where(near, tiles[1], tiles[0])


def final_kernel(mine_ref, swap_ref, mine_q_ref, gq_ref, gk_ref, gv_ref):
    head = head_at()
    gq_ref[0, 0, head, 0] = mine_q_ref[...]
    gq_ref[0, 0, 1 - head, 0] = swap_ref[2]
    for i, ref in enumerate((gk_ref, gv_ref)):
        ref[0, 0, head, 0] = mine_ref[i]
        ref[0, 0, 1 - head, 0] = swap_ref[i]


def body(queries, keys, values, grad_out, attn_out, window_mask):
    tok, width = queries.shape[-2:]
    scale = width ** -0.5
    times, heights = lax.axis_size("tm"), lax.axis_size("height")
    chips = times // 2
    sides = 1 if chips == 2 else 2
    bf16, f32 = jnp.bfloat16, jnp.float32

    def call(kernel, shapes, specs, scratch=(), cost=0):
        return pl.pallas_call(
            kernel,
            out_shape=[jax.ShapeDtypeStruct(*shape) for shape in shapes],
            in_specs=list(specs),
            out_specs=[VMEM] * len(shapes),
            scratch_shapes=list(scratch),
            compiler_params=LIMIT,
            cost_estimate=pl.CostEstimate(flops=cost * 10**9, bytes_accessed=0, transcendentals=0) if cost else None,
        )

    def partner(index, which, size):
        if which is None:
            return index
        at = index + 1 if index % 2 == which else index - 1
        return at if 0 <= at < size else None

    def exchange(block, y_which, z_which):
        pairs = []
        for t in range(times):
            for z in range(heights):
                y_at, z_at = partner(t // 2, y_which, chips), partner(z, z_which, heights)
                at = t * heights + z
                alone = y_at is None or z_at is None
                pairs.append((at, (t ^ 1) * heights + z if alone else (2 * y_at + 1 - t % 2) * heights + z_at))
        return lax.ppermute(block, ("tm", "height"), pairs)

    def swap_cores(block):
        return lax.ppermute(block, "tm", [(t, t ^ 1) for t in range(times)])

    line_shape, tile_shape = ((2, 2 * tok, width), bf16), ((2, tok, width), bf16)
    extra = 64
    arguments = (keys, values, queries, grad_out, attn_out, window_mask)
    kv, rest, other = call(
        functools.partial(pack_kernel, tok),
        [((2 * tok + extra, width), bf16), ((3 * tok + 16, width), bf16), ((5 * tok + 16, width), bf16)],
        [HBM] * 6,
        [pltpu.SMEM(window_mask.shape, jnp.int32), pltpu.SemaphoreType.DMA((11,))],
    )(*(pltpu.with_memory_space_constraint(x, pltpu.HBM) for x in arguments))
    early = [exchange(kv, None, which) for which in (1, 0)]
    par = swap_cores(other)
    border_shape, two = ((2 * tok + 48, width), bf16), 2 * tok
    par_kv, *borders = call(
        functools.partial(line_kernel, tok), [((2 * tok + 32, width), bf16)] + [border_shape] * sides, [VMEM] * 2
    )(rest, par)
    foreign = [exchange(borders[which], which, None) for which in range(sides)]
    late = [exchange(par_kv, None, which) for which in (1, 0)]
    tiles = (kv, par_kv, late[0], early[0], late[1], early[1])
    note_shape, raw_shape = ((8, two), f32), ((width, two), f32)

    def square(count, kind=f32):
        return ((count * tok, two), kind)

    def far_square(kind=f32):
        return ((3 * sides * tok, 2 * width), kind)

    q_all, g_all, table, s_own, d_own = call(
        functools.partial(first_kernel, tok, heights, scale),
        [((two, width), bf16)] * 2 + [note_shape, square(2), square(2)],
        [VMEM] * 4,
    )(kv, par_kv, rest, par)
    qg = (q_all, g_all)
    (message,) = call(
        functools.partial(message_kernel, tok),
        [((4 * tok + sides * (2 * tok + 16), width), bf16)],
        [VMEM] * (2 + sides),
    )(*qg, *foreign)
    queries_in = [exchange(message, None, which) for which in (1, 0)]
    s_early, d_early, part = call(
        functools.partial(early_kernel, tok, scale), [square(2), square(2), note_shape], [VMEM] * 7
    )(*qg, table, s_own, *early, message)
    s_late, s_far, *sent = call(
        functools.partial(score_kernel, tok, chips, heights, sides, scale),
        [square(2), far_square()] + [note_shape] * sides,
        [VMEM] * (10 + sides),
    )(*qg, table, part, *foreign, *tiles)
    came = [exchange(sent[which], which, None) for which in range(sides)]
    far_tile = ((sides * tok, 2 * width), bf16)
    e, ds, e_far, ds_far, raw_dq, *shares = call(
        functools.partial(middle_kernel, tok, sides, scale),
        [square(2, bf16)] * 2 + [far_tile] * 2 + [raw_shape] + [((tok, width), bf16)] * sides,
        [VMEM] * (15 + 2 * sides),
        cost=20,
    )(*qg, table, s_own, d_own, s_early, d_early, s_late, s_far, *tiles, *foreign, *sent)
    (note,) = call(functools.partial(total_kernel, tok, chips, sides), [note_shape], [VMEM] * (2 * sides))(*sent, *came)
    notes = [exchange(note, None, which) for which in (1, 0)]
    shares = [exchange(share, which, None) for which, share in enumerate(shares)]
    sums_shape = ((2, two, width), f32)

    def line_terms(line, *earlier):
        return call(
            functools.partial(line_query_kernel, tok, chips, heights, sides, scale, line),
            [square(2, bf16)] * 2 + [far_tile] * 2 + [note_shape],
            [VMEM] * (4 + len(earlier)),
            cost=20,
        )(kv, par_kv, queries_in[line - 1], late[line - 1], *earlier)

    own, dq = call(
        functools.partial(stay_kernel, tok, chips, sides),
        [sums_shape, ((two, width), f32)],
        [VMEM] * (8 + 2 * sides),
    )(*qg, e, ds, e_far, ds_far, raw_dq, note, *sent, *foreign)
    part_shape = ((2, tok, width), f32)
    even_terms = line_terms(2)
    (joined,) = call(
        functools.partial(join_kernel, tok, heights, sides, 2), [part_shape], [VMEM] * 8
    )(own, queries_in[1], notes[1], *even_terms)
    odd_terms = line_terms(1, joined)
    mine_q, leaving = call(
        functools.partial(leave_kernel, tok, chips, heights, sides, 1),
        [((tok, width), bf16), ((3, tok, width), bf16)],
        [VMEM] * (10 + 2 * sides),
        [pltpu.VMEM(*part_shape)],
    )(joined, dq, note, queries_in[0], notes[0], *odd_terms, *came, *shares)
    (mine,) = call(
        functools.partial(own_kernel, tok, heights, sides),
        [tile_shape],
        [VMEM] * 15,
        [pltpu.VMEM(*part_shape)],
        cost=20,
    )(own, queries_in[1], notes[1], *even_terms, queries_in[0], notes[0], *odd_terms)
    return call(final_kernel, [(queries.shape, bf16)] * 3, [VMEM] * 3)(mine, swap_cores(leaving), mine_q)


def solution(mesh):
    placed = P("tm", "height", "dp", None, None, None)
    return jax.shard_map(
        body,
        mesh=mesh,
        in_specs=(placed,) * 5 + (P("tm", "height", None, None),),
        out_specs=(placed,) * 3,
        check_vma=False,
    )
```

```python
import functools

import jax
import jax.numpy as jnp
from jax import lax
from jax.experimental import pallas as pl
from jax.experimental.pallas import tpu as pltpu
from jax.sharding import PartitionSpec as P

VMEM = pl.BlockSpec(memory_space=pltpu.VMEM)
HBM = pl.BlockSpec(memory_space=pltpu.HBM)
LIMIT = pltpu.CompilerParams(vmem_limit_bytes=32 * 1024 * 1024)
ROWS_T = (((1,), (1,)), ((), ()))
COLS_T = (((0,), (0,)), ((), ()))


def dot(a, b, dims=(((1,), (0,)), ((), ()))):
    return lax.dot_general(a, b, dims, preferred_element_type=jnp.float32)


LATE, EARLY = 0, 1


def place():
    t = lax.axis_index("tm")
    return t // 2, t % 2, lax.axis_index("height")


def head_at():
    y, c, z = place()
    return (c + y + z) % 2


def pair(index, which):
    rising = (index % 2) == (0 if which == 0 else 1)
    return rising, jnp.where(rising, index + 1, index - 1)


def within(index, size):
    return (index >= 0) & (index < size)


def pack_kernel(tok, k_ref, v_ref, q_ref, g_ref, o_ref, mask_ref, kv_ref, rest_ref, other_ref, flags, sems):
    head = head_at()
    copies = [pltpu.make_async_copy(mask_ref, flags, sems.at[10])]
    for i, ref in enumerate((k_ref, v_ref, q_ref, g_ref, o_ref)):
        own = (kv_ref if i < 2 else rest_ref).at[pl.ds((i if i < 2 else i - 2) * tok, tok), :]
        copies.append(pltpu.make_async_copy(ref.at[0, 0, head, 0], own, sems.at[2 * i + 1]))
        copies.append(
            pltpu.make_async_copy(ref.at[0, 0, 1 - head, 0], other_ref.at[pl.ds(i * tok, tok), :], sems.at[2 * i])
        )
    for copy in copies:
        copy.start()
    copies[0].wait()
    row = lax.broadcasted_iota(jnp.int32, (16, rest_ref.shape[1]), 0)
    spread = jnp.zeros(row.shape, jnp.float32)
    for i in range(9):
        on = (flags[0, 0, 0, 9 * (i // 3) + 3 * (i % 3) + 1] != 0).astype(jnp.float32)
        spread = jnp.where(row == i, on, spread)
    rest_ref[pl.ds(3 * tok, 16), :] = spread.astype(jnp.bfloat16)
    other_ref[pl.ds(5 * tok, 16), :] = spread.astype(jnp.bfloat16)
    for copy in copies[1:]:
        copy.wait()


def rows_at(index, tok):
    return pl.ds(index * tok, tok)


def border_is_own(y, c):
    rising, _ = pair(y, 0)
    return (c == 1) == rising


def pick(near, which, own, par):
    return jnp.where(near, own, par) if which == 0 else jnp.where(near, par, own)


def three_terms(row):
    terms = []
    for _ in range(3):
        terms.append(row.astype(jnp.bfloat16).astype(jnp.float32))
        row = row - terms[-1]
    return terms


def line_kernel(tok, rest_ref, par_ref, par_kv_ref, *border_refs):
    y, c, _ = place()
    near = border_is_own(y, c)
    for i in range(2):
        par_kv_ref[rows_at(i, tok), :] = par_ref[rows_at(i, tok), :]
    width = par_ref.shape[1]
    f32 = jnp.float32
    q, g, o = (
        [pick(near, which, rest_ref[rows_at(i, tok), :], par_ref[rows_at(i + 2, tok), :]) for which in range(2)]
        for i in range(3)
    )
    own_flags, par_flags = rest_ref[pl.ds(3 * tok, 16), :].astype(f32), par_ref[pl.ds(5 * tok, 16), :].astype(f32)
    flags = [pick(near, which, own_flags, par_flags)[0:9] for which in range(2)]
    product = jnp.concatenate(g, axis=0).astype(f32) * jnp.concatenate(o, axis=0).astype(f32)
    terms = [
        [term[:, start : start + width] for start in range(0, 2 * tok, width)]
        for term in three_terms(jnp.sum(product.T, axis=0, keepdims=True))
    ]
    for which, ref in enumerate(border_refs):
        ref[rows_at(0, tok), :], ref[rows_at(1, tok), :] = q[which], g[which]
        part = slice(0, 2) if which == 0 else slice(len(terms[0]) - 2, None)
        lines = [flags[which]] + [row for term in terms for row in term[part]] + [jnp.zeros((1, width), f32)]
        ref[pl.ds(2 * tok, 16), :] = jnp.concatenate(lines, axis=0).astype(jnp.bfloat16)
    lines = flags + [row for term in terms for row in term] + [jnp.zeros((5, width), f32)]
    par_kv_ref[pl.ds(2 * tok, 32), :] = jnp.concatenate(lines, axis=0).astype(jnp.bfloat16)


def foreign_delta(ref, tok):
    terms = ref[pl.ds(2 * tok, 16), :].astype(jnp.float32)
    return jnp.concatenate(
        [sum(terms[9 + 2 * i + half : 10 + 2 * i + half] for i in range(3)) for half in range(2)], axis=1
    )


def line_place(z, line, heights):
    if line == 0:
        return True, lambda flags, dt: flags[3 * dt + 1 : 3 * dt + 2]
    rising, at = pair(z, 2 - line)
    return within(at, heights), lambda flags, dt: jnp.where(
        rising, flags[3 * dt + 2 : 3 * dt + 3], flags[3 * dt : 3 * dt + 1]
    )


def lanes_of(tok, border, other):
    width = border.shape[1]
    lane = lax.broadcasted_iota(jnp.int32, (1, width), 1)
    return jnp.concatenate(
        [jnp.where(lane + start < tok, border, other) for start in range(0, 2 * tok, width)], axis=1
    )


def flag_row(tok, slot, at, own_flags, par_flags, own_query):
    y, c, _ = place()
    first, near = c == 0, border_is_own(y, c)
    if slot == 0:
        own, par = at(own_flags, 1), jnp.where(first, at(par_flags, 0), at(par_flags, 2))
    else:
        own, par = jnp.where(first, at(own_flags, 2), at(own_flags, 0)), at(par_flags, 1)
    if own_query:
        centre = jnp.ones_like(own)
        own, par = (centre, par) if slot == 0 else (own, centre)
    return lanes_of(tok, pick(near, 0, own, par), pick(near, 1, own, par))


def first_kernel(tok, heights, scale, kv_ref, par_kv_ref, rest_ref, par_ref, q_all, g_all, table, s_ref, d_ref):
    qg = (q_all, g_all)
    y, c, z = place()
    two = 2 * tok
    width = rest_ref.shape[1]
    f32 = jnp.float32
    near = border_is_own(y, c)
    out = []
    for part in range(3):
        own, par = rest_ref[rows_at(part, tok), :], par_ref[rows_at(part + 2, tok), :]
        tiles = [pick(near, which, own, par) for which in range(2)]
        if part == 2:
            out = jnp.concatenate(tiles, axis=0)
        else:
            for which in range(2):
                qg[part][rows_at(which, tok), :] = tiles[which]
    delta = jnp.sum((qg[1][...].astype(f32) * out.astype(f32)).T, axis=0, keepdims=True)

    own_flags = rest_ref[pl.ds(3 * tok, 16), :].astype(f32)
    par_flags = par_ref[pl.ds(5 * tok, 16), :].astype(f32)
    lines = []
    for line in range(3):
        inside, at = line_place(z, line, heights)
        for slot in range(2):
            row = flag_row(tok, slot, at, own_flags, par_flags, line == 0)
            lines.append(jnp.where(inside, (row - 1.0) * 1e30, -1e30))
    table[...] = jnp.concatenate(lines + [delta, jnp.zeros((1, two), f32)], axis=0)
    for i, source in enumerate((kv_ref, par_kv_ref)):
        rows = rows_at(i, tok)
        s_ref[rows, :] = dot(source[rows_at(0, tok), :], qg[0][...], ROWS_T) * scale + table[i : i + 1, :]
        d_ref[rows, :] = dot(source[rows_at(1, tok), :], qg[1][...], ROWS_T) - table[6:7, :]


def largest(tok, blocks):
    lanes = blocks[0][0].shape[1]
    top = jnp.full((8, lanes), -1e30, jnp.float32)
    for ref, i in blocks:
        top = jnp.maximum(top, jnp.max(ref[rows_at(i, tok), :].reshape(tok // 8, 8, lanes), axis=0))
    return jnp.max(top, axis=0, keepdims=True)


def summed(tok, blocks, top):
    lanes = blocks[0][0].shape[1]
    total = jnp.zeros((8, lanes), jnp.float32)
    for ref, i in blocks:
        weights = jnp.exp(ref[rows_at(i, tok), :] - top)
        total = total + jnp.sum(weights.reshape(tok // 8, 8, lanes), axis=0)
    return jnp.sum(total, axis=0, keepdims=True)


def early_kernel(tok, scale, q_all, g_all, table, s_own, one_ref, two_ref, s_ref, d_ref, part_ref):
    qg = (q_all, g_all)
    for i, source in enumerate((one_ref, two_ref)):
        rows = rows_at(i, tok)
        s_ref[rows, :] = dot(source[rows_at(0, tok), :], qg[0][...], ROWS_T) * scale + table[2 + 2 * i + EARLY : 3 + 2 * i + EARLY, :]
        d_ref[rows, :] = dot(source[rows_at(1, tok), :], qg[1][...], ROWS_T) - table[6:7, :]
    blocks = [(ref, i) for ref in (s_own, s_ref) for i in range(2)]
    top = largest(tok, blocks)
    total = summed(tok, blocks, top)
    part_ref[...] = jnp.concatenate([top, total, jnp.zeros((6, 2 * tok), jnp.float32)], axis=0)


def foreign_rows(ref, part, which, tok):
    block = ref[rows_at(part, tok), :]
    gap = jnp.zeros((2 * block.shape[1] - tok, block.shape[1]), block.dtype)
    return jnp.concatenate([block, gap] if which == 0 else [gap, block], axis=0)


def foreign_lanes(which, tok, width):
    return slice(0, 2 * width) if which == 0 else slice(2 * tok - 2 * width, 2 * tok)


def far_row(tok, which, row):
    lane, width = lax.broadcasted_iota(jnp.int32, row.shape, 1), row.shape[1]
    return jnp.concatenate(
        [
            jnp.where(lane + start < tok if which == 0 else lane + start >= 2 * width - tok, row, 0.0)
            for start in (0, width)
        ],
        axis=1,
    )


def to_lanes(which, tok, row, fill):
    gap = jnp.full((1, 2 * tok - row.shape[1]), fill, jnp.float32)
    return jnp.concatenate([row, gap] if which == 0 else [gap, row], axis=1)


def score_kernel(tok, chips, heights, sides, scale, q_all, g_all, table, part, *refs):
    qg = (q_all, g_all)
    foreign, keys, refs = refs[:sides], refs[sides : 6 + sides], refs[6 + sides :]
    s_late, s_far, *notes = refs
    y, c, z = place()
    near = border_is_own(y, c)
    two = 2 * tok
    f32 = jnp.float32
    far = []
    for which in range(sides):
        rising, y_at = pair(y, which)
        flags = foreign[which][pl.ds(2 * tok, 16), :].astype(f32)
        queries = foreign_rows(foreign[which], 0, which, tok)
        for line in range(3):
            inside, at = line_place(z, line, heights)
            row = far_row(tok, which, jnp.where(rising, at(flags, 0), at(flags, 2)))
            bias = jnp.where(inside & within(y_at, chips), (row - 1.0) * 1e30, -1e30)
            border = pick(near, which, keys[2 * line][rows_at(0, tok), :], keys[2 * line + 1][rows_at(0, tok), :])
            s_far[rows_at(3 * which + line, tok), :] = dot(border, queries, ROWS_T) * scale + bias
        blocks = [(s_far, 3 * which + line) for line in range(3)]
        top = largest(tok, blocks)
        far.append([to_lanes(which, tok, top, -1e30), to_lanes(which, tok, summed(tok, blocks, top), 0.0)])
    for i in range(2):
        at = 2 + 2 * i + LATE
        scores = dot(keys[at][rows_at(0, tok), :], qg[0][...], ROWS_T) * scale
        s_late[rows_at(i, tok), :] = scores + table[at : at + 1, :]
    blocks = [(s_late, i) for i in range(2)]
    top = jnp.maximum(part[0:1, :], largest(tok, blocks))
    total = part[1:2, :] * jnp.exp(part[0:1, :] - top) + summed(tok, blocks, top)
    for which in range(sides):
        notes[which][...] = jnp.concatenate([top, total] + far[which] + [jnp.zeros((4, two), f32)], axis=0)


def middle_kernel(tok, sides, scale, q_all, g_all, table, s_own, d_own, s_early, d_early, s_late, s_far, *refs):
    qg = (q_all, g_all)
    tiles, foreign, sent = refs[:6], refs[6 : 6 + sides], refs[6 + sides : 6 + 2 * sides]
    e_ref, ds_ref, e_far, ds_far, dq_ref, *shares = refs[6 + 2 * sides :]
    y, c, _ = place()
    near = border_is_own(y, c)
    bf16 = jnp.bfloat16

    total, far_total = 0.0, [0.0] * sides
    for line in range(3):
        dq = 0.0
        for slot in range(2):
            i, at = 2 * line + slot, rows_at(line - 1 if line else slot, tok)
            scores = s_own if line == 0 else s_early if slot == EARLY else s_late
            weights = jnp.exp(scores[at, :] - sent[0][0:1, :])
            if line and slot == LATE:
                grads = dot(tiles[i][rows_at(1, tok), :], qg[1][...], ROWS_T) - table[6:7, :]
            else:
                grads = (d_early if line else d_own)[at, :]
            low = (weights * grads * scale).astype(bf16)
            if line == 0:
                e_ref[rows_at(i, tok), :] = weights.astype(bf16)
                ds_ref[rows_at(i, tok), :] = low
            dq = dq + dot(tiles[i][rows_at(0, tok), :], low, COLS_T)
        total = total + dq
        for which in range(sides):
            far_g = foreign_rows(foreign[which], 1, which, tok)
            delta = foreign_delta(foreign[which], tok)
            lanes = foreign_lanes(which, tok, qg[0].shape[1])
            rows = rows_at(3 * which + line, tok)
            own, par = tiles[2 * line], tiles[2 * line + 1]
            key, value = (pick(near, which, own[rows_at(i, tok), :], par[rows_at(i, tok), :]) for i in range(2))
            weights = jnp.exp(s_far[rows, :] - sent[which][2:3, lanes])
            low = (weights * (dot(value, far_g, ROWS_T) - delta) * scale).astype(bf16)
            if line == 0:
                e_far[rows_at(which, tok), :] = weights.astype(bf16)
                ds_far[rows_at(which, tok), :] = low
            far_total[which] = far_total[which] + dot(key, low, COLS_T)

    dq_ref[...] = total
    for which in range(sides):
        shares[which][...] = border_rows(which, tok, far_total[which].T).astype(bf16)


def border_rows(which, tok, block):
    return block[:tok] if which == 0 else block[block.shape[0] - tok :]


def message_kernel(tok, q_all, g_all, *refs):
    *foreign, out_ref = refs
    out_ref[pl.ds(0, 2 * tok), :] = q_all[...]
    out_ref[pl.ds(2 * tok, 2 * tok), :] = g_all[...]
    for which, ref in enumerate(foreign):
        far_part(out_ref, which, tok)[...] = ref[pl.ds(0, 2 * tok + 16), :]


def far_part(ref, which, tok):
    return ref.at[pl.ds(4 * tok + which * (2 * tok + 16), 2 * tok + 16), :]


def total_kernel(tok, chips, sides, *refs):
    sent, came, note_ref = refs[:sides], refs[sides : 2 * sides], refs[2 * sides]
    y, _, _ = place()

    def log_total(top, total, other_top, other_total):
        both = jnp.maximum(top, other_top)
        return both + jnp.log(total * jnp.exp(top - both) + other_total * jnp.exp(other_top - both))

    lse, far_rows = None, []
    for which in range(sides):
        _, y_at = pair(y, which)
        inside = within(y_at, chips)
        note = came[which]
        far_lse = log_total(note[0:1, :], note[1:2, :], sent[which][2:3, :], sent[which][3:4, :])
        far_rows.append(jnp.where(inside, far_lse, 0.0))
        other = jnp.where(inside, note[2:3, :], -1e30), jnp.where(inside, note[3:4, :], 0.0)
        if which == 0:
            lse = log_total(sent[0][0:1, :], sent[0][1:2, :], *other)
        else:
            lse = log_total(lse, jnp.ones_like(lse), *other)
    rows = [lse] + far_rows
    note_ref[...] = jnp.concatenate(rows + [jnp.zeros((8 - len(rows), 2 * tok), jnp.float32)], axis=0)


def line_query_kernel(tok, chips, heights, sides, scale, line, kv_ref, par_kv_ref, message, extras, *outs):
    e_ref, ds_ref, e_far, ds_far, top_ref = outs[-5:]
    y, c, z = place()
    near = border_is_own(y, c)
    two = 2 * tok
    width = kv_ref.shape[1]
    f32, bf16 = jnp.float32, jnp.bfloat16
    tiles = (kv_ref, par_kv_ref)

    def work():
        rising, _ = pair(z, 2 - line)

        def at(flags, dt):
            return jnp.where(rising, flags[3 * dt : 3 * dt + 1], flags[3 * dt + 2 : 3 * dt + 3])

        rows = extras[pl.ds(2 * tok, 32), :].astype(f32)
        own_flags, par_flags = (pick(near, which, rows[0:9], rows[9:18]) for which in range(2))
        delta = [sum(rows[18 + 3 * i + part : 19 + 3 * i + part] for i in range(3)) for part in range(two // width)]
        delta = jnp.concatenate(delta, axis=1)
        line_q, line_g = (message[pl.ds(part * two, two), :] for part in range(2))
        scores = []
        for slot in range(2):
            row = flag_row(tok, slot, at, own_flags, par_flags, False)
            scores.append(dot(tiles[slot][rows_at(0, tok), :], line_q, ROWS_T) * scale + (row - 1.0) * 1e30)
        tops = [jnp.maximum(*(jnp.max(block, axis=0, keepdims=True) for block in scores))]
        for slot in range(2):
            weights = jnp.exp(scores[slot] - tops[0])
            grads = dot(tiles[slot][rows_at(1, tok), :], line_g, ROWS_T) - delta
            kept = rows_at(slot, tok)
            e_ref[kept, :] = weights.astype(bf16)
            ds_ref[kept, :] = (weights * grads * scale).astype(bf16)
        for which in range(sides):
            ref = far_part(message, which, tok)
            y_rising, y_at = pair(y, which)
            flags = ref[pl.ds(2 * tok, 16), :].astype(f32)
            row = far_row(tok, which, jnp.where(y_rising, at(flags, 0), at(flags, 2)))
            bias = jnp.where(within(y_at, chips), (row - 1.0) * 1e30, -1e30)
            key, value = (pick(near, which, *(tile[rows_at(i, tok), :] for tile in tiles)) for i in range(2))
            far_q, far_g = (foreign_rows(ref, part, which, tok) for part in range(2))
            block = dot(key, far_q, ROWS_T) * scale + bias
            top = jnp.max(block, axis=0, keepdims=True)
            tops.append(to_lanes(which, tok, top, -1e30))
            weights = jnp.exp(block - top)
            grads = dot(value, far_g, ROWS_T) - foreign_delta(ref, tok)
            kept = rows_at(which, tok)
            e_far[kept, :] = weights.astype(bf16)
            ds_far[kept, :] = (weights * grads * scale).astype(bf16)
        top_ref[...] = jnp.concatenate(tops + [jnp.zeros((7 - sides, two), f32)], axis=0)

    pl.when(line_place(z, line, heights)[0])(work)


def times(block, factor):
    column = jnp.broadcast_to(factor, (block.shape[1], factor.shape[1])).T
    return (block.astype(jnp.float32) * column).astype(jnp.bfloat16)


def key_sums(tok, near, line, e_ref, ds_ref, scaled, far, slots=(0, 1)):
    rows = [rows_at(2 * line + slot, tok) for slot in slots]
    sums = [[dot(ref[at, :], scaled[i]) for i, ref in enumerate((ds_ref, e_ref))] for at in rows]
    for which, (e_far, ds_far, at, far_scaled) in enumerate(far):
        for i, ref in enumerate((ds_far, e_far)):
            block = dot(ref[at, :], far_scaled[i])
            for at_slot, slot in enumerate(slots):
                mine = near == ((slot == 0) == (which == 0))
                sums[at_slot][i] = sums[at_slot][i] + jnp.where(mine, block, 0.0)
    return sums


def stay_kernel(tok, chips, sides, q_all, g_all, e_ref, ds_ref, e_far, ds_far, raw_dq, note, *refs):
    qg = (q_all, g_all)
    sent, foreign, (own_ref, dq_ref) = refs[:sides], refs[sides : 2 * sides], refs[2 * sides :]
    y, c, _ = place()
    near = border_is_own(y, c)
    width = qg[0].shape[1]
    factor = jnp.exp(sent[0][0:1, :] - note[0:1, :])
    dq_ref[...] = (raw_dq[...] * factor).T
    far = []
    for which in range(sides):
        _, y_at = pair(y, which)
        lanes = foreign_lanes(which, tok, width)
        far_factor = jnp.exp(sent[which][2:3, lanes] - note[1 + which : 2 + which, lanes])
        far_factor = jnp.where(within(y_at, chips), far_factor, 0.0)
        scaled = [times(foreign_rows(foreign[which], part, which, tok), far_factor) for part in range(2)]
        far.append((e_far, ds_far, rows_at(which, tok), scaled))
    sums = key_sums(tok, near, 0, e_ref, ds_ref, [times(qg[part][...], factor) for part in range(2)], far)
    for slot in range(2):
        for i in range(2):
            own_ref[i, rows_at(slot, tok), :] = sums[slot][i]


def line_sums(tok, heights, sides, line, slot, sums, message, note, e_ref, ds_ref, e_far, ds_far, top_ref):
    y, c, z = place()
    near = border_is_own(y, c)

    def work():
        factor = jnp.exp(top_ref[0:1, :] - note[0:1, :])
        scaled = [times(message[pl.ds(part * 2 * tok, 2 * tok), :], factor) for part in range(2)]
        far = []
        for which in range(sides):
            lanes, at = foreign_lanes(which, tok, message.shape[1]), 1 + which
            far_factor = jnp.exp(top_ref[at : at + 1, lanes] - note[at : at + 1, lanes])
            rows = [foreign_rows(far_part(message, which, tok), part, which, tok) for part in range(2)]
            far.append((e_far, ds_far, rows_at(which, tok), [times(block, far_factor) for block in rows]))
        more = key_sums(tok, near, 0, e_ref, ds_ref, scaled, far, (slot,))
        for i in range(2):
            sums[i] += more[0][i]

    pl.when(line_place(z, line, heights)[0])(work)


def join_kernel(tok, heights, sides, line, own_ref, message, note, *refs):
    *terms, sums = refs
    sums[...] = own_ref[:, rows_at(1, tok), :]
    line_sums(tok, heights, sides, line, 1, sums, message, note, *terms)


def own_kernel(tok, heights, sides, own_ref, *refs):
    *refs, mine_ref, sums = refs
    sums[...] = own_ref[:, rows_at(0, tok), :]
    for i, line in enumerate((2, 1)):
        line_sums(tok, heights, sides, line, 0, sums, *refs[7 * i : 7 * i + 7])
    mine_ref[...] = sums[...].astype(jnp.bfloat16)


def leave_kernel(tok, chips, heights, sides, line, own_ref, dq_ref, note, message, note_in, *refs):
    terms, refs = refs[:5], refs[5:]
    came, backs, (mine_q_ref, swap_ref, sums) = refs[:sides], refs[sides : 2 * sides], refs[2 * sides :]
    y, c, _ = place()
    near = border_is_own(y, c)
    f32, bf16 = jnp.float32, jnp.bfloat16
    width = dq_ref.shape[1]
    sums[...] = own_ref[...]
    line_sums(tok, heights, sides, line, 1, sums, message, note_in, *terms)
    for i in range(2):
        swap_ref[i] = sums[i].astype(bf16)
    tiles = []
    for tile in range(2):
        value = dq_ref[rows_at(tile, tok), :]
        if tile < sides:
            _, y_at = pair(y, tile)
            lanes = foreign_lanes(tile, tok, width)
            factor = jnp.exp(came[tile][2:3, lanes] - note[0:1, lanes])
            column = border_rows(tile, tok, jnp.broadcast_to(factor, (width, 2 * width)).T)
            value = value + jnp.where(within(y_at, chips), backs[tile][...].astype(f32) * column, 0.0)
        tiles.append(value.astype(bf16))
    mine_q_ref[...] = jnp.where(near, tiles[0], tiles[1])
    swap_ref[2] = jnp.where(near, tiles[1], tiles[0])


def final_kernel(mine_ref, swap_ref, mine_q_ref, gq_ref, gk_ref, gv_ref):
    head = head_at()
    gq_ref[0, 0, head, 0] = mine_q_ref[...]
    gq_ref[0, 0, 1 - head, 0] = swap_ref[2]
    for i, ref in enumerate((gk_ref, gv_ref)):
        ref[0, 0, head, 0] = mine_ref[i]
        ref[0, 0, 1 - head, 0] = swap_ref[i]


def body(queries, keys, values, grad_out, attn_out, window_mask):
    tok, width = queries.shape[-2:]
    scale = width ** -0.5
    times, heights = lax.axis_size("tm"), lax.axis_size("height")
    chips = times // 2
    sides = 1 if chips == 2 else 2
    bf16, f32 = jnp.bfloat16, jnp.float32

    def call(kernel, shapes, specs, scratch=(), cost=0):
        return pl.pallas_call(
            kernel,
            out_shape=[jax.ShapeDtypeStruct(*shape) for shape in shapes],
            in_specs=list(specs),
            out_specs=[VMEM] * len(shapes),
            scratch_shapes=list(scratch),
            compiler_params=LIMIT,
            cost_estimate=pl.CostEstimate(flops=cost * 10**9, bytes_accessed=0, transcendentals=0) if cost else None,
        )

    def partner(index, which, size):
        if which is None:
            return index
        at = index + 1 if index % 2 == which else index - 1
        return at if 0 <= at < size else None

    def exchange(block, y_which, z_which):
        pairs = []
        for t in range(times):
            for z in range(heights):
                y_at, z_at = partner(t // 2, y_which, chips), partner(z, z_which, heights)
                at = t * heights + z
                alone = y_at is None or z_at is None
                pairs.append((at, (t ^ 1) * heights + z if alone else (2 * y_at + 1 - t % 2) * heights + z_at))
        return lax.ppermute(block, ("tm", "height"), pairs)

    def swap_cores(block):
        return lax.ppermute(block, "tm", [(t, t ^ 1) for t in range(times)])

    line_shape, tile_shape = ((2, 2 * tok, width), bf16), ((2, tok, width), bf16)
    extra = 56
    arguments = (keys, values, queries, grad_out, attn_out, window_mask)
    kv, rest, other = call(
        functools.partial(pack_kernel, tok),
        [((2 * tok + extra, width), bf16), ((3 * tok + 16, width), bf16), ((5 * tok + 16, width), bf16)],
        [HBM] * 6,
        [pltpu.SMEM(window_mask.shape, jnp.int32), pltpu.SemaphoreType.DMA((11,))],
    )(*(pltpu.with_memory_space_constraint(x, pltpu.HBM) for x in arguments))
    early = [exchange(kv, None, which) for which in (1, 0)]
    par = swap_cores(other)
    border_shape, two = ((2 * tok + 48, width), bf16), 2 * tok
    par_kv, *borders = call(
        functools.partial(line_kernel, tok), [((2 * tok + 32, width), bf16)] + [border_shape] * sides, [VMEM] * 2
    )(rest, par)
    foreign = [exchange(borders[which], which, None) for which in range(sides)]
    late = [exchange(par_kv, None, which) for which in (1, 0)]
    tiles = (kv, par_kv, late[0], early[0], late[1], early[1])
    note_shape, raw_shape = ((8, two), f32), ((width, two), f32)

    def square(count, kind=f32):
        return ((count * tok, two), kind)

    def far_square(kind=f32):
        return ((3 * sides * tok, 2 * width), kind)

    q_all, g_all, table, s_own, d_own = call(
        functools.partial(first_kernel, tok, heights, scale),
        [((two, width), bf16)] * 2 + [note_shape, square(2), square(2)],
        [VMEM] * 4,
    )(kv, par_kv, rest, par)
    qg = (q_all, g_all)
    (message,) = call(
        functools.partial(message_kernel, tok),
        [((4 * tok + sides * (2 * tok + 16), width), bf16)],
        [VMEM] * (2 + sides),
    )(*qg, *foreign)
    queries_in = [exchange(message, None, which) for which in (1, 0)]
    s_early, d_early, part = call(
        functools.partial(early_kernel, tok, scale), [square(2), square(2), note_shape], [VMEM] * 6
    )(*qg, table, s_own, *early)
    s_late, s_far, *sent = call(
        functools.partial(score_kernel, tok, chips, heights, sides, scale),
        [square(2), far_square()] + [note_shape] * sides,
        [VMEM] * (10 + sides),
    )(*qg, table, part, *foreign, *tiles)
    came = [exchange(sent[which], which, None) for which in range(sides)]
    far_tile = ((sides * tok, 2 * width), bf16)
    e, ds, e_far, ds_far, raw_dq, *shares = call(
        functools.partial(middle_kernel, tok, sides, scale),
        [square(2, bf16)] * 2 + [far_tile] * 2 + [raw_shape] + [((tok, width), bf16)] * sides,
        [VMEM] * (15 + 2 * sides),
        cost=20,
    )(*qg, table, s_own, d_own, s_early, d_early, s_late, s_far, *tiles, *foreign, *sent)
    (note,) = call(functools.partial(total_kernel, tok, chips, sides), [note_shape], [VMEM] * (2 * sides))(*sent, *came)
    notes = [exchange(note, None, which) for which in (1, 0)]
    shares = [exchange(share, which, None) for which, share in enumerate(shares)]
    sums_shape = ((2, two, width), f32)

    def line_terms(line, *earlier):
        return call(
            functools.partial(line_query_kernel, tok, chips, heights, sides, scale, line),
            [square(2, bf16)] * 2 + [far_tile] * 2 + [note_shape],
            [VMEM] * (4 + len(earlier)),
            cost=20,
        )(kv, par_kv, queries_in[line - 1], late[line - 1], *earlier)

    own, dq = call(
        functools.partial(stay_kernel, tok, chips, sides),
        [sums_shape, ((two, width), f32)],
        [VMEM] * (8 + 2 * sides),
    )(*qg, e, ds, e_far, ds_far, raw_dq, note, *sent, *foreign)
    part_shape = ((2, tok, width), f32)
    even_terms = line_terms(2)
    (joined,) = call(
        functools.partial(join_kernel, tok, heights, sides, 2), [part_shape], [VMEM] * 8
    )(own, queries_in[1], notes[1], *even_terms)
    odd_terms = line_terms(1, joined)
    mine_q, leaving = call(
        functools.partial(leave_kernel, tok, chips, heights, sides, 1),
        [((tok, width), bf16), ((3, tok, width), bf16)],
        [VMEM] * (10 + 2 * sides),
        [pltpu.VMEM(*part_shape)],
    )(joined, dq, note, queries_in[0], notes[0], *odd_terms, *came, *shares)
    (mine,) = call(
        functools.partial(own_kernel, tok, heights, sides),
        [tile_shape],
        [VMEM] * 15,
        [pltpu.VMEM(*part_shape)],
        cost=20,
    )(own, queries_in[1], notes[1], *even_terms, queries_in[0], notes[0], *odd_terms)
    return call(final_kernel, [(queries.shape, bf16)] * 3, [VMEM] * 3)(mine, swap_cores(leaving), mine_q)


def solution(mesh):
    placed = P("tm", "height", "dp", None, None, None)
    return jax.shard_map(
        body,
        mesh=mesh,
        in_specs=(placed,) * 5 + (P("tm", "height", None, None),),
        out_specs=(placed,) * 3,
        check_vma=False,
    )
```
